32 devices in a mesh: dp: 16 (over z, y, core), stream: 2 (over x).
Axes of the slice: x: 2, y: 2, z: 4, core: 2. Of those that a mesh axis runs over, the one named last changes fastest.
Arguments:
- patches: bfloat16 [32768, 768], P(('dp', 'stream')), may hold values from -6 to 6
- embedding: float32 [128, 768], P(('dp', 'stream')), may hold values from -6 to 6
- long_image: int32 [32], P(('dp', 'stream')), may hold values 0 or 1
- routes: int32 [32768, 2], P(('dp', 'stream')), may hold values from 0 to 7, all different within a row; in each aligned block of 1024 rows (0 to 1023, 1024 to 2047, ...) at most 288 rows name the same one
- cotangent: bfloat16 [32768, 768], P(('dp', 'stream')), may hold values from -6 to 6
- ada_weight: bfloat16 [768, 4608], replicated, may hold values from -0.4375 to 0.4375
- qkv_weight: bfloat16 [768, 2304], replicated, may hold values from -0.21875 to 0.21875
- out_weight: bfloat16 [768, 768], replicated, may hold values from -0.875 to 0.875
- shared_up: bfloat16 [768, 3072], replicated, may hold values from -0.21875 to 0.21875
- shared_down: bfloat16 [3072, 768], replicated, may hold values from -0.109375 to 0.109375
- router_weight: bfloat16 [768, 8], replicated, may hold values from -0.15625 to 0.15625
- expert_up: bfloat16 [8, 768, 3072], P('stream'), may hold values from -0.21875 to 0.21875
- expert_down: bfloat16 [8, 3072, 768], P('stream'), may hold values from -0.109375 to 0.109375
Outputs:
- mixed: bfloat16 [32768, 768], P(('dp', 'stream'))
- grad_patches: float32 [32768, 768], P(('dp', 'stream'))
- grad_embedding: float32 [128, 768], P(('dp', 'stream'))
- grad_ada: float32 [768, 4608], P('dp')
- grad_qkv: float32 [768, 2304], P('dp')
- grad_out_weight: float32 [768, 768], P('dp')
- grad_shared_up: float32 [768, 3072], P('dp')
- grad_shared_down: float32 [3072, 768], P('dp')
- grad_router: float32 [768, 8], P('dp')
- grad_expert_up: float32 [8, 768, 3072], P('stream', 'dp')
- grad_expert_down: float32 [8, 3072, 768], P('stream', 'dp')
The draws below stay inside these ranges and needn't reach their ends.
Inputs may be any that keep to these rules, and one draw needn't show every extreme that they name: `routes`: in the rows of one device (aligned blocks of 1024 rows) each expert is named by at most 288 rows; a row names two different experts. `long_image`: 1: the device's patches are one image; 0: they are images of 256 patches.
All inputs are finite; a program needn't handle non-finite values.
Results may differ from the reference program's by a relative error of at most 0.022.
The reference program's roundings to bfloat16 on the way count: a program that leaves them out, or rounds other values in their place, can miss the bound.
Values may be sent and summed in bfloat16 or wider, within the bound.
No kernel may reach another device: no remote copies, remote signals or barrier semaphores. Data moves between devices by JAX's collectives and lax.ppermute only.
A program may use at most 384 MiB of HBM per device.

```python
import math
import jax
import jax.numpy as jnp
import numpy as np
from jax import lax

D = 768
HEADS = 12
HEAD_DIM = 64
FF = 3072
EXPERTS = 8
SHORT = 256
CAP = 288
TOK_DEV = 1024
TOKENS = 32768
BLOCKS = 128
N_DP = 16
N_STREAM = 2
DEVICES = 32


def plant(entries, rng, least, largest):
    shape = entries.shape
    place = [jax.random.randint(jax.random.fold_in(rng, axis), (), 0, shape[axis]) for axis in range(len(shape))]
    entries = entries.at[tuple(place)].set(least)
    longest = shape.index(max(shape))
    place[longest] = (place[longest] + 1) % shape[longest]
    return entries.at[tuple(place)].set(largest)


def block_scale(key, shape, shards, least, largest):
    level = 1.0
    for axis_at, parts in shards:
        heights = jax.random.uniform(jax.random.fold_in(jax.random.fold_in(key, 6), axis_at), (parts,), jnp.float32, least / len(shards), largest / len(shards))
        level = level * jnp.repeat(jnp.exp(heights), shape[axis_at] // parts).reshape((-1,) + (1,) * (len(shape) - 1 - axis_at))
    return level


def deal_out(own_key, own, number, rows, amount, top, reach, lean):
    ranking = jax.random.permutation(own_key, amount)
    crowded, usual = load_shares(amount, rows * top, reach, lean, True), load_shares(amount, rows * top, reach, lean, False)
    places = jnp.arange(amount)

    def named(sizes, turn):
        used = int((sizes > 0).sum())
        fixed = max(1, used // 4)
        shifted = fixed + (places - fixed + turn * (used - fixed)) % max(1, amount - fixed)
        return jnp.zeros((amount,), jnp.int32).at[ranking[jnp.where(places < fixed, places, shifted)]].set(jnp.asarray(sizes, jnp.int32))

    sizes = jnp.where(number % 4 == 0, named(crowded, number // 4), named(usual, number - number // 4 - 1))
    mixed = jax.random.permutation(jax.random.fold_in(own, 3), amount)
    donor, sink = mixed[0:amount // 2 * 2:2], mixed[1:amount // 2 * 2:2]
    margin = jnp.minimum(sizes[donor] - 1, reach - sizes[sink]) // 2
    margin = jnp.where((donor == ranking[0]) | (sink == ranking[0]) | (sizes[sink] == 0), 0, jnp.maximum(margin, 0))
    shifted = jax.random.randint(jax.random.fold_in(own, 4), (amount // 2,), 0, 1 << 20) % (margin + 1)
    sizes = sizes.at[donor].add(-shifted).at[sink].add(shifted)
    items = jnp.searchsorted(jnp.cumsum(sizes), jnp.arange(rows * top), side="right").astype(jnp.int32)
    grid = items.reshape(top, rows).T
    grid = grid[jax.random.permutation(jax.random.fold_in(own, 1), rows)]
    turn = jax.random.randint(jax.random.fold_in(own, 2), (rows, 1), 0, top)
    return jnp.take_along_axis(grid, (jnp.arange(top)[None, :] + turn) % top, axis=1)


def load_shares(amount, total, limit, slope, full):
    weights = [(1 << 20) // math.isqrt(standing ** slope) + 1 for standing in range(1, amount + 1)]
    largest = limit if full else min(limit, max(-(-total // amount), total * weights[0] // sum(weights)))
    least = 1 if total - largest >= amount - 1 else 0
    holding, surplus = [largest] + [least] * (amount - 1), total - largest - least * (amount - 1)
    while surplus > 0:
        movable = [i for i in range(1, amount) if holding[i] < largest] or [i for i in range(1, amount) if holding[i] < limit]
        pool, left = sum([weights[i] for i in movable]), surplus
        for i in movable:
            addition = min(limit - holding[i], max(1, left * weights[i] // pool), surplus)
            holding[i] = holding[i] + addition
            surplus = surplus - addition
    return np.array(holding)


def centred(rng, shape, spread, reach, pieces=(), dtype=jnp.bfloat16):
    drawn = jax.random.normal(rng, shape, jnp.float32) * spread
    if len(pieces) > 0:
        drawn = block_scale(rng, shape, pieces, -0.22, 0.18) * drawn
    return jnp.clip(drawn, min=-reach, max=reach).astype(dtype)


def setup_inputs(seed: int = 0) -> dict:
    keys = jax.random.split(jax.random.key(seed), 14)
    patches = centred(keys[0], (TOKENS, D), 1.0, 6.0, ((0, 32),))
    embedding = centred(keys[1], (BLOCKS, D), 1.0, 6.0, ((0, 32),), jnp.float32)
    long_image = plant((jax.random.randint(keys[2], (DEVICES,), 0, 2) < 1).astype(jnp.int32), jax.random.fold_in(keys[2], 1), 0, 1)
    routes_keys = jax.random.split(jax.random.fold_in(keys[3], 1), TOKENS // TOK_DEV)
    routes_turns = jax.random.permutation(jax.random.fold_in(keys[3], 3), TOKENS // TOK_DEV)
    routes = jax.vmap(lambda own, number: deal_out(jax.random.fold_in(keys[3], 2), own, number, TOK_DEV, EXPERTS, 2, CAP, 1))(routes_keys, routes_turns).reshape((TOKENS, 2))
    cotangent = centred(keys[4], (TOKENS, D), 1.0, 6.0, ((0, 32),))
    ada_weight = centred(keys[5], (D, 6 * D), (D // 4) ** -0.5, 0.4375)
    qkv_weight = centred(keys[6], (D, 3 * D), D ** -0.5, 0.21875)
    out_weight = centred(keys[7], (D, D), (D // 16) ** -0.5, 0.875)
    shared_up = centred(keys[8], (D, FF), D ** -0.5, 0.21875)
    shared_down = centred(keys[9], (FF, D), FF ** -0.5, 0.109375)
    router_weight = centred(keys[10], (D, EXPERTS), (2 * D) ** -0.5, 0.15625)
    expert_up = centred(keys[11], (EXPERTS, D, FF), D ** -0.5, 0.21875, ((0, 2),))
    expert_down = centred(keys[12], (EXPERTS, FF, D), FF ** -0.5, 0.109375, ((0, 2),))
    return dict(patches=patches, embedding=embedding, long_image=long_image, routes=routes, cotangent=cotangent, ada_weight=ada_weight, qkv_weight=qkv_weight, out_weight=out_weight, shared_up=shared_up, shared_down=shared_down, router_weight=router_weight, expert_up=expert_up, expert_down=expert_down)


@jax.custom_vjp
def low(v):
    return lax.optimization_barrier(v.astype(jnp.bfloat16)).astype(jnp.float32)

@jax.custom_vjp
def low_back(v):
    return v

def low_keep(v):
    return (low(v), None)

def low_pass(kept, grad):
    return (grad,)

def back_keep(v):
    return (v, None)

def back_low(kept, grad):
    return (low(grad),)
low.defvjp(low_keep, low_pass)
low_back.defvjp(back_keep, back_low)
HIGH = lax.Precision.HIGHEST
EPSILON = 1e-06

def gelu_tanh(values):
    return jax.nn.gelu(values, approximate=True)

def normalize(values):
    centered = values - lax.optimization_barrier(jnp.mean(values, -1, keepdims=True))
    return centered * lax.rsqrt(lax.optimization_barrier(jnp.mean(centered * centered, -1, keepdims=True)) + EPSILON)

def attend_device(inputs):
    packed, flag = inputs
    queries = packed[:, :D].reshape(TOK_DEV, HEADS, HEAD_DIM)
    key_heads = packed[:, D:2 * D].reshape(TOK_DEV, HEADS, HEAD_DIM)
    values = packed[:, 2 * D:].reshape(TOK_DEV, HEADS, HEAD_DIM)
    scores = jnp.einsum('qhd,khd->hqk', queries, key_heads, precision=HIGH) * HEAD_DIM ** (-0.5)
    scores = low_back(scores)
    seg_len = jnp.where(flag > 0, TOK_DEV, SHORT)
    places = jnp.arange(TOK_DEV)
    same = places[:, None] // seg_len == places[None, :] // seg_len
    scores = jnp.where(same[None], scores, -jnp.inf)
    weights = low(jax.nn.softmax(scores, -1))
    return jnp.einsum('hqk,khd->qhd', weights, values, precision=HIGH).reshape(TOK_DEV, D)

def expert_rows(inputs):
    rows_in, up_weight, down_weight = inputs
    pre_act = low_back(jnp.dot(rows_in, up_weight, precision=HIGH))
    activ = low(gelu_tanh(pre_act))
    return jnp.dot(activ, down_weight, precision=HIGH)

def reference(patches, embedding, long_image, routes, cotangent, ada_weight, qkv_weight, out_weight, shared_up, shared_down, router_weight, expert_up, expert_down):
    device_count = N_DP * N_STREAM
    block_count = TOK_DEV // SHORT
    flat_routes = routes.reshape(device_count, 2 * TOK_DEV)
    route_hits = (flat_routes[:, :, None] == jnp.arange(EXPERTS)[None, None, :]).astype(jnp.int32)
    earlier = jnp.cumsum(route_hits, 1) - route_hits
    slots = lax.optimization_barrier(jnp.sum(earlier * route_hits, 2))
    rows_at = (jnp.arange(device_count)[:, None] * CAP + slots).reshape(-1).astype(jnp.int32)
    experts_at = flat_routes.reshape(-1).astype(jnp.int32)
    chosen_hot = (routes[:, :, None] == jnp.arange(EXPERTS)[None, None, :]).astype(jnp.float32)

    def layer(patches_f, embedding_f, ada_f, qkv_f, out_f, sh_up_f, sh_down_f, router_f, ex_up_f, ex_down_f):
        emb_blocks = embedding_f.reshape(device_count, block_count, D)
        used = jnp.where(long_image[:, None, None] > 0, emb_blocks[:, :1, :], emb_blocks)
        modulation = jnp.einsum('nbd,de->nbe', jax.nn.silu(used), ada_f, precision=HIGH)
        modulation = modulation.reshape(device_count, block_count, 1, 6, D)
        shift_one = modulation[:, :, :, 0]
        scale_one = modulation[:, :, :, 1]
        gate_one = modulation[:, :, :, 2]
        shift_two = modulation[:, :, :, 3]
        scale_two = modulation[:, :, :, 4]
        gate_two = modulation[:, :, :, 5]
        inputs_full = patches_f.reshape(device_count, block_count, SHORT, D)
        hidden_one = low(normalize(inputs_full) * (1.0 + scale_one) + shift_one).reshape(device_count, TOK_DEV, D)
        packed = jnp.einsum('ntd,de->nte', hidden_one, qkv_f, precision=HIGH)
        packed = low_back(low(packed))
        attended = lax.map(jax.checkpoint(attend_device), (packed, long_image))
        attended = low_back(low(attended))
        branch_one = low_back(jnp.einsum('ntd,de->nte', attended, out_f, precision=HIGH))
        branch_one = branch_one.reshape(device_count, block_count, SHORT, D)
        middle = inputs_full + gate_one * branch_one
        hidden_two = low(normalize(middle) * (1.0 + scale_two) + shift_two).reshape(TOKENS, D)
        shared_out = low_back(expert_rows((hidden_two, sh_up_f, sh_down_f)))
        logits = jnp.dot(hidden_two, router_f, precision=HIGH)
        gates = jax.nn.softmax(lax.optimization_barrier(jnp.sum(chosen_hot * logits[:, None, :], -1)), -1)
        buffer = jnp.zeros((EXPERTS, device_count * CAP, D), jnp.float32)
        buffer = buffer.at[experts_at, rows_at].set(jnp.repeat(hidden_two, 2, axis=0))
        buffer = low_back(buffer)
        results = lax.map(jax.checkpoint(expert_rows), (buffer, ex_up_f, ex_down_f))
        results = low(low_back(results))
        picked = results[experts_at, rows_at].reshape(TOKENS, 2, D)
        routed = lax.optimization_barrier(jnp.sum(gates[:, :, None] * picked, 1))
        branch_two = (shared_out + routed).reshape(device_count, block_count, SHORT, D)
        return (middle + gate_two * branch_two).reshape(TOKENS, D)
    output, pullback = jax.vjp(layer, patches.astype(jnp.float32), embedding, ada_weight.astype(jnp.float32), qkv_weight.astype(jnp.float32), out_weight.astype(jnp.float32), shared_up.astype(jnp.float32), shared_down.astype(jnp.float32), router_weight.astype(jnp.float32), expert_up.astype(jnp.float32), expert_down.astype(jnp.float32))
    grads = pullback(cotangent.astype(jnp.float32))
    return (output.astype(jnp.bfloat16), grads[0], grads[1], grads[2], grads[3], grads[4], grads[5], grads[6], grads[7], grads[8], grads[9])
```

```python
import functools
import math

import jax
import jax.numpy as jnp
from jax import lax
from jax.experimental import pallas as pl
from jax.experimental.pallas import tpu as pltpu
from jax.sharding import PartitionSpec as P

HEADS = 12
HEAD_DIM = 64
EXPERTS = 8
CAP = 288


HIGH = lax.Precision.HIGHEST
EPSILON = 1e-06
F32 = jnp.float32
BF16 = jnp.bfloat16
MIB = 1 << 20


def gelu_tanh(values):
    return jax.nn.gelu(values, approximate=True)


def normalize(values):
    centered = values - jnp.mean(values, -1, keepdims=True)
    spread = lax.rsqrt(jnp.mean(centered * centered, -1, keepdims=True) + EPSILON)
    return (centered * spread, spread)


def normalize_back(grad_normed, normed, spread):
    return spread * (
        grad_normed
        - jnp.mean(grad_normed, -1, keepdims=True)
        - normed * jnp.mean(grad_normed * normed, -1, keepdims=True)
    )


def split_packed(packed, seg_len):
    row_count = packed.shape[0]
    model_width = packed.shape[1] // 3
    groups = row_count // seg_len
    block_rows = min(512, seg_len)
    part_count = seg_len // block_rows
    queries = (
        packed[:, :model_width]
        .reshape(groups, part_count, block_rows, HEADS, HEAD_DIM)
        .swapaxes(0, 1)
    )
    key_heads = packed[:, model_width : 2 * model_width].reshape(groups, seg_len, HEADS, HEAD_DIM)
    values = packed[:, 2 * model_width :].reshape(groups, seg_len, HEADS, HEAD_DIM)
    return (queries, key_heads, values, groups, block_rows, part_count)


def attend(packed, seg_len):
    row_count = packed.shape[0]
    model_width = packed.shape[1] // 3
    factor = 1.0 / math.sqrt(HEAD_DIM)
    queries, key_heads, values, groups, block_rows, part_count = split_packed(packed, seg_len)

    def one_block(query_block):
        scores = (
            jnp.einsum(
                "gqhd,gkhd->ghqk", query_block, key_heads, preferred_element_type=jnp.float32
            )
            * factor
        )
        row_max = jnp.max(scores, -1, keepdims=True)
        shifted = jnp.exp(scores - row_max)
        row_sum = jnp.sum(shifted, -1, keepdims=True)
        weights = (shifted / row_sum).astype(jnp.bfloat16)
        mixture = jnp.einsum("ghqk,gkhd->gqhd", weights, values, preferred_element_type=jnp.float32)
        return (mixture, row_max[..., 0] + jnp.log(row_sum[..., 0]))

    mixture, logsum = lax.map(one_block, queries)
    return (mixture.swapaxes(0, 1).reshape(row_count, model_width), logsum.reshape(-1))


def attend_back(packed, logsum, grad_mixture, seg_len):
    row_count = packed.shape[0]
    model_width = packed.shape[1] // 3
    factor = 1.0 / math.sqrt(HEAD_DIM)
    queries, key_heads, values, groups, block_rows, part_count = split_packed(packed, seg_len)
    grad_blocks = grad_mixture.reshape(groups, part_count, block_rows, HEADS, HEAD_DIM).swapaxes(
        0, 1
    )
    logsum_blocks = logsum.reshape(part_count, groups, HEADS, block_rows)

    def one_block(carried, inputs):
        grad_keys, grad_values = carried
        query_block, grad_block, logsum_block = inputs
        scores = (
            jnp.einsum(
                "gqhd,gkhd->ghqk", query_block, key_heads, preferred_element_type=jnp.float32
            )
            * factor
        )
        prob_full = jnp.exp(scores - logsum_block[..., None])
        grad_values = grad_values + jnp.einsum(
            "ghqk,gqhd->gkhd",
            prob_full.astype(jnp.bfloat16),
            grad_block,
            preferred_element_type=jnp.float32,
        )
        grad_probs = jnp.einsum(
            "gqhd,gkhd->ghqk", grad_block, values, preferred_element_type=jnp.float32
        )
        row_inner = jnp.sum(grad_probs * prob_full, -1, keepdims=True)
        grad_scores = (prob_full * (grad_probs - row_inner)).astype(jnp.bfloat16)
        grad_query = (
            jnp.einsum(
                "ghqk,gkhd->gqhd", grad_scores, key_heads, preferred_element_type=jnp.float32
            )
            * factor
        )
        grad_keys = (
            grad_keys
            + jnp.einsum(
                "ghqk,gqhd->gkhd", grad_scores, query_block, preferred_element_type=jnp.float32
            )
            * factor
        )
        return ((grad_keys, grad_values), grad_query)

    zeros_kv = jnp.zeros((groups, seg_len, HEADS, HEAD_DIM), jnp.float32)
    (grad_keys, grad_values), grad_query = lax.scan(
        one_block, (zeros_kv, zeros_kv), (queries, grad_blocks, logsum_blocks)
    )
    return jnp.concatenate(
        [
            grad_query.swapaxes(0, 1).reshape(row_count, model_width),
            grad_keys.reshape(row_count, model_width),
            grad_values.reshape(row_count, model_width),
        ],
        1,
    )


def local_general(
    patches,
    embedding,
    long_image,
    routes,
    cotangent,
    ada_weight,
    qkv_weight,
    out_weight,
    shared_up,
    shared_down,
    router_weight,
    expert_up,
    expert_down,
):
    row_count, model_width = patches.shape
    block_count = embedding.shape[0]
    short_len = row_count // block_count
    lane_count = lax.axis_size("stream")
    local_experts = expert_up.shape[0]
    is_long = long_image[0] > 0

    def blocks(values):
        return values.reshape(block_count, short_len, model_width)

    def flatten(values):
        return values.reshape(row_count, model_width)

    used = jnp.where(is_long, jnp.broadcast_to(embedding[0:1], embedding.shape), embedding)
    activated, silu_back = jax.vjp(jax.nn.silu, used)
    ada_full = ada_weight.astype(jnp.float32)
    modulation = jnp.dot(activated, ada_full, precision=HIGH)
    pieces = [
        modulation[:, column * model_width : (column + 1) * model_width][:, None, :]
        for column in range(6)
    ]
    shift_one, scale_one, gate_one, shift_two, scale_two, gate_two = pieces
    inputs_full = blocks(patches.astype(jnp.float32))
    normed_one, spread_one = normalize(inputs_full)
    hidden_one = flatten(normed_one * (1.0 + scale_one) + shift_one).astype(jnp.bfloat16)
    packed = jnp.dot(hidden_one, qkv_weight, preferred_element_type=jnp.float32).astype(
        jnp.bfloat16
    )
    attended, logsum = lax.cond(
        is_long,
        lambda packed_in: attend(packed_in, row_count),
        lambda packed_in: attend(packed_in, short_len),
        packed,
    )
    attended_low = attended.astype(jnp.bfloat16)
    branch_one = blocks(jnp.dot(attended_low, out_weight, preferred_element_type=jnp.float32))
    middle = inputs_full + gate_one * branch_one
    normed_two, spread_two = normalize(middle)
    hidden_two = flatten(normed_two * (1.0 + scale_two) + shift_two).astype(jnp.bfloat16)
    shared_pre = jnp.dot(hidden_two, shared_up, preferred_element_type=jnp.float32)
    shared_act, shared_back = jax.vjp(gelu_tanh, shared_pre)
    shared_low = shared_act.astype(jnp.bfloat16)
    shared_out = jnp.dot(shared_low, shared_down, preferred_element_type=jnp.float32)
    logits = jnp.dot(hidden_two, router_weight, preferred_element_type=jnp.float32)
    chosen_hot = (routes[:, :, None] == jnp.arange(EXPERTS)[None, None, :]).astype(jnp.float32)
    gates = jax.nn.softmax(jnp.sum(chosen_hot * logits[:, None, :], -1), -1)
    flat_routes = routes.reshape(-1)
    route_hits = (flat_routes[:, None] == jnp.arange(EXPERTS)[None, :]).astype(jnp.int32)
    earlier = jnp.cumsum(route_hits, 0) - route_hits
    target = flat_routes * CAP + jnp.sum(earlier * route_hits, 1)

    def spread_rows(rows_low):
        buffer = jnp.zeros((EXPERTS * CAP, model_width), jnp.bfloat16).at[target].set(rows_low)
        return buffer.reshape(lane_count, local_experts, CAP, model_width)

    def collect(arrived):
        return (
            arrived.reshape(EXPERTS * CAP, model_width)[target]
            .astype(jnp.float32)
            .reshape(row_count, 2, model_width)
        )

    def by_expert(arrived):
        return arrived.swapaxes(0, 1).reshape(local_experts, lane_count * CAP, model_width)

    def by_source(results):
        return results.reshape(local_experts, lane_count, CAP, model_width).swapaxes(0, 1)

    expert_in = by_expert(
        lax.all_to_all(
            spread_rows(jnp.repeat(hidden_two, 2, axis=0)),
            "stream",
            split_axis=0,
            concat_axis=0,
            tiled=True,
        )
    )
    expert_pre = jnp.einsum(
        "jrd,jdf->jrf", expert_in, expert_up, preferred_element_type=jnp.float32
    )
    expert_act, expert_back = jax.vjp(gelu_tanh, expert_pre)
    expert_low = expert_act.astype(jnp.bfloat16)
    expert_out = jnp.einsum(
        "jrf,jfd->jrd", expert_low, expert_down, preferred_element_type=jnp.float32
    ).astype(jnp.bfloat16)
    picked = collect(
        lax.all_to_all(by_source(expert_out), "stream", split_axis=0, concat_axis=0, tiled=True)
    )
    routed = jnp.sum(gates[:, :, None] * picked, 1)
    branch_two = blocks(shared_out + routed)
    mixed = flatten(middle + gate_two * branch_two).astype(jnp.bfloat16)
    grad_top = blocks(cotangent.astype(jnp.float32))
    grad_gate_two = jnp.sum(grad_top * branch_two, 1)
    grad_branch = flatten(grad_top * gate_two)
    grad_pick = (
        (gates[:, :, None] * grad_branch[:, None, :])
        .astype(jnp.bfloat16)
        .reshape(2 * row_count, model_width)
    )
    grad_arrived = by_expert(
        lax.all_to_all(spread_rows(grad_pick), "stream", split_axis=0, concat_axis=0, tiled=True)
    )
    grad_expert_down = jnp.einsum(
        "jrf,jrd->jfd", expert_low, grad_arrived, preferred_element_type=jnp.float32
    )
    grad_expert_act = jnp.einsum(
        "jrd,jfd->jrf", grad_arrived, expert_down, preferred_element_type=jnp.float32
    )
    grad_expert_pre = expert_back(grad_expert_act)[0].astype(jnp.bfloat16)
    grad_expert_up = jnp.einsum(
        "jrd,jrf->jdf", expert_in, grad_expert_pre, preferred_element_type=jnp.float32
    )
    grad_expert_in = jnp.einsum(
        "jrf,jdf->jrd", grad_expert_pre, expert_up, preferred_element_type=jnp.float32
    ).astype(jnp.bfloat16)
    grad_routed = jnp.sum(
        collect(
            lax.all_to_all(
                by_source(grad_expert_in), "stream", split_axis=0, concat_axis=0, tiled=True
            )
        ),
        1,
    )
    grad_shared_low = grad_branch.astype(jnp.bfloat16)
    grad_shared_down = jnp.einsum(
        "rf,rd->fd", shared_low, grad_shared_low, preferred_element_type=jnp.float32
    )
    grad_shared_act = jnp.einsum(
        "rd,fd->rf", grad_shared_low, shared_down, preferred_element_type=jnp.float32
    )
    grad_shared_pre = shared_back(grad_shared_act)[0].astype(jnp.bfloat16)
    grad_shared_up = jnp.einsum(
        "rd,rf->df", hidden_two, grad_shared_pre, preferred_element_type=jnp.float32
    )
    grad_gates = jnp.sum(picked * grad_branch[:, None, :], -1)
    grad_chosen = gates * (grad_gates - jnp.sum(gates * grad_gates, -1, keepdims=True))
    grad_logits = jnp.sum(chosen_hot * grad_chosen[:, :, None], 1)
    hidden_two_full = hidden_two.astype(jnp.float32)
    router_full = router_weight.astype(jnp.float32)
    grad_router = jnp.dot(hidden_two_full.T, grad_logits, precision=HIGH)
    grad_hidden = jnp.dot(grad_logits, router_full.T, precision=HIGH) + grad_routed
    grad_hidden = blocks(
        grad_hidden
        + jnp.einsum("rf,df->rd", grad_shared_pre, shared_up, preferred_element_type=jnp.float32)
    )
    grad_shift_two = jnp.sum(grad_hidden, 1)
    grad_scale_two = jnp.sum(grad_hidden * normed_two, 1)
    grad_middle = grad_top + normalize_back(grad_hidden * (1.0 + scale_two), normed_two, spread_two)
    grad_gate_one = jnp.sum(grad_middle * branch_one, 1)
    grad_branch_one = flatten(grad_middle * gate_one).astype(jnp.bfloat16)
    grad_out_weight = jnp.einsum(
        "rd,re->de", attended_low, grad_branch_one, preferred_element_type=jnp.float32
    )
    grad_attended = jnp.einsum(
        "re,de->rd", grad_branch_one, out_weight, preferred_element_type=jnp.float32
    ).astype(jnp.bfloat16)
    grad_packed = lax.cond(
        is_long,
        lambda packed_in, logsum_in, grad_in: attend_back(packed_in, logsum_in, grad_in, row_count),
        lambda packed_in, logsum_in, grad_in: attend_back(packed_in, logsum_in, grad_in, short_len),
        packed,
        logsum,
        grad_attended,
    ).astype(jnp.bfloat16)
    grad_qkv = jnp.einsum("rd,re->de", hidden_one, grad_packed, preferred_element_type=jnp.float32)
    grad_hidden_one = blocks(
        jnp.einsum("re,de->rd", grad_packed, qkv_weight, preferred_element_type=jnp.float32)
    )
    grad_shift_one = jnp.sum(grad_hidden_one, 1)
    grad_scale_one = jnp.sum(grad_hidden_one * normed_one, 1)
    grad_inputs = grad_middle + normalize_back(
        grad_hidden_one * (1.0 + scale_one), normed_one, spread_one
    )
    grad_modulation = jnp.concatenate(
        [
            grad_shift_one,
            grad_scale_one,
            grad_gate_one,
            grad_shift_two,
            grad_scale_two,
            grad_gate_two,
        ],
        1,
    )
    grad_ada = jnp.dot(activated.T, grad_modulation, precision=HIGH)
    grad_used = silu_back(jnp.dot(grad_modulation, ada_full.T, precision=HIGH))[0]
    grad_embedding = jnp.where(
        is_long, jnp.zeros_like(grad_used).at[0].set(jnp.sum(grad_used, 0)), grad_used
    )
    shares = (
        lax.psum_scatter(
            grad_ada.astype(jnp.bfloat16), "dp", scatter_dimension=0, tiled=True
        ).astype(jnp.float32),
        lax.psum_scatter(
            grad_qkv.astype(jnp.bfloat16), "dp", scatter_dimension=0, tiled=True
        ).astype(jnp.float32),
        lax.psum_scatter(
            grad_out_weight.astype(jnp.bfloat16), "dp", scatter_dimension=0, tiled=True
        ).astype(jnp.float32),
        lax.psum_scatter(
            grad_shared_up.astype(jnp.bfloat16), "dp", scatter_dimension=0, tiled=True
        ).astype(jnp.float32),
        lax.psum_scatter(
            grad_shared_down.astype(jnp.bfloat16), "dp", scatter_dimension=0, tiled=True
        ).astype(jnp.float32),
        lax.psum_scatter(
            grad_router.astype(jnp.bfloat16), "dp", scatter_dimension=0, tiled=True
        ).astype(jnp.float32),
    )
    expert_summed = (
        lax.psum_scatter(
            grad_expert_up.astype(jnp.bfloat16), "dp", scatter_dimension=1, tiled=True
        ).astype(jnp.float32),
        lax.psum_scatter(
            grad_expert_down.astype(jnp.bfloat16), "dp", scatter_dimension=1, tiled=True
        ).astype(jnp.float32),
    )
    summed = (
        lax.psum(shares[0].astype(jnp.bfloat16), "stream").astype(jnp.float32),
        lax.psum(shares[1].astype(jnp.bfloat16), "stream").astype(jnp.float32),
        lax.psum(shares[2].astype(jnp.bfloat16), "stream").astype(jnp.float32),
        lax.psum(shares[3].astype(jnp.bfloat16), "stream").astype(jnp.float32),
        lax.psum(shares[4].astype(jnp.bfloat16), "stream").astype(jnp.float32),
        lax.psum(shares[5].astype(jnp.bfloat16), "stream").astype(jnp.float32),
    )
    return (
        mixed,
        flatten(grad_inputs),
        grad_embedding,
        summed[0],
        summed[1],
        summed[2],
        summed[3],
        summed[4],
        summed[5],
        expert_summed[0],
        expert_summed[1],
    )


def nn(left, right):
    return jnp.dot(left, right, preferred_element_type=F32)


def nt(left, right):
    return lax.dot_general(left, right, (((1,), (1,)), ((), ())), preferred_element_type=F32)


def tn(left, right):
    return lax.dot_general(left, right, (((0,), (0,)), ((), ())), preferred_element_type=F32)


def three_parts(values):
    first = values.astype(BF16)
    rest = values - first.astype(F32)
    second = rest.astype(BF16)
    third = (rest - second.astype(F32)).astype(BF16)
    return first, second, third


def sigmoid(values):
    return 1.0 / (1.0 + jnp.exp(-values))


def gelu_and_slope(values):
    inner = math.sqrt(2.0 / math.pi)
    square = values * values
    bend = jnp.tanh(values * (inner + (inner * 0.044715) * square))
    half = 0.5 + 0.5 * bend
    slope = half + values * (0.5 - 0.5 * bend * bend) * (inner + (3.0 * inner * 0.044715) * square)
    return values * half, slope


def params(limit=56):
    return pltpu.CompilerParams(vmem_limit_bytes=limit * MIB)


def cost(flops, moved):
    return pl.CostEstimate(flops=int(flops), bytes_accessed=int(moved), transcendentals=0)


def full(shape):
    return pl.BlockSpec(shape, lambda *_: (0,) * len(shape))


def modulate_kernel(long_ref, emb_ref, ada_ref, mod_ref, act_ref):
    emb = emb_ref[...]
    used = jnp.where(long_ref[0] > 0, jnp.broadcast_to(emb[0:1], emb.shape), emb)
    act = used * sigmoid(used)
    act_ref[...] = act
    weight = ada_ref[...]
    total = 0.0
    for part in three_parts(act):
        total = total + nn(part, weight)
    mod_ref[0] = total


def modulate(long_image, emb_pad, ada_weight):
    rows, width = emb_pad.shape
    pieces = ada_weight.shape[1] // width
    return pl.pallas_call(
        modulate_kernel,
        grid_spec=pltpu.PrefetchScalarGridSpec(
            num_scalar_prefetch=1,
            grid=(pieces,),
            in_specs=[
                pl.BlockSpec((rows, width), lambda i, *_: (0, 0)),
                pl.BlockSpec((width, width), lambda i, *_: (0, i)),
            ],
            out_specs=[
                pl.BlockSpec((1, rows, width), lambda i, *_: (i, 0, 0)),
                pl.BlockSpec((rows, width), lambda i, *_: (0, 0)),
            ],
        ),
        out_shape=[
            jax.ShapeDtypeStruct((pieces, rows, width), F32),
            jax.ShapeDtypeStruct((rows, width), F32),
        ],
        compiler_params=params(),
        cost_estimate=cost(0, ada_weight.size * 2),
        name="modulate",
    )(long_image, emb_pad, ada_weight)


def norm_parts(values):
    centered = values - jnp.mean(values, -1, keepdims=True)
    spread = lax.rsqrt(jnp.mean(centered * centered, -1, keepdims=True) + EPSILON)
    return centered * spread, spread


def norm_back(grad, normed, spread):
    return spread * (
        grad
        - jnp.mean(grad, -1, keepdims=True)
        - normed * jnp.mean(grad * normed, -1, keepdims=True)
    )


def qkv_kernel(x_ref, mod_ref, w_ref, packed_ref):
    block = pl.program_id(0)
    normed, _ = norm_parts(x_ref[...].astype(F32))
    shift, scale = mod_ref[0, pl.ds(block, 1), :], mod_ref[1, pl.ds(block, 1), :]
    hidden = (normed * (1.0 + scale) + shift).astype(BF16)
    packed_ref[...] = nn(hidden, w_ref[...]).astype(BF16)


def qkv_forward(patches, mod, weight, blocks):
    rows, width = patches.shape
    short = rows // blocks
    wide = weight.shape[1]
    return pl.pallas_call(
        qkv_kernel,
        grid=(blocks,),
        in_specs=[pl.BlockSpec((short, width), lambda i: (i, 0)), full(mod.shape), full(weight.shape)],
        out_specs=pl.BlockSpec((short, wide), lambda i: (i, 0)),
        out_shape=jax.ShapeDtypeStruct((rows, wide), BF16),
        compiler_params=params(),
        cost_estimate=cost(2 * rows * width * wide, rows * wide * 2),
        name="qkv",
    )(patches, mod, weight)


def attend_kernel(short, long_ref, q_ref, k_ref, v_ref, o_ref, lse_ref):
    rows, lanes = q_ref.shape
    first = lax.broadcasted_iota(jnp.int32, (1, lanes), 1) < HEAD_DIM
    factor = 1.0 / math.sqrt(HEAD_DIM)

    def part(query_at, key_at, key_count):
        queries = q_ref[query_at : query_at + short, :]
        keys = k_ref[key_at : key_at + key_count, :]
        values = v_ref[key_at : key_at + key_count, :]
        zero = jnp.zeros_like(queries)
        outs, sums = [], []
        for mine in (first, jnp.logical_not(first)):
            scores = nt(jnp.where(mine, queries, zero), keys) * factor
            top = jnp.max(scores, -1, keepdims=True)
            shifted = jnp.exp(scores - top)
            total = jnp.sum(shifted, -1, keepdims=True)
            outs.append(nn(shifted.astype(BF16), values) * (1.0 / total))
            sums.append(top + jnp.log(total))
        o_ref[query_at : query_at + short, :] = jnp.where(first, outs[0], outs[1]).astype(BF16)
        lse_ref[query_at : query_at + short, :] = jnp.where(first, sums[0], sums[1])

    @pl.when(long_ref[0] > 0)
    def _():
        for at in range(0, rows, short):
            part(at, 0, rows)

    @pl.when(long_ref[0] <= 0)
    def _():
        for at in range(0, rows, short):
            part(at, at, short)


def attend_forward(long_image, packed, short):
    rows = packed.shape[0]
    width = packed.shape[1] // 3
    lanes = 2 * HEAD_DIM
    pairs = width // lanes
    spec = [
        pl.BlockSpec((rows, lanes), functools.partial(lambda shift, i, *_: (0, i + shift), shift))
        for shift in (0, pairs, 2 * pairs)
    ]
    return pl.pallas_call(
        functools.partial(attend_kernel, short),
        grid_spec=pltpu.PrefetchScalarGridSpec(
            num_scalar_prefetch=1, grid=(pairs,), in_specs=spec, out_specs=[spec[0], spec[0]]
        ),
        out_shape=[
            jax.ShapeDtypeStruct((rows, width), BF16),
            jax.ShapeDtypeStruct((rows, width), F32),
        ],
        compiler_params=params(),
        cost_estimate=cost(16 * rows * rows * width, rows * width * 12),
        name="attend",
    )(long_image, packed, packed, packed)


def attend_back_kernel(
    short, long_ref, q_ref, k_ref, v_ref, o_ref, lse_ref, do_ref, dq_ref, dk_ref, dv_ref,
    dk_acc, dv_acc,
):
    rows, lanes = q_ref.shape
    first = lax.broadcasted_iota(jnp.int32, (1, lanes), 1) < HEAD_DIM
    factor = 1.0 / math.sqrt(HEAD_DIM)
    product = do_ref[...].astype(F32) * o_ref[...].astype(F32)
    lse_t = jnp.transpose(lse_ref[...])
    product_t = jnp.transpose(product)
    lse_rows = [lse_t[0:1], lse_t[HEAD_DIM : HEAD_DIM + 1]]
    delta_rows = [
        jnp.sum(product_t[:HEAD_DIM], 0, keepdims=True),
        jnp.sum(product_t[HEAD_DIM:], 0, keepdims=True),
    ]

    def part(query_at, key_at, key_count, fresh):
        chunk = slice(query_at, query_at + short)
        span = slice(key_at, key_at + key_count)
        queries, grads = q_ref[chunk, :], do_ref[chunk, :]
        keys, values = k_ref[span, :], v_ref[span, :]
        zero, zero_keys = jnp.zeros_like(queries), jnp.zeros_like(keys)
        dq = dk = dv = 0.0
        for head, mine in enumerate((first, jnp.logical_not(first))):
            query_own = jnp.where(mine, queries, zero)
            grad_own = jnp.where(mine, grads, zero)
            key_own = jnp.where(mine, keys, zero_keys)
            scores = nt(keys, query_own) * factor
            probs = jnp.exp(scores - lse_rows[head][:, chunk])
            grad_probs = nt(values, grad_own)
            grad_scores = (probs * (grad_probs - delta_rows[head][:, chunk])).astype(BF16)
            dv = dv + nn(probs.astype(BF16), grad_own)
            dk = dk + nn(grad_scores, query_own)
            dq = dq + tn(grad_scores, key_own)
        dq_ref[chunk, :] = (dq * factor).astype(BF16)
        if fresh:
            dk_acc[span, :] = dk
            dv_acc[span, :] = dv
        else:
            dk_acc[span, :] += dk
            dv_acc[span, :] += dv

    @pl.when(long_ref[0] > 0)
    def _():
        for at in range(0, rows, short):
            part(at, 0, rows, at == 0)

    @pl.when(long_ref[0] <= 0)
    def _():
        for at in range(0, rows, short):
            part(at, at, short, True)

    dk_ref[...] = (dk_acc[...] * factor).astype(BF16)
    dv_ref[...] = dv_acc[...].astype(BF16)


def attend_backward(long_image, packed, attended, logsum, grad, short):
    rows, width = attended.shape
    lanes = 2 * HEAD_DIM
    pairs = width // lanes
    spec = [
        pl.BlockSpec((rows, lanes), functools.partial(lambda shift, i, *_: (0, i + shift), shift))
        for shift in (0, pairs, 2 * pairs)
    ]
    return pl.pallas_call(
        functools.partial(attend_back_kernel, short),
        grid_spec=pltpu.PrefetchScalarGridSpec(
            num_scalar_prefetch=1,
            grid=(pairs,),
            in_specs=spec + [spec[0]] * 3,
            out_specs=[spec[0]] * 3,
            scratch_shapes=[pltpu.VMEM((rows, lanes), F32)] * 2,
        ),
        out_shape=[jax.ShapeDtypeStruct((rows, width), BF16)] * 3,
        compiler_params=params(),
        cost_estimate=cost(40 * rows * rows * width, rows * width * 20),
        name="attend_back",
    )(long_image, packed, packed, packed, attended, logsum, grad)


def middle_kernel(att_ref, x_ref, mod_ref, w_ref, branch_ref, hidden_ref):
    block = pl.program_id(0)
    branch = nn(att_ref[...], w_ref[...])
    branch_ref[...] = branch
    middle = x_ref[...].astype(F32) + mod_ref[2, pl.ds(block, 1), :] * branch
    normed, _ = norm_parts(middle)
    shift, scale = mod_ref[3, pl.ds(block, 1), :], mod_ref[4, pl.ds(block, 1), :]
    hidden_ref[...] = (normed * (1.0 + scale) + shift).astype(BF16)


def middle_forward(attended, patches, mod, out_weight, blocks):
    rows, width = patches.shape
    tile = pl.BlockSpec((rows // blocks, width), lambda i: (i, 0))
    return pl.pallas_call(
        middle_kernel,
        grid=(blocks,),
        in_specs=[tile, tile, full(mod.shape), full(out_weight.shape)],
        out_specs=[tile, tile],
        out_shape=[
            jax.ShapeDtypeStruct((rows, width), F32),
            jax.ShapeDtypeStruct((rows, width), BF16),
        ],
        compiler_params=params(),
        cost_estimate=cost(2 * rows * width * width, rows * width * 10),
        name="middle",
    )(attended, patches, mod, out_weight)


def rank_kernel(base_ref, routes_ref, row_ref, col_ref):
    rows = routes_ref.shape[2]
    ids = base_ref[0] + lax.broadcasted_iota(jnp.int32, (8, rows), 0)
    hits = jnp.logical_or(routes_ref[0, 0:1, :] == ids, routes_ref[0, 1:2, :] == ids)
    before = lax.broadcasted_iota(jnp.int32, (rows, rows), 0)
    after = lax.broadcasted_iota(jnp.int32, (rows, rows), 1)
    upper = (before < after).astype(F32).astype(BF16)
    earlier = nn(hits.astype(F32).astype(BF16), upper)
    rank = jnp.where(hits, earlier, -1.0)
    row_ref[0] = rank.astype(jnp.int32)
    tall = jnp.concatenate([rank, jnp.full((120, rows), -1.0, F32)], 0)
    col_ref[0] = jnp.transpose(tall).astype(jnp.int32)


def ranks(base, routes_all):
    count, _, rows = routes_all.shape
    return pl.pallas_call(
        rank_kernel,
        grid_spec=pltpu.PrefetchScalarGridSpec(
            num_scalar_prefetch=1,
            grid=(count,),
            in_specs=[pl.BlockSpec((1, 2, rows), lambda i, *_: (i, 0, 0))],
            out_specs=[
                pl.BlockSpec((1, 8, rows), lambda i, *_: (i, 0, 0)),
                pl.BlockSpec((1, rows, 128), lambda i, *_: (i, 0, 0)),
            ],
        ),
        out_shape=[
            jax.ShapeDtypeStruct((count, 8, rows), jnp.int32),
            jax.ShapeDtypeStruct((count, rows, 128), jnp.int32),
        ],
        compiler_params=params(),
        cost_estimate=cost(0, 4 << 20),
        name="ranks",
    )(base, routes_all)


def gate_rows(hidden, routes, router_t, ids):
    logits = nt(router_t, hidden)
    every = lax.broadcasted_iota(jnp.int32, logits.shape, 0)
    first, second = routes[0:1, :], routes[1:2, :]
    zero = jnp.zeros_like(logits)
    logit_one = jnp.sum(jnp.where(every == first, logits, zero), 0, keepdims=True)
    logit_two = jnp.sum(jnp.where(every == second, logits, zero), 0, keepdims=True)
    gate_one = sigmoid(logit_one - logit_two)
    gate_two = sigmoid(logit_two - logit_one)
    return jnp.where(ids == first, gate_one, 0.0) + jnp.where(ids == second, gate_two, 0.0)


def ffn_phase_one(x, g, up_ref, down_ref, act_ref, pre_ref, step=256):
    wide = act_ref.shape[1]
    for at in range(0, wide, step):
        cols = slice(at, at + step)
        act, slope = gelu_and_slope(nn(x, up_ref[0, :, cols]))
        back = nt(g, down_ref[0, cols, :])
        act_ref[:, cols] = act.astype(BF16)
        pre_ref[:, cols] = (back * slope).astype(BF16)


def expert_kernel(
    slot, has_prior, scal_ref, h0_ref, h1_ref, g0_ref, g1_ref, rank_ref, routes_ref, router_ref,
    up_ref, down_ref, *rest,
):
    if has_prior:
        prior_up_ref, prior_down_ref = rest[:2]
        rest = rest[2:]
    (dup_ref, ddown_ref, out_ref, gx_ref, gg_ref,
     x_s, xt_s, g_s, gt_s, b_s, gate_s, act_s, pre_s, out_acc, gx_acc) = rest
    tile = pl.program_id(0)
    last = pl.num_programs(0) - 1
    rows = h0_ref.shape[0]
    own = lax.broadcasted_iota(jnp.int32, (CAP, rows), 0)

    def hot(source):
        return (own == rank_ref[source, slot : slot + 1, :]).astype(F32)

    @pl.when(tile == 0)
    def _():
        for source, (h_ref, b_ref) in enumerate(((h0_ref, g0_ref), (h1_ref, g1_ref))):
            span = slice(source * CAP, (source + 1) * CAP)
            pick = hot(source)
            pick_low = pick.astype(BF16)
            gate = gate_rows(h_ref[...], routes_ref[source], router_ref[...], scal_ref[1])
            gate_col = jnp.sum(pick * gate[0:1], -1, keepdims=True)
            branch = nn(pick_low, b_ref[...])
            x_s[span, :] = nn(pick_low, h_ref[...]).astype(BF16)
            b_s[span, :] = branch.astype(BF16)
            g_s[span, :] = (branch * gate_col).astype(BF16)
            gate_s[span, :] = jnp.broadcast_to(gate_col, (CAP, 128))
        xt_s[...] = jnp.transpose(x_s[...])
        gt_s[...] = jnp.transpose(g_s[...])
        out_acc[...] = jnp.zeros_like(out_acc)
        gx_acc[...] = jnp.zeros_like(gx_acc)

    ffn_phase_one(x_s[...], g_s[...], up_ref, down_ref, act_s, pre_s)
    act, pre = act_s[...], pre_s[...]
    out_acc[...] += nn(act, down_ref[0])
    gx_acc[...] += nt(pre, up_ref[0])
    dup = nn(xt_s[...], pre)
    ddown = nn(gt_s[...], act)
    if has_prior:
        dup = dup + prior_up_ref[...].astype(F32)
        split = ddown_ref.shape[2]
        for piece in range(ddown_ref.shape[0]):
            ddown_ref[piece] = (
                ddown[:, piece * split : (piece + 1) * split] + prior_down_ref[piece].astype(F32)
            ).astype(BF16)
    else:
        split = ddown_ref.shape[2]
        for piece in range(ddown_ref.shape[0]):
            ddown_ref[piece] = ddown[:, piece * split : (piece + 1) * split].astype(BF16)
    dup_ref[...] = dup.astype(BF16)

    @pl.when(tile == last)
    def _():
        for source in range(2):
            span = slice(source * CAP, (source + 1) * CAP)
            out = out_acc[span, :]
            out_ref[source] = (out * gate_s[span, 0:1]).astype(BF16)
            gx_ref[source] = gx_acc[span, :].astype(BF16)
            inner = jnp.sum(out * b_s[span, :].astype(F32), -1, keepdims=True)
            gg_ref[source] = jnp.sum(hot(source) * inner, 0, keepdims=True)


def expert_call(slot, scal, hiddens, branches, rank_rows, routes, router_t, up, down, prior, zy):
    rows, width = hiddens[0].shape
    wide = up.shape[2]
    tile = width
    tiles = wide // tile
    split = wide // zy
    per = tile // split
    count = 2 * CAP
    weights = [
        pl.BlockSpec((1, width, tile), lambda f, s: (s[0], 0, f)),
        pl.BlockSpec((1, tile, width), lambda f, s: (s[0], f, 0)),
    ]
    grads = [
        pl.BlockSpec((width, tile), lambda f, s: (0, f)),
        pl.BlockSpec((per, width, split), lambda f, s: (f, 0, 0)),
    ]
    whole = lambda a: pl.BlockSpec(a.shape, lambda f, s: (0,) * a.ndim)
    shared = [*hiddens, *branches, rank_rows, routes, router_t]
    out_shape = [
        jax.ShapeDtypeStruct((width, wide), BF16),
        jax.ShapeDtypeStruct((zy, width, split), BF16),
        jax.ShapeDtypeStruct((2, CAP, width), BF16),
        jax.ShapeDtypeStruct((2, CAP, width), BF16),
        jax.ShapeDtypeStruct((2, 1, rows), F32),
    ]
    return pl.pallas_call(
        functools.partial(expert_kernel, slot, prior is not None),
        grid_spec=pltpu.PrefetchScalarGridSpec(
            num_scalar_prefetch=1,
            grid=(tiles,),
            in_specs=[whole(a) for a in shared] + weights + (grads if prior is not None else []),
            out_specs=grads + [whole(a) for a in out_shape[2:]],
            scratch_shapes=[
                pltpu.VMEM((count, width), BF16),
                pltpu.VMEM((width, count), BF16),
                pltpu.VMEM((count, width), BF16),
                pltpu.VMEM((width, count), BF16),
                pltpu.VMEM((count, width), BF16),
                pltpu.VMEM((count, 128), F32),
                pltpu.VMEM((count, tile), BF16),
                pltpu.VMEM((count, tile), BF16),
                pltpu.VMEM((count, width), F32),
                pltpu.VMEM((count, width), F32),
            ],
        ),
        out_shape=out_shape,
        compiler_params=params(),
        cost_estimate=cost(12 * count * width * wide, width * wide * 8),
        name="expert",
    )(scal, *shared, up, down, *(prior if prior is not None else ()))


def shared_kernel(
    h_ref, b_ref, up_ref, down_ref, dup_ref, ddown_ref, out_ref, gx_ref,
    xt_s, gt_s, act_s, pre_s,
):
    @pl.when(pl.program_id(0) == 0)
    def _():
        xt_s[...] = jnp.transpose(h_ref[...])
        gt_s[...] = jnp.transpose(b_ref[...])
        out_ref[...] = jnp.zeros_like(out_ref)
        gx_ref[...] = jnp.zeros_like(gx_ref)

    ffn_phase_one(h_ref[...], b_ref[...], up_ref, down_ref, act_s, pre_s)
    act, pre = act_s[...], pre_s[...]
    out_ref[...] += nn(act, down_ref[0])
    gx_ref[...] += nt(pre, up_ref[0])
    dup_ref[0] = nn(xt_s[...], pre).astype(BF16)
    ddown_ref[0] = nn(gt_s[...], act).astype(BF16)


def shared_call(hidden, branch, up, down):
    rows, width = hidden.shape
    wide = up.shape[1]
    tile = width
    tiles = wide // tile
    whole = lambda a: pl.BlockSpec(a.shape, lambda f: (0,) * a.ndim)
    return pl.pallas_call(
        shared_kernel,
        grid=(tiles,),
        in_specs=[
            whole(hidden),
            whole(branch),
            pl.BlockSpec((1, width, tile), lambda f: (0, 0, f)),
            pl.BlockSpec((1, tile, width), lambda f: (0, f, 0)),
        ],
        out_specs=[
            pl.BlockSpec((1, width, tile), lambda f: (f, 0, 0)),
            pl.BlockSpec((1, width, tile), lambda f: (f, 0, 0)),
            whole(hidden),
            whole(hidden),
        ],
        out_shape=[
            jax.ShapeDtypeStruct((tiles, width, tile), BF16),
            jax.ShapeDtypeStruct((tiles, width, tile), BF16),
            jax.ShapeDtypeStruct((rows, width), F32),
            jax.ShapeDtypeStruct((rows, width), F32),
        ],
        scratch_shapes=[
            pltpu.VMEM((width, rows), BF16),
            pltpu.VMEM((width, rows), BF16),
            pltpu.VMEM((rows, tile), BF16),
            pltpu.VMEM((rows, tile), BF16),
        ],
        compiler_params=params(),
        cost_estimate=cost(12 * rows * width * wide, width * wide * 8),
        name="shared",
    )(hidden, branch, up[None], down[None])


def combine_kernel(slots, col_ref, *rest):
    rows_refs, (out_ref, gx_ref) = rest[: 2 * slots], rest[2 * slots :]
    rows = col_ref.shape[1]
    own = lax.broadcasted_iota(jnp.int32, (rows, CAP), 1)
    out = gx = 0.0
    for slot in range(slots):
        pick = (col_ref[0, :, slot : slot + 1] == own).astype(F32).astype(BF16)
        out = out + nn(pick, rows_refs[2 * slot][0])
        gx = gx + nn(pick, rows_refs[2 * slot + 1][0])
    out_ref[0] = out.astype(BF16)
    gx_ref[0] = gx.astype(BF16)


def combine(rank_cols, pairs):
    count, rows, _ = rank_cols.shape
    width = pairs[0][0].shape[2]
    part = pl.BlockSpec((1, CAP, width), lambda i: (i, 0, 0))
    whole = pl.BlockSpec((1, rows, width), lambda i: (i, 0, 0))
    return pl.pallas_call(
        functools.partial(combine_kernel, len(pairs)),
        grid=(count,),
        in_specs=[pl.BlockSpec((1, rows, 128), lambda i: (i, 0, 0))] + [part] * (2 * len(pairs)),
        out_specs=[whole, whole],
        out_shape=[jax.ShapeDtypeStruct((count, rows, width), BF16)] * 2,
        compiler_params=params(),
        cost_estimate=cost(8 * count * rows * CAP * width, count * rows * width * 8),
        name="combine",
    )(rank_cols, *[a for pair in pairs for a in pair])


def middle_back_kernel(
    gs_ref, ga_ref, gb_ref, gc_ref, gg_ref, ids_ref, routes_ref, router_ref, router_rel_ref,
    hidden_ref, cot_ref, branch_ref, x_ref, mod_ref, w_ref, att_ref,
    gm_ref, gatt_ref, mods_ref, drouter_ref, dout_ref,
):
    block = pl.program_id(0)
    hidden = hidden_ref[...]
    gates = gate_rows(hidden, routes_ref[...], router_ref[...], ids_ref[:, 0:1])
    grad_gates = gg_ref[...]
    inner = jnp.sum(gates * grad_gates, 0, keepdims=True)
    grad_logits = gates * (grad_gates - inner)
    grad = gs_ref[...] + ga_ref[...].astype(F32) + gb_ref[...].astype(F32) + gc_ref[...].astype(F32)
    drouter = 0.0
    for piece in three_parts(grad_logits):
        grad = grad + tn(piece, router_rel_ref[...])
        drouter = drouter + nn(piece, hidden)
    branch = branch_ref[...]
    gate_one = mod_ref[2, pl.ds(block, 1), :]
    middle = x_ref[...].astype(F32) + gate_one * branch
    normed, spread = norm_parts(middle)
    scale = mod_ref[4, pl.ds(block, 1), :]
    mods_ref[1, pl.ds(block, 1), :] = jnp.sum(grad, 0, keepdims=True)
    mods_ref[2, pl.ds(block, 1), :] = jnp.sum(grad * normed, 0, keepdims=True)
    grad_middle = cot_ref[...].astype(F32) + norm_back(grad * (1.0 + scale), normed, spread)
    mods_ref[0, pl.ds(block, 1), :] = jnp.sum(grad_middle * branch, 0, keepdims=True)
    gm_ref[...] = grad_middle
    grad_branch = (grad_middle * gate_one).astype(BF16)
    gatt_ref[...] = nt(grad_branch, w_ref[...]).astype(BF16)
    dout = tn(att_ref[...], grad_branch)

    @pl.when(block == 0)
    def _():
        drouter_ref[...] = drouter
        dout_ref[...] = dout

    @pl.when(block > 0)
    def _():
        drouter_ref[...] += drouter
        dout_ref[...] += dout


def middle_backward(parts, gg, ids, routes_t, router_t, router_rel, hidden, cot, branch, patches, mod,
                    out_weight, attended, blocks):
    rows, width = patches.shape
    short = rows // blocks
    tile = pl.BlockSpec((short, width), lambda i: (i, 0))
    cols = lambda a: pl.BlockSpec((a.shape[0], short), lambda i: (0, i))
    specs = (
        [tile] * 4 + [cols(gg), full(ids.shape), cols(routes_t), full(router_t.shape)]
        + [full(router_rel.shape)] + [tile] * 4 + [full(mod.shape), full(out_weight.shape), tile]
    )
    out_shape = [
        jax.ShapeDtypeStruct((rows, width), F32),
        jax.ShapeDtypeStruct((rows, width), BF16),
        jax.ShapeDtypeStruct((3, 8, width), F32),
        jax.ShapeDtypeStruct((router_rel.shape[0], width), F32),
        jax.ShapeDtypeStruct((width, width), F32),
    ]
    return pl.pallas_call(
        middle_back_kernel,
        grid=(blocks,),
        in_specs=specs,
        out_specs=[tile, tile] + [full(a.shape) for a in out_shape[2:]],
        out_shape=out_shape,
        compiler_params=params(),
        cost_estimate=cost(4 * rows * width * width, rows * width * 30),
        name="middle_back",
    )(*parts, gg, ids, routes_t, router_t, router_rel, hidden, cot, branch, patches, mod, out_weight,
      attended)


def mixed_kernel(so_ref, ra_ref, rb_ref, rc_ref, cot_ref, branch_ref, x_ref, mod_ref, mixed_ref, gate_ref):
    block = pl.program_id(0)
    second = so_ref[...] + ra_ref[...].astype(F32) + rb_ref[...].astype(F32) + rc_ref[...].astype(F32)
    middle = x_ref[...].astype(F32) + mod_ref[2, pl.ds(block, 1), :] * branch_ref[...]
    mixed_ref[...] = (middle + mod_ref[5, pl.ds(block, 1), :] * second).astype(BF16)
    gate_ref[pl.ds(block, 1), :] = jnp.sum(cot_ref[...].astype(F32) * second, 0, keepdims=True)


def mixed_forward(parts, cot, branch, patches, mod, blocks):
    rows, width = patches.shape
    tile = pl.BlockSpec((rows // blocks, width), lambda i: (i, 0))
    return pl.pallas_call(
        mixed_kernel,
        grid=(blocks,),
        in_specs=[tile] * 7 + [full(mod.shape)],
        out_specs=[tile, full((8, width))],
        out_shape=[
            jax.ShapeDtypeStruct((rows, width), BF16),
            jax.ShapeDtypeStruct((8, width), F32),
        ],
        compiler_params=params(),
        cost_estimate=cost(0, rows * width * 22),
        name="mixed",
    )(*parts, cot, branch, patches, mod)


def qkv_weight_kernel(x_ref, mod_ref, dq_ref, dk_ref, dv_ref, dw_ref, hidden_t):
    blocks = mod_ref.shape[1]
    short = x_ref.shape[0] // 4

    @pl.when(pl.program_id(0) == 0)
    def _():
        for block in range(x_ref.shape[0] // short):
            span = slice(block * short, (block + 1) * short)
            normed, _ = norm_parts(x_ref[span, :].astype(F32))
            hidden = normed * (1.0 + mod_ref[1, block : block + 1, :]) + mod_ref[0, block : block + 1, :]
            hidden_t[:, span] = jnp.transpose(hidden.astype(BF16))

    for index, ref in enumerate((dq_ref, dk_ref, dv_ref)):

        @pl.when(pl.program_id(0) == index)
        def _():
            dw_ref[...] = nn(hidden_t[...], ref[...]).astype(BF16)


def qkv_weight_grad(patches, mod, grads):
    rows, width = patches.shape
    return pl.pallas_call(
        qkv_weight_kernel,
        grid=(3,),
        in_specs=[full(patches.shape), full(mod.shape)] + [full(patches.shape)] * 3,
        out_specs=pl.BlockSpec((width, width), lambda i: (0, i)),
        out_shape=jax.ShapeDtypeStruct((width, 3 * width), BF16),
        scratch_shapes=[pltpu.VMEM((width, rows), BF16)],
        compiler_params=params(),
        cost_estimate=cost(6 * rows * width * width, rows * width * 14),
        name="qkv_weight",
    )(patches, mod, *grads)


def inputs_back_kernel(dq_ref, dk_ref, dv_ref, w_ref, x_ref, gm_ref, mod_ref, gp_ref, mods_ref):
    block = pl.program_id(0)
    width = x_ref.shape[1]
    grad = nt(dq_ref[...], w_ref[:, :width])
    grad = grad + nt(dk_ref[...], w_ref[:, width : 2 * width])
    grad = grad + nt(dv_ref[...], w_ref[:, 2 * width :])
    normed, spread = norm_parts(x_ref[...].astype(F32))
    mods_ref[0, pl.ds(block, 1), :] = jnp.sum(grad, 0, keepdims=True)
    mods_ref[1, pl.ds(block, 1), :] = jnp.sum(grad * normed, 0, keepdims=True)
    scale = mod_ref[1, pl.ds(block, 1), :]
    gp_ref[...] = gm_ref[...] + norm_back(grad * (1.0 + scale), normed, spread)


def inputs_backward(grads, weight, patches, grad_middle, mod, blocks):
    rows, width = patches.shape
    tile = pl.BlockSpec((rows // blocks, width), lambda i: (i, 0))
    return pl.pallas_call(
        inputs_back_kernel,
        grid=(blocks,),
        in_specs=[tile] * 3 + [full(weight.shape), tile, tile, full(mod.shape)],
        out_specs=[tile, full((2, 8, width))],
        out_shape=[
            jax.ShapeDtypeStruct((rows, width), F32),
            jax.ShapeDtypeStruct((2, 8, width), F32),
        ],
        compiler_params=params(),
        cost_estimate=cost(6 * rows * width * width, rows * width * 20),
        name="inputs_back",
    )(*grads, weight, patches, grad_middle, mod)


def used_kernel(block_count, long_ref, gm_ref, ada_ref, emb_ref, out_ref):
    piece = pl.program_id(0)

    @pl.when(piece == 0)
    def _():
        out_ref[...] = jnp.zeros_like(out_ref)

    for part in three_parts(gm_ref[0]):
        out_ref[...] += nt(part, ada_ref[...])

    @pl.when(piece == pl.num_programs(0) - 1)
    def _():
        emb = emb_ref[...]
        is_long = long_ref[0] > 0
        used = jnp.where(is_long, jnp.broadcast_to(emb[0:1], emb.shape), emb)
        gate = sigmoid(used)
        grad = out_ref[...] * (gate * (1.0 + used * (1.0 - gate)))
        row = lax.broadcasted_iota(jnp.int32, grad.shape, 0)
        grad = jnp.where(row < block_count, grad, 0.0)
        total = jnp.sum(grad, 0, keepdims=True)
        out_ref[...] = jnp.where(is_long, jnp.where(row == 0, total, 0.0), grad)


def used_backward(long_image, grad_mod, ada_weight, emb_pad, block_count):
    rows, width = emb_pad.shape
    pieces = grad_mod.shape[0]
    return pl.pallas_call(
        functools.partial(used_kernel, block_count),
        grid_spec=pltpu.PrefetchScalarGridSpec(
            num_scalar_prefetch=1,
            grid=(pieces,),
            in_specs=[
                pl.BlockSpec((1, rows, width), lambda i, *_: (i, 0, 0)),
                pl.BlockSpec((width, width), lambda i, *_: (0, i)),
                pl.BlockSpec((rows, width), lambda i, *_: (0, 0)),
            ],
            out_specs=pl.BlockSpec((rows, width), lambda i, *_: (0, 0)),
        ),
        out_shape=jax.ShapeDtypeStruct((rows, width), F32),
        compiler_params=params(),
        cost_estimate=cost(0, ada_weight.size * 2),
        name="used_back",
    )(long_image, grad_mod, ada_weight, emb_pad)


def swap(values, axis, bit):
    size = lax.axis_size(axis)
    return lax.ppermute(values, axis, [(i, i ^ bit) for i in range(size)])


def half_sum(values, at, own, axis, bit):
    keep = lax.dynamic_index_in_dim(values, own, at, keepdims=False)
    send = lax.dynamic_index_in_dim(values, 1 - own, at, keepdims=False)
    arrived = swap(send.astype(BF16), axis, bit)
    return keep.astype(F32) + arrived.astype(F32)


def paired(values, at, own, axis, bit):
    arrived = swap(values, axis, bit)
    ahead = jnp.where(own == 0, values, arrived)
    behind = jnp.where(own == 0, arrived, values)
    return jnp.stack([ahead, behind], at)


def gather_group(values):
    dp = lax.axis_index("dp")
    stream = lax.axis_index("stream")
    held = paired(values, 0, stream, "stream", 1)
    bit = 1
    while bit < lax.axis_size("dp"):
        held = paired(held, 0, (dp // bit) % 2, "dp", bit)
        held = held.reshape((-1,) + values.shape)
        bit *= 2
    return held


def reduce_zy(values, at):
    size = lax.axis_size("dp")
    dp = lax.axis_index("dp")
    order = [2] + [bit for bit in (1 << k for k in range(2, size.bit_length() - 1))]
    groups = values.shape[at]
    lead, tail = values.shape[:at], values.shape[at + 1 :]
    bits = groups.bit_length() - 1
    held = values.reshape(lead + (2,) * bits + tail)
    left = list(range(bits))
    for bit in order:
        place = bit.bit_length() - 2
        position = at + [len(left) - 1 - i for i, b in enumerate(sorted(left))][sorted(left).index(place)]
        held = half_sum(held, position, (dp // bit) % 2, "dp", bit)
        left.remove(place)
    return held


def reduce_copied(values):
    size = lax.axis_size("dp")
    rows, columns = values.shape
    dp, stream = lax.axis_index("dp"), lax.axis_index("stream")
    held = values.reshape(size // 2, 2, rows // size, 2, columns // 2)
    held = half_sum(held, 1, dp % 2, "dp", 1)
    held = half_sum(held, 2, stream, "stream", 1)
    held = reduce_zy(held, 0)
    both = paired(held.astype(BF16), 1, stream, "stream", 1)
    return both.reshape(rows // size, columns).astype(F32)


def local_pair(
    patches, embedding, long_image, routes, cotangent, ada_weight, qkv_weight, out_weight, shared_up,
    shared_down, router_weight, expert_up, expert_down,
):
    rows, width = patches.shape
    blocks = embedding.shape[0]
    short = rows // blocks
    dp_size = lax.axis_size("dp")
    zy = dp_size // 2
    dp, stream = lax.axis_index("dp"), lax.axis_index("stream")
    core = dp % 2
    local_experts = expert_up.shape[0]
    here = local_experts // 2
    group = stream * 2 + core

    emb_pad = jnp.pad(embedding, ((0, 8 - blocks), (0, 0)))
    mod, act = modulate(long_image, emb_pad, ada_weight)
    cot_full = cotangent.astype(F32).reshape(blocks, short, width)
    branch_grad = (cot_full * mod[5, :blocks][:, None, :]).astype(BF16).reshape(rows, width)
    routes_t = routes.T
    routes_x = swap(routes_t, "stream", 1)
    routes_near = jnp.stack([routes_t, swap(routes_t, "dp", 1)])
    routes_far = jnp.stack([routes_x, swap(routes_x, "dp", 1)])
    base = (stream * local_experts + core * here).astype(jnp.int32)
    rank_near, cols_near = ranks(base[None], routes_near)
    rank_far, cols_far = ranks(base[None], routes_far)
    router_t = jnp.pad(router_weight.T, ((0, 16 - router_weight.shape[1]), (0, 0)))
    branch_x = swap(branch_grad, "stream", 1)
    branches_near = (branch_grad, swap(branch_grad, "dp", 1))
    branches_far = (branch_x, swap(branch_x, "dp", 1))

    packed = qkv_forward(patches, mod, qkv_weight, blocks)
    attended, logsum = attend_forward(long_image, packed, short)
    branch_one, hidden = middle_forward(attended, patches, mod, out_weight, blocks)

    hidden_x = swap(hidden, "stream", 1)
    hiddens_near = (hidden, swap(hidden, "dp", 1))
    hiddens_far = (hidden_x, swap(hidden_x, "dp", 1))

    def expert(slot, far, prior):
        scal = jnp.stack([core * here + slot, base + slot]).astype(jnp.int32)
        return expert_call(
            slot, scal, hiddens_far if far else hiddens_near, branches_far if far else branches_near,
            rank_far if far else rank_near, routes_far if far else routes_near, router_t,
            expert_up, expert_down, prior, zy,
        )

    near = [expert(slot, False, None) for slot in range(here)]
    far = [expert(slot, True, near[slot][:2]) for slot in range(here)]
    out_far, gx_far = combine(cols_far, [(r[2], r[3]) for r in far])
    gg_far = jnp.stack([r[4][:, 0] for r in far], 1)
    gx_back = swap(gx_far[0] + swap(gx_far[1], "dp", 1), "stream", 1)
    out_back = swap(out_far[0] + swap(out_far[1], "dp", 1), "stream", 1)
    gg_back = swap(jnp.concatenate([gg_far[0], swap(gg_far[1], "dp", 1)], 0), "stream", 1)
    out_near, gx_near = combine(cols_near, [(r[2], r[3]) for r in near])
    gg_near = jnp.stack([r[4][:, 0] for r in near], 1)
    gx_core = swap(gx_near[1], "dp", 1)
    out_core = swap(out_near[1], "dp", 1)
    gg_core = swap(gg_near[1], "dp", 1)
    gg = jnp.concatenate([gg_near[0], gg_core, gg_back], 0)
    relative = jnp.arange(EXPERTS, dtype=jnp.int32)
    ids = ((relative // here) ^ group) * here + relative % here
    router_rel = router_weight.T[ids]

    dup, ddown, shared_out, shared_gx = shared_call(hidden, branch_grad, shared_up, shared_down)

    pad8 = lambda a: jnp.pad(a, ((0, 16 - EXPERTS),) + ((0, 0),) * (a.ndim - 1))
    ids16 = jnp.broadcast_to(jnp.pad(ids, (0, 16 - EXPERTS), constant_values=-1)[:, None], (16, 128))
    grad_middle, grad_attended, mods_two, drouter, dout = middle_backward(
        (shared_gx, gx_near[0], gx_core, gx_back), pad8(gg), ids16, routes_t, router_t, pad8(router_rel),
        hidden, cotangent, branch_one, patches, mod, out_weight, attended, blocks,
    )
    mixed, gate_two = mixed_forward(
        (shared_out, out_near[0], out_core, out_back), cotangent, branch_one, patches, mod, blocks
    )
    grads = attend_backward(long_image, packed, attended, logsum, grad_attended, short)
    dqkv = qkv_weight_grad(patches, mod, grads)
    grad_patches, mods_one = inputs_backward(grads, qkv_weight, patches, grad_middle, mod, blocks)
    grad_mod = jnp.concatenate([mods_one, mods_two, gate_two[None]], 0)
    grad_embedding = used_backward(long_image, grad_mod, ada_weight, emb_pad, blocks)[:blocks]

    early = jnp.concatenate([act[:blocks], *[a[:blocks] for a in (*mods_two, gate_two)]], 1)
    early = gather_group(early.astype(BF16))
    late = gather_group(jnp.concatenate([mods_one[0, :blocks], mods_one[1, :blocks]], 1).astype(BF16))
    early = early.reshape(-1, early.shape[-1])
    late = late.reshape(-1, late.shape[-1])
    acts = lax.dynamic_slice_in_dim(early, dp * (width // dp_size), width // dp_size, 1)
    factors = jnp.concatenate([late, early[:, width:]], 1)
    grad_ada = lax.dot_general(acts, factors, (((0,), (0,)), ((), ())), preferred_element_type=F32)

    own = jnp.zeros((EXPERTS, EXPERTS), F32).at[ids, jnp.arange(EXPERTS)].set(1.0)
    drouter_abs = jnp.dot(own, drouter[:EXPERTS], precision=HIGH)
    drouter_sum = lax.psum(drouter_abs, ("dp", "stream"))
    grad_router = lax.dynamic_slice_in_dim(drouter_sum, dp * (width // dp_size), width // dp_size, 1).T

    part = width // zy
    wide = expert_up.shape[2]
    ups, downs = [], []
    for slot in range(here):
        up_sum = reduce_zy(far[slot][0].reshape(zy, part, wide), 0)
        down_sum = reduce_zy(far[slot][1], 0)
        ups.append(up_sum)
        downs.append(down_sum.T)

    def to_cores(held):
        halves = jnp.stack(held)
        halves = halves.reshape(here, 2, halves.shape[1] // 2, halves.shape[2])
        keep = lax.dynamic_index_in_dim(halves, core, 1, False)
        send = lax.dynamic_index_in_dim(halves, 1 - core, 1, False)
        arrived = swap(send.astype(BF16), "dp", 1).astype(F32)
        return jnp.concatenate(
            [jnp.where(core == 0, keep, arrived), jnp.where(core == 0, arrived, keep)], 0
        )

    grad_expert_up = to_cores(ups)
    grad_expert_down = to_cores(downs)

    def reduce_tiles(tiles, scatter):
        held = tiles.reshape((2, 2) + tiles.shape[1:])
        held = half_sum(held, 0, core, "dp", 1)
        held = half_sum(held, 0, stream, "stream", 1)
        return reduce_zy(held, scatter)

    up_tiles = dup.reshape(4, zy, part, -1)
    up_own = reduce_tiles(up_tiles, 0).astype(BF16).reshape(2, part // 2, -1)
    keep = lax.dynamic_index_in_dim(up_own, core, 0, False)
    send = lax.dynamic_index_in_dim(up_own, 1 - core, 0, False)
    arrived = swap(send, "dp", 1)
    both = jnp.stack([jnp.where(core == 0, keep, arrived), jnp.where(core == 0, arrived, keep)], 1)
    both = paired(both, 2, stream, "stream", 1)
    grad_shared_up = both.reshape(part // 2, -1).astype(F32)

    down_full = jnp.swapaxes(ddown, 1, 2).reshape(shared_down.shape)
    grad_shared_down = reduce_copied(down_full)
    grad_qkv = reduce_copied(dqkv)
    grad_out_weight = reduce_copied(dout.astype(BF16))
    return (
        mixed, grad_patches, grad_embedding, grad_ada, grad_qkv, grad_out_weight, grad_shared_up,
        grad_shared_down, grad_router, grad_expert_up, grad_expert_down,
    )


def local(*arrays):
    if lax.axis_size("stream") == 2 and arrays[11].shape[0] % 2 == 0:
        return local_pair(*arrays)
    return local_general(*arrays)


def solution(mesh):
    return jax.shard_map(
        local,
        mesh=mesh,
        in_specs=(
            P(("dp", "stream"), None),
            P(("dp", "stream"), None),
            P(("dp", "stream")),
            P(("dp", "stream"), None),
            P(("dp", "stream"), None),
            P(),
            P(),
            P(),
            P(),
            P(),
            P(),
            P("stream", None, None),
            P("stream", None, None),
        ),
        out_specs=(
            P(("dp", "stream"), None),
            P(("dp", "stream"), None),
            P(("dp", "stream"), None),
            P("dp", None),
            P("dp", None),
            P("dp", None),
            P("dp", None),
            P("dp", None),
            P("dp", None),
            P("stream", "dp", None),
            P("stream", "dp", None),
        ),
        check_vma=False,
    )
```

```python
import functools
import math

import jax
import jax.numpy as jnp
from jax import lax
from jax.experimental import pallas as pl
from jax.experimental.pallas import tpu as pltpu
from jax.sharding import PartitionSpec as P

HEADS = 12
HEAD_DIM = 64
EXPERTS = 8
CAP = 288


HIGH = lax.Precision.HIGHEST
EPSILON = 1e-06
F32 = jnp.float32
BF16 = jnp.bfloat16
MIB = 1 << 20


def gelu_tanh(values):
    return jax.nn.gelu(values, approximate=True)


def normalize(values):
    centered = values - jnp.mean(values, -1, keepdims=True)
    spread = lax.rsqrt(jnp.mean(centered * centered, -1, keepdims=True) + EPSILON)
    return (centered * spread, spread)


def normalize_back(grad_normed, normed, spread):
    return spread * (
        grad_normed
        - jnp.mean(grad_normed, -1, keepdims=True)
        - normed * jnp.mean(grad_normed * normed, -1, keepdims=True)
    )


def split_packed(packed, seg_len):
    row_count = packed.shape[0]
    model_width = packed.shape[1] // 3
    groups = row_count // seg_len
    block_rows = min(512, seg_len)
    part_count = seg_len // block_rows
    queries = (
        packed[:, :model_width]
        .reshape(groups, part_count, block_rows, HEADS, HEAD_DIM)
        .swapaxes(0, 1)
    )
    key_heads = packed[:, model_width : 2 * model_width].reshape(groups, seg_len, HEADS, HEAD_DIM)
    values = packed[:, 2 * model_width :].reshape(groups, seg_len, HEADS, HEAD_DIM)
    return (queries, key_heads, values, groups, block_rows, part_count)


def attend(packed, seg_len):
    row_count = packed.shape[0]
    model_width = packed.shape[1] // 3
    factor = 1.0 / math.sqrt(HEAD_DIM)
    queries, key_heads, values, groups, block_rows, part_count = split_packed(packed, seg_len)

    def one_block(query_block):
        scores = (
            jnp.einsum(
                "gqhd,gkhd->ghqk", query_block, key_heads, preferred_element_type=jnp.float32
            )
            * factor
        )
        row_max = jnp.max(scores, -1, keepdims=True)
        shifted = jnp.exp(scores - row_max)
        row_sum = jnp.sum(shifted, -1, keepdims=True)
        weights = (shifted / row_sum).astype(jnp.bfloat16)
        mixture = jnp.einsum("ghqk,gkhd->gqhd", weights, values, preferred_element_type=jnp.float32)
        return (mixture, row_max[..., 0] + jnp.log(row_sum[..., 0]))

    mixture, logsum = lax.map(one_block, queries)
    return (mixture.swapaxes(0, 1).reshape(row_count, model_width), logsum.reshape(-1))


def attend_back(packed, logsum, grad_mixture, seg_len):
    row_count = packed.shape[0]
    model_width = packed.shape[1] // 3
    factor = 1.0 / math.sqrt(HEAD_DIM)
    queries, key_heads, values, groups, block_rows, part_count = split_packed(packed, seg_len)
    grad_blocks = grad_mixture.reshape(groups, part_count, block_rows, HEADS, HEAD_DIM).swapaxes(
        0, 1
    )
    logsum_blocks = logsum.reshape(part_count, groups, HEADS, block_rows)

    def one_block(carried, inputs):
        grad_keys, grad_values = carried
        query_block, grad_block, logsum_block = inputs
        scores = (
            jnp.einsum(
                "gqhd,gkhd->ghqk", query_block, key_heads, preferred_element_type=jnp.float32
            )
            * factor
        )
        prob_full = jnp.exp(scores - logsum_block[..., None])
        grad_values = grad_values + jnp.einsum(
            "ghqk,gqhd->gkhd",
            prob_full.astype(jnp.bfloat16),
            grad_block,
            preferred_element_type=jnp.float32,
        )
        grad_probs = jnp.einsum(
            "gqhd,gkhd->ghqk", grad_block, values, preferred_element_type=jnp.float32
        )
        row_inner = jnp.sum(grad_probs * prob_full, -1, keepdims=True)
        grad_scores = (prob_full * (grad_probs - row_inner)).astype(jnp.bfloat16)
        grad_query = (
            jnp.einsum(
                "ghqk,gkhd->gqhd", grad_scores, key_heads, preferred_element_type=jnp.float32
            )
            * factor
        )
        grad_keys = (
            grad_keys
            + jnp.einsum(
                "ghqk,gqhd->gkhd", grad_scores, query_block, preferred_element_type=jnp.float32
            )
            * factor
        )
        return ((grad_keys, grad_values), grad_query)

    zeros_kv = jnp.zeros((groups, seg_len, HEADS, HEAD_DIM), jnp.float32)
    (grad_keys, grad_values), grad_query = lax.scan(
        one_block, (zeros_kv, zeros_kv), (queries, grad_blocks, logsum_blocks)
    )
    return jnp.concatenate(
        [
            grad_query.swapaxes(0, 1).reshape(row_count, model_width),
            grad_keys.reshape(row_count, model_width),
            grad_values.reshape(row_count, model_width),
        ],
        1,
    )


def local_general(
    patches,
    embedding,
    long_image,
    routes,
    cotangent,
    ada_weight,
    qkv_weight,
    out_weight,
    shared_up,
    shared_down,
    router_weight,
    expert_up,
    expert_down,
):
    row_count, model_width = patches.shape
    block_count = embedding.shape[0]
    short_len = row_count // block_count
    lane_count = lax.axis_size("stream")
    local_experts = expert_up.shape[0]
    is_long = long_image[0] > 0

    def blocks(values):
        return values.reshape(block_count, short_len, model_width)

    def flatten(values):
        return values.reshape(row_count, model_width)

    used = jnp.where(is_long, jnp.broadcast_to(embedding[0:1], embedding.shape), embedding)
    activated, silu_back = jax.vjp(jax.nn.silu, used)
    ada_full = ada_weight.astype(jnp.float32)
    modulation = jnp.dot(activated, ada_full, precision=HIGH)
    pieces = [
        modulation[:, column * model_width : (column + 1) * model_width][:, None, :]
        for column in range(6)
    ]
    shift_one, scale_one, gate_one, shift_two, scale_two, gate_two = pieces
    inputs_full = blocks(patches.astype(jnp.float32))
    normed_one, spread_one = normalize(inputs_full)
    hidden_one = flatten(normed_one * (1.0 + scale_one) + shift_one).astype(jnp.bfloat16)
    packed = jnp.dot(hidden_one, qkv_weight, preferred_element_type=jnp.float32).astype(
        jnp.bfloat16
    )
    attended, logsum = lax.cond(
        is_long,
        lambda packed_in: attend(packed_in, row_count),
        lambda packed_in: attend(packed_in, short_len),
        packed,
    )
    attended_low = attended.astype(jnp.bfloat16)
    branch_one = blocks(jnp.dot(attended_low, out_weight, preferred_element_type=jnp.float32))
    middle = inputs_full + gate_one * branch_one
    normed_two, spread_two = normalize(middle)
    hidden_two = flatten(normed_two * (1.0 + scale_two) + shift_two).astype(jnp.bfloat16)
    shared_pre = jnp.dot(hidden_two, shared_up, preferred_element_type=jnp.float32)
    shared_act, shared_back = jax.vjp(gelu_tanh, shared_pre)
    shared_low = shared_act.astype(jnp.bfloat16)
    shared_out = jnp.dot(shared_low, shared_down, preferred_element_type=jnp.float32)
    logits = jnp.dot(hidden_two, router_weight, preferred_element_type=jnp.float32)
    chosen_hot = (routes[:, :, None] == jnp.arange(EXPERTS)[None, None, :]).astype(jnp.float32)
    gates = jax.nn.softmax(jnp.sum(chosen_hot * logits[:, None, :], -1), -1)
    flat_routes = routes.reshape(-1)
    route_hits = (flat_routes[:, None] == jnp.arange(EXPERTS)[None, :]).astype(jnp.int32)
    earlier = jnp.cumsum(route_hits, 0) - route_hits
    target = flat_routes * CAP + jnp.sum(earlier * route_hits, 1)

    def spread_rows(rows_low):
        buffer = jnp.zeros((EXPERTS * CAP, model_width), jnp.bfloat16).at[target].set(rows_low)
        return buffer.reshape(lane_count, local_experts, CAP, model_width)

    def collect(arrived):
        return (
            arrived.reshape(EXPERTS * CAP, model_width)[target]
            .astype(jnp.float32)
            .reshape(row_count, 2, model_width)
        )

    def by_expert(arrived):
        return arrived.swapaxes(0, 1).reshape(local_experts, lane_count * CAP, model_width)

    def by_source(results):
        return results.reshape(local_experts, lane_count, CAP, model_width).swapaxes(0, 1)

    expert_in = by_expert(
        lax.all_to_all(
            spread_rows(jnp.repeat(hidden_two, 2, axis=0)),
            "stream",
            split_axis=0,
            concat_axis=0,
            tiled=True,
        )
    )
    expert_pre = jnp.einsum(
        "jrd,jdf->jrf", expert_in, expert_up, preferred_element_type=jnp.float32
    )
    expert_act, expert_back = jax.vjp(gelu_tanh, expert_pre)
    expert_low = expert_act.astype(jnp.bfloat16)
    expert_out = jnp.einsum(
        "jrf,jfd->jrd", expert_low, expert_down, preferred_element_type=jnp.float32
    ).astype(jnp.bfloat16)
    picked = collect(
        lax.all_to_all(by_source(expert_out), "stream", split_axis=0, concat_axis=0, tiled=True)
    )
    routed = jnp.sum(gates[:, :, None] * picked, 1)
    branch_two = blocks(shared_out + routed)
    mixed = flatten(middle + gate_two * branch_two).astype(jnp.bfloat16)
    grad_top = blocks(cotangent.astype(jnp.float32))
    grad_gate_two = jnp.sum(grad_top * branch_two, 1)
    grad_branch = flatten(grad_top * gate_two)
    grad_pick = (
        (gates[:, :, None] * grad_branch[:, None, :])
        .astype(jnp.bfloat16)
        .reshape(2 * row_count, model_width)
    )
    grad_arrived = by_expert(
        lax.all_to_all(spread_rows(grad_pick), "stream", split_axis=0, concat_axis=0, tiled=True)
    )
    grad_expert_down = jnp.einsum(
        "jrf,jrd->jfd", expert_low, grad_arrived, preferred_element_type=jnp.float32
    )
    grad_expert_act = jnp.einsum(
        "jrd,jfd->jrf", grad_arrived, expert_down, preferred_element_type=jnp.float32
    )
    grad_expert_pre = expert_back(grad_expert_act)[0].astype(jnp.bfloat16)
    grad_expert_up = jnp.einsum(
        "jrd,jrf->jdf", expert_in, grad_expert_pre, preferred_element_type=jnp.float32
    )
    grad_expert_in = jnp.einsum(
        "jrf,jdf->jrd", grad_expert_pre, expert_up, preferred_element_type=jnp.float32
    ).astype(jnp.bfloat16)
    grad_routed = jnp.sum(
        collect(
            lax.all_to_all(
                by_source(grad_expert_in), "stream", split_axis=0, concat_axis=0, tiled=True
            )
        ),
        1,
    )
    grad_shared_low = grad_branch.astype(jnp.bfloat16)
    grad_shared_down = jnp.einsum(
        "rf,rd->fd", shared_low, grad_shared_low, preferred_element_type=jnp.float32
    )
    grad_shared_act = jnp.einsum(
        "rd,fd->rf", grad_shared_low, shared_down, preferred_element_type=jnp.float32
    )
    grad_shared_pre = shared_back(grad_shared_act)[0].astype(jnp.bfloat16)
    grad_shared_up = jnp.einsum(
        "rd,rf->df", hidden_two, grad_shared_pre, preferred_element_type=jnp.float32
    )
    grad_gates = jnp.sum(picked * grad_branch[:, None, :], -1)
    grad_chosen = gates * (grad_gates - jnp.sum(gates * grad_gates, -1, keepdims=True))
    grad_logits = jnp.sum(chosen_hot * grad_chosen[:, :, None], 1)
    hidden_two_full = hidden_two.astype(jnp.float32)
    router_full = router_weight.astype(jnp.float32)
    grad_router = jnp.dot(hidden_two_full.T, grad_logits, precision=HIGH)
    grad_hidden = jnp.dot(grad_logits, router_full.T, precision=HIGH) + grad_routed
    grad_hidden = blocks(
        grad_hidden
        + jnp.einsum("rf,df->rd", grad_shared_pre, shared_up, preferred_element_type=jnp.float32)
    )
    grad_shift_two = jnp.sum(grad_hidden, 1)
    grad_scale_two = jnp.sum(grad_hidden * normed_two, 1)
    grad_middle = grad_top + normalize_back(grad_hidden * (1.0 + scale_two), normed_two, spread_two)
    grad_gate_one = jnp.sum(grad_middle * branch_one, 1)
    grad_branch_one = flatten(grad_middle * gate_one).astype(jnp.bfloat16)
    grad_out_weight = jnp.einsum(
        "rd,re->de", attended_low, grad_branch_one, preferred_element_type=jnp.float32
    )
    grad_attended = jnp.einsum(
        "re,de->rd", grad_branch_one, out_weight, preferred_element_type=jnp.float32
    ).astype(jnp.bfloat16)
    grad_packed = lax.cond(
        is_long,
        lambda packed_in, logsum_in, grad_in: attend_back(packed_in, logsum_in, grad_in, row_count),
        lambda packed_in, logsum_in, grad_in: attend_back(packed_in, logsum_in, grad_in, short_len),
        packed,
        logsum,
        grad_attended,
    ).astype(jnp.bfloat16)
    grad_qkv = jnp.einsum("rd,re->de", hidden_one, grad_packed, preferred_element_type=jnp.float32)
    grad_hidden_one = blocks(
        jnp.einsum("re,de->rd", grad_packed, qkv_weight, preferred_element_type=jnp.float32)
    )
    grad_shift_one = jnp.sum(grad_hidden_one, 1)
    grad_scale_one = jnp.sum(grad_hidden_one * normed_one, 1)
    grad_inputs = grad_middle + normalize_back(
        grad_hidden_one * (1.0 + scale_one), normed_one, spread_one
    )
    grad_modulation = jnp.concatenate(
        [
            grad_shift_one,
            grad_scale_one,
            grad_gate_one,
            grad_shift_two,
            grad_scale_two,
            grad_gate_two,
        ],
        1,
    )
    grad_ada = jnp.dot(activated.T, grad_modulation, precision=HIGH)
    grad_used = silu_back(jnp.dot(grad_modulation, ada_full.T, precision=HIGH))[0]
    grad_embedding = jnp.where(
        is_long, jnp.zeros_like(grad_used).at[0].set(jnp.sum(grad_used, 0)), grad_used
    )
    shares = (
        lax.psum_scatter(
            grad_ada.astype(jnp.bfloat16), "dp", scatter_dimension=0, tiled=True
        ).astype(jnp.float32),
        lax.psum_scatter(
            grad_qkv.astype(jnp.bfloat16), "dp", scatter_dimension=0, tiled=True
        ).astype(jnp.float32),
        lax.psum_scatter(
            grad_out_weight.astype(jnp.bfloat16), "dp", scatter_dimension=0, tiled=True
        ).astype(jnp.float32),
        lax.psum_scatter(
            grad_shared_up.astype(jnp.bfloat16), "dp", scatter_dimension=0, tiled=True
        ).astype(jnp.float32),
        lax.psum_scatter(
            grad_shared_down.astype(jnp.bfloat16), "dp", scatter_dimension=0, tiled=True
        ).astype(jnp.float32),
        lax.psum_scatter(
            grad_router.astype(jnp.bfloat16), "dp", scatter_dimension=0, tiled=True
        ).astype(jnp.float32),
    )
    expert_summed = (
        lax.psum_scatter(
            grad_expert_up.astype(jnp.bfloat16), "dp", scatter_dimension=1, tiled=True
        ).astype(jnp.float32),
        lax.psum_scatter(
            grad_expert_down.astype(jnp.bfloat16), "dp", scatter_dimension=1, tiled=True
        ).astype(jnp.float32),
    )
    summed = (
        lax.psum(shares[0].astype(jnp.bfloat16), "stream").astype(jnp.float32),
        lax.psum(shares[1].astype(jnp.bfloat16), "stream").astype(jnp.float32),
        lax.psum(shares[2].astype(jnp.bfloat16), "stream").astype(jnp.float32),
        lax.psum(shares[3].astype(jnp.bfloat16), "stream").astype(jnp.float32),
        lax.psum(shares[4].astype(jnp.bfloat16), "stream").astype(jnp.float32),
        lax.psum(shares[5].astype(jnp.bfloat16), "stream").astype(jnp.float32),
    )
    return (
        mixed,
        flatten(grad_inputs),
        grad_embedding,
        summed[0],
        summed[1],
        summed[2],
        summed[3],
        summed[4],
        summed[5],
        expert_summed[0],
        expert_summed[1],
    )


def nn(left, right):
    return jnp.dot(left, right, preferred_element_type=F32)


def nt(left, right):
    return lax.dot_general(left, right, (((1,), (1,)), ((), ())), preferred_element_type=F32)


def tn(left, right):
    return lax.dot_general(left, right, (((0,), (0,)), ((), ())), preferred_element_type=F32)


def three_parts(values):
    first = values.astype(BF16)
    rest = values - first.astype(F32)
    second = rest.astype(BF16)
    third = (rest - second.astype(F32)).astype(BF16)
    return first, second, third


def sigmoid(values):
    return 1.0 / (1.0 + jnp.exp(-values))


def gelu_and_slope(values):
    inner = math.sqrt(2.0 / math.pi)
    square = values * values
    bend = jnp.tanh(values * (inner + (inner * 0.044715) * square))
    half = 0.5 + 0.5 * bend
    slope = half + values * (0.5 - 0.5 * bend * bend) * (inner + (3.0 * inner * 0.044715) * square)
    return values * half, slope


def run(kernel, args, grid, in_specs, out_specs, out_shape, name, scalars=(), scratch=(), after=(), limit=56):
    count = len(scalars) + len(args)

    def body(*refs):
        kernel(*refs[:count], *refs[count + len(after) :])

    return pl.pallas_call(
        body,
        grid_spec=pltpu.PrefetchScalarGridSpec(
            num_scalar_prefetch=len(scalars),
            grid=grid,
            in_specs=list(in_specs) + [pl.BlockSpec(memory_space=pl.ANY)] * len(after),
            out_specs=out_specs,
            scratch_shapes=list(scratch),
        ),
        out_shape=out_shape,
        compiler_params=pltpu.CompilerParams(vmem_limit_bytes=limit * MIB),
        cost_estimate=pl.CostEstimate(flops=1000, bytes_accessed=1000, transcendentals=0),
        name=name,
    )(*scalars, *args, *after)


def full(shape):
    return pl.BlockSpec(shape, lambda *_: (0,) * len(shape))


def like(array):
    return full(array.shape)


def rows_spec(rows, width):
    return pl.BlockSpec((rows, width), lambda i, *_: (i, 0))


def shape(dims, dtype):
    return jax.ShapeDtypeStruct(tuple(dims), dtype)


LONG, CORE, STREAM, ROW_Y, ROW_Z, FIRST_HERE, FIRST_ALL = range(7)


def flipped(value, bits):
    total = 0
    for bit in range(bits):
        total = total + (((value >> bit) & 1) << (bits - 1 - bit))
    return total


def modulate_kernel(blocks, pos_ref, emb_ref, ada_ref, cot_ref, mod_ref, act_ref, branch_ref):
    emb = emb_ref[...]
    used = jnp.where(pos_ref[LONG] > 0, jnp.broadcast_to(emb[0:1], emb.shape), emb)
    act = used * sigmoid(used)
    act_ref[...] = act
    weight = ada_ref[...]
    total = 0.0
    for part in three_parts(act):
        total = total + nn(part, weight)
    mod_ref[0] = total

    @pl.when(pl.program_id(0) == pl.num_programs(0) - 1)
    def _():
        short = cot_ref.shape[0] // blocks
        for block in range(blocks):
            span = slice(block * short, (block + 1) * short)
            branch_ref[span, :] = (cot_ref[span, :].astype(F32) * total[block : block + 1]).astype(BF16)


def modulate(pos, emb_pad, ada_weight, cot, blocks):
    rows, width = emb_pad.shape
    pieces = ada_weight.shape[1] // width
    return run(
        functools.partial(modulate_kernel, blocks), (emb_pad, ada_weight, cot), (pieces,),
        [like(emb_pad), pl.BlockSpec((width, width), lambda i, *_: (0, i)), like(cot)],
        [pl.BlockSpec((1, rows, width), lambda i, *_: (i, 0, 0)), like(emb_pad), like(cot)],
        [shape((pieces, rows, width), F32), shape((rows, width), F32), shape(cot.shape, BF16)],
        "modulate", scalars=(pos,),
    )


def norm_parts(values):
    centered = values - jnp.mean(values, -1, keepdims=True)
    spread = lax.rsqrt(jnp.mean(centered * centered, -1, keepdims=True) + EPSILON)
    return centered * spread, spread


def norm_back(grad, normed, spread):
    return spread * (
        grad
        - jnp.mean(grad, -1, keepdims=True)
        - normed * jnp.mean(grad * normed, -1, keepdims=True)
    )


def qkv_kernel(x_ref, mod_ref, w_ref, packed_ref):
    block = pl.program_id(0)
    normed, _ = norm_parts(x_ref[...].astype(F32))
    shift, scale = mod_ref[0, pl.ds(block, 1), :], mod_ref[1, pl.ds(block, 1), :]
    hidden = (normed * (1.0 + scale) + shift).astype(BF16)
    packed_ref[...] = nn(hidden, w_ref[...]).astype(BF16)


def qkv_forward(patches, mod, weight, blocks, after):
    rows, width = patches.shape
    short = rows // blocks
    wide = weight.shape[1]
    return run(
        qkv_kernel, (patches, mod, weight), (blocks,),
        [rows_spec(short, width), like(mod), like(weight)], rows_spec(short, wide),
        shape((rows, wide), BF16), "qkv", after=after,
    )


def attend_kernel(short, pos_ref, q_ref, k_ref, v_ref, o_ref, lse_ref):
    rows, lanes = q_ref.shape
    first = lax.broadcasted_iota(jnp.int32, (1, lanes), 1) < HEAD_DIM
    factor = 1.0 / math.sqrt(HEAD_DIM)

    def part(query_at, key_at, key_count):
        queries = q_ref[query_at : query_at + short, :]
        keys = k_ref[key_at : key_at + key_count, :]
        values = v_ref[key_at : key_at + key_count, :]
        zero = jnp.zeros_like(queries)
        outs, sums = [], []
        for mine in (first, jnp.logical_not(first)):
            scores = nt(jnp.where(mine, queries, zero), keys) * factor
            top = jnp.max(scores, -1, keepdims=True)
            shifted = jnp.exp(scores - top)
            total = jnp.sum(shifted, -1, keepdims=True)
            outs.append(nn(shifted.astype(BF16), values) * (1.0 / total))
            sums.append(top + jnp.log(total))
        o_ref[query_at : query_at + short, :] = jnp.where(first, outs[0], outs[1]).astype(BF16)
        lse_ref[query_at : query_at + short, :] = jnp.where(first, sums[0], sums[1])

    @pl.when(pos_ref[LONG] > 0)
    def _():
        for at in range(0, rows, short):
            part(at, 0, rows)

    @pl.when(pos_ref[LONG] <= 0)
    def _():
        for at in range(0, rows, short):
            part(at, at, short)


def pair_specs(rows, width):
    lanes = 2 * HEAD_DIM
    pairs = width // lanes
    return [
        pl.BlockSpec((rows, lanes), functools.partial(lambda shift, i, *_: (0, i + shift), shift))
        for shift in (0, pairs, 2 * pairs)
    ]


def attend_forward(pos, packed, short):
    rows = packed.shape[0]
    width = packed.shape[1] // 3
    spec = pair_specs(rows, width)
    return run(
        functools.partial(attend_kernel, short), (packed, packed, packed), (width // (2 * HEAD_DIM),),
        spec, [spec[0], spec[0]], [shape((rows, width), BF16), shape((rows, width), F32)],
        "attend", scalars=(pos,),
    )


def attend_back_kernel(
    short, pos_ref, q_ref, k_ref, v_ref, o_ref, lse_ref, do_ref, dq_ref, dk_ref, dv_ref,
    dk_acc, dv_acc,
):
    rows, lanes = q_ref.shape
    first = lax.broadcasted_iota(jnp.int32, (1, lanes), 1) < HEAD_DIM
    factor = 1.0 / math.sqrt(HEAD_DIM)
    product = do_ref[...].astype(F32) * o_ref[...].astype(F32)
    lse_t = jnp.transpose(lse_ref[...])
    product_t = jnp.transpose(product)
    lse_rows = [lse_t[0:1], lse_t[HEAD_DIM : HEAD_DIM + 1]]
    delta_rows = [
        jnp.sum(product_t[:HEAD_DIM], 0, keepdims=True),
        jnp.sum(product_t[HEAD_DIM:], 0, keepdims=True),
    ]

    def part(query_at, key_at, key_count, fresh):
        chunk = slice(query_at, query_at + short)
        span = slice(key_at, key_at + key_count)
        queries, grads = q_ref[chunk, :], do_ref[chunk, :]
        keys, values = k_ref[span, :], v_ref[span, :]
        zero, zero_keys = jnp.zeros_like(queries), jnp.zeros_like(keys)
        dq = dk = dv = 0.0
        for head, mine in enumerate((first, jnp.logical_not(first))):
            query_own = jnp.where(mine, queries, zero)
            grad_own = jnp.where(mine, grads, zero)
            key_own = jnp.where(mine, keys, zero_keys)
            scores = nt(keys, query_own) * factor
            probs = jnp.exp(scores - lse_rows[head][:, chunk])
            grad_probs = nt(values, grad_own)
            grad_scores = (probs * (grad_probs - delta_rows[head][:, chunk])).astype(BF16)
            dv = dv + nn(probs.astype(BF16), grad_own)
            dk = dk + nn(grad_scores, query_own)
            dq = dq + tn(grad_scores, key_own)
        dq_ref[chunk, :] = (dq * factor).astype(BF16)
        if fresh:
            dk_acc[span, :] = dk
            dv_acc[span, :] = dv
        else:
            dk_acc[span, :] += dk
            dv_acc[span, :] += dv

    @pl.when(pos_ref[LONG] > 0)
    def _():
        for at in range(0, rows, short):
            part(at, 0, rows, at == 0)

    @pl.when(pos_ref[LONG] <= 0)
    def _():
        for at in range(0, rows, short):
            part(at, at, short, True)

    dk_ref[...] = (dk_acc[...] * factor).astype(BF16)
    dv_ref[...] = dv_acc[...].astype(BF16)


def attend_backward(pos, packed, attended, logsum, grad, short, after):
    rows, width = attended.shape
    lanes = 2 * HEAD_DIM
    spec = pair_specs(rows, width)
    return run(
        functools.partial(attend_back_kernel, short),
        (packed, packed, packed, attended, logsum, grad), (width // lanes,),
        spec + [spec[0]] * 3, [spec[0]] * 3, [shape((rows, width), BF16)] * 3,
        "attend_back", scalars=(pos,), scratch=[pltpu.VMEM((rows, lanes), F32)] * 2, after=after,
    )


def middle_kernel(att_ref, x_ref, mod_ref, w_ref, branch_ref, hidden_ref):
    block = pl.program_id(0)
    branch = nn(att_ref[...], w_ref[...])
    branch_ref[...] = branch
    middle = x_ref[...].astype(F32) + mod_ref[2, pl.ds(block, 1), :] * branch
    normed, _ = norm_parts(middle)
    shift, scale = mod_ref[3, pl.ds(block, 1), :], mod_ref[4, pl.ds(block, 1), :]
    hidden_ref[...] = (normed * (1.0 + scale) + shift).astype(BF16)


def middle_forward(attended, patches, mod, out_weight, blocks, after):
    rows, width = patches.shape
    tile = rows_spec(rows // blocks, width)
    return run(
        middle_kernel, (attended, patches, mod, out_weight), (blocks,),
        [tile, tile, like(mod), like(out_weight)], [tile, tile],
        [shape((rows, width), F32), shape((rows, width), BF16)], "middle", after=after,
    )


def rank_kernel(pos_ref, *refs):
    count = (len(refs) - 2) // 1
    routes, (row_ref, col_ref) = refs[:count], refs[count:]
    rows = routes[0].shape[1]
    before = lax.broadcasted_iota(jnp.int32, (rows, rows), 0)
    after = lax.broadcasted_iota(jnp.int32, (rows, rows), 1)
    upper = (before < after).astype(F32).astype(BF16)
    ids = pos_ref[FIRST_ALL] + lax.broadcasted_iota(jnp.int32, (8, rows), 0)
    for source, ref in enumerate(routes):
        hits = jnp.logical_or(ref[0:1, :] == ids, ref[1:2, :] == ids)
        earlier = nn(hits.astype(F32).astype(BF16), upper)
        rank = jnp.where(hits, earlier, -1.0)
        row_ref[source] = rank.astype(jnp.int32)
        tall = jnp.concatenate([rank, jnp.full((120, rows), -1.0, F32)], 0)
        col_ref[source] = jnp.transpose(tall).astype(jnp.int32)


def ranks(pos, routes, after):
    count, rows = len(routes), routes[0].shape[1]
    out = [shape((count, 8, rows), jnp.int32), shape((count, rows, 128), jnp.int32)]
    return run(
        rank_kernel, routes, (1,), [like(a) for a in routes], [like(a) for a in out], out, "ranks",
        scalars=(pos,), after=after,
    )


def touch(array, after):
    count = len(after)

    def body(*refs):
        del refs

    return pl.pallas_call(
        body,
        in_specs=[pl.BlockSpec(memory_space=pl.ANY)] * (1 + count),
        out_specs=pl.BlockSpec(memory_space=pl.ANY),
        out_shape=shape(array.shape, array.dtype),
        input_output_aliases={0: 0},
        name="touch",
    )(array, *after)


def gate_rows(hidden, routes, router_t, ids):
    logits = nt(router_t, hidden)
    every = lax.broadcasted_iota(jnp.int32, logits.shape, 0)
    first, second = routes[0:1, :], routes[1:2, :]
    zero = jnp.zeros_like(logits)
    logit_one = jnp.sum(jnp.where(every == first, logits, zero), 0, keepdims=True)
    logit_two = jnp.sum(jnp.where(every == second, logits, zero), 0, keepdims=True)
    gate_one = sigmoid(logit_one - logit_two)
    gate_two = sigmoid(logit_two - logit_one)
    return jnp.where(ids == first, gate_one, 0.0) + jnp.where(ids == second, gate_two, 0.0)


def ffn_phase_one(x, g, up_ref, down_ref, act_ref, pre_ref, step=256):
    wide = act_ref.shape[1]
    for at in range(0, wide, step):
        cols = slice(at, at + step)
        act, slope = gelu_and_slope(nn(x, up_ref[0, :, cols]))
        back = nt(g, down_ref[0, cols, :])
        act_ref[:, cols] = act.astype(BF16)
        pre_ref[:, cols] = (back * slope).astype(BF16)


def relative_rows(pos_ref, target, values, nz):
    bits = nz.bit_length() - 1
    part = values.shape[0] // (2 * nz)
    for block in range(2 * nz):
        place = (block % 2) ^ pos_ref[ROW_Y]
        place = place * nz + flipped((block // 2) ^ pos_ref[ROW_Z], bits)
        at = pl.multiple_of(place * part, part)
        target[pl.ds(at, part), :] = values[block * part : (block + 1) * part]


def sides(pos_ref, values):
    half = values.shape[1] // 2
    low, high = values[:, :half], values[:, half:]
    own_low = pos_ref[ROW_Y] == 0
    return jnp.where(own_low, low, high), jnp.where(own_low, high, low)


def expert_kernel(
    slot, sends, has_prior, pos_ref, h0_ref, h1_ref, g0_ref, g1_ref, rank_ref, routes0_ref, routes1_ref,
    router_ref, up_ref, down_ref, *rest,
):
    count = 1 + sends
    priors, rest = (rest[:count], rest[count:]) if has_prior else ((), rest)
    targets, rest = rest[:count], rest[count:]
    keep_ref = targets[0]
    (out_ref, gx_ref, gg_ref,
     x_s, xt_s, g_s, gt_s, b_s, gate_s, act_s, pre_s, out_acc, gx_acc) = rest
    tile = pl.program_id(0)
    last = pl.num_programs(0) - 1
    rows = h0_ref.shape[0]
    nz = keep_ref.shape[2] // keep_ref.shape[3] * 2
    part = h0_ref.shape[1] // (2 * nz)
    own = lax.broadcasted_iota(jnp.int32, (CAP, rows), 0)

    def hot(source):
        return (own == rank_ref[source, slot : slot + 1, :]).astype(F32)

    @pl.when(tile == 0)
    def _():
        sources = ((h0_ref, g0_ref, routes0_ref), (h1_ref, g1_ref, routes1_ref))
        for source, (h_ref, b_ref, routes_ref) in enumerate(sources):
            span = slice(source * CAP, (source + 1) * CAP)
            pick = hot(source)
            pick_low = pick.astype(BF16)
            expert = pos_ref[FIRST_ALL] + slot
            gate = gate_rows(h_ref[...], routes_ref[...], router_ref[...], expert)
            gate_col = jnp.sum(pick * gate[0:1], -1, keepdims=True)
            branch = nn(pick_low, b_ref[...])
            x_s[span, :] = nn(pick_low, h_ref[...]).astype(BF16)
            b_s[span, :] = branch.astype(BF16)
            g_s[span, :] = (branch * gate_col).astype(BF16)
            gate_s[span, :] = jnp.broadcast_to(gate_col, (CAP, 128))
        relative_rows(pos_ref, xt_s, jnp.transpose(x_s[...]), nz)
        gt_s[...] = jnp.transpose(g_s[...])
        out_acc[...] = jnp.zeros_like(out_acc)
        gx_acc[...] = jnp.zeros_like(gx_acc)

    ffn_phase_one(x_s[...], g_s[...], up_ref, down_ref, act_s, pre_s)
    act, pre = act_s[...], pre_s[...]
    out_acc[...] += nn(act, down_ref[0])
    gx_acc[...] += nt(pre, up_ref[0])

    def place(side, kind):
        return (0, kind) if side == 0 else (1, kind) if sends == 1 else (1 + kind, 0)

    dup = nn(xt_s[...], pre)
    half = dup.shape[1] // 2
    for side in range(2):
        at, entry = place(side, 0)
        for z in range(nz):
            for lanes in range(2):
                row, into = (side * nz + z) * part, (z * 2 + lanes) * part
                piece = dup[row : row + part, lanes * half : (lanes + 1) * half]
                if has_prior:
                    piece = piece + priors[at][0, entry, into : into + part, :].astype(F32)
                targets[at][0, entry, into : into + part, :] = piece.astype(BF16)
    for side, piece in enumerate(sides(pos_ref, nn(gt_s[...], act))):
        at, entry = place(side, 1)
        if has_prior:
            piece = piece + priors[at][0, entry].astype(F32)
        targets[at][0, entry] = piece.astype(BF16)

    @pl.when(tile == last)
    def _():
        for source in range(2):
            span = slice(source * CAP, (source + 1) * CAP)
            out = out_acc[span, :]
            out_ref[source] = (out * gate_s[span, 0:1]).astype(BF16)
            gx_ref[source] = gx_acc[span, :].astype(BF16)
            inner = jnp.sum(out * b_s[span, :].astype(F32), -1, keepdims=True)
            gg_ref[source] = jnp.sum(hot(source) * inner, 0, keepdims=True)


def expert_call(
    slot, sends, pos, hiddens, branches, rank_rows, routes, router_t, up, down, prior, nz, after
):
    rows, width = hiddens[0].shape
    wide = up.shape[2]
    tile = wide // nz
    bits = nz.bit_length() - 1
    count = 2 * CAP
    weights = [
        pl.BlockSpec((1, width, tile), lambda f, s: (s[FIRST_HERE] + slot, 0, f)),
        pl.BlockSpec((1, tile, width), lambda f, s: (s[FIRST_HERE] + slot, f, 0)),
    ]
    kinds = [2, 2] if sends == 1 else [2, 1, 1]
    grads = [
        pl.BlockSpec((1, kind, width, tile // 2), lambda f, s: (flipped(f ^ s[ROW_Z], bits), 0, 0, 0))
        for kind in kinds
    ]
    once = [*hiddens, *branches, rank_rows, *routes, router_t]
    out_shape = (
        [shape((nz, kind, width, tile // 2), BF16) for kind in kinds]
        + [shape((2, CAP, width), BF16)] * 2
        + [shape((2, 1, rows), F32)]
    )
    prior = () if prior is None else tuple(prior)
    return run(
        functools.partial(expert_kernel, slot, sends, bool(prior)), (*once, up, down, *prior), (nz,),
        [like(a) for a in once] + weights + (grads if prior else []),
        grads + [like(a) for a in out_shape[len(grads) :]], out_shape, "expert", scalars=(pos,), after=after,
        scratch=[
            pltpu.VMEM((count, width), BF16),
            pltpu.VMEM((width, count), BF16),
            pltpu.VMEM((count, width), BF16),
            pltpu.VMEM((width, count), BF16),
            pltpu.VMEM((count, width), BF16),
            pltpu.VMEM((count, 128), F32),
            pltpu.VMEM((count, tile), BF16),
            pltpu.VMEM((count, tile), BF16),
            pltpu.VMEM((count, width), F32),
            pltpu.VMEM((count, width), F32),
        ],
    )


def shared_kernel(
    pos_ref, h_ref, b_ref, up_ref, down_ref, ku_ref, su_ref, kd_ref, sd_ref, out_ref, gx_ref,
    xt_s, gt_s, act_s, pre_s,
):
    step = pl.program_id(0)
    nz, block = 4, kd_ref.shape[3]

    @pl.when(step == 0)
    def _():
        relative_rows(pos_ref, xt_s, jnp.transpose(h_ref[...]), nz)
        turned = jnp.transpose(b_ref[...])
        for slice_at in range(4):
            place = ((slice_at % 2) ^ pos_ref[CORE]) * 2 + ((slice_at // 2) ^ pos_ref[STREAM])
            at = pl.multiple_of(place * block, block)
            gt_s[pl.ds(at, block), :] = turned[slice_at * block : (slice_at + 1) * block]
        out_ref[...] = jnp.zeros_like(out_ref)
        gx_ref[...] = jnp.zeros_like(gx_ref)

    ffn_phase_one(h_ref[...], b_ref[...], up_ref, down_ref, act_s, pre_s)
    act, pre = act_s[...], pre_s[...]
    out_ref[...] += nn(act, down_ref[0])
    gx_ref[...] += nt(pre, up_ref[0])
    dup = nn(xt_s[...], pre).astype(BF16)

    @pl.when(step < 2)
    def _():
        ku_ref[0] = dup

    @pl.when(step >= 2)
    def _():
        su_ref[0] = dup

    for y, piece in enumerate(sides(pos_ref, nn(gt_s[...], act))):
        for place, ref in ((0, kd_ref), (1, kd_ref), (2, sd_ref), (3, sd_ref)):
            ref[place % 2, y, 0] = piece[place * block : (place + 1) * block].astype(BF16)


def shared_call(pos, hidden, branch, up, down, after):
    rows, width = hidden.shape
    wide = up.shape[1]
    nz = 4
    tile = wide // nz
    block = width // 4

    def unit(f, s):
        return (f % 2 ^ s[STREAM]) * 2 + (f // 2 ^ s[CORE])

    keep = pl.BlockSpec((1, width, tile), lambda f, s: (jnp.minimum(f, 1), 0, 0))
    send = pl.BlockSpec((1, width, tile), lambda f, s: (jnp.maximum(f - 2, 0), 0, 0))
    downs = pl.BlockSpec(
        (2, 2, 1, block, tile // 2), lambda f, s: (0, 0, flipped(unit(f, s) ^ s[ROW_Z], 2), 0, 0)
    )
    return run(
        shared_kernel, (hidden, branch, up[None], down[None]), (nz,),
        [
            like(hidden),
            like(branch),
            pl.BlockSpec((1, width, tile), lambda f, s: (0, 0, unit(f, s))),
            pl.BlockSpec((1, tile, width), lambda f, s: (0, unit(f, s), 0)),
        ],
        [keep, send, downs, downs, like(hidden), like(hidden)],
        [shape((2, width, tile), BF16)] * 2
        + [shape((2, 2, nz, block, tile // 2), BF16)] * 2
        + [shape((rows, width), F32)] * 2,
        "shared", scalars=(pos,), after=after,
        scratch=[
            pltpu.VMEM((width, rows), BF16),
            pltpu.VMEM((width, rows), BF16),
            pltpu.VMEM((rows, tile), BF16),
            pltpu.VMEM((rows, tile), BF16),
        ],
    )


def combine_kernel(slots, col_ref, *refs):
    rows_refs, refs = refs[: 2 * slots], refs[2 * slots :]
    targets, stacks = refs[:4], refs[4:]

    @pl.when(pl.program_id(0) == 0)
    def _():
        for slot in range(slots):
            for kind in range(2):
                for source in range(2):
                    stacks[kind][source, slot * CAP : (slot + 1) * CAP, :] = rows_refs[2 * slot + kind][source]

    block = col_ref.shape[1]
    own = lax.broadcasted_iota(jnp.int32, (block, slots * CAP), 1)
    for source in range(2):
        hits = None
        for slot in range(slots):
            rank = col_ref[source, :, slot : slot + 1]
            place = jnp.where(rank < 0, -1, rank + slot * CAP)
            hit = place == own
            hits = hit if hits is None else jnp.logical_or(hits, hit)
        pick = hits.astype(F32).astype(BF16)
        for kind in range(2):
            targets[2 * kind + source][...] = nn(pick, stacks[kind][source]).astype(BF16)


def combine(rank_cols, pairs, after):
    count, rows, _ = rank_cols.shape
    width = pairs[0][0].shape[2]
    block = rows // 4
    flat = [a for pair in pairs for a in pair]
    return run(
        functools.partial(combine_kernel, len(pairs)), (rank_cols, *flat), (rows // block,),
        [pl.BlockSpec((count, block, 128), lambda i: (0, i, 0))] + [like(a) for a in flat],
        [rows_spec(block, width)] * 4, [shape((rows, width), BF16)] * 4, "combine",
        scratch=[pltpu.VMEM((2, len(pairs) * CAP, width), BF16)] * 2, after=after,
    )


def add_kernel(*refs):
    count = len(refs) // 3
    for left, right, out in zip(refs[:count], refs[count : 2 * count], refs[2 * count :]):
        out[...] = (left[...].astype(F32) + right[...].astype(F32)).astype(out.dtype)


def add_rows(lefts, rights, after=()):
    rows, width = lefts[0].shape
    count = len(lefts)
    tile = rows_spec(rows // 4, width)
    return run(
        add_kernel, (*lefts, *rights), (4,), [tile] * (2 * count), [tile] * count,
        [shape((rows, width), BF16)] * count, "add_rows", after=after,
    )


def total_of(keep, arrived):
    return keep.astype(F32) + arrived.astype(F32)


def halve_kinds_kernel(kinds, *refs):
    keep_ref, send_ref = refs[-2:]
    refs = iter(refs[:-2])
    for at, kind in enumerate(kinds):
        if kind == 0:
            total = total_of(next(refs)[0, 0], next(refs)[0, 0])
            half = total.shape[0] // 2
            keep_ref[at, 0], send_ref[at, 0] = total[:half], total[half:].astype(BF16)
        else:
            keep_ref[at, 0] = total_of(next(refs)[0, 0], next(refs)[0, 0])
            send_ref[at, 0] = total_of(next(refs)[0, 0], next(refs)[0, 0]).astype(BF16)


def halve_y(keep, arrived, kinds, after):
    nz, _, rows, cols = keep.shape
    split = lambda a: a.reshape(nz, -1, rows // 2, cols)
    args, specs = [], []
    for at, kind in enumerate(kinds):
        for add in (0, nz // 2) if kind else (0,):
            for array, entry in ((keep, kind), (arrived, at)):
                if kind == 0:
                    args.append(array)
                    index = functools.partial(lambda entry, t: (t, entry, 0, 0), entry)
                    specs.append(pl.BlockSpec((1, 1, rows, cols), index))
                else:
                    args.append(split(array))
                    index = functools.partial(
                        lambda entry, add, t: (t // 2 + add, 2 * entry + t % 2, 0, 0), entry, add
                    )
                    specs.append(pl.BlockSpec((1, 1, rows // 2, cols), index))
    out = pl.BlockSpec((len(kinds), 1, rows // 2, cols), lambda t: (0, t, 0, 0))
    dims = (len(kinds), nz, rows // 2, cols)
    return run(
        functools.partial(halve_kinds_kernel, kinds), args, (nz,), specs, [out, out],
        [shape(dims, F32), shape(dims, BF16)], "halve_y", after=after,
    )


def halve_z(keep, arrived, kinds, after):
    _, nz, rows, cols = keep.shape
    split = lambda a: a.reshape(len(kinds), 2 * nz, rows // 2, cols)
    args, specs = [], []
    for at, kind in enumerate(kinds):
        for add in (0, nz) if kind else (0,):
            for array, flip in ((keep, 0), (arrived, nz // 2)):
                if kind == 0:
                    args.append(array)
                    index = functools.partial(lambda at, flip, t: (at, t ^ flip, 0, 0), at, flip)
                    specs.append(pl.BlockSpec((1, 1, rows, cols), index))
                else:
                    args.append(split(array))
                    index = functools.partial(lambda at, add, t: (at, t + add, 0, 0), at, add)
                    specs.append(pl.BlockSpec((1, 1, rows // 2, cols), index))
    out = pl.BlockSpec((len(kinds), 1, rows // 2, cols), lambda t: (0, t, 0, 0))
    dims = (len(kinds), nz, rows // 2, cols)
    return run(
        functools.partial(halve_kinds_kernel, kinds), args, (nz,), specs, [out, out],
        [shape(dims, F32), shape(dims, BF16)], "halve_z", after=after,
    )


def core_halves(pos_ref, values):
    half = values.shape[0] // 2
    low, high = values[:half], values[half:]
    own_low = pos_ref[CORE] == 0
    return jnp.where(own_low, low, high), jnp.where(own_low, high, low).astype(BF16)


def finish_kinds_kernel(kinds, pos_ref, *refs):
    inputs, outs = refs[: 2 * len(kinds)], refs[2 * len(kinds) :]
    for at, kind in enumerate(kinds):
        keep_ref, arrived_ref = inputs[2 * at : 2 * at + 2]
        mine, sent = outs[2 * at : 2 * at + 2]
        if kind == 0:
            up = total_of(keep_ref[0, 0], arrived_ref[0, 0])
            half = up.shape[0] // 2
            mine[...], sent[...] = core_halves(pos_ref, jnp.concatenate([up[:half], up[half:]], 1))
        else:

            @pl.when(pl.program_id(0) == 0)
            def _():
                down = total_of(keep_ref[0], arrived_ref[0])
                down = down.reshape(down.shape[0] * down.shape[1], down.shape[2])
                mine[...], sent[...] = core_halves(pos_ref, jnp.transpose(down))


def finish_kinds(pos, keep, arrived, kinds, after):
    _, nz, rows, cols = keep.shape
    bits = nz.bit_length() - 1
    args, specs, out_specs, outs = [], [], [], []
    for at, kind in enumerate(kinds):
        args += [keep, arrived]
        if kind == 0:
            for flip in (0, 1):
                index = functools.partial(lambda at, flip, t, s: (at, t ^ flip, 0, 0), at, flip)
                specs.append(pl.BlockSpec((1, 1, rows, cols), index))
            dims = (rows // 4, 2 * cols * nz)
            out = pl.BlockSpec((rows // 4, 2 * cols), lambda t, s: (0, flipped(t, bits) ^ s[ROW_Z]))
        else:
            index = functools.partial(lambda at, t, s: (at, 0, 0, 0), at)
            specs += [pl.BlockSpec((1, nz, rows, cols), index)] * 2
            dims = (cols // 2, nz * rows)
            out = full(dims)
        out_specs += [out, out]
        outs += [shape(dims, F32), shape(dims, BF16)]
    return run(
        functools.partial(finish_kinds_kernel, kinds), args, (nz,), specs, out_specs, outs, "finish_kinds",
        scalars=(pos,), after=after,
    )


def halve_slices_kernel(ku_ref, au_ref, kd_ref, ad_ref, keep_ref, send_ref):
    for at, ref in enumerate((keep_ref, send_ref)):
        up = total_of(ku_ref[at], au_ref[at])
        half = up.shape[1] // 2
        for side in range(2):
            ref[0, side * up.shape[0] : (side + 1) * up.shape[0], :] = up[:, side * half : (side + 1) * half].astype(ref.dtype)
        ref[1] = total_of(kd_ref[at], ad_ref[at]).astype(ref.dtype)


def halve_slices(up_keep, up_arrived, down_keep, down_arrived, after):
    _, rows, cols = up_keep.shape
    steps = 8
    ups = pl.BlockSpec((2, rows // steps, cols), lambda i: (0, i, 0))
    downs = pl.BlockSpec((2, 2 * rows // steps, cols // 2), lambda i: (0, i, 0))
    dims = (2, 2 * rows, cols // 2)
    return run(
        halve_slices_kernel, (up_keep, up_arrived, down_keep, down_arrived), (steps,), [ups, ups, downs, downs],
        [downs, downs], [shape(dims, F32), shape(dims, BF16)], "halve_slices", after=after,
    )


def halve_kernel(keep_ref, arrived_ref, keep_out, send_out):
    keep_out[...] = total_of(keep_ref[:, 0], arrived_ref[:, 0])
    send_out[...] = total_of(keep_ref[:, 1], arrived_ref[:, 1]).astype(BF16)


def halve(keep, arrived, after, steps=2):
    kinds, rows, cols = keep.shape
    split = lambda a: a.reshape(kinds, 2, rows // 2, cols)
    into = pl.BlockSpec((kinds, 2, rows // 2 // steps, cols), lambda i: (0, 0, i, 0))
    out = pl.BlockSpec((kinds, rows // 2 // steps, cols), lambda i: (0, i, 0))
    dims = (kinds, rows // 2, cols)
    return run(
        halve_kernel, (split(keep), split(arrived)), (steps,), [into, into], [out, out],
        [shape(dims, F32), shape(dims, BF16)], "halve", after=after,
    )


def halve_parts_kernel(keep_ref, first_ref, second_ref, keep_out, send_out):
    keep_out[0] = total_of(keep_ref[0], first_ref[...])
    send_out[0] = total_of(keep_ref[1], second_ref[...]).astype(BF16)


def halve_parts(keep, arrived, after, steps=2):
    _, rows, cols = keep.shape
    into = pl.BlockSpec((2, rows // steps, cols), lambda i: (0, i, 0))
    out = pl.BlockSpec((1, rows // steps, cols), lambda i: (0, i, 0))
    return run(
        halve_parts_kernel, (keep, *arrived), (steps,), [into] + [rows_spec(rows // steps, cols)] * 2,
        [out, out], [shape((1, rows, cols), F32), shape((1, rows, cols), BF16)], "halve_parts", after=after,
    )


def finish_slices_kernel(merged, pos_ref, keep_ref, arrived_ref, *outs):
    total = total_of(keep_ref[...], arrived_ref[...])
    up = total[0]
    if merged:
        half = up.shape[0] // 2
        up = jnp.concatenate([up[:half], up[half:]], 1)
        outs[2][...], outs[3][...] = core_halves(pos_ref, jnp.transpose(total[1]))
    outs[0][...], outs[1][...] = core_halves(pos_ref, up)


def finish_slices(pos, keep, arrived, merged, after):
    _, rows, cols = keep.shape
    dims = [(rows // 4, 2 * cols), (cols // 2, rows)] if merged else [(rows // 2, cols)]
    outs = [shape(d, t) for d in dims for t in (F32, BF16)]
    return run(
        functools.partial(finish_slices_kernel, merged), (keep, arrived), (1,), [like(keep), like(arrived)],
        [like(a) for a in outs], outs, "finish_slices", scalars=(pos,), after=after,
    )


def middle_back_kernel(
    gs_ref, ga_ref, gb_ref, gc_ref, gg_ref, routes_ref, router_ref,
    hidden_ref, cot_ref, branch_ref, x_ref, mod_ref, w_ref,
    gm_ref, gatt_ref, back_ref, mods_ref, drouter_ref,
):
    block = pl.program_id(0)
    hidden = hidden_ref[...]
    grad_gates = gg_ref[...]
    ids = lax.broadcasted_iota(jnp.int32, grad_gates.shape, 0)
    gates = gate_rows(hidden, routes_ref[...], router_ref[...], ids)
    inner = jnp.sum(gates * grad_gates, 0, keepdims=True)
    grad_logits = gates * (grad_gates - inner)
    grad = gs_ref[...] + ga_ref[...].astype(F32) + gb_ref[...].astype(F32) + gc_ref[...].astype(F32)
    drouter = 0.0
    for piece in three_parts(grad_logits):
        grad = grad + tn(piece, router_ref[...])
        drouter = drouter + nn(piece, hidden)
    branch = branch_ref[...]
    gate_one = mod_ref[2, pl.ds(block, 1), :]
    middle = x_ref[...].astype(F32) + gate_one * branch
    normed, spread = norm_parts(middle)
    scale = mod_ref[4, pl.ds(block, 1), :]
    mods_ref[1, pl.ds(block, 1), :] = jnp.sum(grad, 0, keepdims=True)
    mods_ref[2, pl.ds(block, 1), :] = jnp.sum(grad * normed, 0, keepdims=True)
    grad_middle = cot_ref[...].astype(F32) + norm_back(grad * (1.0 + scale), normed, spread)
    mods_ref[0, pl.ds(block, 1), :] = jnp.sum(grad_middle * branch, 0, keepdims=True)
    gm_ref[...] = grad_middle
    grad_branch = (grad_middle * gate_one).astype(BF16)
    back_ref[...] = grad_branch
    gatt_ref[...] = nt(grad_branch, w_ref[...]).astype(BF16)

    @pl.when(block == 0)
    def _():
        drouter_ref[...] = drouter

    @pl.when(block > 0)
    def _():
        drouter_ref[...] += drouter


def middle_backward(parts, gg, routes_t, router_t, hidden, cot, branch, patches, mod, out_weight, blocks, after):
    rows, width = patches.shape
    short = rows // blocks
    tile = rows_spec(short, width)
    cols = lambda a: pl.BlockSpec((a.shape[0], short), lambda i: (0, i))
    out_shape = [
        shape((rows, width), F32),
        shape((rows, width), BF16),
        shape((rows, width), BF16),
        shape((3, 8, width), F32),
        shape((router_t.shape[0], width), F32),
    ]
    return run(
        middle_back_kernel,
        (*parts, gg, routes_t, router_t, hidden, cot, branch, patches, mod, out_weight), (blocks,),
        [tile] * 4 + [cols(gg), cols(routes_t), like(router_t)] + [tile] * 4 + [like(mod), like(out_weight)],
        [tile] * 3 + [like(a) for a in out_shape[3:]], out_shape, "middle_back", after=after,
    )


def mixed_kernel(so_ref, ra_ref, rb_ref, rc_ref, cot_ref, branch_ref, x_ref, mod_ref, mixed_ref, gate_ref):
    block = pl.program_id(0)
    second = so_ref[...] + ra_ref[...].astype(F32) + rb_ref[...].astype(F32) + rc_ref[...].astype(F32)
    middle = x_ref[...].astype(F32) + mod_ref[2, pl.ds(block, 1), :] * branch_ref[...]
    mixed_ref[...] = (middle + mod_ref[5, pl.ds(block, 1), :] * second).astype(BF16)
    gate_ref[pl.ds(block, 1), :] = jnp.sum(cot_ref[...].astype(F32) * second, 0, keepdims=True)


def mixed_forward(parts, cot, branch, patches, mod, blocks, after):
    rows, width = patches.shape
    tile = rows_spec(rows // blocks, width)
    return run(
        mixed_kernel, (*parts, cot, branch, patches, mod), (blocks,), [tile] * 7 + [like(mod)],
        [tile, full((8, width))], [shape((rows, width), BF16), shape((8, width), F32)], "mixed", after=after,
    )


def weight_kernel(
    pos_ref, x_ref, mod_ref, dq_ref, dk_ref, dv_ref, att_ref, back_ref, keep_ref, first_ref, second_ref, turned
):
    rows = x_ref.shape[0]
    short = rows // 4
    step = pl.program_id(0)
    matrix = ((step % 2) ^ pos_ref[STREAM]) * 2 + ((step // 2) ^ pos_ref[CORE])
    nz = 4

    @pl.when(step == 0)
    def _():
        for block in range(4):
            span = slice(block * short, (block + 1) * short)
            normed, _ = norm_parts(x_ref[span, :].astype(F32))
            hidden = normed * (1.0 + mod_ref[1, block : block + 1, :]) + mod_ref[0, block : block + 1, :]
            relative_rows(pos_ref, turned.at[0, :, span], jnp.transpose(hidden.astype(BF16)), nz)
        relative_rows(pos_ref, turned.at[1], jnp.transpose(att_ref[...]), nz)

    for index, (left, ref) in enumerate(((0, dq_ref), (0, dk_ref), (0, dv_ref), (1, back_ref))):

        @pl.when(matrix == index)
        def _():
            total = nn(turned[left], ref[...]).astype(BF16)

            @pl.when(step < 2)
            def _():
                keep_ref[0] = total

            @pl.when(step == 2)
            def _():
                first_ref[...] = total

            @pl.when(step == 3)
            def _():
                second_ref[...] = total


def weight_grads(pos, patches, mod, grads, attended, back, after):
    rows, width = patches.shape
    args = (patches, mod, *grads, attended, back)
    keep = pl.BlockSpec((1, width, width), lambda f, s: (jnp.minimum(f, 1), 0, 0))
    send = full((width, width))
    outs = run(
        weight_kernel, args, (4,), [like(a) for a in args], [keep, send, send],
        [shape((2, width, width), BF16)] + [shape((width, width), BF16)] * 2, "weight_grads", scalars=(pos,),
        scratch=[pltpu.VMEM((2, width, rows), BF16)], after=after,
    )
    return outs[0], outs[1:]


def inputs_back_kernel(dq_ref, dk_ref, dv_ref, w_ref, x_ref, gm_ref, mod_ref, gp_ref, mods_ref):
    block = pl.program_id(0)
    width = x_ref.shape[1]
    grad = nt(dq_ref[...], w_ref[:, :width])
    grad = grad + nt(dk_ref[...], w_ref[:, width : 2 * width])
    grad = grad + nt(dv_ref[...], w_ref[:, 2 * width :])
    normed, spread = norm_parts(x_ref[...].astype(F32))
    mods_ref[0, pl.ds(block, 1), :] = jnp.sum(grad, 0, keepdims=True)
    mods_ref[1, pl.ds(block, 1), :] = jnp.sum(grad * normed, 0, keepdims=True)
    scale = mod_ref[1, pl.ds(block, 1), :]
    gp_ref[...] = gm_ref[...] + norm_back(grad * (1.0 + scale), normed, spread)


def inputs_backward(grads, weight, patches, grad_middle, mod, blocks, after):
    rows, width = patches.shape
    tile = rows_spec(rows // blocks, width)
    return run(
        inputs_back_kernel, (*grads, weight, patches, grad_middle, mod), (blocks,),
        [tile] * 3 + [like(weight), tile, tile, like(mod)], [tile, full((2, 8, width))],
        [shape((rows, width), F32), shape((2, 8, width), F32)], "inputs_back", after=after,
    )


def used_kernel(block_count, pos_ref, gm_ref, ada_ref, emb_ref, out_ref):
    piece = pl.program_id(0)

    @pl.when(piece == 0)
    def _():
        out_ref[...] = jnp.zeros_like(out_ref)

    for part in three_parts(gm_ref[0]):
        out_ref[...] += nt(part, ada_ref[...])

    @pl.when(piece == pl.num_programs(0) - 1)
    def _():
        emb = emb_ref[...]
        is_long = pos_ref[LONG] > 0
        used = jnp.where(is_long, jnp.broadcast_to(emb[0:1], emb.shape), emb)
        gate = sigmoid(used)
        grad = out_ref[...] * (gate * (1.0 + used * (1.0 - gate)))
        row = lax.broadcasted_iota(jnp.int32, grad.shape, 0)
        grad = jnp.where(row < block_count, grad, 0.0)
        total = jnp.sum(grad, 0, keepdims=True)
        out_ref[...] = jnp.where(is_long, jnp.where(row == 0, total, 0.0), grad)


def used_backward(pos, grad_mod, ada_weight, emb_pad, block_count, after):
    rows, width = emb_pad.shape
    pieces = grad_mod.shape[0]
    return run(
        functools.partial(used_kernel, block_count), (grad_mod, ada_weight, emb_pad), (pieces,),
        [
            pl.BlockSpec((1, rows, width), lambda i, *_: (i, 0, 0)),
            pl.BlockSpec((width, width), lambda i, *_: (0, i)),
            like(emb_pad),
        ],
        like(emb_pad), shape((rows, width), F32), "used_back", scalars=(pos,), after=after,
    )


def swap(values, axis, bit):
    size = lax.axis_size(axis)
    return lax.ppermute(values, axis, [(i, i ^ bit) for i in range(size)])


def swap_all(arrays, axis, bit):
    return [swap(a, axis, bit) for a in arrays]


def in_order(own, mine, arrived, axis):
    return jnp.concatenate(
        [jnp.where(own == 0, mine, arrived), jnp.where(own == 0, arrived, mine)], axis
    )


def local_pair(
    patches, embedding, long_image, routes, cotangent, ada_weight, qkv_weight, out_weight, shared_up,
    shared_down, router_weight, expert_up, expert_down,
):
    rows, width = patches.shape
    blocks = embedding.shape[0]
    short = rows // blocks
    dp_size = lax.axis_size("dp")
    nz = dp_size // 4
    dp, stream = lax.axis_index("dp"), lax.axis_index("stream")
    core, row_y, row_z = dp % 2, (dp // 2) % 2, dp // 4
    local_experts = expert_up.shape[0]
    here = local_experts // 2
    first_here = core * here
    first_all = stream * local_experts + first_here
    places = [long_image[0], core, stream, row_y, row_z, first_here, first_all, 0]
    pos = jnp.stack([jnp.asarray(a, jnp.int32) for a in places])

    routes_t = routes.T
    routes_x = swap(routes_t, "stream", 1)
    routes_near = (routes_t, swap(routes_t, "dp", 1))
    routes_far = (routes_x, swap(routes_x, "dp", 1))
    emb_pad = jnp.pad(embedding, ((0, 8 - blocks), (0, 0)))
    router_t = jnp.pad(router_weight.T, ((0, 16 - router_weight.shape[1]), (0, 0)))
    mod, act, branch_grad = modulate(pos, emb_pad, ada_weight, cotangent, blocks)
    rank_near, cols_near = ranks(pos, routes_near, (mod,))
    rank_far, cols_far = ranks(pos, routes_far, (rank_near,))
    branch_grad = touch(branch_grad, (rank_far,))
    branch_x = swap(branch_grad, "stream", 1)
    branches_near = (branch_grad, swap(branch_grad, "dp", 1))
    branches_far = (branch_x, swap(branch_x, "dp", 1))

    packed = qkv_forward(patches, mod, qkv_weight, blocks, (branch_grad,))
    attended, logsum = attend_forward(pos, packed, short)
    branch_one, hidden = middle_forward(
        attended, patches, mod, out_weight, blocks, (branch_x, branches_near[1])
    )
    hidden_x = swap(hidden, "stream", 1)
    hiddens_near = (hidden, swap(hidden, "dp", 1))

    def expert(slot, is_far, sends, prior, after):
        group = (
            (hiddens_far, branches_far, rank_far, routes_far)
            if is_far
            else (hiddens_near, branches_near, rank_near, routes_near)
        )
        out = expert_call(slot, sends, pos, *group, router_t, expert_up, expert_down, prior, nz, after)
        return out[: 1 + sends], out[1 + sends :]

    first, first_near = expert(0, False, 1, None, (branches_far[1],))
    hidden_x = touch(hidden_x, (first_near[2],))
    hiddens_far = (hidden_x, swap(hidden_x, "dp", 1))
    first, first_far = expert(0, True, 1, first, ())
    first_arrived = swap(first[1], "dp", 2)
    second, second_near = expert(1, False, 2, None, (first_far[2],))
    second, second_far = expert(1, True, 2, second, ())
    up_half_arrived = swap(second[1], "dp", 2)
    out_x, out_xc, gx_x, gx_xc = combine(cols_far, [r[:2] for r in (first_far, second_far)], ())
    gx_xc, out_xc = swap(gx_xc, "dp", 1), swap(out_xc, "dp", 1)
    out_near, out_core, gx_near, gx_core = combine(
        cols_near, [r[:2] for r in (first_near, second_near)], (gx_x,)
    )
    gx_core = swap(gx_core, "dp", 1)
    out_core = swap(out_core, "dp", 1)
    (gx_sum,) = add_rows([gx_x], [gx_xc], (out_near,))
    gx_back = swap(gx_sum, "stream", 1)
    (out_sum,) = add_rows([out_x], [out_xc], (gx_sum,))
    out_back = swap(out_sum, "stream", 1)
    near, far = (first_near, second_near), (first_far, second_far)
    gg_near = [jnp.concatenate([r[2][source] for r in near], 0) for source in range(2)]
    gg_far = [jnp.concatenate([r[2][source] for r in far], 0) for source in range(2)]
    gg_back = swap(jnp.concatenate([gg_far[0], swap(gg_far[1], "dp", 1)], 0), "stream", 1)
    gg_rel = jnp.concatenate([gg_near[0], swap(gg_near[1], "dp", 1), gg_back], 0)
    order = jnp.arange(4, dtype=jnp.int32) ^ (stream * 2 + core)
    gg = gg_rel.reshape(4, here, rows)[order].reshape(EXPERTS, rows)
    gg = jnp.pad(gg, ((0, 16 - EXPERTS), (0, 0)))

    up_keep, up_send, down_keep, down_send, shared_out, shared_gx = shared_call(
        pos, hidden, branch_grad, shared_up, shared_down, (out_sum, gx_core, out_core, gg)
    )
    up_arrived, down_arrived = swap(up_send, "dp", 1), swap(down_send, "dp", 1)

    grad_middle, grad_attended, back, mods_two, drouter = middle_backward(
        (shared_gx, gx_near, gx_core, gx_back), gg, routes_t, router_t, hidden, cotangent, branch_one,
        patches, mod, out_weight, blocks, (),
    )
    both, up, down = (0, 1), (0,), (1,)
    flat = lambda a: a.reshape(a.shape[0], -1, a.shape[-1])
    ea_keep, ea_send = halve_y(first[0], first_arrived, both, (grad_attended,))
    ea_arrived = swap(ea_send, "dp", 4)
    down_half = touch(second[2], (up_half_arrived, ea_send))
    down_half_arrived = swap(down_half, "dp", 2)
    sh_keep, sh_send = halve_slices(up_keep, up_arrived, flat(down_keep), flat(down_arrived), (down_half,))
    sh_arrived = swap(sh_send, "stream", 1)
    bu_keep, bu_send = halve_y(second[0], up_half_arrived, up, (sh_send,))
    bu_arrived = swap(bu_send, "dp", 4)
    grads = attend_backward(pos, packed, attended, logsum, grad_attended, short, (bu_send,))
    mixed, gate_two = mixed_forward(
        (shared_out, out_near, out_core, out_back), cotangent, branch_one, patches, mod, blocks, (grads[0],)
    )
    qk_keep, qk_send = weight_grads(pos, patches, mod, grads, attended, back, (gate_two,))
    qk_arrived = [swap(a, "dp", 1) for a in qk_send]
    ea_keep, ea_send = halve_z(ea_keep, ea_arrived, both, (qk_send[0],))
    ea_arrived = swap(ea_send, "dp", 8)
    bu_keep, bu_send = halve_z(bu_keep, bu_arrived, up, (ea_send,))
    bu_arrived = swap(bu_send, "dp", 8)
    bd_keep, bd_send = halve_y(second[0], down_half_arrived, down, (bu_send,))
    bd_arrived = swap(bd_send, "dp", 4)
    sh_keep, sh_send = halve(sh_keep, sh_arrived, (bd_send,))
    sh_arrived = swap(sh_send, "dp", 2)
    qk_keep, qk_send = halve_parts(qk_keep, qk_arrived, (sh_send,))
    qk_arrived = swap(qk_send, "stream", 1)
    grad_patches, mods_one = inputs_backward(grads, qkv_weight, patches, grad_middle, mod, blocks, (qk_send,))
    factors = [act, *mods_one, *mods_two, gate_two]
    factors = jnp.concatenate([a[:blocks] for a in factors] + [drouter[:EXPERTS].reshape(blocks, -1)], 1)
    factors = lax.all_gather(factors.astype(BF16), ("dp", "stream"), axis=0, tiled=True)
    grad_mod = jnp.concatenate([mods_one, mods_two, gate_two[None]], 0)
    grad_embedding = used_backward(pos, grad_mod, ada_weight, emb_pad, blocks, (mods_one,))

    bd_keep, bd_send = halve_z(bd_keep, bd_arrived, down, (grad_embedding,))
    bd_arrived = swap(bd_send, "dp", 8)
    sh_keep, sh_send = halve(sh_keep, sh_arrived, (bd_send,))
    sh_arrived = swap(sh_send, "dp", 4)
    qk_keep, qk_send = halve(qk_keep, qk_arrived, (sh_send,))
    qk_arrived = swap(qk_send, "dp", 2)
    ea_done = finish_kinds(pos, ea_keep, ea_arrived, both, (qk_send,))
    ea_others = [swap(ea_done[1], "dp", 1), swap(ea_done[3], "dp", 1)]
    sh_keep, sh_send = halve(sh_keep, sh_arrived, (ea_done[1],))
    sh_arrived = swap(sh_send, "dp", 8)
    qk_keep, qk_send = halve(qk_keep, qk_arrived, (sh_send,))
    qk_arrived = swap(qk_send, "dp", 4)
    bu_done = finish_kinds(pos, bu_keep, bu_arrived, up, (qk_send,))
    bu_others = swap(bu_done[1], "dp", 1)
    qk_keep, qk_send = halve(qk_keep, qk_arrived, (bu_done[1],))
    qk_arrived = swap(qk_send, "dp", 8)
    sh_done = finish_slices(pos, sh_keep, sh_arrived, True, (qk_send,))
    bd_done = finish_kinds(pos, bd_keep, bd_arrived, down, (sh_done[1],))
    bd_others = swap(bd_done[1], "dp", 1)
    qk_done = finish_slices(pos, qk_keep, qk_arrived, False, (bd_done[1],))

    share = width // dp_size
    factors = touch(factors, (sh_done[1],))
    acts = lax.dynamic_slice_in_dim(factors[:, :width], dp * share, share, 1)
    wide = 7 * width
    grad_ada = lax.dot_general(acts, factors[:, width:wide], (((0,), (0,)), ((), ())), preferred_element_type=F32)
    drouter_sum = jnp.sum(factors[:, wide:].astype(F32).reshape(-1, blocks, 2 * width), 0)
    drouter_sum = drouter_sum.reshape(EXPERTS, width)
    grad_router = lax.dynamic_slice_in_dim(drouter_sum, dp * share, share, 1).T

    def experts_out(one, two, one_other, two_other):
        mine, others = jnp.stack([one, two]), jnp.stack([one_other, two_other]).astype(F32)
        return in_order(core, mine, others, 0)

    def slices_out(keep, send):
        chip = in_order(core, keep.astype(BF16), swap(send, "dp", 1), 1)
        return in_order(stream, chip, swap(chip, "stream", 1), 1).astype(F32)

    grad_qkv_out = slices_out(*qk_done)
    return (
        mixed, grad_patches, grad_embedding[:blocks], grad_ada, grad_qkv_out[:, : 3 * width],
        grad_qkv_out[:, 3 * width :], slices_out(*sh_done[:2]), slices_out(*sh_done[2:]), grad_router,
        experts_out(ea_done[0], bu_done[0], ea_others[0], bu_others),
        experts_out(ea_done[2], bd_done[0], ea_others[1], bd_others),
    )


def local(*arrays):
    experts, width, wide = arrays[11].shape
    pair = lax.axis_size("stream") == 2 and experts == 4 and lax.axis_size("dp") == 16
    if pair and wide == 4 * width:
        return local_pair(*arrays)
    return local_general(*arrays)


def solution(mesh):
    return jax.shard_map(
        local,
        mesh=mesh,
        in_specs=(
            P(("dp", "stream"), None),
            P(("dp", "stream"), None),
            P(("dp", "stream")),
            P(("dp", "stream"), None),
            P(("dp", "stream"), None),
            P(),
            P(),
            P(),
            P(),
            P(),
            P(),
            P("stream", None, None),
            P("stream", None, None),
        ),
        out_specs=(
            P(("dp", "stream"), None),
            P(("dp", "stream"), None),
            P(("dp", "stream"), None),
            P("dp", None),
            P("dp", None),
            P("dp", None),
            P("dp", None),
            P("dp", None),
            P("dp", None),
            P("stream", "dp", None),
            P("stream", "dp", None),
        ),
        check_vma=False,
    )
```

```python
import functools
import math

import jax
import jax.numpy as jnp
from jax import lax
from jax.experimental import pallas as pl
from jax.experimental.pallas import tpu as pltpu
from jax.sharding import PartitionSpec as P

HEADS = 12
HEAD_DIM = 64
EXPERTS = 8
CAP = 288


HIGH = lax.Precision.HIGHEST
EPSILON = 1e-06
F32 = jnp.float32
BF16 = jnp.bfloat16
MIB = 1 << 20


def gelu_tanh(values):
    return jax.nn.gelu(values, approximate=True)


def normalize(values):
    centered = values - jnp.mean(values, -1, keepdims=True)
    spread = lax.rsqrt(jnp.mean(centered * centered, -1, keepdims=True) + EPSILON)
    return (centered * spread, spread)


def normalize_back(grad_normed, normed, spread):
    return spread * (
        grad_normed
        - jnp.mean(grad_normed, -1, keepdims=True)
        - normed * jnp.mean(grad_normed * normed, -1, keepdims=True)
    )


def split_packed(packed, seg_len):
    row_count = packed.shape[0]
    model_width = packed.shape[1] // 3
    groups = row_count // seg_len
    block_rows = min(512, seg_len)
    part_count = seg_len // block_rows
    queries = (
        packed[:, :model_width]
        .reshape(groups, part_count, block_rows, HEADS, HEAD_DIM)
        .swapaxes(0, 1)
    )
    key_heads = packed[:, model_width : 2 * model_width].reshape(groups, seg_len, HEADS, HEAD_DIM)
    values = packed[:, 2 * model_width :].reshape(groups, seg_len, HEADS, HEAD_DIM)
    return (queries, key_heads, values, groups, block_rows, part_count)


def attend(packed, seg_len):
    row_count = packed.shape[0]
    model_width = packed.shape[1] // 3
    factor = 1.0 / math.sqrt(HEAD_DIM)
    queries, key_heads, values, groups, block_rows, part_count = split_packed(packed, seg_len)

    def one_block(query_block):
        scores = (
            jnp.einsum(
                "gqhd,gkhd->ghqk", query_block, key_heads, preferred_element_type=jnp.float32
            )
            * factor
        )
        row_max = jnp.max(scores, -1, keepdims=True)
        shifted = jnp.exp(scores - row_max)
        row_sum = jnp.sum(shifted, -1, keepdims=True)
        weights = (shifted / row_sum).astype(jnp.bfloat16)
        mixture = jnp.einsum("ghqk,gkhd->gqhd", weights, values, preferred_element_type=jnp.float32)
        return (mixture, row_max[..., 0] + jnp.log(row_sum[..., 0]))

    mixture, logsum = lax.map(one_block, queries)
    return (mixture.swapaxes(0, 1).reshape(row_count, model_width), logsum.reshape(-1))


def attend_back(packed, logsum, grad_mixture, seg_len):
    row_count = packed.shape[0]
    model_width = packed.shape[1] // 3
    factor = 1.0 / math.sqrt(HEAD_DIM)
    queries, key_heads, values, groups, block_rows, part_count = split_packed(packed, seg_len)
    grad_blocks = grad_mixture.reshape(groups, part_count, block_rows, HEADS, HEAD_DIM).swapaxes(
        0, 1
    )
    logsum_blocks = logsum.reshape(part_count, groups, HEADS, block_rows)

    def one_block(carried, inputs):
        grad_keys, grad_values = carried
        query_block, grad_block, logsum_block = inputs
        scores = (
            jnp.einsum(
                "gqhd,gkhd->ghqk", query_block, key_heads, preferred_element_type=jnp.float32
            )
            * factor
        )
        prob_full = jnp.exp(scores - logsum_block[..., None])
        grad_values = grad_values + jnp.einsum(
            "ghqk,gqhd->gkhd",
            prob_full.astype(jnp.bfloat16),
            grad_block,
            preferred_element_type=jnp.float32,
        )
        grad_probs = jnp.einsum(
            "gqhd,gkhd->ghqk", grad_block, values, preferred_element_type=jnp.float32
        )
        row_inner = jnp.sum(grad_probs * prob_full, -1, keepdims=True)
        grad_scores = (prob_full * (grad_probs - row_inner)).astype(jnp.bfloat16)
        grad_query = (
            jnp.einsum(
                "ghqk,gkhd->gqhd", grad_scores, key_heads, preferred_element_type=jnp.float32
            )
            * factor
        )
        grad_keys = (
            grad_keys
            + jnp.einsum(
                "ghqk,gqhd->gkhd", grad_scores, query_block, preferred_element_type=jnp.float32
            )
            * factor
        )
        return ((grad_keys, grad_values), grad_query)

    zeros_kv = jnp.zeros((groups, seg_len, HEADS, HEAD_DIM), jnp.float32)
    (grad_keys, grad_values), grad_query = lax.scan(
        one_block, (zeros_kv, zeros_kv), (queries, grad_blocks, logsum_blocks)
    )
    return jnp.concatenate(
        [
            grad_query.swapaxes(0, 1).reshape(row_count, model_width),
            grad_keys.reshape(row_count, model_width),
            grad_values.reshape(row_count, model_width),
        ],
        1,
    )


def local_general(
    patches,
    embedding,
    long_image,
    routes,
    cotangent,
    ada_weight,
    qkv_weight,
    out_weight,
    shared_up,
    shared_down,
    router_weight,
    expert_up,
    expert_down,
):
    row_count, model_width = patches.shape
    block_count = embedding.shape[0]
    short_len = row_count // block_count
    lane_count = lax.axis_size("stream")
    local_experts = expert_up.shape[0]
    is_long = long_image[0] > 0

    def blocks(values):
        return values.reshape(block_count, short_len, model_width)

    def flatten(values):
        return values.reshape(row_count, model_width)

    used = jnp.where(is_long, jnp.broadcast_to(embedding[0:1], embedding.shape), embedding)
    activated, silu_back = jax.vjp(jax.nn.silu, used)
    ada_full = ada_weight.astype(jnp.float32)
    modulation = jnp.dot(activated, ada_full, precision=HIGH)
    pieces = [
        modulation[:, column * model_width : (column + 1) * model_width][:, None, :]
        for column in range(6)
    ]
    shift_one, scale_one, gate_one, shift_two, scale_two, gate_two = pieces
    inputs_full = blocks(patches.astype(jnp.float32))
    normed_one, spread_one = normalize(inputs_full)
    hidden_one = flatten(normed_one * (1.0 + scale_one) + shift_one).astype(jnp.bfloat16)
    packed = jnp.dot(hidden_one, qkv_weight, preferred_element_type=jnp.float32).astype(
        jnp.bfloat16
    )
    attended, logsum = lax.cond(
        is_long,
        lambda packed_in: attend(packed_in, row_count),
        lambda packed_in: attend(packed_in, short_len),
        packed,
    )
    attended_low = attended.astype(jnp.bfloat16)
    branch_one = blocks(jnp.dot(attended_low, out_weight, preferred_element_type=jnp.float32))
    middle = inputs_full + gate_one * branch_one
    normed_two, spread_two = normalize(middle)
    hidden_two = flatten(normed_two * (1.0 + scale_two) + shift_two).astype(jnp.bfloat16)
    shared_pre = jnp.dot(hidden_two, shared_up, preferred_element_type=jnp.float32)
    shared_act, shared_back = jax.vjp(gelu_tanh, shared_pre)
    shared_low = shared_act.astype(jnp.bfloat16)
    shared_out = jnp.dot(shared_low, shared_down, preferred_element_type=jnp.float32)
    logits = jnp.dot(hidden_two, router_weight, preferred_element_type=jnp.float32)
    chosen_hot = (routes[:, :, None] == jnp.arange(EXPERTS)[None, None, :]).astype(jnp.float32)
    gates = jax.nn.softmax(jnp.sum(chosen_hot * logits[:, None, :], -1), -1)
    flat_routes = routes.reshape(-1)
    route_hits = (flat_routes[:, None] == jnp.arange(EXPERTS)[None, :]).astype(jnp.int32)
    earlier = jnp.cumsum(route_hits, 0) - route_hits
    target = flat_routes * CAP + jnp.sum(earlier * route_hits, 1)

    def spread_rows(rows_low):
        buffer = jnp.zeros((EXPERTS * CAP, model_width), jnp.bfloat16).at[target].set(rows_low)
        return buffer.reshape(lane_count, local_experts, CAP, model_width)

    def collect(arrived):
        return (
            arrived.reshape(EXPERTS * CAP, model_width)[target]
            .astype(jnp.float32)
            .reshape(row_count, 2, model_width)
        )

    def by_expert(arrived):
        return arrived.swapaxes(0, 1).reshape(local_experts, lane_count * CAP, model_width)

    def by_source(results):
        return results.reshape(local_experts, lane_count, CAP, model_width).swapaxes(0, 1)

    expert_in = by_expert(
        lax.all_to_all(
            spread_rows(jnp.repeat(hidden_two, 2, axis=0)),
            "stream",
            split_axis=0,
            concat_axis=0,
            tiled=True,
        )
    )
    expert_pre = jnp.einsum(
        "jrd,jdf->jrf", expert_in, expert_up, preferred_element_type=jnp.float32
    )
    expert_act, expert_back = jax.vjp(gelu_tanh, expert_pre)
    expert_low = expert_act.astype(jnp.bfloat16)
    expert_out = jnp.einsum(
        "jrf,jfd->jrd", expert_low, expert_down, preferred_element_type=jnp.float32
    ).astype(jnp.bfloat16)
    picked = collect(
        lax.all_to_all(by_source(expert_out), "stream", split_axis=0, concat_axis=0, tiled=True)
    )
    routed = jnp.sum(gates[:, :, None] * picked, 1)
    branch_two = blocks(shared_out + routed)
    mixed = flatten(middle + gate_two * branch_two).astype(jnp.bfloat16)
    grad_top = blocks(cotangent.astype(jnp.float32))
    grad_gate_two = jnp.sum(grad_top * branch_two, 1)
    grad_branch = flatten(grad_top * gate_two)
    grad_pick = (
        (gates[:, :, None] * grad_branch[:, None, :])
        .astype(jnp.bfloat16)
        .reshape(2 * row_count, model_width)
    )
    grad_arrived = by_expert(
        lax.all_to_all(spread_rows(grad_pick), "stream", split_axis=0, concat_axis=0, tiled=True)
    )
    grad_expert_down = jnp.einsum(
        "jrf,jrd->jfd", expert_low, grad_arrived, preferred_element_type=jnp.float32
    )
    grad_expert_act = jnp.einsum(
        "jrd,jfd->jrf", grad_arrived, expert_down, preferred_element_type=jnp.float32
    )
    grad_expert_pre = expert_back(grad_expert_act)[0].astype(jnp.bfloat16)
    grad_expert_up = jnp.einsum(
        "jrd,jrf->jdf", expert_in, grad_expert_pre, preferred_element_type=jnp.float32
    )
    grad_expert_in = jnp.einsum(
        "jrf,jdf->jrd", grad_expert_pre, expert_up, preferred_element_type=jnp.float32
    ).astype(jnp.bfloat16)
    grad_routed = jnp.sum(
        collect(
            lax.all_to_all(
                by_source(grad_expert_in), "stream", split_axis=0, concat_axis=0, tiled=True
            )
        ),
        1,
    )
    grad_shared_low = grad_branch.astype(jnp.bfloat16)
    grad_shared_down = jnp.einsum(
        "rf,rd->fd", shared_low, grad_shared_low, preferred_element_type=jnp.float32
    )
    grad_shared_act = jnp.einsum(
        "rd,fd->rf", grad_shared_low, shared_down, preferred_element_type=jnp.float32
    )
    grad_shared_pre = shared_back(grad_shared_act)[0].astype(jnp.bfloat16)
    grad_shared_up = jnp.einsum(
        "rd,rf->df", hidden_two, grad_shared_pre, preferred_element_type=jnp.float32
    )
    grad_gates = jnp.sum(picked * grad_branch[:, None, :], -1)
    grad_chosen = gates * (grad_gates - jnp.sum(gates * grad_gates, -1, keepdims=True))
    grad_logits = jnp.sum(chosen_hot * grad_chosen[:, :, None], 1)
    hidden_two_full = hidden_two.astype(jnp.float32)
    router_full = router_weight.astype(jnp.float32)
    grad_router = jnp.dot(hidden_two_full.T, grad_logits, precision=HIGH)
    grad_hidden = jnp.dot(grad_logits, router_full.T, precision=HIGH) + grad_routed
    grad_hidden = blocks(
        grad_hidden
        + jnp.einsum("rf,df->rd", grad_shared_pre, shared_up, preferred_element_type=jnp.float32)
    )
    grad_shift_two = jnp.sum(grad_hidden, 1)
    grad_scale_two = jnp.sum(grad_hidden * normed_two, 1)
    grad_middle = grad_top + normalize_back(grad_hidden * (1.0 + scale_two), normed_two, spread_two)
    grad_gate_one = jnp.sum(grad_middle * branch_one, 1)
    grad_branch_one = flatten(grad_middle * gate_one).astype(jnp.bfloat16)
    grad_out_weight = jnp.einsum(
        "rd,re->de", attended_low, grad_branch_one, preferred_element_type=jnp.float32
    )
    grad_attended = jnp.einsum(
        "re,de->rd", grad_branch_one, out_weight, preferred_element_type=jnp.float32
    ).astype(jnp.bfloat16)
    grad_packed = lax.cond(
        is_long,
        lambda packed_in, logsum_in, grad_in: attend_back(packed_in, logsum_in, grad_in, row_count),
        lambda packed_in, logsum_in, grad_in: attend_back(packed_in, logsum_in, grad_in, short_len),
        packed,
        logsum,
        grad_attended,
    ).astype(jnp.bfloat16)
    grad_qkv = jnp.einsum("rd,re->de", hidden_one, grad_packed, preferred_element_type=jnp.float32)
    grad_hidden_one = blocks(
        jnp.einsum("re,de->rd", grad_packed, qkv_weight, preferred_element_type=jnp.float32)
    )
    grad_shift_one = jnp.sum(grad_hidden_one, 1)
    grad_scale_one = jnp.sum(grad_hidden_one * normed_one, 1)
    grad_inputs = grad_middle + normalize_back(
        grad_hidden_one * (1.0 + scale_one), normed_one, spread_one
    )
    grad_modulation = jnp.concatenate(
        [
            grad_shift_one,
            grad_scale_one,
            grad_gate_one,
            grad_shift_two,
            grad_scale_two,
            grad_gate_two,
        ],
        1,
    )
    grad_ada = jnp.dot(activated.T, grad_modulation, precision=HIGH)
    grad_used = silu_back(jnp.dot(grad_modulation, ada_full.T, precision=HIGH))[0]
    grad_embedding = jnp.where(
        is_long, jnp.zeros_like(grad_used).at[0].set(jnp.sum(grad_used, 0)), grad_used
    )
    shares = (
        lax.psum_scatter(
            grad_ada.astype(jnp.bfloat16), "dp", scatter_dimension=0, tiled=True
        ).astype(jnp.float32),
        lax.psum_scatter(
            grad_qkv.astype(jnp.bfloat16), "dp", scatter_dimension=0, tiled=True
        ).astype(jnp.float32),
        lax.psum_scatter(
            grad_out_weight.astype(jnp.bfloat16), "dp", scatter_dimension=0, tiled=True
        ).astype(jnp.float32),
        lax.psum_scatter(
            grad_shared_up.astype(jnp.bfloat16), "dp", scatter_dimension=0, tiled=True
        ).astype(jnp.float32),
        lax.psum_scatter(
            grad_shared_down.astype(jnp.bfloat16), "dp", scatter_dimension=0, tiled=True
        ).astype(jnp.float32),
        lax.psum_scatter(
            grad_router.astype(jnp.bfloat16), "dp", scatter_dimension=0, tiled=True
        ).astype(jnp.float32),
    )
    expert_summed = (
        lax.psum_scatter(
            grad_expert_up.astype(jnp.bfloat16), "dp", scatter_dimension=1, tiled=True
        ).astype(jnp.float32),
        lax.psum_scatter(
            grad_expert_down.astype(jnp.bfloat16), "dp", scatter_dimension=1, tiled=True
        ).astype(jnp.float32),
    )
    summed = (
        lax.psum(shares[0].astype(jnp.bfloat16), "stream").astype(jnp.float32),
        lax.psum(shares[1].astype(jnp.bfloat16), "stream").astype(jnp.float32),
        lax.psum(shares[2].astype(jnp.bfloat16), "stream").astype(jnp.float32),
        lax.psum(shares[3].astype(jnp.bfloat16), "stream").astype(jnp.float32),
        lax.psum(shares[4].astype(jnp.bfloat16), "stream").astype(jnp.float32),
        lax.psum(shares[5].astype(jnp.bfloat16), "stream").astype(jnp.float32),
    )
    return (
        mixed,
        flatten(grad_inputs),
        grad_embedding,
        summed[0],
        summed[1],
        summed[2],
        summed[3],
        summed[4],
        summed[5],
        expert_summed[0],
        expert_summed[1],
    )


def nn(left, right):
    return jnp.dot(left, right, preferred_element_type=F32)


def nt(left, right):
    return lax.dot_general(left, right, (((1,), (1,)), ((), ())), preferred_element_type=F32)


def tn(left, right):
    return lax.dot_general(left, right, (((0,), (0,)), ((), ())), preferred_element_type=F32)


def three_parts(values):
    first = values.astype(BF16)
    rest = values - first.astype(F32)
    second = rest.astype(BF16)
    third = (rest - second.astype(F32)).astype(BF16)
    return first, second, third


def sigmoid(values):
    return 1.0 / (1.0 + jnp.exp(-values))


def gelu_and_slope(values):
    inner = math.sqrt(2.0 / math.pi)
    square = values * values
    bend = jnp.tanh(values * (inner + (inner * 0.044715) * square))
    half = 0.5 + 0.5 * bend
    slope = half + values * (0.5 - 0.5 * bend * bend) * (inner + (3.0 * inner * 0.044715) * square)
    return values * half, slope


def run(kernel, args, grid, in_specs, out_specs, out_shape, name, scalars=(), scratch=(), after=(), limit=56):
    count = len(scalars) + len(args)

    def body(*refs):
        kernel(*refs[:count], *refs[count + len(after) :])

    return pl.pallas_call(
        body,
        grid_spec=pltpu.PrefetchScalarGridSpec(
            num_scalar_prefetch=len(scalars),
            grid=grid,
            in_specs=list(in_specs) + [pl.BlockSpec(memory_space=pl.ANY)] * len(after),
            out_specs=out_specs,
            scratch_shapes=list(scratch),
        ),
        out_shape=out_shape,
        compiler_params=pltpu.CompilerParams(vmem_limit_bytes=limit * MIB),
        cost_estimate=pl.CostEstimate(flops=1000, bytes_accessed=1000, transcendentals=0),
        name=name,
    )(*scalars, *args, *after)


def full(shape):
    return pl.BlockSpec(shape, lambda *_: (0,) * len(shape))


def like(array):
    return full(array.shape)


def rows_spec(rows, width):
    return pl.BlockSpec((rows, width), lambda i, *_: (i, 0))


def shape(dims, dtype):
    return jax.ShapeDtypeStruct(tuple(dims), dtype)


LONG, CORE, STREAM, ROW_Y, ROW_Z, FIRST_HERE, FIRST_ALL = range(7)


def flipped(value, bits):
    total = 0
    for bit in range(bits):
        total = total + (((value >> bit) & 1) << (bits - 1 - bit))
    return total


def modulate_kernel(blocks, pos_ref, emb_ref, ada_ref, cot_ref, mod_ref, act_ref, branch_ref):
    emb = emb_ref[...]
    used = jnp.where(pos_ref[LONG] > 0, jnp.broadcast_to(emb[0:1], emb.shape), emb)
    act = used * sigmoid(used)
    act_ref[...] = act
    weight = ada_ref[...]
    total = 0.0
    for part in three_parts(act):
        total = total + nn(part, weight)
    mod_ref[0] = total

    @pl.when(pl.program_id(0) == pl.num_programs(0) - 1)
    def _():
        short = cot_ref.shape[0] // blocks
        for block in range(blocks):
            span = slice(block * short, (block + 1) * short)
            branch_ref[span, :] = (cot_ref[span, :].astype(F32) * total[block : block + 1]).astype(BF16)


def modulate(pos, emb_pad, ada_weight, cot, blocks):
    rows, width = emb_pad.shape
    pieces = ada_weight.shape[1] // width
    return run(
        functools.partial(modulate_kernel, blocks), (emb_pad, ada_weight, cot), (pieces,),
        [like(emb_pad), pl.BlockSpec((width, width), lambda i, *_: (0, i)), like(cot)],
        [pl.BlockSpec((1, rows, width), lambda i, *_: (i, 0, 0)), like(emb_pad), like(cot)],
        [shape((pieces, rows, width), F32), shape((rows, width), F32), shape(cot.shape, BF16)],
        "modulate", scalars=(pos,),
    )


def norm_parts(values):
    centered = values - jnp.mean(values, -1, keepdims=True)
    spread = lax.rsqrt(jnp.mean(centered * centered, -1, keepdims=True) + EPSILON)
    return centered * spread, spread


def norm_back(grad, normed, spread):
    return spread * (
        grad
        - jnp.mean(grad, -1, keepdims=True)
        - normed * jnp.mean(grad * normed, -1, keepdims=True)
    )


def qkv_kernel(x_ref, mod_ref, w_ref, packed_ref):
    block = pl.program_id(0)
    normed, _ = norm_parts(x_ref[...].astype(F32))
    shift, scale = mod_ref[0, pl.ds(block, 1), :], mod_ref[1, pl.ds(block, 1), :]
    hidden = (normed * (1.0 + scale) + shift).astype(BF16)
    packed_ref[...] = nn(hidden, w_ref[...]).astype(BF16)


def qkv_forward(patches, mod, weight, blocks, after):
    rows, width = patches.shape
    short = rows // blocks
    wide = weight.shape[1]
    return run(
        qkv_kernel, (patches, mod, weight), (blocks,),
        [rows_spec(short, width), like(mod), like(weight)], rows_spec(short, wide),
        shape((rows, wide), BF16), "qkv", after=after,
    )


def attend_kernel(short, pos_ref, q_ref, k_ref, v_ref, o_ref, lse_ref):
    rows, lanes = q_ref.shape
    first = lax.broadcasted_iota(jnp.int32, (1, lanes), 1) < HEAD_DIM
    factor = 1.0 / math.sqrt(HEAD_DIM)

    def part(at, count):
        span = slice(at, at + count)
        queries = (q_ref[span, :].astype(F32) * factor).astype(BF16)
        keys, values = k_ref[span, :], v_ref[span, :]
        zero = jnp.zeros_like(queries)
        wide = jnp.concatenate([values, jnp.ones_like(values)], 1)
        masks = (first, jnp.logical_not(first))
        scores = [nt(jnp.where(mine, queries, zero), keys) for mine in masks]
        tops = [jnp.max(a, -1, keepdims=True) for a in scores]
        shifted = [jnp.exp(a - top).astype(BF16) for a, top in zip(scores, tops)]
        mixtures = [nn(a, wide) for a in shifted]
        totals = [a[:, lanes:] for a in mixtures]
        outs = [a[:, :lanes] / total for a, total in zip(mixtures, totals)]
        sums = [top + jnp.log(total) for top, total in zip(tops, totals)]
        o_ref[span, :] = jnp.where(first, outs[0], outs[1]).astype(BF16)
        lse_ref[span, :] = jnp.where(first, sums[0], sums[1])

    @pl.when(pos_ref[LONG] > 0)
    def _():
        part(0, rows)

    @pl.when(pos_ref[LONG] <= 0)
    def _():
        for at in range(0, rows, short):
            part(at, short)


def pair_specs(rows, width):
    lanes = 2 * HEAD_DIM
    pairs = width // lanes
    return [
        pl.BlockSpec((rows, lanes), functools.partial(lambda shift, i, *_: (0, i + shift), shift))
        for shift in (0, pairs, 2 * pairs)
    ]


def attend_forward(pos, packed, short):
    rows = packed.shape[0]
    width = packed.shape[1] // 3
    spec = pair_specs(rows, width)
    return run(
        functools.partial(attend_kernel, short), (packed, packed, packed), (width // (2 * HEAD_DIM),),
        spec, [spec[0], spec[0]], [shape((rows, width), BF16), shape((rows, width), F32)],
        "attend", scalars=(pos,),
    )


def attend_back_kernel(
    short, pos_ref, q_ref, k_ref, v_ref, o_ref, lse_ref, do_ref, dq_ref, dk_ref, dv_ref,
    dk_acc, dv_acc,
):
    rows, lanes = q_ref.shape
    first = lax.broadcasted_iota(jnp.int32, (1, lanes), 1) < HEAD_DIM
    factor = 1.0 / math.sqrt(HEAD_DIM)
    product = do_ref[...].astype(F32) * o_ref[...].astype(F32)
    lse_t = jnp.transpose(lse_ref[...])
    product_t = jnp.transpose(product)
    lse_rows = [lse_t[0:1], lse_t[HEAD_DIM : HEAD_DIM + 1]]
    delta_rows = [
        jnp.sum(product_t[:HEAD_DIM], 0, keepdims=True),
        jnp.sum(product_t[HEAD_DIM:], 0, keepdims=True),
    ]

    def part(query_at, key_at, key_count, fresh):
        chunk = slice(query_at, query_at + short)
        span = slice(key_at, key_at + key_count)
        queries, grads = (q_ref[chunk, :].astype(F32) * factor).astype(BF16), do_ref[chunk, :]
        keys, values = k_ref[span, :], v_ref[span, :]
        masks = (first, jnp.logical_not(first))

        def apart(array):
            return [jnp.where(mine, array, jnp.zeros_like(array)) for mine in masks]

        query_own, grad_own, key_own = apart(queries), apart(grads), apart(keys)
        probs = [
            jnp.exp(nt(keys, query) - lse[:, chunk]) for query, lse in zip(query_own, lse_rows)
        ]
        grad_probs = [nt(values, grad) for grad in grad_own]
        grad_scores = [
            (prob * (grad - delta[:, chunk])).astype(BF16)
            for prob, grad, delta in zip(probs, grad_probs, delta_rows)
        ]
        low = [prob.astype(BF16) for prob in probs]
        dv = nn(jnp.concatenate(low, 1), jnp.concatenate(grad_own, 0))
        dk = nn(jnp.concatenate(grad_scores, 1), jnp.concatenate(query_own, 0))
        dq = nn(jnp.transpose(jnp.concatenate(key_own, 0)), jnp.concatenate(grad_scores, 0))
        dq_ref[chunk, :] = (jnp.transpose(dq) * factor).astype(BF16)
        if fresh:
            dk_acc[span, :] = dk
            dv_acc[span, :] = dv
        else:
            dk_acc[span, :] += dk
            dv_acc[span, :] += dv

    @pl.when(pos_ref[LONG] > 0)
    def _():
        for at in range(0, rows, short):
            part(at, 0, rows, at == 0)

    @pl.when(pos_ref[LONG] <= 0)
    def _():
        for at in range(0, rows, short):
            part(at, at, short, True)

    dk_ref[...] = dk_acc[...].astype(BF16)
    dv_ref[...] = dv_acc[...].astype(BF16)


def attend_backward(pos, packed, attended, logsum, grad, short, after):
    rows, width = attended.shape
    lanes = 2 * HEAD_DIM
    spec = pair_specs(rows, width)
    return run(
        functools.partial(attend_back_kernel, short),
        (packed, packed, packed, attended, logsum, grad), (width // lanes,),
        spec + [spec[0]] * 3, [spec[0]] * 3, [shape((rows, width), BF16)] * 3,
        "attend_back", scalars=(pos,), scratch=[pltpu.VMEM((rows, lanes), F32)] * 2, after=after,
    )


def middle_kernel(att_ref, x_ref, mod_ref, w_ref, branch_ref, hidden_ref):
    block = pl.program_id(0)
    branch = nn(att_ref[...], w_ref[...])
    branch_ref[...] = branch
    middle = x_ref[...].astype(F32) + mod_ref[2, pl.ds(block, 1), :] * branch
    normed, _ = norm_parts(middle)
    shift, scale = mod_ref[3, pl.ds(block, 1), :], mod_ref[4, pl.ds(block, 1), :]
    hidden_ref[...] = (normed * (1.0 + scale) + shift).astype(BF16)


def middle_forward(attended, patches, mod, out_weight, blocks, after):
    rows, width = patches.shape
    tile = rows_spec(rows // blocks, width)
    return run(
        middle_kernel, (attended, patches, mod, out_weight), (blocks,),
        [tile, tile, like(mod), like(out_weight)], [tile, tile],
        [shape((rows, width), F32), shape((rows, width), BF16)], "middle", after=after,
    )


def rank_kernel(pos_ref, *refs):
    count = (len(refs) - 2) // 1
    routes, (row_ref, col_ref) = refs[:count], refs[count:]
    rows = routes[0].shape[1]
    before = lax.broadcasted_iota(jnp.int32, (rows, rows), 0)
    after = lax.broadcasted_iota(jnp.int32, (rows, rows), 1)
    upper = (before < after).astype(F32).astype(BF16)
    ids = pos_ref[FIRST_ALL] + lax.broadcasted_iota(jnp.int32, (8, rows), 0)
    for source, ref in enumerate(routes):
        hits = jnp.logical_or(ref[0:1, :] == ids, ref[1:2, :] == ids)
        earlier = nn(hits.astype(F32).astype(BF16), upper)
        rank = jnp.where(hits, earlier, -1.0)
        row_ref[source] = rank.astype(jnp.int32)
        tall = jnp.concatenate([rank, jnp.full((120, rows), -1.0, F32)], 0)
        col_ref[source] = jnp.transpose(tall).astype(jnp.int32)


def ranks(pos, routes, after):
    count, rows = len(routes), routes[0].shape[1]
    out = [shape((count, 8, rows), jnp.int32), shape((count, rows, 128), jnp.int32)]
    return run(
        rank_kernel, routes, (1,), [like(a) for a in routes], [like(a) for a in out], out, "ranks",
        scalars=(pos,), after=after,
    )


def touch(array, after):
    count = len(after)

    def body(*refs):
        del refs

    return pl.pallas_call(
        body,
        in_specs=[pl.BlockSpec(memory_space=pl.ANY)] * (1 + count),
        out_specs=pl.BlockSpec(memory_space=pl.ANY),
        out_shape=shape(array.shape, array.dtype),
        input_output_aliases={0: 0},
        name="touch",
    )(array, *after)


def gate_rows(hidden, routes, router_t, ids):
    logits = nt(router_t, hidden)
    every = lax.broadcasted_iota(jnp.int32, logits.shape, 0)
    first, second = routes[0:1, :], routes[1:2, :]
    zero = jnp.zeros_like(logits)
    logit_one = jnp.sum(jnp.where(every == first, logits, zero), 0, keepdims=True)
    logit_two = jnp.sum(jnp.where(every == second, logits, zero), 0, keepdims=True)
    gate_one = sigmoid(logit_one - logit_two)
    gate_two = sigmoid(logit_two - logit_one)
    return jnp.where(ids == first, gate_one, 0.0) + jnp.where(ids == second, gate_two, 0.0)


def ffn_phase_one(x, g, up_ref, down_ref, act_ref, pre_ref, step=256):
    wide = act_ref.shape[1]
    for at in range(0, wide, step):
        cols = slice(at, at + step)
        act, slope = gelu_and_slope(nn(x, up_ref[0, :, cols]))
        back = nt(g, down_ref[0, cols, :])
        act_ref[:, cols] = act.astype(BF16)
        pre_ref[:, cols] = (back * slope).astype(BF16)


def relative_rows(pos_ref, target, values, nz):
    bits = nz.bit_length() - 1
    part = values.shape[0] // (2 * nz)
    for block in range(2 * nz):
        place = (block % 2) ^ pos_ref[ROW_Y]
        place = place * nz + flipped((block // 2) ^ pos_ref[ROW_Z], bits)
        at = pl.multiple_of(place * part, part)
        target[pl.ds(at, part), :] = values[block * part : (block + 1) * part]


def sides(pos_ref, values):
    half = values.shape[1] // 2
    low, high = values[:, :half], values[:, half:]
    own_low = pos_ref[ROW_Y] == 0
    return jnp.where(own_low, low, high), jnp.where(own_low, high, low)


def expert_kernel(
    slot, sends, has_prior, pos_ref, h0_ref, h1_ref, g0_ref, g1_ref, rank_ref, routes0_ref, routes1_ref,
    router_ref, up_ref, down_ref, *rest,
):
    count = 1 + sends
    priors, rest = (rest[:count], rest[count:]) if has_prior else ((), rest)
    targets, rest = rest[:count], rest[count:]
    keep_ref = targets[0]
    (out_ref, gx_ref, gg_ref,
     x_s, xt_s, g_s, gt_s, b_s, gate_s, act_s, pre_s, out_acc, gx_acc) = rest
    tile = pl.program_id(0)
    last = pl.num_programs(0) - 1
    rows = h0_ref.shape[0]
    nz = keep_ref.shape[2] // keep_ref.shape[3] * 2
    part = h0_ref.shape[1] // (2 * nz)
    own = lax.broadcasted_iota(jnp.int32, (CAP, rows), 0)

    def hot(source):
        return (own == rank_ref[source, slot : slot + 1, :]).astype(F32)

    @pl.when(tile == 0)
    def _():
        sources = ((h0_ref, g0_ref, routes0_ref), (h1_ref, g1_ref, routes1_ref))
        for source, (h_ref, b_ref, routes_ref) in enumerate(sources):
            span = slice(source * CAP, (source + 1) * CAP)
            pick = hot(source)
            pick_low = pick.astype(BF16)
            expert = pos_ref[FIRST_ALL] + slot
            gate = gate_rows(h_ref[...], routes_ref[...], router_ref[...], expert)
            gate_col = jnp.sum(pick * gate[0:1], -1, keepdims=True)
            branch = nn(pick_low, b_ref[...])
            x_s[span, :] = nn(pick_low, h_ref[...]).astype(BF16)
            b_s[span, :] = branch.astype(BF16)
            g_s[span, :] = (branch * gate_col).astype(BF16)
            gate_s[span, :] = jnp.broadcast_to(gate_col, (CAP, 128))
        relative_rows(pos_ref, xt_s, jnp.transpose(x_s[...]), nz)
        gt_s[...] = jnp.transpose(g_s[...])
        out_acc[...] = jnp.zeros_like(out_acc)
        gx_acc[...] = jnp.zeros_like(gx_acc)

    ffn_phase_one(x_s[...], g_s[...], up_ref, down_ref, act_s, pre_s)
    act, pre = act_s[...], pre_s[...]
    out_acc[...] += nn(act, down_ref[0])
    gx_acc[...] += nt(pre, up_ref[0])

    def place(side, kind):
        return (0, kind) if side == 0 else (1, kind) if sends == 1 else (1 + kind, 0)

    dup = nn(xt_s[...], pre)
    half = dup.shape[1] // 2
    for side in range(2):
        at, entry = place(side, 0)
        for z in range(nz):
            for lanes in range(2):
                row, into = (side * nz + z) * part, (z * 2 + lanes) * part
                piece = dup[row : row + part, lanes * half : (lanes + 1) * half]
                if has_prior:
                    piece = piece + priors[at][0, entry, into : into + part, :].astype(F32)
                targets[at][0, entry, into : into + part, :] = piece.astype(BF16)
    for side, piece in enumerate(sides(pos_ref, nn(gt_s[...], act))):
        at, entry = place(side, 1)
        if has_prior:
            piece = piece + priors[at][0, entry].astype(F32)
        targets[at][0, entry] = piece.astype(BF16)

    @pl.when(tile == last)
    def _():
        for source in range(2):
            span = slice(source * CAP, (source + 1) * CAP)
            out = out_acc[span, :]
            out_ref[source] = (out * gate_s[span, 0:1]).astype(BF16)
            gx_ref[source] = gx_acc[span, :].astype(BF16)
            inner = jnp.sum(out * b_s[span, :].astype(F32), -1, keepdims=True)
            gg_ref[source] = jnp.sum(hot(source) * inner, 0, keepdims=True)


def expert_call(
    slot, sends, pos, hiddens, branches, rank_rows, routes, router_t, up, down, prior, nz, after
):
    rows, width = hiddens[0].shape
    wide = up.shape[2]
    tile = wide // nz
    bits = nz.bit_length() - 1
    count = 2 * CAP
    weights = [
        pl.BlockSpec((1, width, tile), lambda f, s: (s[FIRST_HERE] + slot, 0, f)),
        pl.BlockSpec((1, tile, width), lambda f, s: (s[FIRST_HERE] + slot, f, 0)),
    ]
    kinds = [2, 2] if sends == 1 else [2, 1, 1]
    grads = [
        pl.BlockSpec((1, kind, width, tile // 2), lambda f, s: (flipped(f ^ s[ROW_Z], bits), 0, 0, 0))
        for kind in kinds
    ]
    once = [*hiddens, *branches, rank_rows, *routes, router_t]
    out_shape = (
        [shape((nz, kind, width, tile // 2), BF16) for kind in kinds]
        + [shape((2, CAP, width), BF16)] * 2
        + [shape((2, 1, rows), F32)]
    )
    prior = () if prior is None else tuple(prior)
    return run(
        functools.partial(expert_kernel, slot, sends, bool(prior)), (*once, up, down, *prior), (nz,),
        [like(a) for a in once] + weights + (grads if prior else []),
        grads + [like(a) for a in out_shape[len(grads) :]], out_shape, "expert", scalars=(pos,), after=after,
        scratch=[
            pltpu.VMEM((count, width), BF16),
            pltpu.VMEM((width, count), BF16),
            pltpu.VMEM((count, width), BF16),
            pltpu.VMEM((width, count), BF16),
            pltpu.VMEM((count, width), BF16),
            pltpu.VMEM((count, 128), F32),
            pltpu.VMEM((count, tile), BF16),
            pltpu.VMEM((count, tile), BF16),
            pltpu.VMEM((count, width), F32),
            pltpu.VMEM((count, width), F32),
        ],
    )


def shared_kernel(
    pos_ref, h_ref, b_ref, up_ref, down_ref, ku_ref, su0_ref, su1_ref, kd_ref, sd0_ref, sd1_ref,
    out_ref, gx_ref, xt_s, gt_s, act_s, pre_s,
):
    step = pl.program_id(0)
    nz, block = 4, kd_ref.shape[3]

    @pl.when(step == 0)
    def _():
        relative_rows(pos_ref, xt_s, jnp.transpose(h_ref[...]), nz)
        turned = jnp.transpose(b_ref[...])
        for slice_at in range(4):
            place = ((slice_at % 2) ^ pos_ref[CORE]) * 2 + ((slice_at // 2) ^ pos_ref[STREAM])
            at = pl.multiple_of(place * block, block)
            gt_s[pl.ds(at, block), :] = turned[slice_at * block : (slice_at + 1) * block]
        out_ref[...] = jnp.zeros_like(out_ref)
        gx_ref[...] = jnp.zeros_like(gx_ref)

    ffn_phase_one(h_ref[...], b_ref[...], up_ref, down_ref, act_s, pre_s)
    act, pre = act_s[...], pre_s[...]
    out_ref[...] += nn(act, down_ref[0])
    gx_ref[...] += nt(pre, up_ref[0])
    dup = nn(xt_s[...], pre).astype(BF16)

    @pl.when(step < 2)
    def _():
        ku_ref[0] = dup

    @pl.when(step == 2)
    def _():
        su0_ref[...] = dup

    @pl.when(step == 3)
    def _():
        su1_ref[...] = dup

    for y, piece in enumerate(sides(pos_ref, nn(gt_s[...], act))):
        pieces = [piece[place * block : (place + 1) * block].astype(BF16) for place in range(4)]
        kd_ref[0, y, 0], kd_ref[1, y, 0] = pieces[0], pieces[1]
        sd0_ref[y, 0], sd1_ref[y, 0] = pieces[2], pieces[3]


def shared_call(pos, hidden, branch, up, down, after):
    rows, width = hidden.shape
    wide = up.shape[1]
    nz = 4
    tile = wide // nz
    block = width // 4

    def unit(f, s):
        return (f % 2 ^ s[STREAM]) * 2 + (f // 2 ^ s[CORE])

    keep = pl.BlockSpec((1, width, tile), lambda f, s: (jnp.minimum(f, 1), 0, 0))
    downs = pl.BlockSpec(
        (2, 2, 1, block, tile // 2), lambda f, s: (0, 0, flipped(unit(f, s) ^ s[ROW_Z], 2), 0, 0)
    )
    sent = pl.BlockSpec((2, 1, block, tile // 2), lambda f, s: (0, flipped(unit(f, s) ^ s[ROW_Z], 2), 0, 0))
    outs = run(
        shared_kernel, (hidden, branch, up[None], down[None]), (nz,),
        [
            like(hidden),
            like(branch),
            pl.BlockSpec((1, width, tile), lambda f, s: (0, 0, unit(f, s))),
            pl.BlockSpec((1, tile, width), lambda f, s: (0, unit(f, s), 0)),
        ],
        [keep] + [full((width, tile))] * 2 + [downs, sent, sent, like(hidden), like(hidden)],
        [shape((2, width, tile), BF16)] + [shape((width, tile), BF16)] * 2
        + [shape((2, 2, nz, block, tile // 2), BF16)] + [shape((2, nz, block, tile // 2), BF16)] * 2
        + [shape((rows, width), F32)] * 2,
        "shared", scalars=(pos,), after=after,
        scratch=[
            pltpu.VMEM((width, rows), BF16),
            pltpu.VMEM((width, rows), BF16),
            pltpu.VMEM((rows, tile), BF16),
            pltpu.VMEM((rows, tile), BF16),
        ],
    )
    return outs[0], outs[1:3], outs[3], outs[4:6], *outs[6:]


def combine_kernel(places, col_ref, *refs):
    slots = len(places)
    rows_refs, refs = refs[: 2 * slots], refs[2 * slots :]
    targets, stacks = refs[:5], refs[5:]

    @pl.when(pl.program_id(0) == 0)
    def _():
        for slot in range(slots):
            for kind in range(2):
                for source in range(2):
                    stacks[kind][source, slot * CAP : (slot + 1) * CAP, :] = rows_refs[2 * slot + kind][places[slot] + source]

    block = col_ref.shape[1]
    own = lax.broadcasted_iota(jnp.int32, (block, slots * CAP), 1)
    for source in range(2):
        hits = None
        for slot in range(slots):
            rank = col_ref[source, :, slot : slot + 1]
            place = jnp.where(rank < 0, -1, rank + slot * CAP)
            hit = place == own
            hits = hit if hits is None else jnp.logical_or(hits, hit)
        pick = hits.astype(F32).astype(BF16)
        for kind in range(2):
            total = nn(pick, stacks[kind][source]).astype(BF16)
            if 2 * kind + source < 3:
                targets[2 * kind + source][...] = total
            else:
                early = pl.program_id(0) < pl.num_programs(0) // 2

                @pl.when(early)
                def _():
                    targets[3][...] = total

                @pl.when(jnp.logical_not(early))
                def _():
                    targets[4][...] = total


def combine(rank_cols, pairs, places, after):
    count, rows, _ = rank_cols.shape
    width = pairs[0][0].shape[2]
    block = rows // 4
    flat = [a for pair in pairs for a in pair]
    halves = [
        pl.BlockSpec((block, width), lambda i: (jnp.minimum(i, 1), 0)),
        pl.BlockSpec((block, width), lambda i: (jnp.maximum(i - 2, 0), 0)),
    ]
    *outs, low, high = run(
        functools.partial(combine_kernel, places), (rank_cols, *flat), (rows // block,),
        [pl.BlockSpec((count, block, 128), lambda i: (0, i, 0))] + [like(a) for a in flat],
        [rows_spec(block, width)] * 3 + halves,
        [shape((rows, width), BF16)] * 3 + [shape((rows // 2, width), BF16)] * 2, "combine",
        scratch=[pltpu.VMEM((2, len(pairs) * CAP, width), BF16)] * 2, after=after,
    )
    return (*outs, (low, high))


def add_kernel(left_ref, low_ref, high_ref, second_ref, third_ref, one_ref, two_ref):
    two_ref[...] = (second_ref[...].astype(F32) + third_ref[...].astype(F32)).astype(BF16)
    low = pl.program_id(0) < pl.num_programs(0) // 2
    right = jnp.where(low, low_ref[...], high_ref[...])
    one_ref[...] = (left_ref[...].astype(F32) + right.astype(F32)).astype(BF16)


def add_rows(left, halves, second, third, after):
    rows, width = left.shape
    tile = rows_spec(rows // 4, width)
    low = pl.BlockSpec((rows // 4, width), lambda i: (jnp.minimum(i, 1), 0))
    high = pl.BlockSpec((rows // 4, width), lambda i: (jnp.maximum(i - 2, 0), 0))
    return run(
        add_kernel, (left, *halves, second, third), (4,), [tile, low, high, tile, tile], [tile] * 2,
        [shape((rows, width), BF16)] * 2, "add_rows", after=after,
    )


def total_of(keep, arrived):
    return keep.astype(F32) + arrived.astype(F32)


def halve_kinds_kernel(kinds, *refs):
    keep_ref, send_ref = refs[-2:]
    refs = iter(refs[:-2])
    for at, kind in enumerate(kinds):
        if kind == 0:
            total = total_of(next(refs)[0, 0], next(refs)[0, 0])
            half = total.shape[0] // 2
            keep_ref[at, 0], send_ref[at, 0] = total[:half], total[half:].astype(BF16)
        else:
            keep_ref[at, 0] = total_of(next(refs)[0, 0], next(refs)[0, 0])
            send_ref[at, 0] = total_of(next(refs)[0, 0], next(refs)[0, 0]).astype(BF16)


def halve_y(keep, arrived, kinds, after):
    nz, _, rows, cols = keep.shape
    split = lambda a: a.reshape(nz, -1, rows // 2, cols)
    args, specs = [], []
    for at, kind in enumerate(kinds):
        for add in (0, nz // 2) if kind else (0,):
            for array, entry in ((keep, kind), (arrived, at)):
                if kind == 0:
                    args.append(array)
                    index = functools.partial(lambda entry, t: (t, entry, 0, 0), entry)
                    specs.append(pl.BlockSpec((1, 1, rows, cols), index))
                else:
                    args.append(split(array))
                    index = functools.partial(
                        lambda entry, add, t: (t // 2 + add, 2 * entry + t % 2, 0, 0), entry, add
                    )
                    specs.append(pl.BlockSpec((1, 1, rows // 2, cols), index))
    out = pl.BlockSpec((len(kinds), 1, rows // 2, cols), lambda t: (0, t, 0, 0))
    dims = (len(kinds), nz, rows // 2, cols)
    return run(
        functools.partial(halve_kinds_kernel, kinds), args, (nz,), specs, [out, out],
        [shape(dims, F32), shape(dims, BF16)], "halve_y", after=after,
    )


def halve_z(keep, arrived, kinds, after):
    _, nz, rows, cols = keep.shape
    split = lambda a: a.reshape(len(kinds), 2 * nz, rows // 2, cols)
    args, specs = [], []
    for at, kind in enumerate(kinds):
        for add in (0, nz) if kind else (0,):
            for array, flip in ((keep, 0), (arrived, nz // 2)):
                if kind == 0:
                    args.append(array)
                    index = functools.partial(lambda at, flip, t: (at, t ^ flip, 0, 0), at, flip)
                    specs.append(pl.BlockSpec((1, 1, rows, cols), index))
                else:
                    args.append(split(array))
                    index = functools.partial(lambda at, add, t: (at, t + add, 0, 0), at, add)
                    specs.append(pl.BlockSpec((1, 1, rows // 2, cols), index))
    out = pl.BlockSpec((len(kinds), 1, rows // 2, cols), lambda t: (0, t, 0, 0))
    dims = (len(kinds), nz, rows // 2, cols)
    return run(
        functools.partial(halve_kinds_kernel, kinds), args, (nz,), specs, [out, out],
        [shape(dims, F32), shape(dims, BF16)], "halve_z", after=after,
    )


def core_halves(pos_ref, values):
    half = values.shape[0] // 2
    low, high = values[:half], values[half:]
    own_low = pos_ref[CORE] == 0
    return jnp.where(own_low, low, high), jnp.where(own_low, high, low).astype(BF16)


def finish_kinds_kernel(kinds, pos_ref, *refs):
    inputs, outs = refs[: 2 * len(kinds)], refs[2 * len(kinds) :]
    for at, kind in enumerate(kinds):
        keep_ref, arrived_ref = inputs[2 * at : 2 * at + 2]
        mine, sent = outs[2 * at : 2 * at + 2]
        if kind == 0:
            up = total_of(keep_ref[0, 0], arrived_ref[0, 0])
            half = up.shape[0] // 2
            mine[...], sent[...] = core_halves(pos_ref, jnp.concatenate([up[:half], up[half:]], 1))
        else:

            @pl.when(pl.program_id(0) == 0)
            def _():
                down = total_of(keep_ref[0], arrived_ref[0])
                down = down.reshape(down.shape[0] * down.shape[1], down.shape[2])
                mine[...], sent[...] = core_halves(pos_ref, jnp.transpose(down))


def finish_kinds(pos, keep, arrived, kinds, after):
    _, nz, rows, cols = keep.shape
    bits = nz.bit_length() - 1
    args, specs, out_specs, outs = [], [], [], []
    for at, kind in enumerate(kinds):
        args += [keep, arrived]
        if kind == 0:
            for flip in (0, 1):
                index = functools.partial(lambda at, flip, t, s: (at, t ^ flip, 0, 0), at, flip)
                specs.append(pl.BlockSpec((1, 1, rows, cols), index))
            dims = (rows // 4, 2 * cols * nz)
            out = pl.BlockSpec((rows // 4, 2 * cols), lambda t, s: (0, flipped(t, bits) ^ s[ROW_Z]))
        else:
            index = functools.partial(lambda at, t, s: (at, 0, 0, 0), at)
            specs += [pl.BlockSpec((1, nz, rows, cols), index)] * 2
            dims = (cols // 2, nz * rows)
            out = full(dims)
        out_specs += [out, out]
        outs += [shape(dims, F32), shape(dims, BF16)]
    return run(
        functools.partial(finish_kinds_kernel, kinds), args, (nz,), specs, out_specs, outs, "finish_kinds",
        scalars=(pos,), after=after,
    )


def halve_slices_kernel(ku_ref, kd_ref, au0_ref, au1_ref, ad0_ref, ad1_ref, keep_ref, send_ref):
    ups, downs = (au0_ref, au1_ref), (ad0_ref, ad1_ref)
    for at, ref in enumerate((keep_ref, send_ref)):
        up = total_of(ku_ref[at], ups[at][...])
        rows, half = up.shape[0], up.shape[1] // 2
        for side in range(2):
            piece = up[:, side * half : (side + 1) * half]
            ref[0, side * rows : (side + 1) * rows, :] = piece.astype(ref.dtype)
        ref[1] = total_of(kd_ref[at], downs[at][...]).astype(ref.dtype)


def halve_slices(up_keep, down_keep, arrived, after):
    _, rows, cols = up_keep.shape
    steps = 8
    down_keep = down_keep.reshape(2, 2 * rows, cols // 2)
    arrived = [a.reshape(-1, a.shape[-1]) for a in arrived]
    ups = pl.BlockSpec((2, rows // steps, cols), lambda i: (0, i, 0))
    downs = pl.BlockSpec((2, 2 * rows // steps, cols // 2), lambda i: (0, i, 0))
    dims = (2, 2 * rows, cols // 2)
    return run(
        halve_slices_kernel, (up_keep, down_keep, *arrived), (steps,),
        [ups, downs] + [rows_spec(a.shape[0] // steps, a.shape[1]) for a in arrived],
        [downs, downs], [shape(dims, F32), shape(dims, BF16)], "halve_slices", after=after,
    )


def halve_kernel(keep_ref, arrived_ref, keep_out, send_out):
    keep_out[...] = total_of(keep_ref[:, 0], arrived_ref[:, 0])
    send_out[...] = total_of(keep_ref[:, 1], arrived_ref[:, 1]).astype(BF16)


def halve(keep, arrived, after, steps=2):
    kinds, rows, cols = keep.shape
    split = lambda a: a.reshape(kinds, 2, rows // 2, cols)
    into = pl.BlockSpec((kinds, 2, rows // 2 // steps, cols), lambda i: (0, 0, i, 0))
    out = pl.BlockSpec((kinds, rows // 2 // steps, cols), lambda i: (0, i, 0))
    dims = (kinds, rows // 2, cols)
    return run(
        halve_kernel, (split(keep), split(arrived)), (steps,), [into, into], [out, out],
        [shape(dims, F32), shape(dims, BF16)], "halve", after=after,
    )


def halve_parts_kernel(keep_ref, first_ref, second_ref, keep_out, send_out):
    keep_out[0] = total_of(keep_ref[0], first_ref[...])
    send_out[0] = total_of(keep_ref[1], second_ref[...]).astype(BF16)


def halve_parts(keep, arrived, after, steps=2):
    _, rows, cols = keep.shape
    into = pl.BlockSpec((2, rows // steps, cols), lambda i: (0, i, 0))
    out = pl.BlockSpec((1, rows // steps, cols), lambda i: (0, i, 0))
    return run(
        halve_parts_kernel, (keep, *arrived), (steps,), [into] + [rows_spec(rows // steps, cols)] * 2,
        [out, out], [shape((1, rows, cols), F32), shape((1, rows, cols), BF16)], "halve_parts", after=after,
    )


def finish_slices_kernel(merged, pos_ref, keep_ref, arrived_ref, *outs):
    total = total_of(keep_ref[...], arrived_ref[...])
    up = total[0]
    if merged:
        half = up.shape[0] // 2
        up = jnp.concatenate([up[:half], up[half:]], 1)
        mine, outs[3][...] = core_halves(pos_ref, jnp.transpose(total[1]))
        outs[2][...] = mine.astype(BF16)
    mine, outs[1][...] = core_halves(pos_ref, up)
    outs[0][...] = mine.astype(BF16)


def finish_slices(pos, keep, arrived, merged, after):
    _, rows, cols = keep.shape
    dims = [(rows // 4, 2 * cols), (cols // 2, rows)] if merged else [(rows // 2, cols)]
    outs = [shape(d, BF16) for d in dims for _ in range(2)]
    return run(
        functools.partial(finish_slices_kernel, merged), (keep, arrived), (1,), [like(keep), like(arrived)],
        [like(a) for a in outs], outs, "finish_slices", scalars=(pos,), after=after,
    )


def middle_back_kernel(
    gs_ref, ga_ref, low_ref, high_ref, gc_ref, gg_ref, routes_ref, router_ref,
    hidden_ref, cot_ref, branch_ref, x_ref, mod_ref, w_ref,
    gm_ref, gatt_ref, back_ref, mods_ref, drouter_ref,
):
    block = pl.program_id(0)
    hidden = hidden_ref[...]
    grad_gates = gg_ref[...]
    ids = lax.broadcasted_iota(jnp.int32, grad_gates.shape, 0)
    gates = gate_rows(hidden, routes_ref[...], router_ref[...], ids)
    inner = jnp.sum(gates * grad_gates, 0, keepdims=True)
    grad_logits = gates * (grad_gates - inner)
    core = jnp.where(block < pl.num_programs(0) // 2, low_ref[...], high_ref[...])
    grad = gs_ref[...] + ga_ref[...].astype(F32) + core.astype(F32) + gc_ref[...].astype(F32)
    drouter = 0.0
    for piece in three_parts(grad_logits):
        grad = grad + tn(piece, router_ref[...])
        drouter = drouter + nn(piece, hidden)
    branch = branch_ref[...]
    gate_one = mod_ref[2, pl.ds(block, 1), :]
    middle = x_ref[...].astype(F32) + gate_one * branch
    normed, spread = norm_parts(middle)
    scale = mod_ref[4, pl.ds(block, 1), :]
    mods_ref[1, pl.ds(block, 1), :] = jnp.sum(grad, 0, keepdims=True)
    mods_ref[2, pl.ds(block, 1), :] = jnp.sum(grad * normed, 0, keepdims=True)
    grad_middle = cot_ref[...].astype(F32) + norm_back(grad * (1.0 + scale), normed, spread)
    mods_ref[0, pl.ds(block, 1), :] = jnp.sum(grad_middle * branch, 0, keepdims=True)
    gm_ref[...] = grad_middle
    grad_branch = (grad_middle * gate_one).astype(BF16)
    back_ref[...] = grad_branch
    gatt_ref[...] = nt(grad_branch, w_ref[...]).astype(BF16)

    @pl.when(block == 0)
    def _():
        drouter_ref[...] = drouter

    @pl.when(block > 0)
    def _():
        drouter_ref[...] += drouter


def middle_backward(parts, gg, routes_t, router_t, hidden, cot, branch, patches, mod, out_weight, blocks, after):
    rows, width = patches.shape
    short = rows // blocks
    tile = rows_spec(short, width)
    cols = lambda a: pl.BlockSpec((a.shape[0], short), lambda i: (0, i))
    half = blocks // 2
    low = pl.BlockSpec((short, width), lambda i: (jnp.minimum(i, half - 1), 0))
    high = pl.BlockSpec((short, width), lambda i: (jnp.maximum(i - half, 0), 0))
    out_shape = [
        shape((rows, width), F32),
        shape((rows, width), BF16),
        shape((rows, width), BF16),
        shape((3, 8, width), F32),
        shape((router_t.shape[0], width), F32),
    ]
    return run(
        middle_back_kernel,
        (*parts, gg, routes_t, router_t, hidden, cot, branch, patches, mod, out_weight), (blocks,),
        [tile, tile, low, high, tile] + [cols(gg), cols(routes_t), like(router_t)] + [tile] * 4 + [like(mod), like(out_weight)],
        [tile] * 3 + [like(a) for a in out_shape[3:]], out_shape, "middle_back", after=after,
    )


def mixed_kernel(so_ref, ra_ref, rb_ref, rc_ref, cot_ref, branch_ref, x_ref, mod_ref, mixed_ref, gate_ref):
    block = pl.program_id(0)
    second = so_ref[...] + ra_ref[...].astype(F32) + rb_ref[...].astype(F32) + rc_ref[...].astype(F32)
    middle = x_ref[...].astype(F32) + mod_ref[2, pl.ds(block, 1), :] * branch_ref[...]
    mixed_ref[...] = (middle + mod_ref[5, pl.ds(block, 1), :] * second).astype(BF16)
    gate_ref[pl.ds(block, 1), :] = jnp.sum(cot_ref[...].astype(F32) * second, 0, keepdims=True)


def mixed_forward(parts, cot, branch, patches, mod, blocks, after):
    rows, width = patches.shape
    tile = rows_spec(rows // blocks, width)
    return run(
        mixed_kernel, (*parts, cot, branch, patches, mod), (blocks,), [tile] * 7 + [like(mod)],
        [tile, full((8, width))], [shape((rows, width), BF16), shape((8, width), F32)], "mixed", after=after,
    )


def weight_kernel(
    pos_ref, x_ref, mod_ref, dq_ref, dk_ref, dv_ref, att_ref, back_ref, keep_ref, first_ref, second_ref, turned
):
    rows = x_ref.shape[0]
    short = rows // 4
    step = pl.program_id(0)
    matrix = ((step % 2) ^ pos_ref[STREAM]) * 2 + ((step // 2) ^ pos_ref[CORE])
    nz = 4

    @pl.when(step == 0)
    def _():
        for block in range(4):
            span = slice(block * short, (block + 1) * short)
            normed, _ = norm_parts(x_ref[span, :].astype(F32))
            hidden = normed * (1.0 + mod_ref[1, block : block + 1, :]) + mod_ref[0, block : block + 1, :]
            relative_rows(pos_ref, turned.at[0, :, span], jnp.transpose(hidden.astype(BF16)), nz)
        relative_rows(pos_ref, turned.at[1], jnp.transpose(att_ref[...]), nz)

    for index, (left, ref) in enumerate(((0, dq_ref), (0, dk_ref), (0, dv_ref), (1, back_ref))):

        @pl.when(matrix == index)
        def _():
            total = nn(turned[left], ref[...]).astype(BF16)

            @pl.when(step < 2)
            def _():
                keep_ref[0] = total

            @pl.when(step == 2)
            def _():
                first_ref[...] = total

            @pl.when(step == 3)
            def _():
                second_ref[...] = total


def weight_grads(pos, patches, mod, grads, attended, back, after):
    rows, width = patches.shape
    args = (patches, mod, *grads, attended, back)
    keep = pl.BlockSpec((1, width, width), lambda f, s: (jnp.minimum(f, 1), 0, 0))
    send = full((width, width))
    outs = run(
        weight_kernel, args, (4,), [like(a) for a in args], [keep, send, send],
        [shape((2, width, width), BF16)] + [shape((width, width), BF16)] * 2, "weight_grads", scalars=(pos,),
        scratch=[pltpu.VMEM((2, width, rows), BF16)], after=after,
    )
    return outs[0], outs[1:]


def inputs_back_kernel(dq_ref, dk_ref, dv_ref, w_ref, x_ref, gm_ref, mod_ref, gp_ref, mods_ref):
    block = pl.program_id(0)
    width = x_ref.shape[1]
    grad = nt(dq_ref[...], w_ref[:, :width])
    grad = grad + nt(dk_ref[...], w_ref[:, width : 2 * width])
    grad = grad + nt(dv_ref[...], w_ref[:, 2 * width :])
    normed, spread = norm_parts(x_ref[...].astype(F32))
    mods_ref[0, pl.ds(block, 1), :] = jnp.sum(grad, 0, keepdims=True)
    mods_ref[1, pl.ds(block, 1), :] = jnp.sum(grad * normed, 0, keepdims=True)
    scale = mod_ref[1, pl.ds(block, 1), :]
    gp_ref[...] = gm_ref[...] + norm_back(grad * (1.0 + scale), normed, spread)


def inputs_backward(grads, weight, patches, grad_middle, mod, blocks, after):
    rows, width = patches.shape
    tile = rows_spec(rows // blocks, width)
    return run(
        inputs_back_kernel, (*grads, weight, patches, grad_middle, mod), (blocks,),
        [tile] * 3 + [like(weight), tile, tile, like(mod)], [tile, full((2, 8, width))],
        [shape((rows, width), F32), shape((2, 8, width), F32)], "inputs_back", after=after,
    )


def used_kernel(block_count, pos_ref, gm_ref, ada_ref, emb_ref, out_ref):
    piece = pl.program_id(0)

    @pl.when(piece == 0)
    def _():
        out_ref[...] = jnp.zeros_like(out_ref)

    for part in three_parts(gm_ref[0]):
        out_ref[...] += nt(part, ada_ref[...])

    @pl.when(piece == pl.num_programs(0) - 1)
    def _():
        emb = emb_ref[...]
        is_long = pos_ref[LONG] > 0
        used = jnp.where(is_long, jnp.broadcast_to(emb[0:1], emb.shape), emb)
        gate = sigmoid(used)
        grad = out_ref[...] * (gate * (1.0 + used * (1.0 - gate)))
        row = lax.broadcasted_iota(jnp.int32, grad.shape, 0)
        grad = jnp.where(row < block_count, grad, 0.0)
        total = jnp.sum(grad, 0, keepdims=True)
        out_ref[...] = jnp.where(is_long, jnp.where(row == 0, total, 0.0), grad)


def used_backward(pos, grad_mod, ada_weight, emb_pad, block_count, after):
    rows, width = emb_pad.shape
    pieces = grad_mod.shape[0]
    return run(
        functools.partial(used_kernel, block_count), (grad_mod, ada_weight, emb_pad), (pieces,),
        [
            pl.BlockSpec((1, rows, width), lambda i, *_: (i, 0, 0)),
            pl.BlockSpec((width, width), lambda i, *_: (0, i)),
            like(emb_pad),
        ],
        like(emb_pad), shape((rows, width), F32), "used_back", scalars=(pos,), after=after,
    )


def swap(values, axis, bit):
    size = lax.axis_size(axis)
    return lax.ppermute(values, axis, [(i, i ^ bit) for i in range(size)])


def swap_all(arrays, axis, bit):
    return [swap(a, axis, bit) for a in arrays]


def swap_across(values):
    stream = lax.axis_size("stream")
    pairs = [
        (i, ((i // stream) ^ 1) * stream + ((i % stream) ^ 1))
        for i in range(lax.axis_size("dp") * stream)
    ]
    return lax.ppermute(values, ("dp", "stream"), pairs)


def in_order(own, mine, arrived, axis):
    return jnp.concatenate(
        [jnp.where(own == 0, mine, arrived), jnp.where(own == 0, arrived, mine)], axis
    )


def local_pair(
    patches, embedding, long_image, routes, cotangent, ada_weight, qkv_weight, out_weight, shared_up,
    shared_down, router_weight, expert_up, expert_down,
):
    rows, width = patches.shape
    blocks = embedding.shape[0]
    short = rows // blocks
    dp_size = lax.axis_size("dp")
    nz = dp_size // 4
    dp, stream = lax.axis_index("dp"), lax.axis_index("stream")
    core, row_y, row_z = dp % 2, (dp // 2) % 2, dp // 4
    local_experts = expert_up.shape[0]
    here = local_experts // 2
    first_here = core * here
    first_all = stream * local_experts + first_here
    places = [long_image[0], core, stream, row_y, row_z, first_here, first_all, 0]
    pos = jnp.stack([jnp.asarray(a, jnp.int32) for a in places])

    routes_t = routes.T
    routes_x = swap(routes_t, "stream", 1)
    routes_near = (routes_t, swap(routes_t, "dp", 1))
    routes_far = (routes_x, swap(routes_x, "dp", 1))
    emb_pad = jnp.pad(embedding, ((0, 8 - blocks), (0, 0)))
    router_t = jnp.pad(router_weight.T, ((0, 16 - router_weight.shape[1]), (0, 0)))
    mod, act, branch_grad = modulate(pos, emb_pad, ada_weight, cotangent, blocks)
    branch_grad = touch(branch_grad, (routes_far[1], routes_near[1]))
    branch_x = swap(branch_grad, "stream", 1)
    branches_near = (branch_grad, swap(branch_grad, "dp", 1))

    packed = qkv_forward(patches, mod, qkv_weight, blocks, (branch_grad,))
    attended, logsum = attend_forward(pos, packed, short)
    branch_one, hidden = middle_forward(
        attended, patches, mod, out_weight, blocks, ()
    )
    hidden_x = swap(hidden, "stream", 1)
    hiddens_near = (hidden, swap(hidden, "dp", 1))
    rank_near, cols_near = ranks(pos, routes_near, (hidden,))
    rank_far, cols_far = ranks(pos, routes_far, (rank_near,))
    branch_x = touch(branch_x, (rank_far,))
    branches_far = (branch_x, swap(branch_x, "dp", 1))

    def expert(slot, is_far, sends, prior, after):
        group = (
            (hiddens_far, branches_far, rank_far, routes_far)
            if is_far
            else (hiddens_near, branches_near, rank_near, routes_near)
        )
        out = expert_call(slot, sends, pos, *group, router_t, expert_up, expert_down, prior, nz, after)
        return out[: 1 + sends], out[1 + sends :]

    first, first_near = expert(0, False, 1, None, (branch_x,))
    hidden_x = touch(hidden_x, (first_near[2],))
    hiddens_far = (hidden_x, swap(hidden_x, "dp", 1))
    first, first_far = expert(0, True, 1, first, ())
    first_arrived = swap(first[1], "dp", 2)

    second, second_near = expert(1, False, 2, None, (first_far[2],))
    second, second_far = expert(1, True, 2, second, ())
    up_half_arrived = swap(second[1], "dp", 2)
    out_x, out_xc, gx_x, gx_xc = combine(cols_far, [r[:2] for r in (first_far, second_far)], (0, 0), ())
    gx_xc, out_xc = swap_all(gx_xc, "dp", 1), swap(out_xc, "dp", 1)
    out_near, out_core, gx_near, gx_core = combine(
        cols_near, [r[:2] for r in (first_near, second_near)], (0, 0), (gx_x,)
    )
    gx_core = swap_all(gx_core, "dp", 1)
    out_core = swap(out_core, "dp", 1)
    gx_sum, out_sum = add_rows(gx_x, gx_xc, out_x, out_xc, (gx_near,))
    gx_back = swap(gx_sum, "stream", 1)
    out_back = swap(out_sum, "stream", 1)
    both, up, down = (0, 1), (0,), (1,)
    ea_keep, ea_send = halve_y(first[0], first_arrived, both, (out_sum,))
    ea_arrived = swap(ea_send, "dp", 4)
    near, far = (first_near, second_near), (first_far, second_far)
    gg_near = [jnp.concatenate([r[2][source] for r in near], 0) for source in range(2)]
    gg_far = [jnp.concatenate([r[2][source] for r in far], 0) for source in range(2)]
    gg_back = swap(jnp.concatenate([gg_far[0], swap(gg_far[1], "dp", 1)], 0), "stream", 1)
    gg_rel = jnp.concatenate([gg_near[0], swap(gg_near[1], "dp", 1), gg_back], 0)
    order = jnp.arange(4, dtype=jnp.int32) ^ (stream * 2 + core)
    gg = gg_rel.reshape(4, here, rows)[order].reshape(EXPERTS, rows)
    gg = jnp.pad(gg, ((0, 16 - EXPERTS), (0, 0)))

    out_core = touch(out_core, (ea_send,))
    down_half = touch(second[2], (out_core,))
    down_half_arrived = swap(down_half, "dp", 2)
    up_keep, up_send, down_keep, down_send, shared_out, shared_gx = shared_call(
        pos, hidden, branch_grad, shared_up, shared_down, (down_half, *gx_core, gg)
    )
    sh_arrived = swap_all([*up_send, *down_send], "dp", 1)

    grad_middle, grad_attended, back, mods_two, drouter = middle_backward(
        (shared_gx, gx_near, *gx_core, gx_back), gg, routes_t, router_t, hidden, cotangent, branch_one,
        patches, mod, out_weight, blocks, (),
    )
    ea_keep, ea_send = halve_z(ea_keep, ea_arrived, both, (grad_attended,))
    ea_arrived = swap(ea_send, "dp", 8)
    bu_keep, bu_send = halve_y(second[0], up_half_arrived, up, (ea_send,))
    bu_arrived = swap(bu_send, "dp", 4)
    sh_keep, sh_send = halve_slices(up_keep, down_keep, sh_arrived, (bu_send,))
    sh_arrived = swap(sh_send, "stream", 1)
    grads = attend_backward(pos, packed, attended, logsum, grad_attended, short, (sh_send,))
    out_back = touch(out_back, (grads[0],))
    bd_keep, bd_send = halve_y(second[0], down_half_arrived, down, (out_back,))
    bd_arrived = swap(bd_send, "dp", 4)
    bu_keep, bu_send = halve_z(bu_keep, bu_arrived, up, (bd_send,))
    bu_arrived = swap(bu_send, "dp", 8)
    ea_arrived = touch(ea_arrived, (bu_send,))
    qk_keep, qk_send = weight_grads(pos, patches, mod, grads, attended, back, (ea_arrived,))
    qk_arrived = swap_all(qk_send, "dp", 1)
    sh_keep, sh_send = halve(sh_keep, sh_arrived, (qk_send[0],))
    sh_arrived = swap(sh_send, "dp", 2)
    qk_keep, qk_send = halve_parts(qk_keep, qk_arrived, (sh_send,))
    qk_arrived = swap(qk_send, "stream", 1)
    mixed, gate_two = mixed_forward(
        (shared_out, out_near, out_core, out_back), cotangent, branch_one, patches, mod, blocks, (qk_send,)
    )
    grad_patches, mods_one = inputs_backward(grads, qkv_weight, patches, grad_middle, mod, blocks, (gate_two,))
    factors = [a[:blocks] for a in (act, *mods_one, *mods_two, gate_two)]
    factors = jnp.concatenate(factors + [drouter[:EXPERTS].reshape(blocks, -1)], 1).astype(BF16)

    def doubled(axis, bit, after):
        return jnp.concatenate([factors, touch(swap(factors, axis, bit), (after,))], 0)

    grad_mod = jnp.concatenate([mods_one, mods_two, gate_two[None]], 0)
    bu_arrived = touch(bu_arrived, (mods_one,))
    bd_keep, bd_send = halve_z(bd_keep, bd_arrived, down, (bu_arrived,))
    bd_arrived = swap(bd_send, "dp", 8)
    qk_keep, qk_send = halve(qk_keep, qk_arrived, (bd_send,))
    qk_arrived = swap(qk_send, "dp", 2)
    factors = doubled("dp", 8, qk_send)
    sh_keep, sh_send = halve(sh_keep, sh_arrived, (qk_send,))
    sh_arrived = swap(sh_send, "dp", 4)
    grad_embedding = used_backward(pos, grad_mod, ada_weight, emb_pad, blocks, (sh_send,))
    factors = doubled("dp", 4, grad_embedding)
    qk_keep, qk_send = halve(qk_keep, qk_arrived, (grad_embedding,))
    qk_arrived = swap(qk_send, "dp", 4)
    bd_arrived = touch(bd_arrived, (qk_send,))
    factors = doubled("dp", 2, bd_arrived)
    ea_done = finish_kinds(pos, ea_keep, ea_arrived, both, (bd_arrived,))
    qk_keep, qk_send = halve(qk_keep, qk_arrived, (ea_done[1],))
    qk_arrived = swap(qk_send, "dp", 8)
    factors = doubled("stream", 1, qk_send)
    sh_keep, sh_send = halve(sh_keep, sh_arrived, (qk_send,))
    sh_arrived = swap(sh_send, "dp", 8)
    bu_done = finish_kinds(pos, bu_keep, bu_arrived, up, (sh_send,))
    bd_done = finish_kinds(pos, bd_keep, bd_arrived, down, (bu_done[1],))
    factors = doubled("dp", 1, bd_done[1])
    ea_others = [touch(swap(a, "dp", 1), (bd_done[1],)) for a in (ea_done[1], ea_done[3])]
    sh_arrived = touch(sh_arrived, (bd_done[1],))

    share = width // dp_size

    def own_share(values):
        return lax.dynamic_slice_in_dim(values, dp * share, share, 1)

    wide = 7 * width
    acts = own_share(factors[:, :width])
    grad_ada = lax.dot_general(acts, factors[:, width:wide], (((0,), (0,)), ((), ())), preferred_element_type=F32)
    drouter_sum = jnp.sum(factors[:, wide:].astype(F32).reshape(-1, blocks, 2 * width), 0)
    grad_router = own_share(drouter_sum.reshape(EXPERTS, width)).T

    qk_done = finish_slices(pos, qk_keep, qk_arrived, False, (grad_ada, sh_arrived, *ea_others))
    bu_others = touch(swap(bu_done[1], "dp", 1), (qk_done[1],))
    bd_others = touch(swap(bd_done[1], "dp", 1), (qk_done[1],))
    sh_done = finish_slices(pos, sh_keep, sh_arrived, True, (qk_done[1],))

    def experts_out(one, two, one_other, two_other):
        mine, others = jnp.stack([one, two]), jnp.stack([one_other, two_other]).astype(F32)
        return in_order(core, mine, others, 0)

    def slices_out(mine, send):
        near = in_order(core, mine, swap(send, "dp", 1), 1)
        far = in_order(core, swap(mine, "stream", 1), swap_across(send), 1)
        return in_order(stream, near, far, 1).astype(F32)

    grad_qkv_out = slices_out(*qk_done)
    return (
        mixed, grad_patches, grad_embedding[:blocks], grad_ada, grad_qkv_out[:, : 3 * width],
        grad_qkv_out[:, 3 * width :], slices_out(*sh_done[:2]), slices_out(*sh_done[2:]), grad_router,
        experts_out(ea_done[0], bu_done[0], ea_others[0], bu_others),
        experts_out(ea_done[2], bd_done[0], ea_others[1], bd_others),
    )


def local(*arrays):
    experts, width, wide = arrays[11].shape
    pair = lax.axis_size("stream") == 2 and experts == 4 and lax.axis_size("dp") == 16
    if pair and wide == 4 * width:
        return local_pair(*arrays)
    return local_general(*arrays)


def solution(mesh):
    return jax.shard_map(
        local,
        mesh=mesh,
        in_specs=(
            P(("dp", "stream"), None),
            P(("dp", "stream"), None),
            P(("dp", "stream")),
            P(("dp", "stream"), None),
            P(("dp", "stream"), None),
            P(),
            P(),
            P(),
            P(),
            P(),
            P(),
            P("stream", None, None),
            P("stream", None, None),
        ),
        out_specs=(
            P(("dp", "stream"), None),
            P(("dp", "stream"), None),
            P(("dp", "stream"), None),
            P("dp", None),
            P("dp", None),
            P("dp", None),
            P("dp", None),
            P("dp", None),
            P("dp", None),
            P("stream", "dp", None),
            P("stream", "dp", None),
        ),
        check_vma=False,
    )
```

```python
import functools
import math

import jax
import jax.numpy as jnp
from jax import lax
from jax.experimental import pallas as pl
from jax.experimental.pallas import tpu as pltpu
from jax.sharding import PartitionSpec as P

HEADS = 12
HEAD_DIM = 64
EXPERTS = 8
CAP = 288


HIGH = lax.Precision.HIGHEST
EPSILON = 1e-06
F32 = jnp.float32
BF16 = jnp.bfloat16
MIB = 1 << 20


def gelu_tanh(values):
    return jax.nn.gelu(values, approximate=True)


def normalize(values):
    centered = values - jnp.mean(values, -1, keepdims=True)
    spread = lax.rsqrt(jnp.mean(centered * centered, -1, keepdims=True) + EPSILON)
    return (centered * spread, spread)


def normalize_back(grad_normed, normed, spread):
    return spread * (
        grad_normed
        - jnp.mean(grad_normed, -1, keepdims=True)
        - normed * jnp.mean(grad_normed * normed, -1, keepdims=True)
    )


def split_packed(packed, seg_len):
    row_count = packed.shape[0]
    model_width = packed.shape[1] // 3
    groups = row_count // seg_len
    block_rows = min(512, seg_len)
    part_count = seg_len // block_rows
    queries = (
        packed[:, :model_width]
        .reshape(groups, part_count, block_rows, HEADS, HEAD_DIM)
        .swapaxes(0, 1)
    )
    key_heads = packed[:, model_width : 2 * model_width].reshape(groups, seg_len, HEADS, HEAD_DIM)
    values = packed[:, 2 * model_width :].reshape(groups, seg_len, HEADS, HEAD_DIM)
    return (queries, key_heads, values, groups, block_rows, part_count)


def attend(packed, seg_len):
    row_count = packed.shape[0]
    model_width = packed.shape[1] // 3
    factor = 1.0 / math.sqrt(HEAD_DIM)
    queries, key_heads, values, groups, block_rows, part_count = split_packed(packed, seg_len)

    def one_block(query_block):
        scores = (
            jnp.einsum(
                "gqhd,gkhd->ghqk", query_block, key_heads, preferred_element_type=jnp.float32
            )
            * factor
        )
        row_max = jnp.max(scores, -1, keepdims=True)
        shifted = jnp.exp(scores - row_max)
        row_sum = jnp.sum(shifted, -1, keepdims=True)
        weights = (shifted / row_sum).astype(jnp.bfloat16)
        mixture = jnp.einsum("ghqk,gkhd->gqhd", weights, values, preferred_element_type=jnp.float32)
        return (mixture, row_max[..., 0] + jnp.log(row_sum[..., 0]))

    mixture, logsum = lax.map(one_block, queries)
    return (mixture.swapaxes(0, 1).reshape(row_count, model_width), logsum.reshape(-1))


def attend_back(packed, logsum, grad_mixture, seg_len):
    row_count = packed.shape[0]
    model_width = packed.shape[1] // 3
    factor = 1.0 / math.sqrt(HEAD_DIM)
    queries, key_heads, values, groups, block_rows, part_count = split_packed(packed, seg_len)
    grad_blocks = grad_mixture.reshape(groups, part_count, block_rows, HEADS, HEAD_DIM).swapaxes(
        0, 1
    )
    logsum_blocks = logsum.reshape(part_count, groups, HEADS, block_rows)

    def one_block(carried, inputs):
        grad_keys, grad_values = carried
        query_block, grad_block, logsum_block = inputs
        scores = (
            jnp.einsum(
                "gqhd,gkhd->ghqk", query_block, key_heads, preferred_element_type=jnp.float32
            )
            * factor
        )
        prob_full = jnp.exp(scores - logsum_block[..., None])
        grad_values = grad_values + jnp.einsum(
            "ghqk,gqhd->gkhd",
            prob_full.astype(jnp.bfloat16),
            grad_block,
            preferred_element_type=jnp.float32,
        )
        grad_probs = jnp.einsum(
            "gqhd,gkhd->ghqk", grad_block, values, preferred_element_type=jnp.float32
        )
        row_inner = jnp.sum(grad_probs * prob_full, -1, keepdims=True)
        grad_scores = (prob_full * (grad_probs - row_inner)).astype(jnp.bfloat16)
        grad_query = (
            jnp.einsum(
                "ghqk,gkhd->gqhd", grad_scores, key_heads, preferred_element_type=jnp.float32
            )
            * factor
        )
        grad_keys = (
            grad_keys
            + jnp.einsum(
                "ghqk,gqhd->gkhd", grad_scores, query_block, preferred_element_type=jnp.float32
            )
            * factor
        )
        return ((grad_keys, grad_values), grad_query)

    zeros_kv = jnp.zeros((groups, seg_len, HEADS, HEAD_DIM), jnp.float32)
    (grad_keys, grad_values), grad_query = lax.scan(
        one_block, (zeros_kv, zeros_kv), (queries, grad_blocks, logsum_blocks)
    )
    return jnp.concatenate(
        [
            grad_query.swapaxes(0, 1).reshape(row_count, model_width),
            grad_keys.reshape(row_count, model_width),
            grad_values.reshape(row_count, model_width),
        ],
        1,
    )


def local_general(
    patches,
    embedding,
    long_image,
    routes,
    cotangent,
    ada_weight,
    qkv_weight,
    out_weight,
    shared_up,
    shared_down,
    router_weight,
    expert_up,
    expert_down,
):
    row_count, model_width = patches.shape
    block_count = embedding.shape[0]
    short_len = row_count // block_count
    lane_count = lax.axis_size("stream")
    local_experts = expert_up.shape[0]
    is_long = long_image[0] > 0

    def blocks(values):
        return values.reshape(block_count, short_len, model_width)

    def flatten(values):
        return values.reshape(row_count, model_width)

    used = jnp.where(is_long, jnp.broadcast_to(embedding[0:1], embedding.shape), embedding)
    activated, silu_back = jax.vjp(jax.nn.silu, used)
    ada_full = ada_weight.astype(jnp.float32)
    modulation = jnp.dot(activated, ada_full, precision=HIGH)
    pieces = [
        modulation[:, column * model_width : (column + 1) * model_width][:, None, :]
        for column in range(6)
    ]
    shift_one, scale_one, gate_one, shift_two, scale_two, gate_two = pieces
    inputs_full = blocks(patches.astype(jnp.float32))
    normed_one, spread_one = normalize(inputs_full)
    hidden_one = flatten(normed_one * (1.0 + scale_one) + shift_one).astype(jnp.bfloat16)
    packed = jnp.dot(hidden_one, qkv_weight, preferred_element_type=jnp.float32).astype(
        jnp.bfloat16
    )
    attended, logsum = lax.cond(
        is_long,
        lambda packed_in: attend(packed_in, row_count),
        lambda packed_in: attend(packed_in, short_len),
        packed,
    )
    attended_low = attended.astype(jnp.bfloat16)
    branch_one = blocks(jnp.dot(attended_low, out_weight, preferred_element_type=jnp.float32))
    middle = inputs_full + gate_one * branch_one
    normed_two, spread_two = normalize(middle)
    hidden_two = flatten(normed_two * (1.0 + scale_two) + shift_two).astype(jnp.bfloat16)
    shared_pre = jnp.dot(hidden_two, shared_up, preferred_element_type=jnp.float32)
    shared_act, shared_back = jax.vjp(gelu_tanh, shared_pre)
    shared_low = shared_act.astype(jnp.bfloat16)
    shared_out = jnp.dot(shared_low, shared_down, preferred_element_type=jnp.float32)
    logits = jnp.dot(hidden_two, router_weight, preferred_element_type=jnp.float32)
    chosen_hot = (routes[:, :, None] == jnp.arange(EXPERTS)[None, None, :]).astype(jnp.float32)
    gates = jax.nn.softmax(jnp.sum(chosen_hot * logits[:, None, :], -1), -1)
    flat_routes = routes.reshape(-1)
    route_hits = (flat_routes[:, None] == jnp.arange(EXPERTS)[None, :]).astype(jnp.int32)
    earlier = jnp.cumsum(route_hits, 0) - route_hits
    target = flat_routes * CAP + jnp.sum(earlier * route_hits, 1)

    def spread_rows(rows_low):
        buffer = jnp.zeros((EXPERTS * CAP, model_width), jnp.bfloat16).at[target].set(rows_low)
        return buffer.reshape(lane_count, local_experts, CAP, model_width)

    def collect(arrived):
        return (
            arrived.reshape(EXPERTS * CAP, model_width)[target]
            .astype(jnp.float32)
            .reshape(row_count, 2, model_width)
        )

    def by_expert(arrived):
        return arrived.swapaxes(0, 1).reshape(local_experts, lane_count * CAP, model_width)

    def by_source(results):
        return results.reshape(local_experts, lane_count, CAP, model_width).swapaxes(0, 1)

    expert_in = by_expert(
        lax.all_to_all(
            spread_rows(jnp.repeat(hidden_two, 2, axis=0)),
            "stream",
            split_axis=0,
            concat_axis=0,
            tiled=True,
        )
    )
    expert_pre = jnp.einsum(
        "jrd,jdf->jrf", expert_in, expert_up, preferred_element_type=jnp.float32
    )
    expert_act, expert_back = jax.vjp(gelu_tanh, expert_pre)
    expert_low = expert_act.astype(jnp.bfloat16)
    expert_out = jnp.einsum(
        "jrf,jfd->jrd", expert_low, expert_down, preferred_element_type=jnp.float32
    ).astype(jnp.bfloat16)
    picked = collect(
        lax.all_to_all(by_source(expert_out), "stream", split_axis=0, concat_axis=0, tiled=True)
    )
    routed = jnp.sum(gates[:, :, None] * picked, 1)
    branch_two = blocks(shared_out + routed)
    mixed = flatten(middle + gate_two * branch_two).astype(jnp.bfloat16)
    grad_top = blocks(cotangent.astype(jnp.float32))
    grad_gate_two = jnp.sum(grad_top * branch_two, 1)
    grad_branch = flatten(grad_top * gate_two)
    grad_pick = (
        (gates[:, :, None] * grad_branch[:, None, :])
        .astype(jnp.bfloat16)
        .reshape(2 * row_count, model_width)
    )
    grad_arrived = by_expert(
        lax.all_to_all(spread_rows(grad_pick), "stream", split_axis=0, concat_axis=0, tiled=True)
    )
    grad_expert_down = jnp.einsum(
        "jrf,jrd->jfd", expert_low, grad_arrived, preferred_element_type=jnp.float32
    )
    grad_expert_act = jnp.einsum(
        "jrd,jfd->jrf", grad_arrived, expert_down, preferred_element_type=jnp.float32
    )
    grad_expert_pre = expert_back(grad_expert_act)[0].astype(jnp.bfloat16)
    grad_expert_up = jnp.einsum(
        "jrd,jrf->jdf", expert_in, grad_expert_pre, preferred_element_type=jnp.float32
    )
    grad_expert_in = jnp.einsum(
        "jrf,jdf->jrd", grad_expert_pre, expert_up, preferred_element_type=jnp.float32
    ).astype(jnp.bfloat16)
    grad_routed = jnp.sum(
        collect(
            lax.all_to_all(
                by_source(grad_expert_in), "stream", split_axis=0, concat_axis=0, tiled=True
            )
        ),
        1,
    )
    grad_shared_low = grad_branch.astype(jnp.bfloat16)
    grad_shared_down = jnp.einsum(
        "rf,rd->fd", shared_low, grad_shared_low, preferred_element_type=jnp.float32
    )
    grad_shared_act = jnp.einsum(
        "rd,fd->rf", grad_shared_low, shared_down, preferred_element_type=jnp.float32
    )
    grad_shared_pre = shared_back(grad_shared_act)[0].astype(jnp.bfloat16)
    grad_shared_up = jnp.einsum(
        "rd,rf->df", hidden_two, grad_shared_pre, preferred_element_type=jnp.float32
    )
    grad_gates = jnp.sum(picked * grad_branch[:, None, :], -1)
    grad_chosen = gates * (grad_gates - jnp.sum(gates * grad_gates, -1, keepdims=True))
    grad_logits = jnp.sum(chosen_hot * grad_chosen[:, :, None], 1)
    hidden_two_full = hidden_two.astype(jnp.float32)
    router_full = router_weight.astype(jnp.float32)
    grad_router = jnp.dot(hidden_two_full.T, grad_logits, precision=HIGH)
    grad_hidden = jnp.dot(grad_logits, router_full.T, precision=HIGH) + grad_routed
    grad_hidden = blocks(
        grad_hidden
        + jnp.einsum("rf,df->rd", grad_shared_pre, shared_up, preferred_element_type=jnp.float32)
    )
    grad_shift_two = jnp.sum(grad_hidden, 1)
    grad_scale_two = jnp.sum(grad_hidden * normed_two, 1)
    grad_middle = grad_top + normalize_back(grad_hidden * (1.0 + scale_two), normed_two, spread_two)
    grad_gate_one = jnp.sum(grad_middle * branch_one, 1)
    grad_branch_one = flatten(grad_middle * gate_one).astype(jnp.bfloat16)
    grad_out_weight = jnp.einsum(
        "rd,re->de", attended_low, grad_branch_one, preferred_element_type=jnp.float32
    )
    grad_attended = jnp.einsum(
        "re,de->rd", grad_branch_one, out_weight, preferred_element_type=jnp.float32
    ).astype(jnp.bfloat16)
    grad_packed = lax.cond(
        is_long,
        lambda packed_in, logsum_in, grad_in: attend_back(packed_in, logsum_in, grad_in, row_count),
        lambda packed_in, logsum_in, grad_in: attend_back(packed_in, logsum_in, grad_in, short_len),
        packed,
        logsum,
        grad_attended,
    ).astype(jnp.bfloat16)
    grad_qkv = jnp.einsum("rd,re->de", hidden_one, grad_packed, preferred_element_type=jnp.float32)
    grad_hidden_one = blocks(
        jnp.einsum("re,de->rd", grad_packed, qkv_weight, preferred_element_type=jnp.float32)
    )
    grad_shift_one = jnp.sum(grad_hidden_one, 1)
    grad_scale_one = jnp.sum(grad_hidden_one * normed_one, 1)
    grad_inputs = grad_middle + normalize_back(
        grad_hidden_one * (1.0 + scale_one), normed_one, spread_one
    )
    grad_modulation = jnp.concatenate(
        [
            grad_shift_one,
            grad_scale_one,
            grad_gate_one,
            grad_shift_two,
            grad_scale_two,
            grad_gate_two,
        ],
        1,
    )
    grad_ada = jnp.dot(activated.T, grad_modulation, precision=HIGH)
    grad_used = silu_back(jnp.dot(grad_modulation, ada_full.T, precision=HIGH))[0]
    grad_embedding = jnp.where(
        is_long, jnp.zeros_like(grad_used).at[0].set(jnp.sum(grad_used, 0)), grad_used
    )
    shares = (
        lax.psum_scatter(
            grad_ada.astype(jnp.bfloat16), "dp", scatter_dimension=0, tiled=True
        ).astype(jnp.float32),
        lax.psum_scatter(
            grad_qkv.astype(jnp.bfloat16), "dp", scatter_dimension=0, tiled=True
        ).astype(jnp.float32),
        lax.psum_scatter(
            grad_out_weight.astype(jnp.bfloat16), "dp", scatter_dimension=0, tiled=True
        ).astype(jnp.float32),
        lax.psum_scatter(
            grad_shared_up.astype(jnp.bfloat16), "dp", scatter_dimension=0, tiled=True
        ).astype(jnp.float32),
        lax.psum_scatter(
            grad_shared_down.astype(jnp.bfloat16), "dp", scatter_dimension=0, tiled=True
        ).astype(jnp.float32),
        lax.psum_scatter(
            grad_router.astype(jnp.bfloat16), "dp", scatter_dimension=0, tiled=True
        ).astype(jnp.float32),
    )
    expert_summed = (
        lax.psum_scatter(
            grad_expert_up.astype(jnp.bfloat16), "dp", scatter_dimension=1, tiled=True
        ).astype(jnp.float32),
        lax.psum_scatter(
            grad_expert_down.astype(jnp.bfloat16), "dp", scatter_dimension=1, tiled=True
        ).astype(jnp.float32),
    )
    summed = (
        lax.psum(shares[0].astype(jnp.bfloat16), "stream").astype(jnp.float32),
        lax.psum(shares[1].astype(jnp.bfloat16), "stream").astype(jnp.float32),
        lax.psum(shares[2].astype(jnp.bfloat16), "stream").astype(jnp.float32),
        lax.psum(shares[3].astype(jnp.bfloat16), "stream").astype(jnp.float32),
        lax.psum(shares[4].astype(jnp.bfloat16), "stream").astype(jnp.float32),
        lax.psum(shares[5].astype(jnp.bfloat16), "stream").astype(jnp.float32),
    )
    return (
        mixed,
        flatten(grad_inputs),
        grad_embedding,
        summed[0],
        summed[1],
        summed[2],
        summed[3],
        summed[4],
        summed[5],
        expert_summed[0],
        expert_summed[1],
    )


def nn(left, right):
    return jnp.dot(left, right, preferred_element_type=F32)


def nt(left, right):
    return lax.dot_general(left, right, (((1,), (1,)), ((), ())), preferred_element_type=F32)


def tn(left, right):
    return lax.dot_general(left, right, (((0,), (0,)), ((), ())), preferred_element_type=F32)


def three_parts(values):
    first = values.astype(BF16)
    rest = values - first.astype(F32)
    second = rest.astype(BF16)
    third = (rest - second.astype(F32)).astype(BF16)
    return first, second, third


def stacked(values):
    return jnp.concatenate(three_parts(values), 0)


def unstacked(product):
    rows = product.shape[0] // 3
    return product[:rows] + product[rows : 2 * rows] + product[2 * rows :]


def sigmoid(values):
    return 1.0 / (1.0 + jnp.exp(-values))


def gelu_and_slope(values):
    inner = math.sqrt(2.0 / math.pi)
    square = values * values
    bend = jnp.tanh(values * (inner + (inner * 0.044715) * square))
    half = 0.5 + 0.5 * bend
    slope = half + values * (0.5 - 0.5 * bend * bend) * (inner + (3.0 * inner * 0.044715) * square)
    return values * half, slope


def run(kernel, args, grid, in_specs, out_specs, out_shape, name, scalars=(), scratch=(), after=(), limit=56):
    count = len(scalars) + len(args)

    def body(*refs):
        kernel(*refs[:count], *refs[count + len(after) :])

    return pl.pallas_call(
        body,
        grid_spec=pltpu.PrefetchScalarGridSpec(
            num_scalar_prefetch=len(scalars),
            grid=grid,
            in_specs=list(in_specs) + [pl.BlockSpec(memory_space=pl.ANY)] * len(after),
            out_specs=out_specs,
            scratch_shapes=list(scratch),
        ),
        out_shape=out_shape,
        compiler_params=pltpu.CompilerParams(vmem_limit_bytes=limit * MIB),
        cost_estimate=pl.CostEstimate(flops=1000, bytes_accessed=1000, transcendentals=0),
        name=name,
    )(*scalars, *args, *after)


def full(shape):
    return pl.BlockSpec(shape, lambda *_: (0,) * len(shape))


def like(array):
    return full(array.shape)


def rows_spec(rows, width):
    return pl.BlockSpec((rows, width), lambda i, *_: (i, 0))


def shape(dims, dtype):
    return jax.ShapeDtypeStruct(tuple(dims), dtype)


LONG, CORE, STREAM, ROW_Y, ROW_Z, FIRST_HERE, FIRST_ALL = range(7)


def flipped(value, bits):
    total = 0
    for bit in range(bits):
        total = total + (((value >> bit) & 1) << (bits - 1 - bit))
    return total


def modulate_kernel(blocks, pos_ref, emb_ref, ada_ref, cot_ref, mod_ref, act_ref, branch_ref, sent_ref):
    emb = emb_ref[...]
    used = jnp.where(pos_ref[LONG] > 0, jnp.broadcast_to(emb[0:1], emb.shape), emb)
    act = used * sigmoid(used)
    act_ref[...] = act
    total = unstacked(nn(stacked(act), ada_ref[...]))
    mod_ref[0] = total

    @pl.when(pl.program_id(0) == pl.num_programs(0) - 1)
    def _():
        short = cot_ref.shape[0] // blocks
        for block in range(blocks):
            span = slice(block * short, (block + 1) * short)
            branch = (cot_ref[span, :].astype(F32) * total[block : block + 1]).astype(BF16)
            branch_ref[span, :] = branch
            sent_ref[span, :] = branch
        sent_ref[cot_ref.shape[0] :, :] = jnp.zeros((sent_ref.shape[0] - cot_ref.shape[0], cot_ref.shape[1]), BF16)


def modulate(pos, emb_pad, ada_weight, cot, blocks):
    rows, width = emb_pad.shape
    pieces = ada_weight.shape[1] // width
    sent = (cot.shape[0] + 32, width)
    return run(
        functools.partial(modulate_kernel, blocks), (emb_pad, ada_weight, cot), (pieces,),
        [like(emb_pad), pl.BlockSpec((width, width), lambda i, *_: (0, i)), like(cot)],
        [pl.BlockSpec((1, rows, width), lambda i, *_: (i, 0, 0)), like(emb_pad), like(cot), full(sent)],
        [shape((pieces, rows, width), F32), shape((rows, width), F32), shape(cot.shape, BF16), shape(sent, BF16)],
        "modulate", scalars=(pos,),
    )


def norm_parts(values):
    centered = values - jnp.mean(values, -1, keepdims=True)
    spread = lax.rsqrt(jnp.mean(centered * centered, -1, keepdims=True) + EPSILON)
    return centered * spread, spread


def norm_back(grad, normed, spread):
    return spread * (
        grad
        - jnp.mean(grad, -1, keepdims=True)
        - normed * jnp.mean(grad * normed, -1, keepdims=True)
    )


def qkv_kernel(x_ref, mod_ref, w_ref, packed_ref):
    block = pl.program_id(0)
    normed, _ = norm_parts(x_ref[...].astype(F32))
    shift, scale = mod_ref[0, pl.ds(block, 1), :], mod_ref[1, pl.ds(block, 1), :]
    hidden = (normed * (1.0 + scale) + shift).astype(BF16)
    packed_ref[...] = nn(hidden, w_ref[...]).astype(BF16)


def qkv_forward(patches, mod, weight, blocks, after):
    rows, width = patches.shape
    short = rows // blocks
    wide = weight.shape[1]
    return run(
        qkv_kernel, (patches, mod, weight), (blocks,),
        [rows_spec(short, width), like(mod), like(weight)], rows_spec(short, wide),
        shape((rows, wide), BF16), "qkv", after=after,
    )


def attend_kernel(short, pos_ref, q_ref, k_ref, v_ref, o_ref, lse_ref):
    rows, lanes = q_ref.shape
    first = lax.broadcasted_iota(jnp.int32, (1, lanes), 1) < HEAD_DIM
    factor = 1.0 / math.sqrt(HEAD_DIM)

    def part(at, count):
        span = slice(at, at + count)
        queries = (q_ref[span, :].astype(F32) * factor).astype(BF16)
        keys, values = k_ref[span, :], v_ref[span, :]
        zero = jnp.zeros_like(queries)
        wide = jnp.concatenate([values, jnp.ones_like(values)], 1)
        masks = (first, jnp.logical_not(first))
        scores = [nt(jnp.where(mine, queries, zero), keys) for mine in masks]
        tops = [jnp.max(a, -1, keepdims=True) for a in scores]
        shifted = [jnp.exp(a - top).astype(BF16) for a, top in zip(scores, tops)]
        mixtures = [nn(a, wide) for a in shifted]
        totals = [a[:, lanes:] for a in mixtures]
        outs = [a[:, :lanes] / total for a, total in zip(mixtures, totals)]
        sums = [top + jnp.log(total) for top, total in zip(tops, totals)]
        o_ref[span, :] = jnp.where(first, outs[0], outs[1]).astype(BF16)
        lse_ref[span, :] = jnp.where(first, sums[0], sums[1])

    @pl.when(pos_ref[LONG] > 0)
    def _():
        part(0, rows)

    @pl.when(pos_ref[LONG] <= 0)
    def _():
        for at in range(0, rows, short):
            part(at, short)


def pair_specs(rows, width):
    lanes = 2 * HEAD_DIM
    pairs = width // lanes
    return [
        pl.BlockSpec((rows, lanes), functools.partial(lambda shift, i, *_: (0, i + shift), shift))
        for shift in (0, pairs, 2 * pairs)
    ]


def attend_forward(pos, packed, short):
    rows = packed.shape[0]
    width = packed.shape[1] // 3
    spec = pair_specs(rows, width)
    return run(
        functools.partial(attend_kernel, short), (packed, packed, packed), (width // (2 * HEAD_DIM),),
        spec, [spec[0], spec[0]], [shape((rows, width), BF16), shape((rows, width), F32)],
        "attend", scalars=(pos,),
    )


def attend_back_kernel(
    short, pos_ref, q_ref, k_ref, v_ref, o_ref, lse_ref, do_ref, dq_ref, dk_ref, dv_ref,
    dk_acc, dv_acc,
):
    rows, lanes = q_ref.shape
    first = lax.broadcasted_iota(jnp.int32, (1, lanes), 1) < HEAD_DIM
    factor = 1.0 / math.sqrt(HEAD_DIM)
    product = do_ref[...].astype(F32) * o_ref[...].astype(F32)
    lse_t = jnp.transpose(lse_ref[...])
    product_t = jnp.transpose(product)
    lse_rows = [lse_t[0:1], lse_t[HEAD_DIM : HEAD_DIM + 1]]
    delta_rows = [
        jnp.sum(product_t[:HEAD_DIM], 0, keepdims=True),
        jnp.sum(product_t[HEAD_DIM:], 0, keepdims=True),
    ]

    def part(query_at, key_at, key_count, fresh):
        chunk = slice(query_at, query_at + short)
        span = slice(key_at, key_at + key_count)
        queries, grads = (q_ref[chunk, :].astype(F32) * factor).astype(BF16), do_ref[chunk, :]
        keys, values = k_ref[span, :], v_ref[span, :]
        masks = (first, jnp.logical_not(first))

        def apart(array):
            return [jnp.where(mine, array, jnp.zeros_like(array)) for mine in masks]

        query_own, grad_own, key_own = apart(queries), apart(grads), apart(keys)
        probs = [
            jnp.exp(nt(keys, query) - lse[:, chunk]) for query, lse in zip(query_own, lse_rows)
        ]
        grad_probs = [nt(values, grad) for grad in grad_own]
        grad_scores = [
            (prob * (grad - delta[:, chunk])).astype(BF16)
            for prob, grad, delta in zip(probs, grad_probs, delta_rows)
        ]
        low = [prob.astype(BF16) for prob in probs]
        dv = nn(jnp.concatenate(low, 1), jnp.concatenate(grad_own, 0))
        dk = nn(jnp.concatenate(grad_scores, 1), jnp.concatenate(query_own, 0))
        dq = nn(jnp.transpose(jnp.concatenate(key_own, 0)), jnp.concatenate(grad_scores, 0))
        dq_ref[chunk, :] = (jnp.transpose(dq) * factor).astype(BF16)
        if fresh:
            dk_acc[span, :] = dk
            dv_acc[span, :] = dv
        else:
            dk_acc[span, :] += dk
            dv_acc[span, :] += dv

    @pl.when(pos_ref[LONG] > 0)
    def _():
        for at in range(0, rows, short):
            part(at, 0, rows, at == 0)

    @pl.when(pos_ref[LONG] <= 0)
    def _():
        for at in range(0, rows, short):
            part(at, at, short, True)

    dk_ref[...] = dk_acc[...].astype(BF16)
    dv_ref[...] = dv_acc[...].astype(BF16)


def attend_backward(pos, packed, attended, logsum, grad, short, after):
    rows, width = attended.shape
    lanes = 2 * HEAD_DIM
    spec = pair_specs(rows, width)
    return run(
        functools.partial(attend_back_kernel, short),
        (packed, packed, packed, attended, logsum, grad), (width // lanes,),
        spec + [spec[0]] * 3, [spec[0]] * 3, [shape((rows, width), BF16)] * 3,
        "attend_back", scalars=(pos,), scratch=[pltpu.VMEM((rows, lanes), F32)] * 2, after=after,
    )


def middle_kernel(att_ref, x_ref, mod_ref, w_ref, branch_ref, hidden_ref):
    block = pl.program_id(0)
    branch = nn(att_ref[...], w_ref[...])
    branch_ref[...] = branch
    middle = x_ref[...].astype(F32) + mod_ref[2, pl.ds(block, 1), :] * branch
    normed, _ = norm_parts(middle)
    shift, scale = mod_ref[3, pl.ds(block, 1), :], mod_ref[4, pl.ds(block, 1), :]
    hidden_ref[...] = (normed * (1.0 + scale) + shift).astype(BF16)


def middle_forward(attended, patches, mod, out_weight, blocks, after):
    rows, width = patches.shape
    tile = rows_spec(rows // blocks, width)
    return run(
        middle_kernel, (attended, patches, mod, out_weight), (blocks,),
        [tile, tile, like(mod), like(out_weight)], [tile, tile],
        [shape((rows, width), F32), shape((rows, width), BF16)], "middle", after=after,
    )


def rank_kernel(pos_ref, *refs):
    count = (len(refs) - 2) // 1
    routes, (row_ref, col_ref) = refs[:count], refs[count:]
    rows = routes[0].shape[1]
    before = lax.broadcasted_iota(jnp.int32, (rows, rows), 0)
    after = lax.broadcasted_iota(jnp.int32, (rows, rows), 1)
    upper = (before < after).astype(F32).astype(BF16)
    ids = pos_ref[FIRST_ALL] + lax.broadcasted_iota(jnp.int32, (8, rows), 0)
    for source, ref in enumerate(routes):
        hits = jnp.logical_or(ref[0:1, :] == ids, ref[1:2, :] == ids)
        earlier = nn(hits.astype(F32).astype(BF16), upper)
        rank = jnp.where(hits, earlier, -1.0)
        row_ref[source] = rank.astype(jnp.int32)
        tall = jnp.concatenate([rank, jnp.full((120, rows), -1.0, F32)], 0)
        col_ref[source] = jnp.transpose(tall).astype(jnp.int32)


def ranks(pos, routes, after):
    count, rows = len(routes), routes[0].shape[1]
    out = [shape((count, 8, rows), jnp.int32), shape((count, rows, 128), jnp.int32)]
    return run(
        rank_kernel, routes, (1,), [like(a) for a in routes], [like(a) for a in out], out, "ranks",
        scalars=(pos,), after=after,
    )


def touch(array, after):
    count = len(after)

    def body(*refs):
        del refs

    return pl.pallas_call(
        body,
        in_specs=[pl.BlockSpec(memory_space=pl.ANY)] * (1 + count),
        out_specs=pl.BlockSpec(memory_space=pl.ANY),
        out_shape=shape(array.shape, array.dtype),
        input_output_aliases={0: 0},
        name="touch",
    )(array, *after)


def gate_rows(hidden, routes, router_t, ids):
    logits = nt(router_t, hidden)
    every = lax.broadcasted_iota(jnp.int32, logits.shape, 0)
    first, second = routes[0:1, :], routes[1:2, :]
    zero = jnp.zeros_like(logits)
    logit_one = jnp.sum(jnp.where(every == first, logits, zero), 0, keepdims=True)
    logit_two = jnp.sum(jnp.where(every == second, logits, zero), 0, keepdims=True)
    gate_one = sigmoid(logit_one - logit_two)
    gate_two = sigmoid(logit_two - logit_one)
    return jnp.where(ids == first, gate_one, 0.0) + jnp.where(ids == second, gate_two, 0.0)


def ffn_phase_one(x, g, up_ref, down_ref, act_ref, pre_ref, step=256):
    wide = act_ref.shape[1]
    for at in range(0, wide, step):
        cols = slice(at, at + step)
        act, slope = gelu_and_slope(nn(x, up_ref[0, :, cols]))
        back = nt(g, down_ref[0, cols, :])
        act_ref[:, cols] = act.astype(BF16)
        pre_ref[:, cols] = (back * slope).astype(BF16)


def relative_rows(pos_ref, target, values, nz):
    bits = nz.bit_length() - 1
    part = values.shape[0] // (2 * nz)
    for block in range(2 * nz):
        place = (block % 2) ^ pos_ref[ROW_Y]
        place = place * nz + flipped((block // 2) ^ pos_ref[ROW_Z], bits)
        at = pl.multiple_of(place * part, part)
        target[pl.ds(at, part), :] = values[block * part : (block + 1) * part]


def sides(pos_ref, values):
    half = values.shape[1] // 2
    low, high = values[:, :half], values[:, half:]
    own_low = pos_ref[ROW_Y] == 0
    return jnp.where(own_low, low, high), jnp.where(own_low, high, low)


def expert_kernel(
    slot, sends, has_prior, pos_ref, h0_ref, h1_ref, g0_ref, g1_ref, rank_ref, routes0_ref, routes1_ref,
    router_ref, up_ref, down_ref, *rest,
):
    count = 1 + sends
    priors, rest = (rest[:count], rest[count:]) if has_prior else ((), rest)
    targets, rest = rest[:count], rest[count:]
    keep_ref = targets[0]
    (out_ref, gx_ref, gg_ref,
     x_s, xt_s, g_s, gt_s, b_s, gate_s, act_s, pre_s, out_acc, gx_acc) = rest
    tile = pl.program_id(0)
    last = pl.num_programs(0) - 1
    rows = h0_ref.shape[0]
    nz = keep_ref.shape[2] // keep_ref.shape[3] * 2
    part = h0_ref.shape[1] // (2 * nz)
    own = lax.broadcasted_iota(jnp.int32, (CAP, rows), 0)

    def hot(source):
        return (own == rank_ref[source, slot : slot + 1, :]).astype(F32)

    @pl.when(tile == 0)
    def _():
        sources = ((h0_ref, g0_ref, routes0_ref), (h1_ref, g1_ref, routes1_ref))
        for source, (h_ref, b_ref, routes_ref) in enumerate(sources):
            span = slice(source * CAP, (source + 1) * CAP)
            pick = hot(source)
            pick_low = pick.astype(BF16)
            expert = pos_ref[FIRST_ALL] + slot
            gate = gate_rows(h_ref[...], routes_ref[...], router_ref[...], expert)
            gate_col = jnp.sum(pick * gate[0:1], -1, keepdims=True)
            branch = nn(pick_low, b_ref[:rows, :])
            x_s[span, :] = nn(pick_low, h_ref[...]).astype(BF16)
            b_s[span, :] = branch.astype(BF16)
            g_s[span, :] = (branch * gate_col).astype(BF16)
            gate_s[span, :] = jnp.broadcast_to(gate_col, (CAP, 128))
        relative_rows(pos_ref, xt_s, jnp.transpose(x_s[...]), nz)
        gt_s[...] = jnp.transpose(g_s[...])
        out_acc[...] = jnp.zeros_like(out_acc)
        gx_acc[...] = jnp.zeros_like(gx_acc)

    ffn_phase_one(x_s[...], g_s[...], up_ref, down_ref, act_s, pre_s)
    act, pre = act_s[...], pre_s[...]
    out_acc[...] += nn(act, down_ref[0])
    gx_acc[...] += nt(pre, up_ref[0])

    def place(side, kind):
        return (0, kind) if side == 0 else (1, kind) if sends == 1 else (1 + kind, 0)

    dup = nn(xt_s[...], pre)
    half = dup.shape[1] // 2
    for side in range(2):
        at, entry = place(side, 0)
        for z in range(nz):
            for lanes in range(2):
                row, into = (side * nz + z) * part, (z * 2 + lanes) * part
                piece = dup[row : row + part, lanes * half : (lanes + 1) * half]
                if has_prior:
                    piece = piece + priors[at][0, entry, into : into + part, :].astype(F32)
                targets[at][0, entry, into : into + part, :] = piece.astype(BF16)
    for side, piece in enumerate(sides(pos_ref, nn(gt_s[...], act))):
        at, entry = place(side, 1)
        if has_prior:
            piece = piece + priors[at][0, entry].astype(F32)
        targets[at][0, entry] = piece.astype(BF16)

    @pl.when(tile == last)
    def _():
        for source in range(2):
            span = slice(source * CAP, (source + 1) * CAP)
            out = out_acc[span, :]
            out_ref[source] = (out * gate_s[span, 0:1]).astype(BF16)
            gx_ref[source] = gx_acc[span, :].astype(BF16)
            inner = jnp.sum(out * b_s[span, :].astype(F32), -1, keepdims=True)
            gg_ref[source] = jnp.sum(hot(source) * inner, 0, keepdims=True)


def expert_call(
    slot, sends, pos, hiddens, branches, rank_rows, routes, router_t, up, down, prior, nz, after
):
    rows, width = hiddens[0].shape
    wide = up.shape[2]
    tile = wide // nz
    bits = nz.bit_length() - 1
    count = 2 * CAP
    weights = [
        pl.BlockSpec((1, width, tile), lambda f, s: (s[FIRST_HERE] + slot, 0, f)),
        pl.BlockSpec((1, tile, width), lambda f, s: (s[FIRST_HERE] + slot, f, 0)),
    ]
    kinds = [2, 2] if sends == 1 else [2, 1, 1]
    grads = [
        pl.BlockSpec((1, kind, width, tile // 2), lambda f, s: (flipped(f ^ s[ROW_Z], bits), 0, 0, 0))
        for kind in kinds
    ]
    once = [*hiddens, *branches, rank_rows, *routes, router_t]
    out_shape = (
        [shape((nz, kind, width, tile // 2), BF16) for kind in kinds]
        + [shape((2, CAP, width), BF16)] * 2
        + [shape((2, 1, rows), F32)]
    )
    prior = () if prior is None else tuple(prior)
    return run(
        functools.partial(expert_kernel, slot, sends, bool(prior)), (*once, up, down, *prior), (nz,),
        [like(a) for a in once] + weights + (grads if prior else []),
        grads + [like(a) for a in out_shape[len(grads) :]], out_shape, "expert", scalars=(pos,), after=after,
        scratch=[
            pltpu.VMEM((count, width), BF16),
            pltpu.VMEM((width, count), BF16),
            pltpu.VMEM((count, width), BF16),
            pltpu.VMEM((width, count), BF16),
            pltpu.VMEM((count, width), BF16),
            pltpu.VMEM((count, 128), F32),
            pltpu.VMEM((count, tile), BF16),
            pltpu.VMEM((count, tile), BF16),
            pltpu.VMEM((count, width), F32),
            pltpu.VMEM((count, width), F32),
        ],
    )


def shared_kernel(
    pos_ref, h_ref, b_ref, up_ref, down_ref, ku_ref, su0_ref, su1_ref, kd_ref, sd0_ref, sd1_ref,
    out_ref, gx_ref, xt_s, gt_s, act_s, pre_s,
):
    step = pl.program_id(0)
    nz, block = 4, kd_ref.shape[3]

    @pl.when(step == 0)
    def _():
        relative_rows(pos_ref, xt_s, jnp.transpose(h_ref[...]), nz)
        turned = jnp.transpose(b_ref[...])
        for slice_at in range(4):
            place = ((slice_at % 2) ^ pos_ref[CORE]) * 2 + ((slice_at // 2) ^ pos_ref[STREAM])
            at = pl.multiple_of(place * block, block)
            gt_s[pl.ds(at, block), :] = turned[slice_at * block : (slice_at + 1) * block]
        out_ref[...] = jnp.zeros_like(out_ref)
        gx_ref[...] = jnp.zeros_like(gx_ref)

    ffn_phase_one(h_ref[...], b_ref[...], up_ref, down_ref, act_s, pre_s)
    act, pre = act_s[...], pre_s[...]
    out_ref[...] += nn(act, down_ref[0])
    gx_ref[...] += nt(pre, up_ref[0])
    dup = nn(xt_s[...], pre).astype(BF16)

    @pl.when(step < 2)
    def _():
        ku_ref[0] = dup

    @pl.when(step == 2)
    def _():
        su0_ref[...] = dup

    @pl.when(step == 3)
    def _():
        su1_ref[...] = dup

    for y, piece in enumerate(sides(pos_ref, nn(gt_s[...], act))):
        pieces = [piece[place * block : (place + 1) * block].astype(BF16) for place in range(4)]
        kd_ref[0, y, 0], kd_ref[1, y, 0] = pieces[0], pieces[1]
        sd0_ref[y, 0], sd1_ref[y, 0] = pieces[2], pieces[3]


def shared_call(pos, hidden, branch, up, down, after):
    rows, width = hidden.shape
    wide = up.shape[1]
    nz = 4
    tile = wide // nz
    block = width // 4

    def unit(f, s):
        return (f % 2 ^ s[STREAM]) * 2 + (f // 2 ^ s[CORE])

    keep = pl.BlockSpec((1, width, tile), lambda f, s: (jnp.minimum(f, 1), 0, 0))
    downs = pl.BlockSpec(
        (2, 2, 1, block, tile // 2), lambda f, s: (0, 0, flipped(unit(f, s) ^ s[ROW_Z], 2), 0, 0)
    )
    sent = pl.BlockSpec((2, 1, block, tile // 2), lambda f, s: (0, flipped(unit(f, s) ^ s[ROW_Z], 2), 0, 0))
    outs = run(
        shared_kernel, (hidden, branch, up[None], down[None]), (nz,),
        [
            like(hidden),
            like(branch),
            pl.BlockSpec((1, width, tile), lambda f, s: (0, 0, unit(f, s))),
            pl.BlockSpec((1, tile, width), lambda f, s: (0, unit(f, s), 0)),
        ],
        [keep] + [full((width, tile))] * 2 + [downs, sent, sent, like(hidden), like(hidden)],
        [shape((2, width, tile), BF16)] + [shape((width, tile), BF16)] * 2
        + [shape((2, 2, nz, block, tile // 2), BF16)] + [shape((2, nz, block, tile // 2), BF16)] * 2
        + [shape((rows, width), F32)] * 2,
        "shared", scalars=(pos,), after=after,
        scratch=[
            pltpu.VMEM((width, rows), BF16),
            pltpu.VMEM((width, rows), BF16),
            pltpu.VMEM((rows, tile), BF16),
            pltpu.VMEM((rows, tile), BF16),
        ],
    )
    return outs[0], outs[1:3], outs[3], outs[4:6], *outs[6:]


def combine_kernel(places, col_ref, *refs):
    slots = len(places)
    rows_refs, refs = refs[: 2 * slots], refs[2 * slots :]
    targets, stacks = refs[:5], refs[5:]

    @pl.when(pl.program_id(0) == 0)
    def _():
        for slot in range(slots):
            for kind in range(2):
                for source in range(2):
                    stacks[kind][source, slot * CAP : (slot + 1) * CAP, :] = rows_refs[2 * slot + kind][places[slot] + source]

    block = col_ref.shape[1]
    own = lax.broadcasted_iota(jnp.int32, (block, slots * CAP), 1)
    for source in range(2):
        hits = None
        for slot in range(slots):
            rank = col_ref[source, :, slot : slot + 1]
            place = jnp.where(rank < 0, -1, rank + slot * CAP)
            hit = place == own
            hits = hit if hits is None else jnp.logical_or(hits, hit)
        pick = hits.astype(F32).astype(BF16)
        for kind in range(2):
            total = nn(pick, stacks[kind][source]).astype(BF16)
            if 2 * kind + source < 3:
                targets[2 * kind + source][...] = total
            else:
                early = pl.program_id(0) < pl.num_programs(0) // 2

                @pl.when(early)
                def _():
                    targets[3][...] = total

                @pl.when(jnp.logical_not(early))
                def _():
                    targets[4][...] = total


def combine(rank_cols, pairs, places, after):
    count, rows, _ = rank_cols.shape
    width = pairs[0][0].shape[2]
    block = rows // 4
    flat = [a for pair in pairs for a in pair]
    halves = [
        pl.BlockSpec((block, width), lambda i: (jnp.minimum(i, 1), 0)),
        pl.BlockSpec((block, width), lambda i: (jnp.maximum(i - 2, 0), 0)),
    ]
    *outs, low, high = run(
        functools.partial(combine_kernel, places), (rank_cols, *flat), (rows // block,),
        [pl.BlockSpec((count, block, 128), lambda i: (0, i, 0))] + [like(a) for a in flat],
        [rows_spec(block, width)] * 3 + halves,
        [shape((rows, width), BF16)] * 3 + [shape((rows // 2, width), BF16)] * 2, "combine",
        scratch=[pltpu.VMEM((2, len(pairs) * CAP, width), BF16)] * 2, after=after,
    )
    return (*outs, (low, high))


def add_kernel(left_ref, low_ref, high_ref, second_ref, third_ref, one_ref, two_ref):
    two_ref[...] = (second_ref[...].astype(F32) + third_ref[...].astype(F32)).astype(BF16)
    low = pl.program_id(0) < pl.num_programs(0) // 2
    right = jnp.where(low, low_ref[...], high_ref[...])
    one_ref[...] = (left_ref[...].astype(F32) + right.astype(F32)).astype(BF16)


def add_rows(left, halves, second, third, after):
    rows, width = left.shape
    tile = rows_spec(rows // 4, width)
    low = pl.BlockSpec((rows // 4, width), lambda i: (jnp.minimum(i, 1), 0))
    high = pl.BlockSpec((rows // 4, width), lambda i: (jnp.maximum(i - 2, 0), 0))
    return run(
        add_kernel, (left, *halves, second, third), (4,), [tile, low, high, tile, tile], [tile] * 2,
        [shape((rows, width), BF16)] * 2, "add_rows", after=after,
    )


def total_of(keep, arrived):
    return keep.astype(F32) + arrived.astype(F32)


def halve_kinds_kernel(kinds, *refs):
    keep_ref, send_ref = refs[-2:]
    refs = iter(refs[:-2])
    for at, kind in enumerate(kinds):
        if kind == 0:
            total = total_of(next(refs)[0, 0], next(refs)[0, 0])
            half = total.shape[0] // 2
            keep_ref[at, 0], send_ref[at, 0] = total[:half], total[half:].astype(BF16)
        else:
            keep_ref[at, 0] = total_of(next(refs)[0, 0], next(refs)[0, 0])
            send_ref[at, 0] = total_of(next(refs)[0, 0], next(refs)[0, 0]).astype(BF16)


def halve_y(keep, arrived, kinds, after):
    nz, _, rows, cols = keep.shape
    split = lambda a: a.reshape(nz, -1, rows // 2, cols)
    args, specs = [], []
    for at, kind in enumerate(kinds):
        for add in (0, nz // 2) if kind else (0,):
            for array, entry in ((keep, kind), (arrived, at)):
                if kind == 0:
                    args.append(array)
                    index = functools.partial(lambda entry, t: (t, entry, 0, 0), entry)
                    specs.append(pl.BlockSpec((1, 1, rows, cols), index))
                else:
                    args.append(split(array))
                    index = functools.partial(
                        lambda entry, add, t: (t // 2 + add, 2 * entry + t % 2, 0, 0), entry, add
                    )
                    specs.append(pl.BlockSpec((1, 1, rows // 2, cols), index))
    out = pl.BlockSpec((len(kinds), 1, rows // 2, cols), lambda t: (0, t, 0, 0))
    dims = (len(kinds), nz, rows // 2, cols)
    return run(
        functools.partial(halve_kinds_kernel, kinds), args, (nz,), specs, [out, out],
        [shape(dims, F32), shape(dims, BF16)], "halve_y", after=after,
    )


def halve_z(keep, arrived, kinds, after):
    _, nz, rows, cols = keep.shape
    split = lambda a: a.reshape(len(kinds), 2 * nz, rows // 2, cols)
    args, specs = [], []
    for at, kind in enumerate(kinds):
        for add in (0, nz) if kind else (0,):
            for array, flip in ((keep, 0), (arrived, nz // 2)):
                if kind == 0:
                    args.append(array)
                    index = functools.partial(lambda at, flip, t: (at, t ^ flip, 0, 0), at, flip)
                    specs.append(pl.BlockSpec((1, 1, rows, cols), index))
                else:
                    args.append(split(array))
                    index = functools.partial(lambda at, add, t: (at, t + add, 0, 0), at, add)
                    specs.append(pl.BlockSpec((1, 1, rows // 2, cols), index))
    out = pl.BlockSpec((len(kinds), 1, rows // 2, cols), lambda t: (0, t, 0, 0))
    dims = (len(kinds), nz, rows // 2, cols)
    return run(
        functools.partial(halve_kinds_kernel, kinds), args, (nz,), specs, [out, out],
        [shape(dims, F32), shape(dims, BF16)], "halve_z", after=after,
    )


def core_halves(pos_ref, values):
    half = values.shape[0] // 2
    low, high = values[:half], values[half:]
    own_low = pos_ref[CORE] == 0
    return jnp.where(own_low, low, high), jnp.where(own_low, high, low).astype(BF16)


def finish_kinds_kernel(kinds, pos_ref, *refs):
    inputs, outs = refs[: 2 * len(kinds)], refs[2 * len(kinds) :]
    for at, kind in enumerate(kinds):
        keep_ref, arrived_ref = inputs[2 * at : 2 * at + 2]
        mine, sent = outs[2 * at : 2 * at + 2]
        if kind == 0:
            up = total_of(keep_ref[0, 0], arrived_ref[0, 0])
            half = up.shape[0] // 2
            mine[...], sent[...] = core_halves(pos_ref, jnp.concatenate([up[:half], up[half:]], 1))
        else:

            @pl.when(pl.program_id(0) == 0)
            def _():
                down = total_of(keep_ref[0], arrived_ref[0])
                down = down.reshape(down.shape[0] * down.shape[1], down.shape[2])
                mine[...], sent[...] = core_halves(pos_ref, jnp.transpose(down))


def finish_kinds(pos, keep, arrived, kinds, after):
    _, nz, rows, cols = keep.shape
    bits = nz.bit_length() - 1
    args, specs, out_specs, outs = [], [], [], []
    for at, kind in enumerate(kinds):
        args += [keep, arrived]
        if kind == 0:
            for flip in (0, 1):
                index = functools.partial(lambda at, flip, t, s: (at, t ^ flip, 0, 0), at, flip)
                specs.append(pl.BlockSpec((1, 1, rows, cols), index))
            dims = (rows // 4, 2 * cols * nz)
            out = pl.BlockSpec((rows // 4, 2 * cols), lambda t, s: (0, flipped(t, bits) ^ s[ROW_Z]))
        else:
            index = functools.partial(lambda at, t, s: (at, 0, 0, 0), at)
            specs += [pl.BlockSpec((1, nz, rows, cols), index)] * 2
            dims = (cols // 2, nz * rows)
            out = full(dims)
        out_specs += [out, out]
        outs += [shape(dims, F32), shape(dims, BF16)]
    return run(
        functools.partial(finish_kinds_kernel, kinds), args, (nz,), specs, out_specs, outs, "finish_kinds",
        scalars=(pos,), after=after,
    )


def halve_slices_kernel(ku_ref, kd_ref, au0_ref, au1_ref, ad0_ref, ad1_ref, keep_ref, send_ref):
    ups, downs = (au0_ref, au1_ref), (ad0_ref, ad1_ref)
    for at, ref in enumerate((keep_ref, send_ref)):
        up = total_of(ku_ref[at], ups[at][...])
        rows, half = up.shape[0], up.shape[1] // 2
        for side in range(2):
            piece = up[:, side * half : (side + 1) * half]
            ref[0, side * rows : (side + 1) * rows, :] = piece.astype(ref.dtype)
        ref[1] = total_of(kd_ref[at], downs[at][...]).astype(ref.dtype)


def halve_slices(up_keep, down_keep, arrived, after):
    _, rows, cols = up_keep.shape
    steps = 8
    down_keep = down_keep.reshape(2, 2 * rows, cols // 2)
    arrived = [a.reshape(-1, a.shape[-1]) for a in arrived]
    ups = pl.BlockSpec((2, rows // steps, cols), lambda i: (0, i, 0))
    downs = pl.BlockSpec((2, 2 * rows // steps, cols // 2), lambda i: (0, i, 0))
    dims = (2, 2 * rows, cols // 2)
    return run(
        halve_slices_kernel, (up_keep, down_keep, *arrived), (steps,),
        [ups, downs] + [rows_spec(a.shape[0] // steps, a.shape[1]) for a in arrived],
        [downs, downs], [shape(dims, F32), shape(dims, BF16)], "halve_slices", after=after,
    )


def halve_kernel(keep_ref, arrived_ref, keep_out, send_out):
    keep_out[...] = total_of(keep_ref[:, 0], arrived_ref[:, 0])
    send_out[...] = total_of(keep_ref[:, 1], arrived_ref[:, 1]).astype(BF16)


def halve(keep, arrived, after, steps=2):
    kinds, rows, cols = keep.shape
    split = lambda a: a.reshape(kinds, 2, rows // 2, cols)
    into = pl.BlockSpec((kinds, 2, rows // 2 // steps, cols), lambda i: (0, 0, i, 0))
    out = pl.BlockSpec((kinds, rows // 2 // steps, cols), lambda i: (0, i, 0))
    dims = (kinds, rows // 2, cols)
    return run(
        halve_kernel, (split(keep), split(arrived)), (steps,), [into, into], [out, out],
        [shape(dims, F32), shape(dims, BF16)], "halve", after=after,
    )


def halve_parts_kernel(keep_ref, first_ref, second_ref, keep_out, send_out):
    keep_out[0] = total_of(keep_ref[0], first_ref[...])
    send_out[0] = total_of(keep_ref[1], second_ref[...]).astype(BF16)


def halve_parts(keep, arrived, after, steps=2):
    _, rows, cols = keep.shape
    into = pl.BlockSpec((2, rows // steps, cols), lambda i: (0, i, 0))
    out = pl.BlockSpec((1, rows // steps, cols), lambda i: (0, i, 0))
    return run(
        halve_parts_kernel, (keep, *arrived), (steps,), [into] + [rows_spec(rows // steps, cols)] * 2,
        [out, out], [shape((1, rows, cols), F32), shape((1, rows, cols), BF16)], "halve_parts", after=after,
    )


def finish_slices_kernel(pos_ref, sk_ref, sa_ref, qk_ref, qa_ref, mine_ref, sent_ref, mine_down_ref, sent_down_ref):
    total = total_of(sk_ref[...], sa_ref[...])
    half = total.shape[1] // 2
    up = jnp.concatenate([total[0, :half], total[0, half:]], 1)
    for at, values in enumerate((total_of(qk_ref[0], qa_ref[0]), up)):
        mine, sent_ref[at] = core_halves(pos_ref, values)
        mine_ref[at] = mine.astype(BF16)
    mine, sent_down_ref[...] = core_halves(pos_ref, jnp.transpose(total[1]))
    mine_down_ref[...] = mine.astype(BF16)


def finish_slices(pos, shared, shared_arrived, queries, queries_arrived, after):
    _, rows, cols = shared.shape
    args = (shared, shared_arrived, queries, queries_arrived)
    outs = [shape((2, rows // 4, 2 * cols), BF16)] * 2 + [shape((cols // 2, rows), BF16)] * 2
    return run(
        finish_slices_kernel, args, (1,), [like(a) for a in args], [like(a) for a in outs], outs,
        "finish_slices", scalars=(pos,), after=after,
    )


def middle_back_kernel(
    gs_ref, ga_ref, low_ref, high_ref, gc_ref, gg_ref, routes_ref, router_ref,
    hidden_ref, cot_ref, branch_ref, x_ref, mod_ref, w_ref,
    gm_ref, gatt_ref, back_ref, mods_ref, drouter_ref,
):
    block = pl.program_id(0)
    hidden = hidden_ref[...]
    grad_gates = gg_ref[...]
    ids = lax.broadcasted_iota(jnp.int32, grad_gates.shape, 0)
    gates = gate_rows(hidden, routes_ref[...], router_ref[...], ids)
    inner = jnp.sum(gates * grad_gates, 0, keepdims=True)
    grad_logits = gates * (grad_gates - inner)
    core = jnp.where(block < pl.num_programs(0) // 2, low_ref[...], high_ref[...])
    grad = gs_ref[...] + ga_ref[...].astype(F32) + core.astype(F32) + gc_ref[...].astype(F32)
    pieces = stacked(grad_logits)
    router = router_ref[...]
    grad = grad + tn(pieces, jnp.concatenate([router] * 3, 0))
    drouter = unstacked(nn(pieces, hidden))
    branch = branch_ref[...]
    gate_one = mod_ref[2, pl.ds(block, 1), :]
    middle = x_ref[...].astype(F32) + gate_one * branch
    normed, spread = norm_parts(middle)
    scale = mod_ref[4, pl.ds(block, 1), :]
    mods_ref[1, pl.ds(block, 1), :] = jnp.sum(grad, 0, keepdims=True)
    mods_ref[2, pl.ds(block, 1), :] = jnp.sum(grad * normed, 0, keepdims=True)
    grad_middle = cot_ref[...].astype(F32) + norm_back(grad * (1.0 + scale), normed, spread)
    mods_ref[0, pl.ds(block, 1), :] = jnp.sum(grad_middle * branch, 0, keepdims=True)
    gm_ref[...] = grad_middle
    grad_branch = (grad_middle * gate_one).astype(BF16)
    back_ref[...] = grad_branch
    gatt_ref[...] = nt(grad_branch, w_ref[...]).astype(BF16)

    @pl.when(block == 0)
    def _():
        drouter_ref[...] = drouter

    @pl.when(block > 0)
    def _():
        drouter_ref[...] += drouter


def middle_backward(parts, gg, routes_t, router_t, hidden, cot, branch, patches, mod, out_weight, blocks, after):
    rows, width = patches.shape
    short = rows // blocks
    tile = rows_spec(short, width)
    cols = lambda a: pl.BlockSpec((a.shape[0], short), lambda i: (0, i))
    half = blocks // 2
    low = pl.BlockSpec((short, width), lambda i: (jnp.minimum(i, half - 1), 0))
    high = pl.BlockSpec((short, width), lambda i: (jnp.maximum(i - half, 0), 0))
    out_shape = [
        shape((rows, width), F32),
        shape((rows, width), BF16),
        shape((rows, width), BF16),
        shape((3, 8, width), F32),
        shape((router_t.shape[0], width), F32),
    ]
    return run(
        middle_back_kernel,
        (*parts, gg, routes_t, router_t, hidden, cot, branch, patches, mod, out_weight), (blocks,),
        [tile, tile, low, high, tile] + [cols(gg), cols(routes_t), like(router_t)] + [tile] * 4 + [like(mod), like(out_weight)],
        [tile] * 3 + [like(a) for a in out_shape[3:]], out_shape, "middle_back", after=after,
    )


def mixed_kernel(so_ref, ra_ref, rb_ref, rc_ref, cot_ref, branch_ref, x_ref, mod_ref, mixed_ref, gate_ref):
    block = pl.program_id(0)
    second = so_ref[...] + ra_ref[...].astype(F32) + rb_ref[...].astype(F32) + rc_ref[...].astype(F32)
    middle = x_ref[...].astype(F32) + mod_ref[2, pl.ds(block, 1), :] * branch_ref[...]
    mixed_ref[...] = (middle + mod_ref[5, pl.ds(block, 1), :] * second).astype(BF16)
    gate_ref[pl.ds(block, 1), :] = jnp.sum(cot_ref[...].astype(F32) * second, 0, keepdims=True)


def mixed_forward(parts, cot, branch, patches, mod, blocks, after):
    rows, width = patches.shape
    tile = rows_spec(rows // blocks, width)
    return run(
        mixed_kernel, (*parts, cot, branch, patches, mod), (blocks,), [tile] * 7 + [like(mod)],
        [tile, full((8, width))], [shape((rows, width), BF16), shape((8, width), F32)], "mixed", after=after,
    )


def weight_kernel(
    pos_ref, x_ref, mod_ref, dq_ref, dk_ref, dv_ref, att_ref, back_ref, keep_ref, first_ref, second_ref, turned
):
    rows = x_ref.shape[0]
    short = rows // 4
    step = pl.program_id(0)
    matrix = ((step % 2) ^ pos_ref[STREAM]) * 2 + ((step // 2) ^ pos_ref[CORE])
    nz = 4

    @pl.when(step == 0)
    def _():
        for block in range(4):
            span = slice(block * short, (block + 1) * short)
            normed, _ = norm_parts(x_ref[span, :].astype(F32))
            hidden = normed * (1.0 + mod_ref[1, block : block + 1, :]) + mod_ref[0, block : block + 1, :]
            relative_rows(pos_ref, turned.at[0, :, span], jnp.transpose(hidden.astype(BF16)), nz)
        relative_rows(pos_ref, turned.at[1], jnp.transpose(att_ref[...]), nz)

    for index, (left, ref) in enumerate(((0, dq_ref), (0, dk_ref), (0, dv_ref), (1, back_ref))):

        @pl.when(matrix == index)
        def _():
            total = nn(turned[left], ref[...]).astype(BF16)

            @pl.when(step < 2)
            def _():
                keep_ref[0] = total

            @pl.when(step == 2)
            def _():
                first_ref[...] = total

            @pl.when(step == 3)
            def _():
                second_ref[...] = total


def weight_grads(pos, patches, mod, grads, attended, back, after):
    rows, width = patches.shape
    args = (patches, mod, *grads, attended, back)
    keep = pl.BlockSpec((1, width, width), lambda f, s: (jnp.minimum(f, 1), 0, 0))
    send = full((width, width))
    outs = run(
        weight_kernel, args, (4,), [like(a) for a in args], [keep, send, send],
        [shape((2, width, width), BF16)] + [shape((width, width), BF16)] * 2, "weight_grads", scalars=(pos,),
        scratch=[pltpu.VMEM((2, width, rows), BF16)], after=after,
    )
    return outs[0], outs[1:]


def inputs_back_kernel(dq_ref, dk_ref, dv_ref, w_ref, x_ref, gm_ref, mod_ref, gp_ref, mods_ref):
    block = pl.program_id(0)
    width = x_ref.shape[1]
    grad = nt(dq_ref[...], w_ref[:, :width])
    grad = grad + nt(dk_ref[...], w_ref[:, width : 2 * width])
    grad = grad + nt(dv_ref[...], w_ref[:, 2 * width :])
    normed, spread = norm_parts(x_ref[...].astype(F32))
    mods_ref[0, pl.ds(block, 1), :] = jnp.sum(grad, 0, keepdims=True)
    mods_ref[1, pl.ds(block, 1), :] = jnp.sum(grad * normed, 0, keepdims=True)
    scale = mod_ref[1, pl.ds(block, 1), :]
    gp_ref[...] = gm_ref[...] + norm_back(grad * (1.0 + scale), normed, spread)


def inputs_backward(grads, weight, patches, grad_middle, mod, blocks, after):
    rows, width = patches.shape
    tile = rows_spec(rows // blocks, width)
    return run(
        inputs_back_kernel, (*grads, weight, patches, grad_middle, mod), (blocks,),
        [tile] * 3 + [like(weight), tile, tile, like(mod)], [tile, full((2, 8, width))],
        [shape((rows, width), F32), shape((2, 8, width), F32)], "inputs_back", after=after,
    )


def used_kernel(block_count, pos_ref, gm_ref, ada_ref, emb_ref, out_ref):
    piece = pl.program_id(0)

    @pl.when(piece == 0)
    def _():
        out_ref[...] = jnp.zeros_like(out_ref)

    out_ref[...] += unstacked(nt(stacked(gm_ref[0]), ada_ref[...]))

    @pl.when(piece == pl.num_programs(0) - 1)
    def _():
        emb = emb_ref[...]
        is_long = pos_ref[LONG] > 0
        used = jnp.where(is_long, jnp.broadcast_to(emb[0:1], emb.shape), emb)
        gate = sigmoid(used)
        grad = out_ref[...] * (gate * (1.0 + used * (1.0 - gate)))
        row = lax.broadcasted_iota(jnp.int32, grad.shape, 0)
        grad = jnp.where(row < block_count, grad, 0.0)
        total = jnp.sum(grad, 0, keepdims=True)
        out_ref[...] = jnp.where(is_long, jnp.where(row == 0, total, 0.0), grad)


def used_backward(pos, grad_mod, ada_weight, emb_pad, block_count, after):
    rows, width = emb_pad.shape
    pieces = grad_mod.shape[0]
    return run(
        functools.partial(used_kernel, block_count), (grad_mod, ada_weight, emb_pad), (pieces,),
        [
            pl.BlockSpec((1, rows, width), lambda i, *_: (i, 0, 0)),
            pl.BlockSpec((width, width), lambda i, *_: (0, i)),
            like(emb_pad),
        ],
        like(emb_pad), shape((rows, width), F32), "used_back", scalars=(pos,), after=after,
    )


def swap(values, axis, bit):
    size = lax.axis_size(axis)
    return lax.ppermute(values, axis, [(i, i ^ bit) for i in range(size)])


def swap_all(arrays, axis, bit):
    return [swap(a, axis, bit) for a in arrays]


def swap_across(values):
    stream = lax.axis_size("stream")
    pairs = [
        (i, ((i // stream) ^ 1) * stream + ((i % stream) ^ 1))
        for i in range(lax.axis_size("dp") * stream)
    ]
    return lax.ppermute(values, ("dp", "stream"), pairs)


def in_order(own, mine, arrived, axis):
    return jnp.concatenate(
        [jnp.where(own == 0, mine, arrived), jnp.where(own == 0, arrived, mine)], axis
    )


def local_pair(
    patches, embedding, long_image, routes, cotangent, ada_weight, qkv_weight, out_weight, shared_up,
    shared_down, router_weight, expert_up, expert_down,
):
    rows, width = patches.shape
    blocks = embedding.shape[0]
    short = rows // blocks
    dp_size = lax.axis_size("dp")
    nz = dp_size // 4
    dp, stream = lax.axis_index("dp"), lax.axis_index("stream")
    core, row_y, row_z = dp % 2, (dp // 2) % 2, dp // 4
    local_experts = expert_up.shape[0]
    here = local_experts // 2
    first_here = core * here
    first_all = stream * local_experts + first_here
    places = [long_image[0], core, stream, row_y, row_z, first_here, first_all, 0]
    pos = jnp.stack([jnp.asarray(a, jnp.int32) for a in places])

    routes_t = routes.T
    routes_x = swap(routes_t, "stream", 1)
    routes_near = (routes_t, swap(routes_t, "dp", 1))
    emb_pad = jnp.pad(embedding, ((0, 8 - blocks), (0, 0)))
    router_t = jnp.pad(router_weight.T, ((0, 16 - router_weight.shape[1]), (0, 0)))
    mod, act, branch_grad, branch_sent = modulate(pos, emb_pad, ada_weight, cotangent, blocks)
    routes_x = touch(routes_x, (mod,))
    branch_grad = touch(branch_grad, (routes_x, routes_near[1]))
    routes_far = (routes_x, swap(routes_x, "dp", 1))
    branch_x = swap(touch(branch_sent, (branch_grad,)), "stream", 1)
    branches_near = (branch_grad, swap(branch_grad, "dp", 1))

    packed = qkv_forward(patches, mod, qkv_weight, blocks, (branch_grad,))
    attended, logsum = attend_forward(pos, packed, short)
    branch_one, hidden = middle_forward(
        attended, patches, mod, out_weight, blocks, ()
    )
    hidden_x = swap(hidden, "stream", 1)
    hiddens_near = (hidden, swap(hidden, "dp", 1))
    rank_near, cols_near = ranks(pos, routes_near, (hidden,))
    branch_x = touch(branch_x, (rank_near,))
    branches_far = (branch_x, swap(branch_x, "dp", 1))

    def expert(slot, is_far, sends, prior, after):
        group = (
            (hiddens_far, branches_far, rank_far, routes_far)
            if is_far
            else (hiddens_near, branches_near, rank_near, routes_near)
        )
        out = expert_call(slot, sends, pos, *group, router_t, expert_up, expert_down, prior, nz, after)
        return out[: 1 + sends], out[1 + sends :]

    first, first_near = expert(0, False, 1, None, (branch_x,))
    hidden_x = touch(hidden_x, (first_near[2],))
    hiddens_far = (hidden_x, swap(hidden_x, "dp", 1))
    rank_far, cols_far = ranks(pos, routes_far, (hidden_x,))
    first, first_far = expert(0, True, 1, first, ())
    first_arrived = swap(first[1], "dp", 2)

    second, second_near = expert(1, False, 2, None, (first_far[2],))
    second, second_far = expert(1, True, 2, second, ())
    up_half_arrived = swap(second[1], "dp", 2)
    out_x, out_xc, gx_x, gx_xc = combine(cols_far, [r[:2] for r in (first_far, second_far)], (0, 0), ())
    gx_xc, out_xc = swap_all(gx_xc, "dp", 1), swap(out_xc, "dp", 1)
    out_near, out_core, gx_near, gx_core = combine(
        cols_near, [r[:2] for r in (first_near, second_near)], (0, 0), (gx_x,)
    )
    gx_core = [touch(a, (gx_near,)) for a in swap_all(gx_core, "dp", 1)]
    out_core = touch(swap(out_core, "dp", 1), (gx_near,))
    near, far = (first_near, second_near), (first_far, second_far)
    gg_near = [jnp.concatenate([r[2][source] for r in near], 0) for source in range(2)]
    gg_far = [jnp.concatenate([r[2][source] for r in far], 0) for source in range(2)]
    gg_back = swap(jnp.concatenate([gg_far[0], swap(gg_far[1], "dp", 1)], 0), "stream", 1)
    gg_back = touch(gg_back, (gx_near,))
    gg_rel = jnp.concatenate([gg_near[0], swap(gg_near[1], "dp", 1), gg_back], 0)
    gx_sum, out_sum = add_rows(gx_x, gx_xc, out_x, out_xc, (gg_back, *gx_core, out_core))
    gx_back = swap(gx_sum, "stream", 1)
    out_back = swap(out_sum, "stream", 1)
    both, up, down = (0, 1), (0,), (1,)
    ea_keep, ea_send = halve_y(first[0], first_arrived, both, (out_sum,))
    ea_arrived = swap(ea_send, "dp", 4)
    order = jnp.arange(4, dtype=jnp.int32) ^ (stream * 2 + core)
    gg = gg_rel.reshape(4, here, rows)[order].reshape(EXPERTS, rows)
    gg = jnp.pad(gg, ((0, 16 - EXPERTS), (0, 0)))

    down_half = touch(second[2], (ea_send,))
    down_half_arrived = swap(down_half, "dp", 2)
    up_keep, up_send, down_keep, down_send, shared_out, shared_gx = shared_call(
        pos, hidden, branch_grad, shared_up, shared_down, (down_half, *gx_core, gg)
    )
    sh_arrived = swap_all([*up_send, *down_send], "dp", 1)

    grad_middle, grad_attended, back, mods_two, drouter = middle_backward(
        (shared_gx, gx_near, *gx_core, gx_back), gg, routes_t, router_t, hidden, cotangent, branch_one,
        patches, mod, out_weight, blocks, (),
    )
    ea_keep, ea_send = halve_z(ea_keep, ea_arrived, both, (grad_attended,))
    ea_arrived = swap(ea_send, "dp", 8)
    bu_keep, bu_send = halve_y(second[0], up_half_arrived, up, (ea_send,))
    bu_arrived = swap(bu_send, "dp", 4)
    sh_keep, sh_send = halve_slices(up_keep, down_keep, sh_arrived, (bu_send,))
    sh_arrived = swap(sh_send, "stream", 1)
    grads = attend_backward(pos, packed, attended, logsum, grad_attended, short, (sh_send,))
    out_back = touch(out_back, (grads[0],))
    bd_keep, bd_send = halve_y(second[0], down_half_arrived, down, (out_back,))
    bd_arrived = swap(bd_send, "dp", 4)
    bu_keep, bu_send = halve_z(bu_keep, bu_arrived, up, (bd_send,))
    bu_arrived = swap(bu_send, "dp", 8)
    ea_arrived = touch(ea_arrived, (bu_send,))
    qk_keep, qk_send = weight_grads(pos, patches, mod, grads, attended, back, (ea_arrived,))
    qk_arrived = swap_all(qk_send, "dp", 1)
    sh_keep, sh_send = halve(sh_keep, sh_arrived, (qk_send[0],))
    sh_arrived = swap(sh_send, "dp", 2)
    qk_keep, qk_send = halve_parts(qk_keep, qk_arrived, (sh_send,))
    qk_arrived = swap(qk_send, "stream", 1)
    mixed, gate_two = mixed_forward(
        (shared_out, out_near, out_core, out_back), cotangent, branch_one, patches, mod, blocks, (qk_send,)
    )
    grad_patches, mods_one = inputs_backward(grads, qkv_weight, patches, grad_middle, mod, blocks, (gate_two,))
    factors = [a[:blocks] for a in (act, *mods_one, *mods_two, gate_two)]
    factors = jnp.concatenate(factors + [drouter[:EXPERTS].reshape(blocks, -1)], 1).astype(BF16)

    def doubled(axis, bit, after):
        return jnp.concatenate([factors, touch(swap(factors, axis, bit), (after,))], 0)

    grad_mod = jnp.concatenate([mods_one, mods_two, gate_two[None]], 0)
    sh_keep, sh_send = halve(sh_keep, sh_arrived, (mods_one,))
    sh_arrived = swap(sh_send, "dp", 4)
    qk_keep, qk_send = halve(qk_keep, qk_arrived, (sh_send,))
    qk_arrived = swap(qk_send, "dp", 2)
    bd_keep, bd_send = halve_z(bd_keep, bd_arrived, down, (qk_send,))
    bd_arrived = swap(bd_send, "dp", 8)
    bu_arrived = touch(bu_arrived, (bd_send,))
    factors = doubled("dp", 8, bu_arrived)
    grad_embedding = used_backward(pos, grad_mod, ada_weight, emb_pad, blocks, (bu_arrived,))
    factors = doubled("dp", 4, grad_embedding)
    qk_keep, qk_send = halve(qk_keep, qk_arrived, (grad_embedding,))
    qk_arrived = swap(qk_send, "dp", 4)
    sh_keep, sh_send = halve(sh_keep, sh_arrived, (qk_send,))
    sh_arrived = swap(sh_send, "dp", 8)
    factors = doubled("dp", 2, sh_send)
    ea_done = finish_kinds(pos, ea_keep, ea_arrived, both, (sh_send,))
    qk_keep, qk_send = halve(qk_keep, qk_arrived, (ea_done[1],))
    qk_arrived = swap(qk_send, "dp", 8)
    bd_arrived = touch(bd_arrived, (qk_send,))
    bu_done = finish_kinds(pos, bu_keep, bu_arrived, up, (bd_arrived,))
    factors_x = touch(swap(factors, "stream", 1), (bu_done[1],))
    bd_done = finish_kinds(pos, bd_keep, bd_arrived, down, (factors_x,))
    bu_others = touch(swap(bu_done[1], "dp", 1), (bd_done[1],))
    ea_others = [touch(swap(a, "dp", 1), (bd_done[1],)) for a in (ea_done[1], ea_done[3])]
    bd_others = touch(swap(bd_done[1], "dp", 1), (bu_others,))
    done = finish_slices(
        pos, sh_keep, sh_arrived, qk_keep, qk_arrived, (bu_others, bd_others, *ea_others)
    )
    pieces = [factors, factors_x, swap(factors, "dp", 1), swap(factors_x, "dp", 1)]

    pieces[:2] = [touch(a, (done[0],)) for a in pieces[:2]]
    ea_others = [touch(a, (done[0],)) for a in ea_others]

    def slices_out(mine, send):
        near = in_order(core, mine, swap(send, "dp", 1), mine.ndim - 1)
        far = in_order(core, swap(mine, "stream", 1), swap_across(send), mine.ndim - 1)
        return in_order(stream, near, far, mine.ndim - 1).astype(F32)

    rows_out = slices_out(*done[:2])
    grad_qkv_out, grad_shared_up = rows_out[0], rows_out[1]
    grad_shared_down = slices_out(*done[2:])

    share = width // dp_size

    def own_share(values):
        return lax.dynamic_slice_in_dim(values, dp * share, share, 1)

    grad_ada, drouter_sum = 0.0, 0.0
    for piece in pieces:
        acts = own_share(piece[:, :width])
        grad_ada = grad_ada + lax.dot_general(
            acts, piece[:, width : 7 * width], (((0,), (0,)), ((), ())), preferred_element_type=F32
        )
        drouter_sum = drouter_sum + jnp.sum(piece[:, 7 * width :].astype(F32).reshape(-1, blocks, 2 * width), 0)
    grad_router = own_share(drouter_sum.reshape(EXPERTS, width)).T

    def experts_out(one, two, one_other, two_other):
        mine, others = jnp.stack([one, two]), jnp.stack([one_other, two_other]).astype(F32)
        return in_order(core, mine, others, 0)

    return (
        mixed, grad_patches, grad_embedding[:blocks], grad_ada, grad_qkv_out[:, : 3 * width],
        grad_qkv_out[:, 3 * width :], grad_shared_up, grad_shared_down, grad_router,
        experts_out(ea_done[0], bu_done[0], ea_others[0], bu_others),
        experts_out(ea_done[2], bd_done[0], ea_others[1], bd_others),
    )


def local(*arrays):
    experts, width, wide = arrays[11].shape
    pair = lax.axis_size("stream") == 2 and experts == 4 and lax.axis_size("dp") == 16
    if pair and wide == 4 * width:
        return local_pair(*arrays)
    return local_general(*arrays)


def solution(mesh):
    return jax.shard_map(
        local,
        mesh=mesh,
        in_specs=(
            P(("dp", "stream"), None),
            P(("dp", "stream"), None),
            P(("dp", "stream")),
            P(("dp", "stream"), None),
            P(("dp", "stream"), None),
            P(),
            P(),
            P(),
            P(),
            P(),
            P(),
            P("stream", None, None),
            P("stream", None, None),
        ),
        out_specs=(
            P(("dp", "stream"), None),
            P(("dp", "stream"), None),
            P(("dp", "stream"), None),
            P("dp", None),
            P("dp", None),
            P("dp", None),
            P("dp", None),
            P("dp", None),
            P("dp", None),
            P("stream", "dp", None),
            P("stream", "dp", None),
        ),
        check_vma=False,
    )
```

```python
import functools
import math

import jax
import jax.numpy as jnp
from jax import lax
from jax.experimental import pallas as pl
from jax.experimental.pallas import tpu as pltpu
from jax.sharding import PartitionSpec as P

HEADS = 12
HEAD_DIM = 64
EXPERTS = 8
CAP = 288


HIGH = lax.Precision.HIGHEST
EPSILON = 1e-06
F32 = jnp.float32
BF16 = jnp.bfloat16
MIB = 1 << 20


def gelu_tanh(values):
    return jax.nn.gelu(values, approximate=True)


def normalize(values):
    centered = values - jnp.mean(values, -1, keepdims=True)
    spread = lax.rsqrt(jnp.mean(centered * centered, -1, keepdims=True) + EPSILON)
    return (centered * spread, spread)


def normalize_back(grad_normed, normed, spread):
    return spread * (
        grad_normed
        - jnp.mean(grad_normed, -1, keepdims=True)
        - normed * jnp.mean(grad_normed * normed, -1, keepdims=True)
    )


def split_packed(packed, seg_len):
    row_count = packed.shape[0]
    model_width = packed.shape[1] // 3
    groups = row_count // seg_len
    block_rows = min(512, seg_len)
    part_count = seg_len // block_rows
    queries = (
        packed[:, :model_width]
        .reshape(groups, part_count, block_rows, HEADS, HEAD_DIM)
        .swapaxes(0, 1)
    )
    key_heads = packed[:, model_width : 2 * model_width].reshape(groups, seg_len, HEADS, HEAD_DIM)
    values = packed[:, 2 * model_width :].reshape(groups, seg_len, HEADS, HEAD_DIM)
    return (queries, key_heads, values, groups, block_rows, part_count)


def attend(packed, seg_len):
    row_count = packed.shape[0]
    model_width = packed.shape[1] // 3
    factor = 1.0 / math.sqrt(HEAD_DIM)
    queries, key_heads, values, groups, block_rows, part_count = split_packed(packed, seg_len)

    def one_block(query_block):
        scores = (
            jnp.einsum(
                "gqhd,gkhd->ghqk", query_block, key_heads, preferred_element_type=jnp.float32
            )
            * factor
        )
        row_max = jnp.max(scores, -1, keepdims=True)
        shifted = jnp.exp(scores - row_max)
        row_sum = jnp.sum(shifted, -1, keepdims=True)
        weights = (shifted / row_sum).astype(jnp.bfloat16)
        mixture = jnp.einsum("ghqk,gkhd->gqhd", weights, values, preferred_element_type=jnp.float32)
        return (mixture, row_max[..., 0] + jnp.log(row_sum[..., 0]))

    mixture, logsum = lax.map(one_block, queries)
    return (mixture.swapaxes(0, 1).reshape(row_count, model_width), logsum.reshape(-1))


def attend_back(packed, logsum, grad_mixture, seg_len):
    row_count = packed.shape[0]
    model_width = packed.shape[1] // 3
    factor = 1.0 / math.sqrt(HEAD_DIM)
    queries, key_heads, values, groups, block_rows, part_count = split_packed(packed, seg_len)
    grad_blocks = grad_mixture.reshape(groups, part_count, block_rows, HEADS, HEAD_DIM).swapaxes(
        0, 1
    )
    logsum_blocks = logsum.reshape(part_count, groups, HEADS, block_rows)

    def one_block(carried, inputs):
        grad_keys, grad_values = carried
        query_block, grad_block, logsum_block = inputs
        scores = (
            jnp.einsum(
                "gqhd,gkhd->ghqk", query_block, key_heads, preferred_element_type=jnp.float32
            )
            * factor
        )
        prob_full = jnp.exp(scores - logsum_block[..., None])
        grad_values = grad_values + jnp.einsum(
            "ghqk,gqhd->gkhd",
            prob_full.astype(jnp.bfloat16),
            grad_block,
            preferred_element_type=jnp.float32,
        )
        grad_probs = jnp.einsum(
            "gqhd,gkhd->ghqk", grad_block, values, preferred_element_type=jnp.float32
        )
        row_inner = jnp.sum(grad_probs * prob_full, -1, keepdims=True)
        grad_scores = (prob_full * (grad_probs - row_inner)).astype(jnp.bfloat16)
        grad_query = (
            jnp.einsum(
                "ghqk,gkhd->gqhd", grad_scores, key_heads, preferred_element_type=jnp.float32
            )
            * factor
        )
        grad_keys = (
            grad_keys
            + jnp.einsum(
                "ghqk,gqhd->gkhd", grad_scores, query_block, preferred_element_type=jnp.float32
            )
            * factor
        )
        return ((grad_keys, grad_values), grad_query)

    zeros_kv = jnp.zeros((groups, seg_len, HEADS, HEAD_DIM), jnp.float32)
    (grad_keys, grad_values), grad_query = lax.scan(
        one_block, (zeros_kv, zeros_kv), (queries, grad_blocks, logsum_blocks)
    )
    return jnp.concatenate(
        [
            grad_query.swapaxes(0, 1).reshape(row_count, model_width),
            grad_keys.reshape(row_count, model_width),
            grad_values.reshape(row_count, model_width),
        ],
        1,
    )


def local_general(
    patches,
    embedding,
    long_image,
    routes,
    cotangent,
    ada_weight,
    qkv_weight,
    out_weight,
    shared_up,
    shared_down,
    router_weight,
    expert_up,
    expert_down,
):
    row_count, model_width = patches.shape
    block_count = embedding.shape[0]
    short_len = row_count // block_count
    lane_count = lax.axis_size("stream")
    local_experts = expert_up.shape[0]
    is_long = long_image[0] > 0

    def blocks(values):
        return values.reshape(block_count, short_len, model_width)

    def flatten(values):
        return values.reshape(row_count, model_width)

    used = jnp.where(is_long, jnp.broadcast_to(embedding[0:1], embedding.shape), embedding)
    activated, silu_back = jax.vjp(jax.nn.silu, used)
    ada_full = ada_weight.astype(jnp.float32)
    modulation = jnp.dot(activated, ada_full, precision=HIGH)
    pieces = [
        modulation[:, column * model_width : (column + 1) * model_width][:, None, :]
        for column in range(6)
    ]
    shift_one, scale_one, gate_one, shift_two, scale_two, gate_two = pieces
    inputs_full = blocks(patches.astype(jnp.float32))
    normed_one, spread_one = normalize(inputs_full)
    hidden_one = flatten(normed_one * (1.0 + scale_one) + shift_one).astype(jnp.bfloat16)
    packed = jnp.dot(hidden_one, qkv_weight, preferred_element_type=jnp.float32).astype(
        jnp.bfloat16
    )
    attended, logsum = lax.cond(
        is_long,
        lambda packed_in: attend(packed_in, row_count),
        lambda packed_in: attend(packed_in, short_len),
        packed,
    )
    attended_low = attended.astype(jnp.bfloat16)
    branch_one = blocks(jnp.dot(attended_low, out_weight, preferred_element_type=jnp.float32))
    middle = inputs_full + gate_one * branch_one
    normed_two, spread_two = normalize(middle)
    hidden_two = flatten(normed_two * (1.0 + scale_two) + shift_two).astype(jnp.bfloat16)
    shared_pre = jnp.dot(hidden_two, shared_up, preferred_element_type=jnp.float32)
    shared_act, shared_back = jax.vjp(gelu_tanh, shared_pre)
    shared_low = shared_act.astype(jnp.bfloat16)
    shared_out = jnp.dot(shared_low, shared_down, preferred_element_type=jnp.float32)
    logits = jnp.dot(hidden_two, router_weight, preferred_element_type=jnp.float32)
    chosen_hot = (routes[:, :, None] == jnp.arange(EXPERTS)[None, None, :]).astype(jnp.float32)
    gates = jax.nn.softmax(jnp.sum(chosen_hot * logits[:, None, :], -1), -1)
    flat_routes = routes.reshape(-1)
    route_hits = (flat_routes[:, None] == jnp.arange(EXPERTS)[None, :]).astype(jnp.int32)
    earlier = jnp.cumsum(route_hits, 0) - route_hits
    target = flat_routes * CAP + jnp.sum(earlier * route_hits, 1)

    def spread_rows(rows_low):
        buffer = jnp.zeros((EXPERTS * CAP, model_width), jnp.bfloat16).at[target].set(rows_low)
        return buffer.reshape(lane_count, local_experts, CAP, model_width)

    def collect(arrived):
        return (
            arrived.reshape(EXPERTS * CAP, model_width)[target]
            .astype(jnp.float32)
            .reshape(row_count, 2, model_width)
        )

    def by_expert(arrived):
        return arrived.swapaxes(0, 1).reshape(local_experts, lane_count * CAP, model_width)

    def by_source(results):
        return results.reshape(local_experts, lane_count, CAP, model_width).swapaxes(0, 1)

    expert_in = by_expert(
        lax.all_to_all(
            spread_rows(jnp.repeat(hidden_two, 2, axis=0)),
            "stream",
            split_axis=0,
            concat_axis=0,
            tiled=True,
        )
    )
    expert_pre = jnp.einsum(
        "jrd,jdf->jrf", expert_in, expert_up, preferred_element_type=jnp.float32
    )
    expert_act, expert_back = jax.vjp(gelu_tanh, expert_pre)
    expert_low = expert_act.astype(jnp.bfloat16)
    expert_out = jnp.einsum(
        "jrf,jfd->jrd", expert_low, expert_down, preferred_element_type=jnp.float32
    ).astype(jnp.bfloat16)
    picked = collect(
        lax.all_to_all(by_source(expert_out), "stream", split_axis=0, concat_axis=0, tiled=True)
    )
    routed = jnp.sum(gates[:, :, None] * picked, 1)
    branch_two = blocks(shared_out + routed)
    mixed = flatten(middle + gate_two * branch_two).astype(jnp.bfloat16)
    grad_top = blocks(cotangent.astype(jnp.float32))
    grad_gate_two = jnp.sum(grad_top * branch_two, 1)
    grad_branch = flatten(grad_top * gate_two)
    grad_pick = (
        (gates[:, :, None] * grad_branch[:, None, :])
        .astype(jnp.bfloat16)
        .reshape(2 * row_count, model_width)
    )
    grad_arrived = by_expert(
        lax.all_to_all(spread_rows(grad_pick), "stream", split_axis=0, concat_axis=0, tiled=True)
    )
    grad_expert_down = jnp.einsum(
        "jrf,jrd->jfd", expert_low, grad_arrived, preferred_element_type=jnp.float32
    )
    grad_expert_act = jnp.einsum(
        "jrd,jfd->jrf", grad_arrived, expert_down, preferred_element_type=jnp.float32
    )
    grad_expert_pre = expert_back(grad_expert_act)[0].astype(jnp.bfloat16)
    grad_expert_up = jnp.einsum(
        "jrd,jrf->jdf", expert_in, grad_expert_pre, preferred_element_type=jnp.float32
    )
    grad_expert_in = jnp.einsum(
        "jrf,jdf->jrd", grad_expert_pre, expert_up, preferred_element_type=jnp.float32
    ).astype(jnp.bfloat16)
    grad_routed = jnp.sum(
        collect(
            lax.all_to_all(
                by_source(grad_expert_in), "stream", split_axis=0, concat_axis=0, tiled=True
            )
        ),
        1,
    )
    grad_shared_low = grad_branch.astype(jnp.bfloat16)
    grad_shared_down = jnp.einsum(
        "rf,rd->fd", shared_low, grad_shared_low, preferred_element_type=jnp.float32
    )
    grad_shared_act = jnp.einsum(
        "rd,fd->rf", grad_shared_low, shared_down, preferred_element_type=jnp.float32
    )
    grad_shared_pre = shared_back(grad_shared_act)[0].astype(jnp.bfloat16)
    grad_shared_up = jnp.einsum(
        "rd,rf->df", hidden_two, grad_shared_pre, preferred_element_type=jnp.float32
    )
    grad_gates = jnp.sum(picked * grad_branch[:, None, :], -1)
    grad_chosen = gates * (grad_gates - jnp.sum(gates * grad_gates, -1, keepdims=True))
    grad_logits = jnp.sum(chosen_hot * grad_chosen[:, :, None], 1)
    hidden_two_full = hidden_two.astype(jnp.float32)
    router_full = router_weight.astype(jnp.float32)
    grad_router = jnp.dot(hidden_two_full.T, grad_logits, precision=HIGH)
    grad_hidden = jnp.dot(grad_logits, router_full.T, precision=HIGH) + grad_routed
    grad_hidden = blocks(
        grad_hidden
        + jnp.einsum("rf,df->rd", grad_shared_pre, shared_up, preferred_element_type=jnp.float32)
    )
    grad_shift_two = jnp.sum(grad_hidden, 1)
    grad_scale_two = jnp.sum(grad_hidden * normed_two, 1)
    grad_middle = grad_top + normalize_back(grad_hidden * (1.0 + scale_two), normed_two, spread_two)
    grad_gate_one = jnp.sum(grad_middle * branch_one, 1)
    grad_branch_one = flatten(grad_middle * gate_one).astype(jnp.bfloat16)
    grad_out_weight = jnp.einsum(
        "rd,re->de", attended_low, grad_branch_one, preferred_element_type=jnp.float32
    )
    grad_attended = jnp.einsum(
        "re,de->rd", grad_branch_one, out_weight, preferred_element_type=jnp.float32
    ).astype(jnp.bfloat16)
    grad_packed = lax.cond(
        is_long,
        lambda packed_in, logsum_in, grad_in: attend_back(packed_in, logsum_in, grad_in, row_count),
        lambda packed_in, logsum_in, grad_in: attend_back(packed_in, logsum_in, grad_in, short_len),
        packed,
        logsum,
        grad_attended,
    ).astype(jnp.bfloat16)
    grad_qkv = jnp.einsum("rd,re->de", hidden_one, grad_packed, preferred_element_type=jnp.float32)
    grad_hidden_one = blocks(
        jnp.einsum("re,de->rd", grad_packed, qkv_weight, preferred_element_type=jnp.float32)
    )
    grad_shift_one = jnp.sum(grad_hidden_one, 1)
    grad_scale_one = jnp.sum(grad_hidden_one * normed_one, 1)
    grad_inputs = grad_middle + normalize_back(
        grad_hidden_one * (1.0 + scale_one), normed_one, spread_one
    )
    grad_modulation = jnp.concatenate(
        [
            grad_shift_one,
            grad_scale_one,
            grad_gate_one,
            grad_shift_two,
            grad_scale_two,
            grad_gate_two,
        ],
        1,
    )
    grad_ada = jnp.dot(activated.T, grad_modulation, precision=HIGH)
    grad_used = silu_back(jnp.dot(grad_modulation, ada_full.T, precision=HIGH))[0]
    grad_embedding = jnp.where(
        is_long, jnp.zeros_like(grad_used).at[0].set(jnp.sum(grad_used, 0)), grad_used
    )
    shares = (
        lax.psum_scatter(
            grad_ada.astype(jnp.bfloat16), "dp", scatter_dimension=0, tiled=True
        ).astype(jnp.float32),
        lax.psum_scatter(
            grad_qkv.astype(jnp.bfloat16), "dp", scatter_dimension=0, tiled=True
        ).astype(jnp.float32),
        lax.psum_scatter(
            grad_out_weight.astype(jnp.bfloat16), "dp", scatter_dimension=0, tiled=True
        ).astype(jnp.float32),
        lax.psum_scatter(
            grad_shared_up.astype(jnp.bfloat16), "dp", scatter_dimension=0, tiled=True
        ).astype(jnp.float32),
        lax.psum_scatter(
            grad_shared_down.astype(jnp.bfloat16), "dp", scatter_dimension=0, tiled=True
        ).astype(jnp.float32),
        lax.psum_scatter(
            grad_router.astype(jnp.bfloat16), "dp", scatter_dimension=0, tiled=True
        ).astype(jnp.float32),
    )
    expert_summed = (
        lax.psum_scatter(
            grad_expert_up.astype(jnp.bfloat16), "dp", scatter_dimension=1, tiled=True
        ).astype(jnp.float32),
        lax.psum_scatter(
            grad_expert_down.astype(jnp.bfloat16), "dp", scatter_dimension=1, tiled=True
        ).astype(jnp.float32),
    )
    summed = (
        lax.psum(shares[0].astype(jnp.bfloat16), "stream").astype(jnp.float32),
        lax.psum(shares[1].astype(jnp.bfloat16), "stream").astype(jnp.float32),
        lax.psum(shares[2].astype(jnp.bfloat16), "stream").astype(jnp.float32),
        lax.psum(shares[3].astype(jnp.bfloat16), "stream").astype(jnp.float32),
        lax.psum(shares[4].astype(jnp.bfloat16), "stream").astype(jnp.float32),
        lax.psum(shares[5].astype(jnp.bfloat16), "stream").astype(jnp.float32),
    )
    return (
        mixed,
        flatten(grad_inputs),
        grad_embedding,
        summed[0],
        summed[1],
        summed[2],
        summed[3],
        summed[4],
        summed[5],
        expert_summed[0],
        expert_summed[1],
    )


def nn(left, right):
    return jnp.dot(left, right, preferred_element_type=F32)


def nt(left, right):
    return lax.dot_general(left, right, (((1,), (1,)), ((), ())), preferred_element_type=F32)


def tn(left, right):
    return lax.dot_general(left, right, (((0,), (0,)), ((), ())), preferred_element_type=F32)


def three_parts(values):
    first = values.astype(BF16)
    rest = values - first.astype(F32)
    second = rest.astype(BF16)
    third = (rest - second.astype(F32)).astype(BF16)
    return first, second, third


def stacked(values):
    return jnp.concatenate(three_parts(values), 0)


def unstacked(product):
    rows = product.shape[0] // 3
    return product[:rows] + product[rows : 2 * rows] + product[2 * rows :]


def sigmoid(values):
    return 1.0 / (1.0 + jnp.exp(-values))


def gelu_and_slope(values):
    inner = math.sqrt(2.0 / math.pi)
    square = values * values
    bend = jnp.tanh(values * (inner + (inner * 0.044715) * square))
    half = 0.5 + 0.5 * bend
    slope = half + values * (0.5 - 0.5 * bend * bend) * (inner + (3.0 * inner * 0.044715) * square)
    return values * half, slope


def run(kernel, args, grid, in_specs, out_specs, out_shape, name, scalars=(), scratch=(), after=(), limit=56):
    count = len(scalars) + len(args)

    def body(*refs):
        kernel(*refs[:count], *refs[count + len(after) :])

    return pl.pallas_call(
        body,
        grid_spec=pltpu.PrefetchScalarGridSpec(
            num_scalar_prefetch=len(scalars),
            grid=grid,
            in_specs=list(in_specs) + [pl.BlockSpec(memory_space=pl.ANY)] * len(after),
            out_specs=out_specs,
            scratch_shapes=list(scratch),
        ),
        out_shape=out_shape,
        compiler_params=pltpu.CompilerParams(vmem_limit_bytes=limit * MIB),
        cost_estimate=pl.CostEstimate(flops=1000, bytes_accessed=1000, transcendentals=0),
        name=name,
    )(*scalars, *args, *after)


def full(shape):
    return pl.BlockSpec(shape, lambda *_: (0,) * len(shape))


def like(array):
    return full(array.shape)


def rows_spec(rows, width):
    return pl.BlockSpec((rows, width), lambda i, *_: (i, 0))


def shape(dims, dtype):
    return jax.ShapeDtypeStruct(tuple(dims), dtype)


LONG, CORE, STREAM, ROW_Y, ROW_Z, FIRST_HERE, FIRST_ALL = range(7)


def flipped(value, bits):
    total = 0
    for bit in range(bits):
        total = total + (((value >> bit) & 1) << (bits - 1 - bit))
    return total


def modulate_kernel(blocks, pos_ref, emb_ref, ada_ref, cot_ref, mod_ref, act_ref, branch_ref, sent_ref):
    emb = emb_ref[...]
    used = jnp.where(pos_ref[LONG] > 0, jnp.broadcast_to(emb[0:1], emb.shape), emb)
    act = used * sigmoid(used)
    act_ref[...] = act
    total = unstacked(nn(stacked(act), ada_ref[...]))
    mod_ref[0] = total

    @pl.when(pl.program_id(0) == pl.num_programs(0) - 1)
    def _():
        short = cot_ref.shape[0] // blocks
        for block in range(blocks):
            span = slice(block * short, (block + 1) * short)
            branch = (cot_ref[span, :].astype(F32) * total[block : block + 1]).astype(BF16)
            branch_ref[span, :] = branch
            sent_ref[span, :] = branch
        sent_ref[cot_ref.shape[0] :, :] = jnp.zeros((sent_ref.shape[0] - cot_ref.shape[0], cot_ref.shape[1]), BF16)


def modulate(pos, emb_pad, ada_weight, cot, blocks):
    rows, width = emb_pad.shape
    pieces = ada_weight.shape[1] // width
    sent = (cot.shape[0] + 32, width)
    return run(
        functools.partial(modulate_kernel, blocks), (emb_pad, ada_weight, cot), (pieces,),
        [like(emb_pad), pl.BlockSpec((width, width), lambda i, *_: (0, i)), like(cot)],
        [pl.BlockSpec((1, rows, width), lambda i, *_: (i, 0, 0)), like(emb_pad), like(cot), full(sent)],
        [shape((pieces, rows, width), F32), shape((rows, width), F32), shape(cot.shape, BF16), shape(sent, BF16)],
        "modulate", scalars=(pos,),
    )


def norm_parts(values):
    centered = values - jnp.mean(values, -1, keepdims=True)
    spread = lax.rsqrt(jnp.mean(centered * centered, -1, keepdims=True) + EPSILON)
    return centered * spread, spread


def norm_back(grad, normed, spread):
    return spread * (
        grad
        - jnp.mean(grad, -1, keepdims=True)
        - normed * jnp.mean(grad * normed, -1, keepdims=True)
    )


def qkv_kernel(x_ref, mod_ref, w_ref, packed_ref):
    short = x_ref.shape[0] // 2
    halves = []
    for at in range(2):
        block = pl.program_id(0) * 2 + at
        normed, _ = norm_parts(x_ref[at * short : (at + 1) * short, :].astype(F32))
        shift, scale = mod_ref[0, pl.ds(block, 1), :], mod_ref[1, pl.ds(block, 1), :]
        halves.append((normed * (1.0 + scale) + shift).astype(BF16))
    packed_ref[...] = nn(jnp.concatenate(halves, 0), w_ref[...]).astype(BF16)


def qkv_forward(patches, mod, weight, blocks, after):
    rows, width = patches.shape
    short = 2 * rows // blocks
    wide = weight.shape[1]
    return run(
        qkv_kernel, (patches, mod, weight), (blocks // 2,),
        [rows_spec(short, width), like(mod), like(weight)], rows_spec(short, wide),
        shape((rows, wide), BF16), "qkv", after=after,
    )


def attend_kernel(short, pos_ref, q_ref, k_ref, v_ref, o_ref, lse_ref):
    rows, lanes = q_ref.shape
    first = lax.broadcasted_iota(jnp.int32, (1, lanes), 1) < HEAD_DIM
    factor = 1.0 / math.sqrt(HEAD_DIM)

    def part(at, count):
        span = slice(at, at + count)
        queries = (q_ref[span, :].astype(F32) * factor).astype(BF16)
        keys, values = k_ref[span, :], v_ref[span, :]
        zero = jnp.zeros_like(queries)
        wide = jnp.concatenate([values, jnp.ones_like(values)], 1)
        masks = (first, jnp.logical_not(first))
        scores = [nt(jnp.where(mine, queries, zero), keys) for mine in masks]
        tops = [jnp.max(a, -1, keepdims=True) for a in scores]
        shifted = [jnp.exp(a - top).astype(BF16) for a, top in zip(scores, tops)]
        mixtures = [nn(a, wide) for a in shifted]
        totals = [a[:, lanes:] for a in mixtures]
        outs = [a[:, :lanes] / total for a, total in zip(mixtures, totals)]
        sums = [top + jnp.log(total) for top, total in zip(tops, totals)]
        o_ref[span, :] = jnp.where(first, outs[0], outs[1]).astype(BF16)
        lse_ref[span, :] = jnp.where(first, sums[0], sums[1])

    @pl.when(pos_ref[LONG] > 0)
    def _():
        part(0, rows)

    @pl.when(pos_ref[LONG] <= 0)
    def _():
        for at in range(0, rows, short):
            part(at, short)


def pair_specs(rows, width):
    lanes = 2 * HEAD_DIM
    pairs = width // lanes
    return [
        pl.BlockSpec((rows, lanes), functools.partial(lambda shift, i, *_: (0, i + shift), shift))
        for shift in (0, pairs, 2 * pairs)
    ]


def attend_forward(pos, packed, short):
    rows = packed.shape[0]
    width = packed.shape[1] // 3
    spec = pair_specs(rows, width)
    return run(
        functools.partial(attend_kernel, short), (packed, packed, packed), (width // (2 * HEAD_DIM),),
        spec, [spec[0], spec[0]], [shape((rows, width), BF16), shape((rows, width), F32)],
        "attend", scalars=(pos,),
    )


def attend_back_kernel(
    short, pos_ref, q_ref, k_ref, v_ref, o_ref, lse_ref, do_ref, dq_ref, dk_ref, dv_ref,
    dk_acc, dv_acc,
):
    rows, lanes = q_ref.shape
    first = lax.broadcasted_iota(jnp.int32, (1, lanes), 1) < HEAD_DIM
    factor = 1.0 / math.sqrt(HEAD_DIM)
    product = do_ref[...].astype(F32) * o_ref[...].astype(F32)
    lse_t = jnp.transpose(lse_ref[...])
    product_t = jnp.transpose(product)
    lse_rows = [lse_t[0:1], lse_t[HEAD_DIM : HEAD_DIM + 1]]
    delta_rows = [
        jnp.sum(product_t[:HEAD_DIM], 0, keepdims=True),
        jnp.sum(product_t[HEAD_DIM:], 0, keepdims=True),
    ]

    def part(query_at, key_at, key_count, fresh):
        chunk = slice(query_at, query_at + short)
        span = slice(key_at, key_at + key_count)
        queries, grads = (q_ref[chunk, :].astype(F32) * factor).astype(BF16), do_ref[chunk, :]
        keys, values = k_ref[span, :], v_ref[span, :]
        masks = (first, jnp.logical_not(first))

        def apart(array):
            return [jnp.where(mine, array, jnp.zeros_like(array)) for mine in masks]

        query_own, grad_own, key_own = apart(queries), apart(grads), apart(keys)
        probs = [
            jnp.exp(nt(keys, query) - lse[:, chunk]) for query, lse in zip(query_own, lse_rows)
        ]
        grad_probs = [nt(values, grad) for grad in grad_own]
        grad_scores = [
            (prob * (grad - delta[:, chunk])).astype(BF16)
            for prob, grad, delta in zip(probs, grad_probs, delta_rows)
        ]
        low = [prob.astype(BF16) for prob in probs]
        dv = nn(jnp.concatenate(low, 1), jnp.concatenate(grad_own, 0))
        dk = nn(jnp.concatenate(grad_scores, 1), jnp.concatenate(query_own, 0))
        dq = nn(jnp.transpose(jnp.concatenate(key_own, 0)), jnp.concatenate(grad_scores, 0))
        dq_ref[chunk, :] = (jnp.transpose(dq) * factor).astype(BF16)
        if fresh:
            dk_acc[span, :] = dk
            dv_acc[span, :] = dv
        else:
            dk_acc[span, :] += dk
            dv_acc[span, :] += dv

    @pl.when(pos_ref[LONG] > 0)
    def _():
        for at in range(0, rows, short):
            part(at, 0, rows, at == 0)

    @pl.when(pos_ref[LONG] <= 0)
    def _():
        for at in range(0, rows, short):
            part(at, at, short, True)

    dk_ref[...] = dk_acc[...].astype(BF16)
    dv_ref[...] = dv_acc[...].astype(BF16)


def attend_backward(pos, packed, attended, logsum, grad, short, after):
    rows, width = attended.shape
    lanes = 2 * HEAD_DIM
    spec = pair_specs(rows, width)
    return run(
        functools.partial(attend_back_kernel, short),
        (packed, packed, packed, attended, logsum, grad), (width // lanes,),
        spec + [spec[0]] * 3, [spec[0]] * 3, [shape((rows, width), BF16)] * 3,
        "attend_back", scalars=(pos,), scratch=[pltpu.VMEM((rows, lanes), F32)] * 2, after=after,
    )


def middle_kernel(att_ref, x_ref, mod_ref, w_ref, branch_ref, hidden_ref):
    short = x_ref.shape[0] // 2
    branch = nn(att_ref[...], w_ref[...])
    branch_ref[...] = branch
    for at in range(2):
        block, span = pl.program_id(0) * 2 + at, slice(at * short, (at + 1) * short)
        middle = x_ref[span, :].astype(F32) + mod_ref[2, pl.ds(block, 1), :] * branch[span]
        normed, _ = norm_parts(middle)
        shift, scale = mod_ref[3, pl.ds(block, 1), :], mod_ref[4, pl.ds(block, 1), :]
        hidden_ref[span, :] = (normed * (1.0 + scale) + shift).astype(BF16)


def middle_forward(attended, patches, mod, out_weight, blocks, after):
    rows, width = patches.shape
    tile = rows_spec(2 * rows // blocks, width)
    return run(
        middle_kernel, (attended, patches, mod, out_weight), (blocks // 2,),
        [tile, tile, like(mod), like(out_weight)], [tile, tile],
        [shape((rows, width), F32), shape((rows, width), BF16)], "middle", after=after,
    )


def rank_kernel(pos_ref, *refs):
    count = (len(refs) - 2) // 1
    routes, (row_ref, col_ref) = refs[:count], refs[count:]
    rows = routes[0].shape[1]
    before = lax.broadcasted_iota(jnp.int32, (rows, rows), 0)
    after = lax.broadcasted_iota(jnp.int32, (rows, rows), 1)
    upper = (before < after).astype(F32).astype(BF16)
    ids = pos_ref[FIRST_ALL] + lax.broadcasted_iota(jnp.int32, (8, rows), 0)
    for source, ref in enumerate(routes):
        hits = jnp.logical_or(ref[0:1, :] == ids, ref[1:2, :] == ids)
        earlier = nn(hits.astype(F32).astype(BF16), upper)
        rank = jnp.where(hits, earlier, -1.0)
        row_ref[source] = rank.astype(jnp.int32)
        tall = jnp.concatenate([rank, jnp.full((120, rows), -1.0, F32)], 0)
        col_ref[source] = jnp.transpose(tall).astype(jnp.int32)


def ranks(pos, routes, after):
    count, rows = len(routes), routes[0].shape[1]
    out = [shape((count, 8, rows), jnp.int32), shape((count, rows, 128), jnp.int32)]
    return run(
        rank_kernel, routes, (1,), [like(a) for a in routes], [like(a) for a in out], out, "ranks",
        scalars=(pos,), after=after,
    )


def touch(array, after):
    count = len(after)

    def body(*refs):
        del refs

    return pl.pallas_call(
        body,
        in_specs=[pl.BlockSpec(memory_space=pl.ANY)] * (1 + count),
        out_specs=pl.BlockSpec(memory_space=pl.ANY),
        out_shape=shape(array.shape, array.dtype),
        input_output_aliases={0: 0},
        name="touch",
    )(array, *after)


def gate_rows(hidden, routes, router_t, ids):
    logits = nt(router_t, hidden)
    every = lax.broadcasted_iota(jnp.int32, logits.shape, 0)
    first, second = routes[0:1, :], routes[1:2, :]
    zero = jnp.zeros_like(logits)
    logit_one = jnp.sum(jnp.where(every == first, logits, zero), 0, keepdims=True)
    logit_two = jnp.sum(jnp.where(every == second, logits, zero), 0, keepdims=True)
    gate_one = sigmoid(logit_one - logit_two)
    gate_two = sigmoid(logit_two - logit_one)
    return jnp.where(ids == first, gate_one, 0.0) + jnp.where(ids == second, gate_two, 0.0)


def ffn_phase_one(x, g, up_ref, down_ref, act_ref, pre_ref, step=768):
    wide = act_ref.shape[1]
    for at in range(0, wide, step):
        cols = slice(at, at + step)
        act, slope = gelu_and_slope(nn(x, up_ref[0, :, cols]))
        back = nt(g, down_ref[0, cols, :])
        act_ref[:, cols] = act.astype(BF16)
        pre_ref[:, cols] = (back * slope).astype(BF16)


def relative_rows(pos_ref, target, values, nz):
    bits = nz.bit_length() - 1
    part = values.shape[0] // (2 * nz)
    for block in range(2 * nz):
        place = (block % 2) ^ pos_ref[ROW_Y]
        place = place * nz + flipped((block // 2) ^ pos_ref[ROW_Z], bits)
        at = pl.multiple_of(place * part, part)
        target[pl.ds(at, part), :] = values[block * part : (block + 1) * part]


def sides(pos_ref, values):
    half = values.shape[1] // 2
    low, high = values[:, :half], values[:, half:]
    own_low = pos_ref[ROW_Y] == 0
    return jnp.where(own_low, low, high), jnp.where(own_low, high, low)


def expert_kernel(
    slot, sends, has_prior, pos_ref, h0_ref, h1_ref, g0_ref, g1_ref, rank_ref, routes0_ref, routes1_ref,
    router_ref, up_ref, down_ref, *rest,
):
    count = 1 + sends
    priors, rest = (rest[:count], rest[count:]) if has_prior else ((), rest)
    targets, rest = rest[:count], rest[count:]
    keep_ref = targets[0]
    (out_ref, gx_ref, gg_ref,
     x_s, xt_s, g_s, gt_s, b_s, gate_s, act_s, pre_s, out_acc, gx_acc) = rest
    tile = pl.program_id(0)
    last = pl.num_programs(0) - 1
    rows = h0_ref.shape[0]
    nz = keep_ref.shape[2] // keep_ref.shape[3] * 2
    part = h0_ref.shape[1] // (2 * nz)
    own = lax.broadcasted_iota(jnp.int32, (CAP, rows), 0)

    def hot(source):
        return (own == rank_ref[source, slot : slot + 1, :]).astype(F32)

    @pl.when(tile == 0)
    def _():
        sources = ((h0_ref, g0_ref, routes0_ref), (h1_ref, g1_ref, routes1_ref))
        for source, (h_ref, b_ref, routes_ref) in enumerate(sources):
            span = slice(source * CAP, (source + 1) * CAP)
            pick = hot(source)
            pick_low = pick.astype(BF16)
            expert = pos_ref[FIRST_ALL] + slot
            gate = gate_rows(h_ref[...], routes_ref[...], router_ref[...], expert)
            gate_col = jnp.sum(pick * gate[0:1], -1, keepdims=True)
            branch = nn(pick_low, b_ref[:rows, :])
            x_s[span, :] = nn(pick_low, h_ref[...]).astype(BF16)
            b_s[span, :] = branch.astype(BF16)
            g_s[span, :] = (branch * gate_col).astype(BF16)
            gate_s[span, :] = jnp.broadcast_to(gate_col, (CAP, 128))
        relative_rows(pos_ref, xt_s, jnp.transpose(x_s[...]), nz)
        gt_s[...] = jnp.transpose(g_s[...])
        out_acc[...] = jnp.zeros_like(out_acc)
        gx_acc[...] = jnp.zeros_like(gx_acc)

    ffn_phase_one(x_s[...], g_s[...], up_ref, down_ref, act_s, pre_s)
    act, pre = act_s[...], pre_s[...]
    out_acc[...] += nn(act, down_ref[0])
    gx_acc[...] += nt(pre, up_ref[0])

    def place(side, kind):
        return (0, kind) if side == 0 else (1, kind) if sends == 1 else (1 + kind, 0)

    dup = nn(xt_s[...], pre)
    half = dup.shape[1] // 2
    for side in range(2):
        at, entry = place(side, 0)
        for z in range(nz):
            for lanes in range(2):
                row, into = (side * nz + z) * part, (z * 2 + lanes) * part
                piece = dup[row : row + part, lanes * half : (lanes + 1) * half]
                if has_prior:
                    piece = piece + priors[at][0, entry, into : into + part, :].astype(F32)
                targets[at][0, entry, into : into + part, :] = piece.astype(BF16)
    for side, piece in enumerate(sides(pos_ref, nn(gt_s[...], act))):
        at, entry = place(side, 1)
        if has_prior:
            piece = piece + priors[at][0, entry].astype(F32)
        targets[at][0, entry] = piece.astype(BF16)

    @pl.when(tile == last)
    def _():
        for source in range(2):
            span = slice(source * CAP, (source + 1) * CAP)
            out = out_acc[span, :]
            out_ref[source] = (out * gate_s[span, 0:1]).astype(BF16)
            gx_ref[source] = gx_acc[span, :].astype(BF16)
            inner = jnp.sum(out * b_s[span, :].astype(F32), -1, keepdims=True)
            gg_ref[source] = jnp.sum(hot(source) * inner, 0, keepdims=True)


def expert_call(
    slot, sends, pos, hiddens, branches, rank_rows, routes, router_t, up, down, prior, nz, after
):
    rows, width = hiddens[0].shape
    wide = up.shape[2]
    tile = wide // nz
    bits = nz.bit_length() - 1
    count = 2 * CAP
    weights = [
        pl.BlockSpec((1, width, tile), lambda f, s: (s[FIRST_HERE] + slot, 0, f)),
        pl.BlockSpec((1, tile, width), lambda f, s: (s[FIRST_HERE] + slot, f, 0)),
    ]
    kinds = [2, 2] if sends == 1 else [2, 1, 1]
    grads = [
        pl.BlockSpec((1, kind, width, tile // 2), lambda f, s: (flipped(f ^ s[ROW_Z], bits), 0, 0, 0))
        for kind in kinds
    ]
    once = [*hiddens, *branches, rank_rows, *routes, router_t]
    out_shape = (
        [shape((nz, kind, width, tile // 2), BF16) for kind in kinds]
        + [shape((2, CAP, width), BF16)] * 2
        + [shape((2, 1, rows), F32)]
    )
    prior = () if prior is None else tuple(prior)
    return run(
        functools.partial(expert_kernel, slot, sends, bool(prior)), (*once, up, down, *prior), (nz,),
        [like(a) for a in once] + weights + (grads if prior else []),
        grads + [like(a) for a in out_shape[len(grads) :]], out_shape, "expert", scalars=(pos,), after=after,
        scratch=[
            pltpu.VMEM((count, width), BF16),
            pltpu.VMEM((width, count), BF16),
            pltpu.VMEM((count, width), BF16),
            pltpu.VMEM((width, count), BF16),
            pltpu.VMEM((count, width), BF16),
            pltpu.VMEM((count, 128), F32),
            pltpu.VMEM((count, tile), BF16),
            pltpu.VMEM((count, tile), BF16),
            pltpu.VMEM((count, width), F32),
            pltpu.VMEM((count, width), F32),
        ],
    )


def shared_kernel(
    pos_ref, h_ref, b_ref, up_ref, down_ref, ku_ref, su0_ref, su1_ref, kd_ref, sd0_ref, sd1_ref,
    out_ref, gx_ref, xt_s, gt_s, act_s, pre_s,
):
    step = pl.program_id(0)
    nz, block = 4, kd_ref.shape[3]

    @pl.when(step == 0)
    def _():
        relative_rows(pos_ref, xt_s, jnp.transpose(h_ref[...]), nz)
        turned = jnp.transpose(b_ref[...])
        for slice_at in range(4):
            place = ((slice_at % 2) ^ pos_ref[CORE]) * 2 + ((slice_at // 2) ^ pos_ref[STREAM])
            at = pl.multiple_of(place * block, block)
            gt_s[pl.ds(at, block), :] = turned[slice_at * block : (slice_at + 1) * block]
        out_ref[...] = jnp.zeros_like(out_ref)
        gx_ref[...] = jnp.zeros_like(gx_ref)

    ffn_phase_one(h_ref[...], b_ref[...], up_ref, down_ref, act_s, pre_s)
    act, pre = act_s[...], pre_s[...]
    out_ref[...] += nn(act, down_ref[0])
    gx_ref[...] += nt(pre, up_ref[0])
    dup = nn(xt_s[...], pre).astype(BF16)

    @pl.when(step < 2)
    def _():
        ku_ref[0] = dup

    @pl.when(step == 2)
    def _():
        su0_ref[...] = dup

    @pl.when(step == 3)
    def _():
        su1_ref[...] = dup

    for y, piece in enumerate(sides(pos_ref, nn(gt_s[...], act))):
        pieces = [piece[place * block : (place + 1) * block].astype(BF16) for place in range(4)]
        kd_ref[0, y, 0], kd_ref[1, y, 0] = pieces[0], pieces[1]
        sd0_ref[y, 0], sd1_ref[y, 0] = pieces[2], pieces[3]


def shared_call(pos, hidden, branch, up, down, after):
    rows, width = hidden.shape
    wide = up.shape[1]
    nz = 4
    tile = wide // nz
    block = width // 4

    def unit(f, s):
        return (f % 2 ^ s[STREAM]) * 2 + (f // 2 ^ s[CORE])

    keep = pl.BlockSpec((1, width, tile), lambda f, s: (jnp.minimum(f, 1), 0, 0))
    downs = pl.BlockSpec(
        (2, 2, 1, block, tile // 2), lambda f, s: (0, 0, flipped(unit(f, s) ^ s[ROW_Z], 2), 0, 0)
    )
    sent = pl.BlockSpec((2, 1, block, tile // 2), lambda f, s: (0, flipped(unit(f, s) ^ s[ROW_Z], 2), 0, 0))
    outs = run(
        shared_kernel, (hidden, branch, up[None], down[None]), (nz,),
        [
            like(hidden),
            like(branch),
            pl.BlockSpec((1, width, tile), lambda f, s: (0, 0, unit(f, s))),
            pl.BlockSpec((1, tile, width), lambda f, s: (0, unit(f, s), 0)),
        ],
        [keep] + [full((width, tile))] * 2 + [downs, sent, sent, like(hidden), like(hidden)],
        [shape((2, width, tile), BF16)] + [shape((width, tile), BF16)] * 2
        + [shape((2, 2, nz, block, tile // 2), BF16)] + [shape((2, nz, block, tile // 2), BF16)] * 2
        + [shape((rows, width), F32)] * 2,
        "shared", scalars=(pos,), after=after,
        scratch=[
            pltpu.VMEM((width, rows), BF16),
            pltpu.VMEM((width, rows), BF16),
            pltpu.VMEM((rows, tile), BF16),
            pltpu.VMEM((rows, tile), BF16),
        ],
    )
    return outs[0], outs[1:3], outs[3], outs[4:6], *outs[6:]


def combine_kernel(places, col_ref, *refs):
    slots = len(places)
    rows_refs, refs = refs[: 2 * slots], refs[2 * slots :]
    targets, stacks = refs[:5], refs[5:]

    @pl.when(pl.program_id(0) == 0)
    def _():
        for slot in range(slots):
            for kind in range(2):
                for source in range(2):
                    stacks[kind][source, slot * CAP : (slot + 1) * CAP, :] = rows_refs[2 * slot + kind][places[slot] + source]

    block = col_ref.shape[1]
    own = lax.broadcasted_iota(jnp.int32, (block, slots * CAP), 1)
    for source in range(2):
        hits = None
        for slot in range(slots):
            rank = col_ref[source, :, slot : slot + 1]
            place = jnp.where(rank < 0, -1, rank + slot * CAP)
            hit = place == own
            hits = hit if hits is None else jnp.logical_or(hits, hit)
        pick = hits.astype(F32).astype(BF16)
        for kind in range(2):
            total = nn(pick, stacks[kind][source]).astype(BF16)
            if 2 * kind + source < 3:
                targets[2 * kind + source][...] = total
            else:
                early = pl.program_id(0) < pl.num_programs(0) // 2

                @pl.when(early)
                def _():
                    targets[3][...] = total

                @pl.when(jnp.logical_not(early))
                def _():
                    targets[4][...] = total


def combine(rank_cols, pairs, places, after):
    count, rows, _ = rank_cols.shape
    width = pairs[0][0].shape[2]
    block = rows // 2
    flat = [a for pair in pairs for a in pair]
    halves = [pl.BlockSpec((block, width), lambda i: (0, 0))] * 2
    *outs, low, high = run(
        functools.partial(combine_kernel, places), (rank_cols, *flat), (rows // block,),
        [pl.BlockSpec((count, block, 128), lambda i: (0, i, 0))] + [like(a) for a in flat],
        [rows_spec(block, width)] * 3 + halves,
        [shape((rows, width), BF16)] * 3 + [shape((rows // 2, width), BF16)] * 2, "combine",
        scratch=[pltpu.VMEM((2, len(pairs) * CAP, width), BF16)] * 2, after=after,
    )
    return (*outs, (low, high))


def add_kernel(left_ref, low_ref, high_ref, second_ref, third_ref, one_ref, two_ref):
    two_ref[...] = (second_ref[...].astype(F32) + third_ref[...].astype(F32)).astype(BF16)
    low = pl.program_id(0) < pl.num_programs(0) // 2
    right = jnp.where(low, low_ref[...], high_ref[...])
    one_ref[...] = (left_ref[...].astype(F32) + right.astype(F32)).astype(BF16)


def add_rows(left, halves, second, third, after):
    rows, width = left.shape
    tile = rows_spec(rows // 4, width)
    low = pl.BlockSpec((rows // 4, width), lambda i: (jnp.minimum(i, 1), 0))
    high = pl.BlockSpec((rows // 4, width), lambda i: (jnp.maximum(i - 2, 0), 0))
    return run(
        add_kernel, (left, *halves, second, third), (4,), [tile, low, high, tile, tile], [tile] * 2,
        [shape((rows, width), BF16)] * 2, "add_rows", after=after,
    )


def total_of(keep, arrived):
    return keep.astype(F32) + arrived.astype(F32)


def halve_kinds_kernel(kinds, *refs):
    keep_ref, send_ref = refs[-2:]
    refs = iter(refs[:-2])
    for at, kind in enumerate(kinds):
        if kind == 0:
            total = total_of(next(refs)[0, 0], next(refs)[0, 0])
            half = total.shape[0] // 2
            keep_ref[at, 0], send_ref[at, 0] = total[:half], total[half:].astype(BF16)
        else:
            keep_ref[at, 0] = total_of(next(refs)[0, 0], next(refs)[0, 0])
            send_ref[at, 0] = total_of(next(refs)[0, 0], next(refs)[0, 0]).astype(BF16)


def halve_y(keep, arrived, kinds, after):
    nz, _, rows, cols = keep.shape
    split = lambda a: a.reshape(nz, -1, rows // 2, cols)
    args, specs = [], []
    for at, kind in enumerate(kinds):
        for add in (0, nz // 2) if kind else (0,):
            for array, entry in ((keep, kind), (arrived, at)):
                if kind == 0:
                    args.append(array)
                    index = functools.partial(lambda entry, t: (t, entry, 0, 0), entry)
                    specs.append(pl.BlockSpec((1, 1, rows, cols), index))
                else:
                    args.append(split(array))
                    index = functools.partial(
                        lambda entry, add, t: (t // 2 + add, 2 * entry + t % 2, 0, 0), entry, add
                    )
                    specs.append(pl.BlockSpec((1, 1, rows // 2, cols), index))
    out = pl.BlockSpec((len(kinds), 1, rows // 2, cols), lambda t: (0, t, 0, 0))
    dims = (len(kinds), nz, rows // 2, cols)
    return run(
        functools.partial(halve_kinds_kernel, kinds), args, (nz,), specs, [out, out],
        [shape(dims, F32), shape(dims, BF16)], "halve_y", after=after,
    )


def halve_z(keep, arrived, kinds, after):
    _, nz, rows, cols = keep.shape
    split = lambda a: a.reshape(len(kinds), 2 * nz, rows // 2, cols)
    args, specs = [], []
    for at, kind in enumerate(kinds):
        for add in (0, nz) if kind else (0,):
            for array, flip in ((keep, 0), (arrived, nz // 2)):
                if kind == 0:
                    args.append(array)
                    index = functools.partial(lambda at, flip, t: (at, t ^ flip, 0, 0), at, flip)
                    specs.append(pl.BlockSpec((1, 1, rows, cols), index))
                else:
                    args.append(split(array))
                    index = functools.partial(lambda at, add, t: (at, t + add, 0, 0), at, add)
                    specs.append(pl.BlockSpec((1, 1, rows // 2, cols), index))
    out = pl.BlockSpec((len(kinds), 1, rows // 2, cols), lambda t: (0, t, 0, 0))
    dims = (len(kinds), nz, rows // 2, cols)
    return run(
        functools.partial(halve_kinds_kernel, kinds), args, (nz,), specs, [out, out],
        [shape(dims, F32), shape(dims, BF16)], "halve_z", after=after,
    )


def core_halves(pos_ref, values):
    half = values.shape[0] // 2
    low, high = values[:half], values[half:]
    own_low = pos_ref[CORE] == 0
    return jnp.where(own_low, low, high), jnp.where(own_low, high, low).astype(BF16)


def finish_kinds_kernel(kinds, pos_ref, *refs):
    inputs, outs = refs[: 2 * len(kinds)], refs[2 * len(kinds) :]
    for at, kind in enumerate(kinds):
        keep_ref, arrived_ref = inputs[2 * at : 2 * at + 2]
        mine, sent = outs[2 * at : 2 * at + 2]
        if kind == 0:
            up = total_of(keep_ref[0, 0], arrived_ref[0, 0])
            half = up.shape[0] // 2
            mine[...], sent[...] = core_halves(pos_ref, jnp.concatenate([up[:half], up[half:]], 1))
        else:

            @pl.when(pl.program_id(0) == 0)
            def _():
                down = total_of(keep_ref[0], arrived_ref[0])
                down = down.reshape(down.shape[0] * down.shape[1], down.shape[2])
                mine[...], sent[...] = core_halves(pos_ref, jnp.transpose(down))


def finish_kinds(pos, keep, arrived, kinds, after):
    _, nz, rows, cols = keep.shape
    bits = nz.bit_length() - 1
    args, specs, out_specs, outs = [], [], [], []
    for at, kind in enumerate(kinds):
        args += [keep, arrived]
        if kind == 0:
            for flip in (0, 1):
                index = functools.partial(lambda at, flip, t, s: (at, t ^ flip, 0, 0), at, flip)
                specs.append(pl.BlockSpec((1, 1, rows, cols), index))
            dims = (rows // 4, 2 * cols * nz)
            out = pl.BlockSpec((rows // 4, 2 * cols), lambda t, s: (0, flipped(t, bits) ^ s[ROW_Z]))
        else:
            index = functools.partial(lambda at, t, s: (at, 0, 0, 0), at)
            specs += [pl.BlockSpec((1, nz, rows, cols), index)] * 2
            dims = (cols // 2, nz * rows)
            out = full(dims)
        out_specs += [out, out]
        outs += [shape(dims, F32), shape(dims, BF16)]
    return run(
        functools.partial(finish_kinds_kernel, kinds), args, (nz,), specs, out_specs, outs, "finish_kinds",
        scalars=(pos,), after=after,
    )


def halve_slices_kernel(ku_ref, kd_ref, au0_ref, au1_ref, ad0_ref, ad1_ref, keep_ref, send_ref):
    ups, downs = (au0_ref, au1_ref), (ad0_ref, ad1_ref)
    for at, ref in enumerate((keep_ref, send_ref)):
        up = total_of(ku_ref[at], ups[at][...])
        rows, half = up.shape[0], up.shape[1] // 2
        for side in range(2):
            piece = up[:, side * half : (side + 1) * half]
            ref[0, side * rows : (side + 1) * rows, :] = piece.astype(ref.dtype)
        ref[1] = total_of(kd_ref[at], downs[at][...]).astype(ref.dtype)


def halve_slices(up_keep, down_keep, arrived, after):
    _, rows, cols = up_keep.shape
    steps = 8
    down_keep = down_keep.reshape(2, 2 * rows, cols // 2)
    arrived = [a.reshape(-1, a.shape[-1]) for a in arrived]
    ups = pl.BlockSpec((2, rows // steps, cols), lambda i: (0, i, 0))
    downs = pl.BlockSpec((2, 2 * rows // steps, cols // 2), lambda i: (0, i, 0))
    dims = (2, 2 * rows, cols // 2)
    return run(
        halve_slices_kernel, (up_keep, down_keep, *arrived), (steps,),
        [ups, downs] + [rows_spec(a.shape[0] // steps, a.shape[1]) for a in arrived],
        [downs, downs], [shape(dims, F32), shape(dims, BF16)], "halve_slices", after=after,
    )


def halve_kernel(keep_ref, arrived_ref, keep_out, send_out):
    keep_out[...] = total_of(keep_ref[:, 0], arrived_ref[:, 0])
    send_out[...] = total_of(keep_ref[:, 1], arrived_ref[:, 1]).astype(BF16)


def halve(keep, arrived, after, steps=2):
    kinds, rows, cols = keep.shape
    split = lambda a: a.reshape(kinds, 2, rows // 2, cols)
    into = pl.BlockSpec((kinds, 2, rows // 2 // steps, cols), lambda i: (0, 0, i, 0))
    out = pl.BlockSpec((kinds, rows // 2 // steps, cols), lambda i: (0, i, 0))
    dims = (kinds, rows // 2, cols)
    return run(
        halve_kernel, (split(keep), split(arrived)), (steps,), [into, into], [out, out],
        [shape(dims, F32), shape(dims, BF16)], "halve", after=after,
    )


def halve_parts_kernel(keep_ref, first_ref, second_ref, keep_out, send_out):
    keep_out[0] = total_of(keep_ref[0], first_ref[...])
    send_out[0] = total_of(keep_ref[1], second_ref[...]).astype(BF16)


def halve_parts(keep, arrived, after, steps=2):
    _, rows, cols = keep.shape
    into = pl.BlockSpec((2, rows // steps, cols), lambda i: (0, i, 0))
    out = pl.BlockSpec((1, rows // steps, cols), lambda i: (0, i, 0))
    return run(
        halve_parts_kernel, (keep, *arrived), (steps,), [into] + [rows_spec(rows // steps, cols)] * 2,
        [out, out], [shape((1, rows, cols), F32), shape((1, rows, cols), BF16)], "halve_parts", after=after,
    )


def finish_slices_kernel(pos_ref, sk_ref, sa_ref, qk_ref, qa_ref, mine_ref, sent_ref, mine_down_ref, sent_down_ref):
    total = total_of(sk_ref[...], sa_ref[...])
    half = total.shape[1] // 2
    up = jnp.concatenate([total[0, :half], total[0, half:]], 1)
    for at, values in enumerate((total_of(qk_ref[0], qa_ref[0]), up)):
        mine, sent_ref[at] = core_halves(pos_ref, values)
        mine_ref[at] = mine.astype(BF16)
    mine, sent_down_ref[...] = core_halves(pos_ref, jnp.transpose(total[1]))
    mine_down_ref[...] = mine.astype(BF16)


def finish_slices(pos, shared, shared_arrived, queries, queries_arrived, after):
    _, rows, cols = shared.shape
    args = (shared, shared_arrived, queries, queries_arrived)
    outs = [shape((2, rows // 4, 2 * cols), BF16)] * 2 + [shape((cols // 2, rows), BF16)] * 2
    return run(
        finish_slices_kernel, args, (1,), [like(a) for a in args], [like(a) for a in outs], outs,
        "finish_slices", scalars=(pos,), after=after,
    )


def middle_back_kernel(
    gs_ref, ga_ref, low_ref, high_ref, gc_ref, gg_ref, routes_ref, router_ref,
    hidden_ref, cot_ref, branch_ref, x_ref, mod_ref, w_ref,
    gm_ref, gatt_ref, back_ref, mods_ref, drouter_ref,
):
    block = pl.program_id(0)
    hidden = hidden_ref[...]
    grad_gates = gg_ref[...]
    ids = lax.broadcasted_iota(jnp.int32, grad_gates.shape, 0)
    gates = gate_rows(hidden, routes_ref[...], router_ref[...], ids)
    inner = jnp.sum(gates * grad_gates, 0, keepdims=True)
    grad_logits = gates * (grad_gates - inner)
    core = jnp.where(block < pl.num_programs(0) // 2, low_ref[...], high_ref[...])
    grad = gs_ref[...] + ga_ref[...].astype(F32) + core.astype(F32) + gc_ref[...].astype(F32)
    pieces = stacked(grad_logits)
    router = router_ref[...]
    grad = grad + tn(pieces, jnp.concatenate([router] * 3, 0))
    drouter = unstacked(nn(pieces, hidden))
    branch = branch_ref[...]
    gate_one = mod_ref[2, pl.ds(block, 1), :]
    middle = x_ref[...].astype(F32) + gate_one * branch
    normed, spread = norm_parts(middle)
    scale = mod_ref[4, pl.ds(block, 1), :]
    mods_ref[1, pl.ds(block, 1), :] = jnp.sum(grad, 0, keepdims=True)
    mods_ref[2, pl.ds(block, 1), :] = jnp.sum(grad * normed, 0, keepdims=True)
    grad_middle = cot_ref[...].astype(F32) + norm_back(grad * (1.0 + scale), normed, spread)
    mods_ref[0, pl.ds(block, 1), :] = jnp.sum(grad_middle * branch, 0, keepdims=True)
    gm_ref[...] = grad_middle
    grad_branch = (grad_middle * gate_one).astype(BF16)
    back_ref[...] = grad_branch
    gatt_ref[...] = nt(grad_branch, w_ref[...]).astype(BF16)

    @pl.when(block == 0)
    def _():
        drouter_ref[...] = drouter

    @pl.when(block > 0)
    def _():
        drouter_ref[...] += drouter


def middle_backward(parts, gg, routes_t, router_t, hidden, cot, branch, patches, mod, out_weight, blocks, after):
    rows, width = patches.shape
    short = rows // blocks
    tile = rows_spec(short, width)
    cols = lambda a: pl.BlockSpec((a.shape[0], short), lambda i: (0, i))
    half = blocks // 2
    low = pl.BlockSpec((short, width), lambda i: (jnp.minimum(i, half - 1), 0))
    high = pl.BlockSpec((short, width), lambda i: (jnp.maximum(i - half, 0), 0))
    out_shape = [
        shape((rows, width), F32),
        shape((rows, width), BF16),
        shape((rows, width), BF16),
        shape((3, 8, width), F32),
        shape((router_t.shape[0], width), F32),
    ]
    return run(
        middle_back_kernel,
        (*parts, gg, routes_t, router_t, hidden, cot, branch, patches, mod, out_weight), (blocks,),
        [tile, tile, low, high, tile] + [cols(gg), cols(routes_t), like(router_t)] + [tile] * 4 + [like(mod), like(out_weight)],
        [tile] * 3 + [like(a) for a in out_shape[3:]], out_shape, "middle_back", after=after,
    )


def mixed_kernel(so_ref, ra_ref, rb_ref, rc_ref, cot_ref, branch_ref, x_ref, mod_ref, mixed_ref, gate_ref):
    block = pl.program_id(0)
    second = so_ref[...] + ra_ref[...].astype(F32) + rb_ref[...].astype(F32) + rc_ref[...].astype(F32)
    middle = x_ref[...].astype(F32) + mod_ref[2, pl.ds(block, 1), :] * branch_ref[...]
    mixed_ref[...] = (middle + mod_ref[5, pl.ds(block, 1), :] * second).astype(BF16)
    gate_ref[pl.ds(block, 1), :] = jnp.sum(cot_ref[...].astype(F32) * second, 0, keepdims=True)


def mixed_forward(parts, cot, branch, patches, mod, blocks, after):
    rows, width = patches.shape
    tile = rows_spec(rows // blocks, width)
    return run(
        mixed_kernel, (*parts, cot, branch, patches, mod), (blocks,), [tile] * 7 + [like(mod)],
        [tile, full((8, width))], [shape((rows, width), BF16), shape((8, width), F32)], "mixed", after=after,
    )


def weight_kernel(
    pos_ref, x_ref, mod_ref, dq_ref, dk_ref, dv_ref, att_ref, back_ref, keep_ref, first_ref, second_ref, turned
):
    rows = x_ref.shape[0]
    short = rows // 4
    step = pl.program_id(0)
    matrix = ((step % 2) ^ pos_ref[STREAM]) * 2 + ((step // 2) ^ pos_ref[CORE])
    nz = 4

    @pl.when(step == 0)
    def _():
        for block in range(4):
            span = slice(block * short, (block + 1) * short)
            normed, _ = norm_parts(x_ref[span, :].astype(F32))
            hidden = normed * (1.0 + mod_ref[1, block : block + 1, :]) + mod_ref[0, block : block + 1, :]
            relative_rows(pos_ref, turned.at[0, :, span], jnp.transpose(hidden.astype(BF16)), nz)
        relative_rows(pos_ref, turned.at[1], jnp.transpose(att_ref[...]), nz)

    for index, (left, ref) in enumerate(((0, dq_ref), (0, dk_ref), (0, dv_ref), (1, back_ref))):

        @pl.when(matrix == index)
        def _():
            total = nn(turned[left], ref[...]).astype(BF16)

            @pl.when(step < 2)
            def _():
                keep_ref[0] = total

            @pl.when(step == 2)
            def _():
                first_ref[...] = total

            @pl.when(step == 3)
            def _():
                second_ref[...] = total


def weight_grads(pos, patches, mod, grads, attended, back, after):
    rows, width = patches.shape
    args = (patches, mod, *grads, attended, back)
    keep = pl.BlockSpec((1, width, width), lambda f, s: (jnp.minimum(f, 1), 0, 0))
    send = full((width, width))
    outs = run(
        weight_kernel, args, (4,), [like(a) for a in args], [keep, send, send],
        [shape((2, width, width), BF16)] + [shape((width, width), BF16)] * 2, "weight_grads", scalars=(pos,),
        scratch=[pltpu.VMEM((2, width, rows), BF16)], after=after,
    )
    return outs[0], outs[1:]


def inputs_back_kernel(dq_ref, dk_ref, dv_ref, w_ref, x_ref, gm_ref, mod_ref, gp_ref, mods_ref):
    width = x_ref.shape[1]
    short = x_ref.shape[0] // 2
    both = nt(dq_ref[...], w_ref[:, :width])
    both = both + nt(dk_ref[...], w_ref[:, width : 2 * width])
    both = both + nt(dv_ref[...], w_ref[:, 2 * width :])
    for at in range(2):
        block, span = pl.program_id(0) * 2 + at, slice(at * short, (at + 1) * short)
        grad = both[span]
        normed, spread = norm_parts(x_ref[span, :].astype(F32))
        mods_ref[0, pl.ds(block, 1), :] = jnp.sum(grad, 0, keepdims=True)
        mods_ref[1, pl.ds(block, 1), :] = jnp.sum(grad * normed, 0, keepdims=True)
        scale = mod_ref[1, pl.ds(block, 1), :]
        gp_ref[span, :] = gm_ref[span, :] + norm_back(grad * (1.0 + scale), normed, spread)


def inputs_backward(grads, weight, patches, grad_middle, mod, blocks, after):
    rows, width = patches.shape
    tile = rows_spec(2 * rows // blocks, width)
    return run(
        inputs_back_kernel, (*grads, weight, patches, grad_middle, mod), (blocks // 2,),
        [tile] * 3 + [like(weight), tile, tile, like(mod)], [tile, full((2, 8, width))],
        [shape((rows, width), F32), shape((2, 8, width), F32)], "inputs_back", after=after,
    )


def used_kernel(block_count, pos_ref, gm_ref, ada_ref, emb_ref, out_ref):
    piece = pl.program_id(0)

    @pl.when(piece == 0)
    def _():
        out_ref[...] = jnp.zeros_like(out_ref)

    out_ref[...] += unstacked(nt(stacked(gm_ref[0]), ada_ref[...]))

    @pl.when(piece == pl.num_programs(0) - 1)
    def _():
        emb = emb_ref[...]
        is_long = pos_ref[LONG] > 0
        used = jnp.where(is_long, jnp.broadcast_to(emb[0:1], emb.shape), emb)
        gate = sigmoid(used)
        grad = out_ref[...] * (gate * (1.0 + used * (1.0 - gate)))
        row = lax.broadcasted_iota(jnp.int32, grad.shape, 0)
        grad = jnp.where(row < block_count, grad, 0.0)
        total = jnp.sum(grad, 0, keepdims=True)
        out_ref[...] = jnp.where(is_long, jnp.where(row == 0, total, 0.0), grad)


def used_backward(pos, grad_mod, ada_weight, emb_pad, block_count, after):
    rows, width = emb_pad.shape
    pieces = grad_mod.shape[0]
    return run(
        functools.partial(used_kernel, block_count), (grad_mod, ada_weight, emb_pad), (pieces,),
        [
            pl.BlockSpec((1, rows, width), lambda i, *_: (i, 0, 0)),
            pl.BlockSpec((width, width), lambda i, *_: (0, i)),
            like(emb_pad),
        ],
        like(emb_pad), shape((rows, width), F32), "used_back", scalars=(pos,), after=after,
    )


def swap(values, axis, bit):
    size = lax.axis_size(axis)
    return lax.ppermute(values, axis, [(i, i ^ bit) for i in range(size)])


def swap_all(arrays, axis, bit):
    return [swap(a, axis, bit) for a in arrays]


def swap_across(values):
    stream = lax.axis_size("stream")
    pairs = [
        (i, ((i // stream) ^ 1) * stream + ((i % stream) ^ 1))
        for i in range(lax.axis_size("dp") * stream)
    ]
    return lax.ppermute(values, ("dp", "stream"), pairs)


def in_order(own, mine, arrived, axis):
    return jnp.concatenate(
        [jnp.where(own == 0, mine, arrived), jnp.where(own == 0, arrived, mine)], axis
    )


def local_pair(
    patches, embedding, long_image, routes, cotangent, ada_weight, qkv_weight, out_weight, shared_up,
    shared_down, router_weight, expert_up, expert_down,
):
    rows, width = patches.shape
    blocks = embedding.shape[0]
    short = rows // blocks
    dp_size = lax.axis_size("dp")
    nz = dp_size // 4
    dp, stream = lax.axis_index("dp"), lax.axis_index("stream")
    core, row_y, row_z = dp % 2, (dp // 2) % 2, dp // 4
    local_experts = expert_up.shape[0]
    here = local_experts // 2
    first_here = core * here
    first_all = stream * local_experts + first_here
    places = [long_image[0], core, stream, row_y, row_z, first_here, first_all, 0]
    pos = jnp.stack([jnp.asarray(a, jnp.int32) for a in places])

    routes_t = routes.T
    routes_x = swap(routes_t, "stream", 1)
    routes_near = (routes_t, swap(routes_t, "dp", 1))
    emb_pad = jnp.pad(embedding, ((0, 8 - blocks), (0, 0)))
    router_t = jnp.pad(router_weight.T, ((0, 16 - router_weight.shape[1]), (0, 0)))
    mod, act, branch_grad, branch_sent = modulate(pos, emb_pad, ada_weight, cotangent, blocks)
    routes_x = touch(routes_x, (mod,))
    branch_grad = touch(branch_grad, (routes_x, routes_near[1]))
    routes_far = (routes_x, swap(routes_x, "dp", 1))
    branch_x = swap(touch(branch_sent, (branch_grad,)), "stream", 1)
    branches_near = (branch_grad, swap(branch_grad, "dp", 1))

    packed = qkv_forward(patches, mod, qkv_weight, blocks, (branch_grad,))
    attended, logsum = attend_forward(pos, packed, short)
    branch_one, hidden = middle_forward(
        attended, patches, mod, out_weight, blocks, ()
    )
    hidden_x = swap(hidden, "stream", 1)
    hiddens_near = (hidden, swap(hidden, "dp", 1))
    rank_near, cols_near = ranks(pos, routes_near, (hidden,))
    branch_x = touch(branch_x, (rank_near,))
    branches_far = (branch_x, swap(branch_x, "dp", 1))

    def expert(slot, is_far, sends, prior, after):
        group = (
            (hiddens_far, branches_far, rank_far, routes_far)
            if is_far
            else (hiddens_near, branches_near, rank_near, routes_near)
        )
        out = expert_call(slot, sends, pos, *group, router_t, expert_up, expert_down, prior, nz, after)
        return out[: 1 + sends], out[1 + sends :]

    first, first_near = expert(0, False, 1, None, (branch_x,))
    hidden_x = touch(hidden_x, (first_near[2],))
    hiddens_far = (hidden_x, swap(hidden_x, "dp", 1))
    rank_far, cols_far = ranks(pos, routes_far, (hidden_x,))
    first, first_far = expert(0, True, 1, first, ())
    first_arrived = swap(first[1], "dp", 2)

    second, second_near = expert(1, False, 2, None, (first_far[2],))
    second, second_far = expert(1, True, 2, second, ())
    up_half_arrived = swap(second[1], "dp", 2)
    out_x, out_xc, gx_x, gx_xc = combine(cols_far, [r[:2] for r in (first_far, second_far)], (0, 0), ())
    gx_xc, out_xc = swap_all(gx_xc, "dp", 1), swap(out_xc, "dp", 1)
    out_near, out_core, gx_near, gx_core = combine(
        cols_near, [r[:2] for r in (first_near, second_near)], (0, 0), (gx_x,)
    )
    gx_core = [touch(a, (gx_near,)) for a in swap_all(gx_core, "dp", 1)]
    out_core = touch(swap(out_core, "dp", 1), (gx_near,))
    near, far = (first_near, second_near), (first_far, second_far)
    gg_near = [jnp.concatenate([r[2][source] for r in near], 0) for source in range(2)]
    gg_far = [jnp.concatenate([r[2][source] for r in far], 0) for source in range(2)]
    gg_back = swap(jnp.concatenate([gg_far[0], swap(gg_far[1], "dp", 1)], 0), "stream", 1)
    gg_back = touch(gg_back, (gx_near,))
    gg_rel = jnp.concatenate([gg_near[0], swap(gg_near[1], "dp", 1), gg_back], 0)
    gx_sum, out_sum = add_rows(gx_x, gx_xc, out_x, out_xc, (gg_back, *gx_core, out_core))
    gx_back = swap(gx_sum, "stream", 1)
    out_back = swap(out_sum, "stream", 1)
    both, up, down = (0, 1), (0,), (1,)
    ea_keep, ea_send = halve_y(first[0], first_arrived, both, (out_sum,))
    ea_arrived = swap(ea_send, "dp", 4)
    order = jnp.arange(4, dtype=jnp.int32) ^ (stream * 2 + core)
    gg = gg_rel.reshape(4, here, rows)[order].reshape(EXPERTS, rows)
    gg = jnp.pad(gg, ((0, 16 - EXPERTS), (0, 0)))

    down_half = touch(second[2], (ea_send,))
    down_half_arrived = swap(down_half, "dp", 2)
    up_keep, up_send, down_keep, down_send, shared_out, shared_gx = shared_call(
        pos, hidden, branch_grad, shared_up, shared_down, (down_half, *gx_core, gg)
    )
    sh_arrived = swap_all([*up_send, *down_send], "dp", 1)

    grad_middle, grad_attended, back, mods_two, drouter = middle_backward(
        (shared_gx, gx_near, *gx_core, gx_back), gg, routes_t, router_t, hidden, cotangent, branch_one,
        patches, mod, out_weight, blocks, (),
    )
    ea_keep, ea_send = halve_z(ea_keep, ea_arrived, both, (grad_attended,))
    ea_arrived = swap(ea_send, "dp", 8)
    bu_keep, bu_send = halve_y(second[0], up_half_arrived, up, (ea_send,))
    bu_arrived = swap(bu_send, "dp", 4)
    sh_keep, sh_send = halve_slices(up_keep, down_keep, sh_arrived, (bu_send,))
    sh_arrived = swap(sh_send, "stream", 1)
    grads = attend_backward(pos, packed, attended, logsum, grad_attended, short, (sh_send,))
    out_back = touch(out_back, (grads[0],))
    bd_keep, bd_send = halve_y(second[0], down_half_arrived, down, (out_back,))
    bd_arrived = swap(bd_send, "dp", 4)
    bu_keep, bu_send = halve_z(bu_keep, bu_arrived, up, (bd_send,))
    bu_arrived = swap(bu_send, "dp", 8)
    ea_arrived = touch(ea_arrived, (bu_send,))
    qk_keep, qk_send = weight_grads(pos, patches, mod, grads, attended, back, (ea_arrived,))
    qk_arrived = swap_all(qk_send, "dp", 1)
    sh_keep, sh_send = halve(sh_keep, sh_arrived, (qk_send[0],))
    sh_arrived = swap(sh_send, "dp", 2)
    qk_keep, qk_send = halve_parts(qk_keep, qk_arrived, (sh_send,))
    qk_arrived = swap(qk_send, "stream", 1)
    mixed, gate_two = mixed_forward(
        (shared_out, out_near, out_core, out_back), cotangent, branch_one, patches, mod, blocks, (qk_send,)
    )
    grad_patches, mods_one = inputs_backward(grads, qkv_weight, patches, grad_middle, mod, blocks, (gate_two,))
    factors = [a[:blocks] for a in (act, *mods_one, *mods_two, gate_two)]
    factors = jnp.concatenate(factors + [drouter[:EXPERTS].reshape(blocks, -1)], 1).astype(BF16)

    def doubled(axis, bit, after):
        return jnp.concatenate([factors, touch(swap(factors, axis, bit), (after,))], 0)

    grad_mod = jnp.concatenate([mods_one, mods_two, gate_two[None]], 0)
    sh_keep, sh_send = halve(sh_keep, sh_arrived, (mods_one,))
    sh_arrived = swap(sh_send, "dp", 4)
    qk_keep, qk_send = halve(qk_keep, qk_arrived, (sh_send,))
    qk_arrived = swap(qk_send, "dp", 2)
    bd_keep, bd_send = halve_z(bd_keep, bd_arrived, down, (qk_send,))
    bd_arrived = swap(bd_send, "dp", 8)
    bu_arrived = touch(bu_arrived, (bd_send,))
    factors = doubled("dp", 8, bu_arrived)
    grad_embedding = used_backward(pos, grad_mod, ada_weight, emb_pad, blocks, (bu_arrived,))
    factors = doubled("dp", 4, grad_embedding)
    qk_keep, qk_send = halve(qk_keep, qk_arrived, (grad_embedding,))
    qk_arrived = swap(qk_send, "dp", 4)
    sh_keep, sh_send = halve(sh_keep, sh_arrived, (qk_send,))
    sh_arrived = swap(sh_send, "dp", 8)
    factors = doubled("dp", 2, sh_send)
    ea_done = finish_kinds(pos, ea_keep, ea_arrived, both, (sh_send,))
    qk_keep, qk_send = halve(qk_keep, qk_arrived, (ea_done[1],))
    qk_arrived = swap(qk_send, "dp", 8)
    bd_arrived = touch(bd_arrived, (qk_send,))
    bu_done = finish_kinds(pos, bu_keep, bu_arrived, up, (bd_arrived,))
    factors_x = touch(swap(factors, "stream", 1), (bu_done[1],))
    bd_done = finish_kinds(pos, bd_keep, bd_arrived, down, (factors_x,))
    bu_others = touch(swap(bu_done[1], "dp", 1), (bd_done[1],))
    ea_others = [touch(swap(a, "dp", 1), (bd_done[1],)) for a in (ea_done[1], ea_done[3])]
    bd_others = touch(swap(bd_done[1], "dp", 1), (bu_others,))
    done = finish_slices(
        pos, sh_keep, sh_arrived, qk_keep, qk_arrived, (bu_others, bd_others, *ea_others)
    )
    pieces = [factors, factors_x, swap(factors, "dp", 1), swap(factors_x, "dp", 1)]

    pieces[:2] = [touch(a, (done[0],)) for a in pieces[:2]]
    ea_others = [touch(a, (done[0],)) for a in ea_others]

    def slices_out(mine, send):
        near = in_order(core, mine, swap(send, "dp", 1), mine.ndim - 1)
        far = in_order(core, swap(mine, "stream", 1), swap_across(send), mine.ndim - 1)
        return in_order(stream, near, far, mine.ndim - 1).astype(F32)

    rows_out = slices_out(*done[:2])
    grad_qkv_out, grad_shared_up = rows_out[0], rows_out[1]
    grad_shared_down = slices_out(*done[2:])

    share = width // dp_size

    def own_share(values):
        return lax.dynamic_slice_in_dim(values, dp * share, share, 1)

    grad_ada, drouter_sum = 0.0, 0.0
    for piece in pieces:
        acts = own_share(piece[:, :width])
        grad_ada = grad_ada + lax.dot_general(
            acts, piece[:, width : 7 * width], (((0,), (0,)), ((), ())), preferred_element_type=F32
        )
        drouter_sum = drouter_sum + jnp.sum(piece[:, 7 * width :].astype(F32).reshape(-1, blocks, 2 * width), 0)
    grad_router = own_share(drouter_sum.reshape(EXPERTS, width)).T

    def experts_out(one, two, one_other, two_other):
        mine, others = jnp.stack([one, two]), jnp.stack([one_other, two_other]).astype(F32)
        return in_order(core, mine, others, 0)

    return (
        mixed, grad_patches, grad_embedding[:blocks], grad_ada, grad_qkv_out[:, : 3 * width],
        grad_qkv_out[:, 3 * width :], grad_shared_up, grad_shared_down, grad_router,
        experts_out(ea_done[0], bu_done[0], ea_others[0], bu_others),
        experts_out(ea_done[2], bd_done[0], ea_others[1], bd_others),
    )


def local(*arrays):
    experts, width, wide = arrays[11].shape
    pair = lax.axis_size("stream") == 2 and experts == 4 and lax.axis_size("dp") == 16
    if pair and wide == 4 * width:
        return local_pair(*arrays)
    return local_general(*arrays)


def solution(mesh):
    return jax.shard_map(
        local,
        mesh=mesh,
        in_specs=(
            P(("dp", "stream"), None),
            P(("dp", "stream"), None),
            P(("dp", "stream")),
            P(("dp", "stream"), None),
            P(("dp", "stream"), None),
            P(),
            P(),
            P(),
            P(),
            P(),
            P(),
            P("stream", None, None),
            P("stream", None, None),
        ),
        out_specs=(
            P(("dp", "stream"), None),
            P(("dp", "stream"), None),
            P(("dp", "stream"), None),
            P("dp", None),
            P("dp", None),
            P("dp", None),
            P("dp", None),
            P("dp", None),
            P("dp", None),
            P("stream", "dp", None),
            P("stream", "dp", None),
        ),
        check_vma=False,
    )
```

```python
import functools
import math

import jax
import jax.numpy as jnp
from jax import lax
from jax.experimental import pallas as pl
from jax.experimental.pallas import tpu as pltpu
from jax.sharding import PartitionSpec as P

HEADS = 12
HEAD_DIM = 64
EXPERTS = 8
CAP = 288


HIGH = lax.Precision.HIGHEST
EPSILON = 1e-06
F32 = jnp.float32
BF16 = jnp.bfloat16
MIB = 1 << 20


def gelu_tanh(values):
    return jax.nn.gelu(values, approximate=True)


def normalize(values):
    centered = values - jnp.mean(values, -1, keepdims=True)
    spread = lax.rsqrt(jnp.mean(centered * centered, -1, keepdims=True) + EPSILON)
    return (centered * spread, spread)


def normalize_back(grad_normed, normed, spread):
    return spread * (
        grad_normed
        - jnp.mean(grad_normed, -1, keepdims=True)
        - normed * jnp.mean(grad_normed * normed, -1, keepdims=True)
    )


def split_packed(packed, seg_len):
    row_count = packed.shape[0]
    model_width = packed.shape[1] // 3
    groups = row_count // seg_len
    block_rows = min(512, seg_len)
    part_count = seg_len // block_rows
    queries = (
        packed[:, :model_width]
        .reshape(groups, part_count, block_rows, HEADS, HEAD_DIM)
        .swapaxes(0, 1)
    )
    key_heads = packed[:, model_width : 2 * model_width].reshape(groups, seg_len, HEADS, HEAD_DIM)
    values = packed[:, 2 * model_width :].reshape(groups, seg_len, HEADS, HEAD_DIM)
    return (queries, key_heads, values, groups, block_rows, part_count)


def attend(packed, seg_len):
    row_count = packed.shape[0]
    model_width = packed.shape[1] // 3
    factor = 1.0 / math.sqrt(HEAD_DIM)
    queries, key_heads, values, groups, block_rows, part_count = split_packed(packed, seg_len)

    def one_block(query_block):
        scores = (
            jnp.einsum(
                "gqhd,gkhd->ghqk", query_block, key_heads, preferred_element_type=jnp.float32
            )
            * factor
        )
        row_max = jnp.max(scores, -1, keepdims=True)
        shifted = jnp.exp(scores - row_max)
        row_sum = jnp.sum(shifted, -1, keepdims=True)
        weights = (shifted / row_sum).astype(jnp.bfloat16)
        mixture = jnp.einsum("ghqk,gkhd->gqhd", weights, values, preferred_element_type=jnp.float32)
        return (mixture, row_max[..., 0] + jnp.log(row_sum[..., 0]))

    mixture, logsum = lax.map(one_block, queries)
    return (mixture.swapaxes(0, 1).reshape(row_count, model_width), logsum.reshape(-1))


def attend_back(packed, logsum, grad_mixture, seg_len):
    row_count = packed.shape[0]
    model_width = packed.shape[1] // 3
    factor = 1.0 / math.sqrt(HEAD_DIM)
    queries, key_heads, values, groups, block_rows, part_count = split_packed(packed, seg_len)
    grad_blocks = grad_mixture.reshape(groups, part_count, block_rows, HEADS, HEAD_DIM).swapaxes(
        0, 1
    )
    logsum_blocks = logsum.reshape(part_count, groups, HEADS, block_rows)

    def one_block(carried, inputs):
        grad_keys, grad_values = carried
        query_block, grad_block, logsum_block = inputs
        scores = (
            jnp.einsum(
                "gqhd,gkhd->ghqk", query_block, key_heads, preferred_element_type=jnp.float32
            )
            * factor
        )
        prob_full = jnp.exp(scores - logsum_block[..., None])
        grad_values = grad_values + jnp.einsum(
            "ghqk,gqhd->gkhd",
            prob_full.astype(jnp.bfloat16),
            grad_block,
            preferred_element_type=jnp.float32,
        )
        grad_probs = jnp.einsum(
            "gqhd,gkhd->ghqk", grad_block, values, preferred_element_type=jnp.float32
        )
        row_inner = jnp.sum(grad_probs * prob_full, -1, keepdims=True)
        grad_scores = (prob_full * (grad_probs - row_inner)).astype(jnp.bfloat16)
        grad_query = (
            jnp.einsum(
                "ghqk,gkhd->gqhd", grad_scores, key_heads, preferred_element_type=jnp.float32
            )
            * factor
        )
        grad_keys = (
            grad_keys
            + jnp.einsum(
                "ghqk,gqhd->gkhd", grad_scores, query_block, preferred_element_type=jnp.float32
            )
            * factor
        )
        return ((grad_keys, grad_values), grad_query)

    zeros_kv = jnp.zeros((groups, seg_len, HEADS, HEAD_DIM), jnp.float32)
    (grad_keys, grad_values), grad_query = lax.scan(
        one_block, (zeros_kv, zeros_kv), (queries, grad_blocks, logsum_blocks)
    )
    return jnp.concatenate(
        [
            grad_query.swapaxes(0, 1).reshape(row_count, model_width),
            grad_keys.reshape(row_count, model_width),
            grad_values.reshape(row_count, model_width),
        ],
        1,
    )


def local_general(
    patches,
    embedding,
    long_image,
    routes,
    cotangent,
    ada_weight,
    qkv_weight,
    out_weight,
    shared_up,
    shared_down,
    router_weight,
    expert_up,
    expert_down,
):
    row_count, model_width = patches.shape
    block_count = embedding.shape[0]
    short_len = row_count // block_count
    lane_count = lax.axis_size("stream")
    local_experts = expert_up.shape[0]
    is_long = long_image[0] > 0

    def blocks(values):
        return values.reshape(block_count, short_len, model_width)

    def flatten(values):
        return values.reshape(row_count, model_width)

    used = jnp.where(is_long, jnp.broadcast_to(embedding[0:1], embedding.shape), embedding)
    activated, silu_back = jax.vjp(jax.nn.silu, used)
    ada_full = ada_weight.astype(jnp.float32)
    modulation = jnp.dot(activated, ada_full, precision=HIGH)
    pieces = [
        modulation[:, column * model_width : (column + 1) * model_width][:, None, :]
        for column in range(6)
    ]
    shift_one, scale_one, gate_one, shift_two, scale_two, gate_two = pieces
    inputs_full = blocks(patches.astype(jnp.float32))
    normed_one, spread_one = normalize(inputs_full)
    hidden_one = flatten(normed_one * (1.0 + scale_one) + shift_one).astype(jnp.bfloat16)
    packed = jnp.dot(hidden_one, qkv_weight, preferred_element_type=jnp.float32).astype(
        jnp.bfloat16
    )
    attended, logsum = lax.cond(
        is_long,
        lambda packed_in: attend(packed_in, row_count),
        lambda packed_in: attend(packed_in, short_len),
        packed,
    )
    attended_low = attended.astype(jnp.bfloat16)
    branch_one = blocks(jnp.dot(attended_low, out_weight, preferred_element_type=jnp.float32))
    middle = inputs_full + gate_one * branch_one
    normed_two, spread_two = normalize(middle)
    hidden_two = flatten(normed_two * (1.0 + scale_two) + shift_two).astype(jnp.bfloat16)
    shared_pre = jnp.dot(hidden_two, shared_up, preferred_element_type=jnp.float32)
    shared_act, shared_back = jax.vjp(gelu_tanh, shared_pre)
    shared_low = shared_act.astype(jnp.bfloat16)
    shared_out = jnp.dot(shared_low, shared_down, preferred_element_type=jnp.float32)
    logits = jnp.dot(hidden_two, router_weight, preferred_element_type=jnp.float32)
    chosen_hot = (routes[:, :, None] == jnp.arange(EXPERTS)[None, None, :]).astype(jnp.float32)
    gates = jax.nn.softmax(jnp.sum(chosen_hot * logits[:, None, :], -1), -1)
    flat_routes = routes.reshape(-1)
    route_hits = (flat_routes[:, None] == jnp.arange(EXPERTS)[None, :]).astype(jnp.int32)
    earlier = jnp.cumsum(route_hits, 0) - route_hits
    target = flat_routes * CAP + jnp.sum(earlier * route_hits, 1)

    def spread_rows(rows_low):
        buffer = jnp.zeros((EXPERTS * CAP, model_width), jnp.bfloat16).at[target].set(rows_low)
        return buffer.reshape(lane_count, local_experts, CAP, model_width)

    def collect(arrived):
        return (
            arrived.reshape(EXPERTS * CAP, model_width)[target]
            .astype(jnp.float32)
            .reshape(row_count, 2, model_width)
        )

    def by_expert(arrived):
        return arrived.swapaxes(0, 1).reshape(local_experts, lane_count * CAP, model_width)

    def by_source(results):
        return results.reshape(local_experts, lane_count, CAP, model_width).swapaxes(0, 1)

    expert_in = by_expert(
        lax.all_to_all(
            spread_rows(jnp.repeat(hidden_two, 2, axis=0)),
            "stream",
            split_axis=0,
            concat_axis=0,
            tiled=True,
        )
    )
    expert_pre = jnp.einsum(
        "jrd,jdf->jrf", expert_in, expert_up, preferred_element_type=jnp.float32
    )
    expert_act, expert_back = jax.vjp(gelu_tanh, expert_pre)
    expert_low = expert_act.astype(jnp.bfloat16)
    expert_out = jnp.einsum(
        "jrf,jfd->jrd", expert_low, expert_down, preferred_element_type=jnp.float32
    ).astype(jnp.bfloat16)
    picked = collect(
        lax.all_to_all(by_source(expert_out), "stream", split_axis=0, concat_axis=0, tiled=True)
    )
    routed = jnp.sum(gates[:, :, None] * picked, 1)
    branch_two = blocks(shared_out + routed)
    mixed = flatten(middle + gate_two * branch_two).astype(jnp.bfloat16)
    grad_top = blocks(cotangent.astype(jnp.float32))
    grad_gate_two = jnp.sum(grad_top * branch_two, 1)
    grad_branch = flatten(grad_top * gate_two)
    grad_pick = (
        (gates[:, :, None] * grad_branch[:, None, :])
        .astype(jnp.bfloat16)
        .reshape(2 * row_count, model_width)
    )
    grad_arrived = by_expert(
        lax.all_to_all(spread_rows(grad_pick), "stream", split_axis=0, concat_axis=0, tiled=True)
    )
    grad_expert_down = jnp.einsum(
        "jrf,jrd->jfd", expert_low, grad_arrived, preferred_element_type=jnp.float32
    )
    grad_expert_act = jnp.einsum(
        "jrd,jfd->jrf", grad_arrived, expert_down, preferred_element_type=jnp.float32
    )
    grad_expert_pre = expert_back(grad_expert_act)[0].astype(jnp.bfloat16)
    grad_expert_up = jnp.einsum(
        "jrd,jrf->jdf", expert_in, grad_expert_pre, preferred_element_type=jnp.float32
    )
    grad_expert_in = jnp.einsum(
        "jrf,jdf->jrd", grad_expert_pre, expert_up, preferred_element_type=jnp.float32
    ).astype(jnp.bfloat16)
    grad_routed = jnp.sum(
        collect(
            lax.all_to_all(
                by_source(grad_expert_in), "stream", split_axis=0, concat_axis=0, tiled=True
            )
        ),
        1,
    )
    grad_shared_low = grad_branch.astype(jnp.bfloat16)
    grad_shared_down = jnp.einsum(
        "rf,rd->fd", shared_low, grad_shared_low, preferred_element_type=jnp.float32
    )
    grad_shared_act = jnp.einsum(
        "rd,fd->rf", grad_shared_low, shared_down, preferred_element_type=jnp.float32
    )
    grad_shared_pre = shared_back(grad_shared_act)[0].astype(jnp.bfloat16)
    grad_shared_up = jnp.einsum(
        "rd,rf->df", hidden_two, grad_shared_pre, preferred_element_type=jnp.float32
    )
    grad_gates = jnp.sum(picked * grad_branch[:, None, :], -1)
    grad_chosen = gates * (grad_gates - jnp.sum(gates * grad_gates, -1, keepdims=True))
    grad_logits = jnp.sum(chosen_hot * grad_chosen[:, :, None], 1)
    hidden_two_full = hidden_two.astype(jnp.float32)
    router_full = router_weight.astype(jnp.float32)
    grad_router = jnp.dot(hidden_two_full.T, grad_logits, precision=HIGH)
    grad_hidden = jnp.dot(grad_logits, router_full.T, precision=HIGH) + grad_routed
    grad_hidden = blocks(
        grad_hidden
        + jnp.einsum("rf,df->rd", grad_shared_pre, shared_up, preferred_element_type=jnp.float32)
    )
    grad_shift_two = jnp.sum(grad_hidden, 1)
    grad_scale_two = jnp.sum(grad_hidden * normed_two, 1)
    grad_middle = grad_top + normalize_back(grad_hidden * (1.0 + scale_two), normed_two, spread_two)
    grad_gate_one = jnp.sum(grad_middle * branch_one, 1)
    grad_branch_one = flatten(grad_middle * gate_one).astype(jnp.bfloat16)
    grad_out_weight = jnp.einsum(
        "rd,re->de", attended_low, grad_branch_one, preferred_element_type=jnp.float32
    )
    grad_attended = jnp.einsum(
        "re,de->rd", grad_branch_one, out_weight, preferred_element_type=jnp.float32
    ).astype(jnp.bfloat16)
    grad_packed = lax.cond(
        is_long,
        lambda packed_in, logsum_in, grad_in: attend_back(packed_in, logsum_in, grad_in, row_count),
        lambda packed_in, logsum_in, grad_in: attend_back(packed_in, logsum_in, grad_in, short_len),
        packed,
        logsum,
        grad_attended,
    ).astype(jnp.bfloat16)
    grad_qkv = jnp.einsum("rd,re->de", hidden_one, grad_packed, preferred_element_type=jnp.float32)
    grad_hidden_one = blocks(
        jnp.einsum("re,de->rd", grad_packed, qkv_weight, preferred_element_type=jnp.float32)
    )
    grad_shift_one = jnp.sum(grad_hidden_one, 1)
    grad_scale_one = jnp.sum(grad_hidden_one * normed_one, 1)
    grad_inputs = grad_middle + normalize_back(
        grad_hidden_one * (1.0 + scale_one), normed_one, spread_one
    )
    grad_modulation = jnp.concatenate(
        [
            grad_shift_one,
            grad_scale_one,
            grad_gate_one,
            grad_shift_two,
            grad_scale_two,
            grad_gate_two,
        ],
        1,
    )
    grad_ada = jnp.dot(activated.T, grad_modulation, precision=HIGH)
    grad_used = silu_back(jnp.dot(grad_modulation, ada_full.T, precision=HIGH))[0]
    grad_embedding = jnp.where(
        is_long, jnp.zeros_like(grad_used).at[0].set(jnp.sum(grad_used, 0)), grad_used
    )
    shares = (
        lax.psum_scatter(
            grad_ada.astype(jnp.bfloat16), "dp", scatter_dimension=0, tiled=True
        ).astype(jnp.float32),
        lax.psum_scatter(
            grad_qkv.astype(jnp.bfloat16), "dp", scatter_dimension=0, tiled=True
        ).astype(jnp.float32),
        lax.psum_scatter(
            grad_out_weight.astype(jnp.bfloat16), "dp", scatter_dimension=0, tiled=True
        ).astype(jnp.float32),
        lax.psum_scatter(
            grad_shared_up.astype(jnp.bfloat16), "dp", scatter_dimension=0, tiled=True
        ).astype(jnp.float32),
        lax.psum_scatter(
            grad_shared_down.astype(jnp.bfloat16), "dp", scatter_dimension=0, tiled=True
        ).astype(jnp.float32),
        lax.psum_scatter(
            grad_router.astype(jnp.bfloat16), "dp", scatter_dimension=0, tiled=True
        ).astype(jnp.float32),
    )
    expert_summed = (
        lax.psum_scatter(
            grad_expert_up.astype(jnp.bfloat16), "dp", scatter_dimension=1, tiled=True
        ).astype(jnp.float32),
        lax.psum_scatter(
            grad_expert_down.astype(jnp.bfloat16), "dp", scatter_dimension=1, tiled=True
        ).astype(jnp.float32),
    )
    summed = (
        lax.psum(shares[0].astype(jnp.bfloat16), "stream").astype(jnp.float32),
        lax.psum(shares[1].astype(jnp.bfloat16), "stream").astype(jnp.float32),
        lax.psum(shares[2].astype(jnp.bfloat16), "stream").astype(jnp.float32),
        lax.psum(shares[3].astype(jnp.bfloat16), "stream").astype(jnp.float32),
        lax.psum(shares[4].astype(jnp.bfloat16), "stream").astype(jnp.float32),
        lax.psum(shares[5].astype(jnp.bfloat16), "stream").astype(jnp.float32),
    )
    return (
        mixed,
        flatten(grad_inputs),
        grad_embedding,
        summed[0],
        summed[1],
        summed[2],
        summed[3],
        summed[4],
        summed[5],
        expert_summed[0],
        expert_summed[1],
    )


def nn(left, right):
    return jnp.dot(left, right, preferred_element_type=F32)


def nt(left, right):
    return lax.dot_general(left, right, (((1,), (1,)), ((), ())), preferred_element_type=F32)


def tn(left, right):
    return lax.dot_general(left, right, (((0,), (0,)), ((), ())), preferred_element_type=F32)


def three_parts(values):
    first = values.astype(BF16)
    rest = values - first.astype(F32)
    second = rest.astype(BF16)
    third = (rest - second.astype(F32)).astype(BF16)
    return first, second, third


def stacked(values):
    return jnp.concatenate(three_parts(values), 0)


def unstacked(product):
    rows = product.shape[0] // 3
    return product[:rows] + product[rows : 2 * rows] + product[2 * rows :]


def sigmoid(values):
    return 1.0 / (1.0 + jnp.exp(-values))


def gelu_and_slope(values):
    inner = math.sqrt(2.0 / math.pi)
    square = values * values
    bend = jnp.tanh(values * (inner + (inner * 0.044715) * square))
    half = 0.5 + 0.5 * bend
    slope = half + values * (0.5 - 0.5 * bend * bend) * (inner + (3.0 * inner * 0.044715) * square)
    return values * half, slope


def run(kernel, args, grid, in_specs, out_specs, out_shape, name, scalars=(), scratch=(), after=(), limit=56):
    count = len(scalars) + len(args)

    def body(*refs):
        kernel(*refs[:count], *refs[count + len(after) :])

    return pl.pallas_call(
        body,
        grid_spec=pltpu.PrefetchScalarGridSpec(
            num_scalar_prefetch=len(scalars),
            grid=grid,
            in_specs=list(in_specs) + [pl.BlockSpec(memory_space=pl.ANY)] * len(after),
            out_specs=out_specs,
            scratch_shapes=list(scratch),
        ),
        out_shape=out_shape,
        compiler_params=pltpu.CompilerParams(vmem_limit_bytes=limit * MIB),
        cost_estimate=pl.CostEstimate(flops=1000, bytes_accessed=1000, transcendentals=0),
        name=name,
    )(*scalars, *args, *after)


def full(shape):
    return pl.BlockSpec(shape, lambda *_: (0,) * len(shape))


def like(array):
    return full(array.shape)


def rows_spec(rows, width):
    return pl.BlockSpec((rows, width), lambda i, *_: (i, 0))


def shape(dims, dtype):
    return jax.ShapeDtypeStruct(tuple(dims), dtype)


LONG, CORE, STREAM, ROW_Y, ROW_Z, FIRST_HERE, FIRST_ALL = range(7)


def flipped(value, bits):
    total = 0
    for bit in range(bits):
        total = total + (((value >> bit) & 1) << (bits - 1 - bit))
    return total


def modulate_kernel(blocks, pos_ref, emb_ref, ada_ref, cot_ref, mod_ref, act_ref, branch_ref, sent_ref):
    emb = emb_ref[...]
    used = jnp.where(pos_ref[LONG] > 0, jnp.broadcast_to(emb[0:1], emb.shape), emb)
    act = used * sigmoid(used)
    act_ref[...] = act
    total = unstacked(nn(stacked(act), ada_ref[...]))
    mod_ref[0] = total

    @pl.when(pl.program_id(0) == pl.num_programs(0) - 1)
    def _():
        short = cot_ref.shape[0] // blocks
        for block in range(blocks):
            span = slice(block * short, (block + 1) * short)
            branch = (cot_ref[span, :].astype(F32) * total[block : block + 1]).astype(BF16)
            branch_ref[span, :] = branch
            sent_ref[span, :] = branch
        sent_ref[cot_ref.shape[0] :, :] = jnp.zeros((sent_ref.shape[0] - cot_ref.shape[0], cot_ref.shape[1]), BF16)


def modulate(pos, emb_pad, ada_weight, cot, blocks):
    rows, width = emb_pad.shape
    pieces = ada_weight.shape[1] // width
    sent = (cot.shape[0] + 32, width)
    return run(
        functools.partial(modulate_kernel, blocks), (emb_pad, ada_weight, cot), (pieces,),
        [like(emb_pad), pl.BlockSpec((width, width), lambda i, *_: (0, i)), like(cot)],
        [pl.BlockSpec((1, rows, width), lambda i, *_: (i, 0, 0)), like(emb_pad), like(cot), full(sent)],
        [shape((pieces, rows, width), F32), shape((rows, width), F32), shape(cot.shape, BF16), shape(sent, BF16)],
        "modulate", scalars=(pos,),
    )


def norm_parts(values):
    centered = values - jnp.mean(values, -1, keepdims=True)
    spread = lax.rsqrt(jnp.mean(centered * centered, -1, keepdims=True) + EPSILON)
    return centered * spread, spread


def norm_back(grad, normed, spread):
    return spread * (
        grad
        - jnp.mean(grad, -1, keepdims=True)
        - normed * jnp.mean(grad * normed, -1, keepdims=True)
    )


def qkv_kernel(x_ref, mod_ref, w_ref, packed_ref):
    short = x_ref.shape[0] // 2
    halves = []
    for at in range(2):
        block = pl.program_id(0) * 2 + at
        normed, _ = norm_parts(x_ref[at * short : (at + 1) * short, :].astype(F32))
        shift, scale = mod_ref[0, pl.ds(block, 1), :], mod_ref[1, pl.ds(block, 1), :]
        halves.append((normed * (1.0 + scale) + shift).astype(BF16))
    packed_ref[...] = nn(jnp.concatenate(halves, 0), w_ref[...]).astype(BF16)


def qkv_forward(patches, mod, weight, blocks, after):
    rows, width = patches.shape
    short = 2 * rows // blocks
    wide = weight.shape[1]
    return run(
        qkv_kernel, (patches, mod, weight), (blocks // 2,),
        [rows_spec(short, width), like(mod), like(weight)], rows_spec(short, wide),
        shape((rows, wide), BF16), "qkv", after=after,
    )


def attend_kernel(short, pos_ref, q_ref, k_ref, v_ref, o_ref, lse_ref):
    rows, lanes = q_ref.shape
    first = lax.broadcasted_iota(jnp.int32, (1, lanes), 1) < HEAD_DIM
    factor = 1.0 / math.sqrt(HEAD_DIM)

    def part(at, count):
        span = slice(at, at + count)
        queries = (q_ref[span, :].astype(F32) * factor).astype(BF16)
        keys, values = k_ref[span, :], v_ref[span, :]
        zero = jnp.zeros_like(queries)
        wide = jnp.concatenate([values, jnp.ones_like(values)], 1)
        masks = (first, jnp.logical_not(first))
        scores = [nt(jnp.where(mine, queries, zero), keys) for mine in masks]
        tops = [jnp.max(a, -1, keepdims=True) for a in scores]
        shifted = [jnp.exp(a - top).astype(BF16) for a, top in zip(scores, tops)]
        mixtures = [nn(a, wide) for a in shifted]
        totals = [a[:, lanes:] for a in mixtures]
        outs = [a[:, :lanes] / total for a, total in zip(mixtures, totals)]
        sums = [top + jnp.log(total) for top, total in zip(tops, totals)]
        o_ref[span, :] = jnp.where(first, outs[0], outs[1]).astype(BF16)
        lse_ref[span, :] = jnp.where(first, sums[0], sums[1])

    @pl.when(pos_ref[LONG] > 0)
    def _():
        part(0, rows)

    @pl.when(pos_ref[LONG] <= 0)
    def _():
        for at in range(0, rows, short):
            part(at, short)


def pair_specs(rows, width):
    lanes = 2 * HEAD_DIM
    pairs = width // lanes
    return [
        pl.BlockSpec((rows, lanes), functools.partial(lambda shift, i, *_: (0, i + shift), shift))
        for shift in (0, pairs, 2 * pairs)
    ]


def attend_forward(pos, packed, short):
    rows = packed.shape[0]
    width = packed.shape[1] // 3
    spec = pair_specs(rows, width)
    return run(
        functools.partial(attend_kernel, short), (packed, packed, packed), (width // (2 * HEAD_DIM),),
        spec, [spec[0], spec[0]], [shape((rows, width), BF16), shape((rows, width), F32)],
        "attend", scalars=(pos,),
    )


def attend_back_kernel(
    short, pos_ref, q_ref, k_ref, v_ref, o_ref, lse_ref, do_ref, dq_ref, dk_ref, dv_ref,
    dk_acc, dv_acc,
):
    rows, lanes = q_ref.shape
    first = lax.broadcasted_iota(jnp.int32, (1, lanes), 1) < HEAD_DIM
    factor = 1.0 / math.sqrt(HEAD_DIM)
    product = do_ref[...].astype(F32) * o_ref[...].astype(F32)
    lse_t = jnp.transpose(lse_ref[...])
    product_t = jnp.transpose(product)
    lse_rows = [lse_t[0:1], lse_t[HEAD_DIM : HEAD_DIM + 1]]
    delta_rows = [
        jnp.sum(product_t[:HEAD_DIM], 0, keepdims=True),
        jnp.sum(product_t[HEAD_DIM:], 0, keepdims=True),
    ]

    def part(query_at, key_at, key_count, fresh):
        chunk = slice(query_at, query_at + short)
        span = slice(key_at, key_at + key_count)
        queries, grads = (q_ref[chunk, :].astype(F32) * factor).astype(BF16), do_ref[chunk, :]
        keys, values = k_ref[span, :], v_ref[span, :]
        masks = (first, jnp.logical_not(first))

        def apart(array):
            return [jnp.where(mine, array, jnp.zeros_like(array)) for mine in masks]

        query_own, grad_own, key_own = apart(queries), apart(grads), apart(keys)
        probs = [
            jnp.exp(nt(keys, query) - lse[:, chunk]) for query, lse in zip(query_own, lse_rows)
        ]
        grad_probs = [nt(values, grad) for grad in grad_own]
        grad_scores = [
            (prob * (grad - delta[:, chunk])).astype(BF16)
            for prob, grad, delta in zip(probs, grad_probs, delta_rows)
        ]
        low = [prob.astype(BF16) for prob in probs]
        dv = nn(jnp.concatenate(low, 1), jnp.concatenate(grad_own, 0))
        dk = nn(jnp.concatenate(grad_scores, 1), jnp.concatenate(query_own, 0))
        dq = nn(jnp.transpose(jnp.concatenate(key_own, 0)), jnp.concatenate(grad_scores, 0))
        dq_ref[chunk, :] = (jnp.transpose(dq) * factor).astype(BF16)
        if fresh:
            dk_acc[span, :] = dk
            dv_acc[span, :] = dv
        else:
            dk_acc[span, :] += dk
            dv_acc[span, :] += dv

    @pl.when(pos_ref[LONG] > 0)
    def _():
        for at in range(0, rows, short):
            part(at, 0, rows, at == 0)

    @pl.when(pos_ref[LONG] <= 0)
    def _():
        for at in range(0, rows, short):
            part(at, at, short, True)

    dk_ref[...] = dk_acc[...].astype(BF16)
    dv_ref[...] = dv_acc[...].astype(BF16)


def attend_backward(pos, packed, attended, logsum, grad, short, after):
    rows, width = attended.shape
    lanes = 2 * HEAD_DIM
    spec = pair_specs(rows, width)
    return run(
        functools.partial(attend_back_kernel, short),
        (packed, packed, packed, attended, logsum, grad), (width // lanes,),
        spec + [spec[0]] * 3, [spec[0]] * 3, [shape((rows, width), BF16)] * 3,
        "attend_back", scalars=(pos,), scratch=[pltpu.VMEM((rows, lanes), F32)] * 2, after=after,
    )


def middle_kernel(att_ref, x_ref, mod_ref, w_ref, branch_ref, hidden_ref):
    short = x_ref.shape[0] // 2
    branch = nn(att_ref[...], w_ref[...])
    branch_ref[...] = branch
    for at in range(2):
        block, span = pl.program_id(0) * 2 + at, slice(at * short, (at + 1) * short)
        middle = x_ref[span, :].astype(F32) + mod_ref[2, pl.ds(block, 1), :] * branch[span]
        normed, _ = norm_parts(middle)
        shift, scale = mod_ref[3, pl.ds(block, 1), :], mod_ref[4, pl.ds(block, 1), :]
        hidden_ref[span, :] = (normed * (1.0 + scale) + shift).astype(BF16)


def middle_forward(attended, patches, mod, out_weight, blocks, after):
    rows, width = patches.shape
    tile = rows_spec(2 * rows // blocks, width)
    return run(
        middle_kernel, (attended, patches, mod, out_weight), (blocks // 2,),
        [tile, tile, like(mod), like(out_weight)], [tile, tile],
        [shape((rows, width), F32), shape((rows, width), BF16)], "middle", after=after,
    )


def rank_kernel(pos_ref, *refs):
    count = (len(refs) - 2) // 1
    routes, (row_ref, col_ref) = refs[:count], refs[count:]
    rows = routes[0].shape[1]
    before = lax.broadcasted_iota(jnp.int32, (rows, rows), 0)
    after = lax.broadcasted_iota(jnp.int32, (rows, rows), 1)
    upper = (before < after).astype(F32).astype(BF16)
    ids = pos_ref[FIRST_ALL] + lax.broadcasted_iota(jnp.int32, (8, rows), 0)
    for source, ref in enumerate(routes):
        hits = jnp.logical_or(ref[0:1, :] == ids, ref[1:2, :] == ids)
        earlier = nn(hits.astype(F32).astype(BF16), upper)
        rank = jnp.where(hits, earlier, -1.0)
        row_ref[source] = rank.astype(jnp.int32)
        tall = jnp.concatenate([rank, jnp.full((120, rows), -1.0, F32)], 0)
        col_ref[source] = jnp.transpose(tall).astype(jnp.int32)


def ranks(pos, routes, after):
    count, rows = len(routes), routes[0].shape[1]
    out = [shape((count, 8, rows), jnp.int32), shape((count, rows, 128), jnp.int32)]
    return run(
        rank_kernel, routes, (1,), [like(a) for a in routes], [like(a) for a in out], out, "ranks",
        scalars=(pos,), after=after,
    )


def touch(array, after):
    count = len(after)

    def body(*refs):
        del refs

    return pl.pallas_call(
        body,
        in_specs=[pl.BlockSpec(memory_space=pl.ANY)] * (1 + count),
        out_specs=pl.BlockSpec(memory_space=pl.ANY),
        out_shape=shape(array.shape, array.dtype),
        input_output_aliases={0: 0},
        name="touch",
    )(array, *after)


def gate_rows(hidden, routes, router_t, ids):
    logits = nt(router_t, hidden)
    every = lax.broadcasted_iota(jnp.int32, logits.shape, 0)
    first, second = routes[0:1, :], routes[1:2, :]
    zero = jnp.zeros_like(logits)
    logit_one = jnp.sum(jnp.where(every == first, logits, zero), 0, keepdims=True)
    logit_two = jnp.sum(jnp.where(every == second, logits, zero), 0, keepdims=True)
    gate_one = sigmoid(logit_one - logit_two)
    gate_two = sigmoid(logit_two - logit_one)
    return jnp.where(ids == first, gate_one, 0.0) + jnp.where(ids == second, gate_two, 0.0)


def ffn_phase_one(x, g, up_ref, down_ref, act_ref, pre_ref, step=768):
    wide = act_ref.shape[1]
    for at in range(0, wide, step):
        cols = slice(at, at + step)
        act, slope = gelu_and_slope(nn(x, up_ref[0, :, cols]))
        back = nt(g, down_ref[0, cols, :])
        act_ref[:, cols] = act.astype(BF16)
        pre_ref[:, cols] = (back * slope).astype(BF16)


def relative_rows(pos_ref, target, values, nz):
    bits = nz.bit_length() - 1
    part = values.shape[0] // (2 * nz)
    for block in range(2 * nz):
        place = (block % 2) ^ pos_ref[ROW_Y]
        place = place * nz + flipped((block // 2) ^ pos_ref[ROW_Z], bits)
        at = pl.multiple_of(place * part, part)
        target[pl.ds(at, part), :] = values[block * part : (block + 1) * part]


def sides(pos_ref, values):
    half = values.shape[1] // 2
    low, high = values[:, :half], values[:, half:]
    own_low = pos_ref[ROW_Y] == 0
    return jnp.where(own_low, low, high), jnp.where(own_low, high, low)


def expert_kernel(
    slot, sends, has_prior, pos_ref, h0_ref, h1_ref, g0_ref, g1_ref, rank_ref, routes0_ref, routes1_ref,
    router_ref, up_ref, down_ref, *rest,
):
    count = 1 + sends
    priors, rest = (rest[:count], rest[count:]) if has_prior else ((), rest)
    targets, rest = rest[:count], rest[count:]
    keep_ref = targets[0]
    (out_ref, gx_ref, gg_ref,
     x_s, xt_s, g_s, gt_s, b_s, gate_s, act_s, pre_s, out_acc, gx_acc) = rest
    tile = pl.program_id(0)
    last = pl.num_programs(0) - 1
    rows = h0_ref.shape[0]
    nz = keep_ref.shape[2] // keep_ref.shape[3] * 2
    part = h0_ref.shape[1] // (2 * nz)
    own = lax.broadcasted_iota(jnp.int32, (CAP, rows), 0)

    def hot(source):
        return (own == rank_ref[source, slot : slot + 1, :]).astype(F32)

    @pl.when(tile == 0)
    def _():
        sources = ((h0_ref, g0_ref, routes0_ref), (h1_ref, g1_ref, routes1_ref))
        for source, (h_ref, b_ref, routes_ref) in enumerate(sources):
            span = slice(source * CAP, (source + 1) * CAP)
            pick = hot(source)
            pick_low = pick.astype(BF16)
            expert = pos_ref[FIRST_ALL] + slot
            gate = gate_rows(h_ref[...], routes_ref[...], router_ref[...], expert)
            gate_col = jnp.sum(pick * gate[0:1], -1, keepdims=True)
            branch = nn(pick_low, b_ref[:rows, :])
            x_s[span, :] = nn(pick_low, h_ref[...]).astype(BF16)
            b_s[span, :] = branch.astype(BF16)
            g_s[span, :] = (branch * gate_col).astype(BF16)
            gate_s[span, :] = jnp.broadcast_to(gate_col, (CAP, 128))
        relative_rows(pos_ref, xt_s, jnp.transpose(x_s[...]), nz)
        gt_s[...] = jnp.transpose(g_s[...])
        out_acc[...] = jnp.zeros_like(out_acc)
        gx_acc[...] = jnp.zeros_like(gx_acc)

    ffn_phase_one(x_s[...], g_s[...], up_ref, down_ref, act_s, pre_s)
    act, pre = act_s[...], pre_s[...]
    out_acc[...] += nn(act, down_ref[0])
    gx_acc[...] += nt(pre, up_ref[0])

    def place(side, kind):
        return (0, kind) if side == 0 else (1, kind) if sends == 1 else (1 + kind, 0)

    dup = nn(xt_s[...], pre)
    half = dup.shape[1] // 2
    for side in range(2):
        at, entry = place(side, 0)
        for z in range(nz):
            for lanes in range(2):
                row, into = (side * nz + z) * part, (z * 2 + lanes) * part
                piece = dup[row : row + part, lanes * half : (lanes + 1) * half]
                if has_prior:
                    piece = piece + priors[at][0, entry, into : into + part, :].astype(F32)
                targets[at][0, entry, into : into + part, :] = piece.astype(BF16)
    for side, piece in enumerate(sides(pos_ref, nn(gt_s[...], act))):
        at, entry = place(side, 1)
        if has_prior:
            piece = piece + priors[at][0, entry].astype(F32)
        targets[at][0, entry] = piece.astype(BF16)

    @pl.when(tile == last)
    def _():
        for source in range(2):
            span = slice(source * CAP, (source + 1) * CAP)
            out = out_acc[span, :]
            out_ref[source] = (out * gate_s[span, 0:1]).astype(BF16)
            gx_ref[source] = gx_acc[span, :].astype(BF16)
            inner = jnp.sum(out * b_s[span, :].astype(F32), -1, keepdims=True)
            gg_ref[source] = jnp.sum(hot(source) * inner, 0, keepdims=True)


def expert_call(
    slot, sends, pos, hiddens, branches, rank_rows, routes, router_t, up, down, prior, nz, after
):
    rows, width = hiddens[0].shape
    wide = up.shape[2]
    tile = wide // nz
    bits = nz.bit_length() - 1
    count = 2 * CAP
    weights = [
        pl.BlockSpec((1, width, tile), lambda f, s: (s[FIRST_HERE] + slot, 0, f)),
        pl.BlockSpec((1, tile, width), lambda f, s: (s[FIRST_HERE] + slot, f, 0)),
    ]
    kinds = [2, 2] if sends == 1 else [2, 1, 1]
    grads = [
        pl.BlockSpec((1, kind, width, tile // 2), lambda f, s: (flipped(f ^ s[ROW_Z], bits), 0, 0, 0))
        for kind in kinds
    ]
    once = [*hiddens, *branches, rank_rows, *routes, router_t]
    out_shape = (
        [shape((nz, kind, width, tile // 2), BF16) for kind in kinds]
        + [shape((2, CAP, width), BF16)] * 2
        + [shape((2, 1, rows), F32)]
    )
    prior = () if prior is None else tuple(prior)
    return run(
        functools.partial(expert_kernel, slot, sends, bool(prior)), (*once, up, down, *prior), (nz,),
        [like(a) for a in once] + weights + (grads if prior else []),
        grads + [like(a) for a in out_shape[len(grads) :]], out_shape, "expert", scalars=(pos,), after=after,
        scratch=[
            pltpu.VMEM((count, width), BF16),
            pltpu.VMEM((width, count), BF16),
            pltpu.VMEM((count, width), BF16),
            pltpu.VMEM((width, count), BF16),
            pltpu.VMEM((count, width), BF16),
            pltpu.VMEM((count, 128), F32),
            pltpu.VMEM((count, tile), BF16),
            pltpu.VMEM((count, tile), BF16),
            pltpu.VMEM((count, width), F32),
            pltpu.VMEM((count, width), F32),
        ],
    )


def shared_kernel(
    pos_ref, h_ref, b_ref, up_ref, down_ref, ku_ref, su0_ref, su1_ref, kd_ref, sd0_ref, sd1_ref,
    out_ref, gx_ref, xt_s, gt_s, act_s, pre_s, out_acc, gx_acc,
):
    step = pl.program_id(0)
    nz, block = 4, kd_ref.shape[3]

    @pl.when(step == 0)
    def _():
        relative_rows(pos_ref, xt_s, jnp.transpose(h_ref[...]), nz)
        turned = jnp.transpose(b_ref[...])
        for slice_at in range(4):
            place = ((slice_at % 2) ^ pos_ref[CORE]) * 2 + ((slice_at // 2) ^ pos_ref[STREAM])
            at = pl.multiple_of(place * block, block)
            gt_s[pl.ds(at, block), :] = turned[slice_at * block : (slice_at + 1) * block]
        out_acc[...] = jnp.zeros_like(out_acc)
        gx_acc[...] = jnp.zeros_like(gx_acc)

    ffn_phase_one(h_ref[...], b_ref[...], up_ref, down_ref, act_s, pre_s)
    act, pre = act_s[...], pre_s[...]
    out_acc[...] += nn(act, down_ref[0])
    gx_acc[...] += nt(pre, up_ref[0])

    @pl.when(step == nz - 1)
    def _():
        out_ref[...] = out_acc[...].astype(BF16)
        gx_ref[...] = gx_acc[...].astype(BF16)

    dup = nn(xt_s[...], pre).astype(BF16)

    @pl.when(step < 2)
    def _():
        ku_ref[0] = dup

    @pl.when(step == 2)
    def _():
        su0_ref[...] = dup

    @pl.when(step == 3)
    def _():
        su1_ref[...] = dup

    for y, piece in enumerate(sides(pos_ref, nn(gt_s[...], act))):
        pieces = [piece[place * block : (place + 1) * block].astype(BF16) for place in range(4)]
        kd_ref[0, y, 0], kd_ref[1, y, 0] = pieces[0], pieces[1]
        sd0_ref[y, 0], sd1_ref[y, 0] = pieces[2], pieces[3]


def shared_call(pos, hidden, branch, up, down, after):
    rows, width = hidden.shape
    wide = up.shape[1]
    nz = 4
    tile = wide // nz
    block = width // 4

    def unit(f, s):
        return (f % 2 ^ s[STREAM]) * 2 + (f // 2 ^ s[CORE])

    keep = pl.BlockSpec((1, width, tile), lambda f, s: (jnp.minimum(f, 1), 0, 0))
    downs = pl.BlockSpec(
        (2, 2, 1, block, tile // 2), lambda f, s: (0, 0, flipped(unit(f, s) ^ s[ROW_Z], 2), 0, 0)
    )
    sent = pl.BlockSpec((2, 1, block, tile // 2), lambda f, s: (0, flipped(unit(f, s) ^ s[ROW_Z], 2), 0, 0))
    outs = run(
        shared_kernel, (hidden, branch, up[None], down[None]), (nz,),
        [
            like(hidden),
            like(branch),
            pl.BlockSpec((1, width, tile), lambda f, s: (0, 0, unit(f, s))),
            pl.BlockSpec((1, tile, width), lambda f, s: (0, unit(f, s), 0)),
        ],
        [keep] + [full((width, tile))] * 2 + [downs, sent, sent, like(hidden), like(hidden)],
        [shape((2, width, tile), BF16)] + [shape((width, tile), BF16)] * 2
        + [shape((2, 2, nz, block, tile // 2), BF16)] + [shape((2, nz, block, tile // 2), BF16)] * 2
        + [shape((rows, width), BF16)] * 2,
        "shared", scalars=(pos,), after=after,
        scratch=[
            pltpu.VMEM((width, rows), BF16),
            pltpu.VMEM((width, rows), BF16),
            pltpu.VMEM((rows, tile), BF16),
            pltpu.VMEM((rows, tile), BF16),
            pltpu.VMEM((rows, width), F32),
            pltpu.VMEM((rows, width), F32),
        ],
    )
    return outs[0], outs[1:3], outs[3], outs[4:6], *outs[6:]


def combine_kernel(places, col_ref, *refs):
    slots = len(places)
    rows_refs, refs = refs[: 2 * slots], refs[2 * slots :]
    targets, stacks = refs[:5], refs[5:]

    @pl.when(pl.program_id(0) == 0)
    def _():
        for slot in range(slots):
            for kind in range(2):
                for source in range(2):
                    stacks[kind][source, slot * CAP : (slot + 1) * CAP, :] = rows_refs[2 * slot + kind][places[slot] + source]

    block = col_ref.shape[1]
    own = lax.broadcasted_iota(jnp.int32, (block, slots * CAP), 1)
    for source in range(2):
        hits = None
        for slot in range(slots):
            rank = col_ref[source, :, slot : slot + 1]
            place = jnp.where(rank < 0, -1, rank + slot * CAP)
            hit = place == own
            hits = hit if hits is None else jnp.logical_or(hits, hit)
        pick = hits.astype(F32).astype(BF16)
        for kind in range(2):
            total = nn(pick, stacks[kind][source]).astype(BF16)
            if 2 * kind + source < 3:
                targets[2 * kind + source][...] = total
            else:
                early = pl.program_id(0) < pl.num_programs(0) // 2

                @pl.when(early)
                def _():
                    targets[3][...] = total

                @pl.when(jnp.logical_not(early))
                def _():
                    targets[4][...] = total


def combine(rank_cols, pairs, places, after):
    count, rows, _ = rank_cols.shape
    width = pairs[0][0].shape[2]
    block = rows // 2
    flat = [a for pair in pairs for a in pair]
    halves = [pl.BlockSpec((block, width), lambda i: (0, 0))] * 2
    *outs, low, high = run(
        functools.partial(combine_kernel, places), (rank_cols, *flat), (rows // block,),
        [pl.BlockSpec((count, block, 128), lambda i: (0, i, 0))] + [like(a) for a in flat],
        [rows_spec(block, width)] * 3 + halves,
        [shape((rows, width), BF16)] * 3 + [shape((rows // 2, width), BF16)] * 2, "combine",
        scratch=[pltpu.VMEM((2, len(pairs) * CAP, width), BF16)] * 2, after=after,
    )
    return (*outs, (low, high))


def add_kernel(left_ref, low_ref, high_ref, second_ref, third_ref, one_ref, two_ref):
    two_ref[...] = (second_ref[...].astype(F32) + third_ref[...].astype(F32)).astype(BF16)
    low = pl.program_id(0) < pl.num_programs(0) // 2
    right = jnp.where(low, low_ref[...], high_ref[...])
    one_ref[...] = (left_ref[...].astype(F32) + right.astype(F32)).astype(BF16)


def add_rows(left, halves, second, third, after):
    rows, width = left.shape
    tile = rows_spec(rows // 4, width)
    low = pl.BlockSpec((rows // 4, width), lambda i: (jnp.minimum(i, 1), 0))
    high = pl.BlockSpec((rows // 4, width), lambda i: (jnp.maximum(i - 2, 0), 0))
    return run(
        add_kernel, (left, *halves, second, third), (4,), [tile, low, high, tile, tile], [tile] * 2,
        [shape((rows, width), BF16)] * 2, "add_rows", after=after,
    )


def total_of(keep, arrived):
    return keep.astype(F32) + arrived.astype(F32)


def halve_kinds_kernel(kinds, *refs):
    keep_ref, send_ref = refs[-2:]
    refs = iter(refs[:-2])
    for at, kind in enumerate(kinds):
        if kind == 0:
            total = total_of(next(refs)[0, 0], next(refs)[0, 0])
            half = total.shape[0] // 2
            keep_ref[at, 0], send_ref[at, 0] = total[:half], total[half:].astype(BF16)
        else:
            keep_ref[at, 0] = total_of(next(refs)[0, 0], next(refs)[0, 0])
            send_ref[at, 0] = total_of(next(refs)[0, 0], next(refs)[0, 0]).astype(BF16)


def halve_y(keep, arrived, kinds, after):
    nz, _, rows, cols = keep.shape
    split = lambda a: a.reshape(nz, -1, rows // 2, cols)
    args, specs = [], []
    for at, kind in enumerate(kinds):
        for add in (0, nz // 2) if kind else (0,):
            for array, entry in ((keep, kind), (arrived, at)):
                if kind == 0:
                    args.append(array)
                    index = functools.partial(lambda entry, t: (t, entry, 0, 0), entry)
                    specs.append(pl.BlockSpec((1, 1, rows, cols), index))
                else:
                    args.append(split(array))
                    index = functools.partial(
                        lambda entry, add, t: (t // 2 + add, 2 * entry + t % 2, 0, 0), entry, add
                    )
                    specs.append(pl.BlockSpec((1, 1, rows // 2, cols), index))
    out = pl.BlockSpec((len(kinds), 1, rows // 2, cols), lambda t: (0, t, 0, 0))
    dims = (len(kinds), nz, rows // 2, cols)
    return run(
        functools.partial(halve_kinds_kernel, kinds), args, (nz,), specs, [out, out],
        [shape(dims, F32), shape(dims, BF16)], "halve_y", after=after,
    )


def halve_z(keep, arrived, kinds, after):
    _, nz, rows, cols = keep.shape
    split = lambda a: a.reshape(len(kinds), 2 * nz, rows // 2, cols)
    args, specs = [], []
    for at, kind in enumerate(kinds):
        for add in (0, nz) if kind else (0,):
            for array, flip in ((keep, 0), (arrived, nz // 2)):
                if kind == 0:
                    args.append(array)
                    index = functools.partial(lambda at, flip, t: (at, t ^ flip, 0, 0), at, flip)
                    specs.append(pl.BlockSpec((1, 1, rows, cols), index))
                else:
                    args.append(split(array))
                    index = functools.partial(lambda at, add, t: (at, t + add, 0, 0), at, add)
                    specs.append(pl.BlockSpec((1, 1, rows // 2, cols), index))
    out = pl.BlockSpec((len(kinds), 1, rows // 2, cols), lambda t: (0, t, 0, 0))
    dims = (len(kinds), nz, rows // 2, cols)
    return run(
        functools.partial(halve_kinds_kernel, kinds), args, (nz,), specs, [out, out],
        [shape(dims, F32), shape(dims, BF16)], "halve_z", after=after,
    )


def core_halves(pos_ref, values):
    half = values.shape[0] // 2
    low, high = values[:half], values[half:]
    own_low = pos_ref[CORE] == 0
    return jnp.where(own_low, low, high), jnp.where(own_low, high, low).astype(BF16)


def finish_kinds_kernel(kinds, pos_ref, *refs):
    inputs, outs = refs[: 2 * len(kinds)], refs[2 * len(kinds) :]
    for at, kind in enumerate(kinds):
        keep_ref, arrived_ref = inputs[2 * at : 2 * at + 2]
        mine, sent = outs[2 * at : 2 * at + 2]
        if kind == 0:
            up = total_of(keep_ref[0, 0], arrived_ref[0, 0])
            half = up.shape[0] // 2
            mine[...], sent[...] = core_halves(pos_ref, jnp.concatenate([up[:half], up[half:]], 1))
        else:

            @pl.when(pl.program_id(0) == 0)
            def _():
                down = total_of(keep_ref[0], arrived_ref[0])
                down = down.reshape(down.shape[0] * down.shape[1], down.shape[2])
                mine[...], sent[...] = core_halves(pos_ref, jnp.transpose(down))


def finish_kinds(pos, keep, arrived, kinds, after):
    _, nz, rows, cols = keep.shape
    bits = nz.bit_length() - 1
    args, specs, out_specs, outs = [], [], [], []
    for at, kind in enumerate(kinds):
        args += [keep, arrived]
        if kind == 0:
            for flip in (0, 1):
                index = functools.partial(lambda at, flip, t, s: (at, t ^ flip, 0, 0), at, flip)
                specs.append(pl.BlockSpec((1, 1, rows, cols), index))
            dims = (rows // 4, 2 * cols * nz)
            out = pl.BlockSpec((rows // 4, 2 * cols), lambda t, s: (0, flipped(t, bits) ^ s[ROW_Z]))
        else:
            index = functools.partial(lambda at, t, s: (at, 0, 0, 0), at)
            specs += [pl.BlockSpec((1, nz, rows, cols), index)] * 2
            dims = (cols // 2, nz * rows)
            out = full(dims)
        out_specs += [out, out]
        outs += [shape(dims, F32), shape(dims, BF16)]
    return run(
        functools.partial(finish_kinds_kernel, kinds), args, (nz,), specs, out_specs, outs, "finish_kinds",
        scalars=(pos,), after=after,
    )


def halve_slices_kernel(ku_ref, kd_ref, au0_ref, au1_ref, ad0_ref, ad1_ref, keep_ref, send_ref):
    ups, downs = (au0_ref, au1_ref), (ad0_ref, ad1_ref)
    for at, ref in enumerate((keep_ref, send_ref)):
        up = total_of(ku_ref[at], ups[at][...])
        rows, half = up.shape[0], up.shape[1] // 2
        for side in range(2):
            piece = up[:, side * half : (side + 1) * half]
            ref[0, side * rows : (side + 1) * rows, :] = piece.astype(ref.dtype)
        ref[1] = total_of(kd_ref[at], downs[at][...]).astype(ref.dtype)


def halve_slices(up_keep, down_keep, arrived, after):
    _, rows, cols = up_keep.shape
    steps = 8
    down_keep = down_keep.reshape(2, 2 * rows, cols // 2)
    arrived = [a.reshape(-1, a.shape[-1]) for a in arrived]
    ups = pl.BlockSpec((2, rows // steps, cols), lambda i: (0, i, 0))
    downs = pl.BlockSpec((2, 2 * rows // steps, cols // 2), lambda i: (0, i, 0))
    dims = (2, 2 * rows, cols // 2)
    return run(
        halve_slices_kernel, (up_keep, down_keep, *arrived), (steps,),
        [ups, downs] + [rows_spec(a.shape[0] // steps, a.shape[1]) for a in arrived],
        [downs, downs], [shape(dims, F32), shape(dims, BF16)], "halve_slices", after=after,
    )


def halve_kernel(keep_ref, arrived_ref, keep_out, send_out):
    keep_out[...] = total_of(keep_ref[:, 0], arrived_ref[:, 0])
    send_out[...] = total_of(keep_ref[:, 1], arrived_ref[:, 1]).astype(BF16)


def halve(keep, arrived, after, steps=2):
    kinds, rows, cols = keep.shape
    split = lambda a: a.reshape(kinds, 2, rows // 2, cols)
    into = pl.BlockSpec((kinds, 2, rows // 2 // steps, cols), lambda i: (0, 0, i, 0))
    out = pl.BlockSpec((kinds, rows // 2 // steps, cols), lambda i: (0, i, 0))
    dims = (kinds, rows // 2, cols)
    return run(
        halve_kernel, (split(keep), split(arrived)), (steps,), [into, into], [out, out],
        [shape(dims, F32), shape(dims, BF16)], "halve", after=after,
    )


def halve_parts_kernel(keep_ref, first_ref, second_ref, keep_out, send_out):
    keep_out[0] = total_of(keep_ref[0], first_ref[...])
    send_out[0] = total_of(keep_ref[1], second_ref[...]).astype(BF16)


def halve_parts(keep, arrived, after, steps=2):
    _, rows, cols = keep.shape
    into = pl.BlockSpec((2, rows // steps, cols), lambda i: (0, i, 0))
    out = pl.BlockSpec((1, rows // steps, cols), lambda i: (0, i, 0))
    return run(
        halve_parts_kernel, (keep, *arrived), (steps,), [into] + [rows_spec(rows // steps, cols)] * 2,
        [out, out], [shape((1, rows, cols), F32), shape((1, rows, cols), BF16)], "halve_parts", after=after,
    )


def finish_slices_kernel(pos_ref, sk_ref, sa_ref, qk_ref, qa_ref, mine_ref, sent_ref, mine_down_ref, sent_down_ref):
    total = total_of(sk_ref[...], sa_ref[...])
    half = total.shape[1] // 2
    up = jnp.concatenate([total[0, :half], total[0, half:]], 1)
    for at, values in enumerate((total_of(qk_ref[0], qa_ref[0]), up)):
        mine, sent_ref[at] = core_halves(pos_ref, values)
        mine_ref[at] = mine.astype(BF16)
    mine, sent_down_ref[...] = core_halves(pos_ref, jnp.transpose(total[1]))
    mine_down_ref[...] = mine.astype(BF16)


def finish_slices(pos, shared, shared_arrived, queries, queries_arrived, after):
    _, rows, cols = shared.shape
    args = (shared, shared_arrived, queries, queries_arrived)
    outs = [shape((2, rows // 4, 2 * cols), BF16)] * 2 + [shape((cols // 2, rows), BF16)] * 2
    return run(
        finish_slices_kernel, args, (1,), [like(a) for a in args], [like(a) for a in outs], outs,
        "finish_slices", scalars=(pos,), after=after,
    )


def middle_back_kernel(
    gs_ref, ga_ref, low_ref, high_ref, gc_ref, gg_ref, routes_ref, router_ref,
    hidden_ref, cot_ref, branch_ref, x_ref, mod_ref, w_ref,
    gm_ref, gatt_ref, back_ref, mods_ref, drouter_ref,
):
    block = pl.program_id(0)
    hidden = hidden_ref[...]
    grad_gates = gg_ref[...]
    ids = lax.broadcasted_iota(jnp.int32, grad_gates.shape, 0)
    gates = gate_rows(hidden, routes_ref[...], router_ref[...], ids)
    inner = jnp.sum(gates * grad_gates, 0, keepdims=True)
    grad_logits = gates * (grad_gates - inner)
    core = jnp.where(block < pl.num_programs(0) // 2, low_ref[...], high_ref[...])
    grad = gs_ref[...].astype(F32) + ga_ref[...].astype(F32) + core.astype(F32) + gc_ref[...].astype(F32)
    pieces = stacked(grad_logits)
    router = router_ref[...]
    grad = grad + tn(pieces, jnp.concatenate([router] * 3, 0))
    drouter = unstacked(nn(pieces, hidden))
    branch = branch_ref[...]
    gate_one = mod_ref[2, pl.ds(block, 1), :]
    middle = x_ref[...].astype(F32) + gate_one * branch
    normed, spread = norm_parts(middle)
    scale = mod_ref[4, pl.ds(block, 1), :]
    mods_ref[1, pl.ds(block, 1), :] = jnp.sum(grad, 0, keepdims=True)
    mods_ref[2, pl.ds(block, 1), :] = jnp.sum(grad * normed, 0, keepdims=True)
    grad_middle = cot_ref[...].astype(F32) + norm_back(grad * (1.0 + scale), normed, spread)
    mods_ref[0, pl.ds(block, 1), :] = jnp.sum(grad_middle * branch, 0, keepdims=True)
    gm_ref[...] = grad_middle
    grad_branch = (grad_middle * gate_one).astype(BF16)
    back_ref[...] = grad_branch
    gatt_ref[...] = nt(grad_branch, w_ref[...]).astype(BF16)

    @pl.when(block == 0)
    def _():
        drouter_ref[...] = drouter

    @pl.when(block > 0)
    def _():
        drouter_ref[...] += drouter


def middle_backward(parts, gg, routes_t, router_t, hidden, cot, branch, patches, mod, out_weight, blocks, after):
    rows, width = patches.shape
    short = rows // blocks
    tile = rows_spec(short, width)
    cols = lambda a: pl.BlockSpec((a.shape[0], short), lambda i: (0, i))
    half = blocks // 2
    low = pl.BlockSpec((short, width), lambda i: (jnp.minimum(i, half - 1), 0))
    high = pl.BlockSpec((short, width), lambda i: (jnp.maximum(i - half, 0), 0))
    out_shape = [
        shape((rows, width), F32),
        shape((rows, width), BF16),
        shape((rows, width), BF16),
        shape((3, 8, width), F32),
        shape((router_t.shape[0], width), F32),
    ]
    return run(
        middle_back_kernel,
        (*parts, gg, routes_t, router_t, hidden, cot, branch, patches, mod, out_weight), (blocks,),
        [tile, tile, low, high, tile] + [cols(gg), cols(routes_t), like(router_t)] + [tile] * 4 + [like(mod), like(out_weight)],
        [tile] * 3 + [like(a) for a in out_shape[3:]], out_shape, "middle_back", after=after,
    )


def mixed_kernel(so_ref, ra_ref, rb_ref, rc_ref, cot_ref, branch_ref, x_ref, mod_ref, mixed_ref, gate_ref):
    block = pl.program_id(0)
    second = so_ref[...].astype(F32) + ra_ref[...].astype(F32) + rb_ref[...].astype(F32) + rc_ref[...].astype(F32)
    middle = x_ref[...].astype(F32) + mod_ref[2, pl.ds(block, 1), :] * branch_ref[...]
    mixed_ref[...] = (middle + mod_ref[5, pl.ds(block, 1), :] * second).astype(BF16)
    gate_ref[pl.ds(block, 1), :] = jnp.sum(cot_ref[...].astype(F32) * second, 0, keepdims=True)


def mixed_forward(parts, cot, branch, patches, mod, blocks, after):
    rows, width = patches.shape
    tile = rows_spec(rows // blocks, width)
    return run(
        mixed_kernel, (*parts, cot, branch, patches, mod), (blocks,), [tile] * 7 + [like(mod)],
        [tile, full((8, width))], [shape((rows, width), BF16), shape((8, width), F32)], "mixed", after=after,
    )


def weight_kernel(
    pos_ref, x_ref, mod_ref, dq_ref, dk_ref, dv_ref, att_ref, back_ref, keep_ref, first_ref, second_ref, turned
):
    rows = x_ref.shape[0]
    short = rows // 4
    step = pl.program_id(0)
    matrix = ((step % 2) ^ pos_ref[STREAM]) * 2 + ((step // 2) ^ pos_ref[CORE])
    nz = 4

    @pl.when(step == 0)
    def _():
        for block in range(4):
            span = slice(block * short, (block + 1) * short)
            normed, _ = norm_parts(x_ref[span, :].astype(F32))
            hidden = normed * (1.0 + mod_ref[1, block : block + 1, :]) + mod_ref[0, block : block + 1, :]
            relative_rows(pos_ref, turned.at[0, :, span], jnp.transpose(hidden.astype(BF16)), nz)
        relative_rows(pos_ref, turned.at[1], jnp.transpose(att_ref[...]), nz)

    for index, (left, ref) in enumerate(((0, dq_ref), (0, dk_ref), (0, dv_ref), (1, back_ref))):

        @pl.when(matrix == index)
        def _():
            total = nn(turned[left], ref[...]).astype(BF16)

            @pl.when(step < 2)
            def _():
                keep_ref[0] = total

            @pl.when(step == 2)
            def _():
                first_ref[...] = total

            @pl.when(step == 3)
            def _():
                second_ref[...] = total


def weight_grads(pos, patches, mod, grads, attended, back, after):
    rows, width = patches.shape
    args = (patches, mod, *grads, attended, back)
    keep = pl.BlockSpec((1, width, width), lambda f, s: (jnp.minimum(f, 1), 0, 0))
    send = full((width, width))
    outs = run(
        weight_kernel, args, (4,), [like(a) for a in args], [keep, send, send],
        [shape((2, width, width), BF16)] + [shape((width, width), BF16)] * 2, "weight_grads", scalars=(pos,),
        scratch=[pltpu.VMEM((2, width, rows), BF16)], after=after,
    )
    return outs[0], outs[1:]


def inputs_back_kernel(dq_ref, dk_ref, dv_ref, w_ref, x_ref, gm_ref, mod_ref, gp_ref, mods_ref):
    width = x_ref.shape[1]
    short = x_ref.shape[0] // 2
    both = nt(dq_ref[...], w_ref[:, :width])
    both = both + nt(dk_ref[...], w_ref[:, width : 2 * width])
    both = both + nt(dv_ref[...], w_ref[:, 2 * width :])
    for at in range(2):
        block, span = pl.program_id(0) * 2 + at, slice(at * short, (at + 1) * short)
        grad = both[span]
        normed, spread = norm_parts(x_ref[span, :].astype(F32))
        mods_ref[0, pl.ds(block, 1), :] = jnp.sum(grad, 0, keepdims=True)
        mods_ref[1, pl.ds(block, 1), :] = jnp.sum(grad * normed, 0, keepdims=True)
        scale = mod_ref[1, pl.ds(block, 1), :]
        gp_ref[span, :] = gm_ref[span, :] + norm_back(grad * (1.0 + scale), normed, spread)


def inputs_backward(grads, weight, patches, grad_middle, mod, blocks, after):
    rows, width = patches.shape
    tile = rows_spec(2 * rows // blocks, width)
    return run(
        inputs_back_kernel, (*grads, weight, patches, grad_middle, mod), (blocks // 2,),
        [tile] * 3 + [like(weight), tile, tile, like(mod)], [tile, full((2, 8, width))],
        [shape((rows, width), F32), shape((2, 8, width), F32)], "inputs_back", after=after,
    )


def used_kernel(block_count, pos_ref, gm_ref, ada_ref, emb_ref, out_ref):
    piece = pl.program_id(0)

    @pl.when(piece == 0)
    def _():
        out_ref[...] = jnp.zeros_like(out_ref)

    out_ref[...] += unstacked(nt(stacked(gm_ref[0]), ada_ref[...]))

    @pl.when(piece == pl.num_programs(0) - 1)
    def _():
        emb = emb_ref[...]
        is_long = pos_ref[LONG] > 0
        used = jnp.where(is_long, jnp.broadcast_to(emb[0:1], emb.shape), emb)
        gate = sigmoid(used)
        grad = out_ref[...] * (gate * (1.0 + used * (1.0 - gate)))
        row = lax.broadcasted_iota(jnp.int32, grad.shape, 0)
        grad = jnp.where(row < block_count, grad, 0.0)
        total = jnp.sum(grad, 0, keepdims=True)
        out_ref[...] = jnp.where(is_long, jnp.where(row == 0, total, 0.0), grad)


def used_backward(pos, grad_mod, ada_weight, emb_pad, block_count, after):
    rows, width = emb_pad.shape
    pieces = grad_mod.shape[0]
    return run(
        functools.partial(used_kernel, block_count), (grad_mod, ada_weight, emb_pad), (pieces,),
        [
            pl.BlockSpec((1, rows, width), lambda i, *_: (i, 0, 0)),
            pl.BlockSpec((width, width), lambda i, *_: (0, i)),
            like(emb_pad),
        ],
        like(emb_pad), shape((rows, width), F32), "used_back", scalars=(pos,), after=after,
    )


def swap(values, axis, bit):
    size = lax.axis_size(axis)
    return lax.ppermute(values, axis, [(i, i ^ bit) for i in range(size)])


def swap_all(arrays, axis, bit):
    return [swap(a, axis, bit) for a in arrays]


def swap_across(values):
    stream = lax.axis_size("stream")
    pairs = [
        (i, ((i // stream) ^ 1) * stream + ((i % stream) ^ 1))
        for i in range(lax.axis_size("dp") * stream)
    ]
    return lax.ppermute(values, ("dp", "stream"), pairs)


def in_order(own, mine, arrived, axis):
    return jnp.concatenate(
        [jnp.where(own == 0, mine, arrived), jnp.where(own == 0, arrived, mine)], axis
    )


def local_pair(
    patches, embedding, long_image, routes, cotangent, ada_weight, qkv_weight, out_weight, shared_up,
    shared_down, router_weight, expert_up, expert_down,
):
    rows, width = patches.shape
    blocks = embedding.shape[0]
    short = rows // blocks
    dp_size = lax.axis_size("dp")
    nz = dp_size // 4
    dp, stream = lax.axis_index("dp"), lax.axis_index("stream")
    core, row_y, row_z = dp % 2, (dp // 2) % 2, dp // 4
    local_experts = expert_up.shape[0]
    here = local_experts // 2
    first_here = core * here
    first_all = stream * local_experts + first_here
    places = [long_image[0], core, stream, row_y, row_z, first_here, first_all, 0]
    pos = jnp.stack([jnp.asarray(a, jnp.int32) for a in places])

    routes_t = routes.T
    routes_x = swap(routes_t, "stream", 1)
    routes_near = (routes_t, swap(routes_t, "dp", 1))
    emb_pad = jnp.pad(embedding, ((0, 8 - blocks), (0, 0)))
    router_t = jnp.pad(router_weight.T, ((0, 16 - router_weight.shape[1]), (0, 0)))
    mod, act, branch_grad, branch_sent = modulate(pos, emb_pad, ada_weight, cotangent, blocks)
    routes_x = touch(routes_x, (mod,))
    branch_grad = touch(branch_grad, (routes_x, routes_near[1]))
    routes_far = (routes_x, swap(routes_x, "dp", 1))
    branch_x = swap(touch(branch_sent, (branch_grad,)), "stream", 1)
    branches_near = (branch_grad, swap(branch_grad, "dp", 1))

    packed = qkv_forward(patches, mod, qkv_weight, blocks, (branch_grad,))
    attended, logsum = attend_forward(pos, packed, short)
    branch_one, hidden = middle_forward(
        attended, patches, mod, out_weight, blocks, ()
    )
    hidden_x = swap(hidden, "stream", 1)
    hiddens_near = (hidden, swap(hidden, "dp", 1))
    rank_near, cols_near = ranks(pos, routes_near, (hidden,))
    branch_x = touch(branch_x, (rank_near,))
    branches_far = (branch_x, swap(branch_x, "dp", 1))

    def expert(slot, is_far, sends, prior, after):
        group = (
            (hiddens_far, branches_far, rank_far, routes_far)
            if is_far
            else (hiddens_near, branches_near, rank_near, routes_near)
        )
        out = expert_call(slot, sends, pos, *group, router_t, expert_up, expert_down, prior, nz, after)
        return out[: 1 + sends], out[1 + sends :]

    first, first_near = expert(0, False, 1, None, (branch_x,))
    hidden_x = touch(hidden_x, (first_near[2],))
    hiddens_far = (hidden_x, swap(hidden_x, "dp", 1))
    rank_far, cols_far = ranks(pos, routes_far, (hidden_x,))
    first, first_far = expert(0, True, 1, first, ())
    first_arrived = swap(first[1], "dp", 2)

    second, second_near = expert(1, False, 2, None, (first_far[2],))
    second, second_far = expert(1, True, 2, second, ())
    up_half_arrived = swap(second[1], "dp", 2)
    out_x, out_xc, gx_x, gx_xc = combine(cols_far, [r[:2] for r in (first_far, second_far)], (0, 0), ())
    gx_xc, out_xc = swap_all(gx_xc, "dp", 1), swap(out_xc, "dp", 1)
    out_near, out_core, gx_near, gx_core = combine(
        cols_near, [r[:2] for r in (first_near, second_near)], (0, 0), (gx_x,)
    )
    gx_core = [touch(a, (gx_near,)) for a in swap_all(gx_core, "dp", 1)]
    out_core = touch(swap(out_core, "dp", 1), (gx_near,))
    near, far = (first_near, second_near), (first_far, second_far)
    gg_near = [jnp.concatenate([r[2][source] for r in near], 0) for source in range(2)]
    gg_far = [jnp.concatenate([r[2][source] for r in far], 0) for source in range(2)]
    gg_back = swap(jnp.concatenate([gg_far[0], swap(gg_far[1], "dp", 1)], 0), "stream", 1)
    gg_back = touch(gg_back, (gx_near,))
    gg_rel = jnp.concatenate([gg_near[0], swap(gg_near[1], "dp", 1), gg_back], 0)
    gx_sum, out_sum = add_rows(gx_x, gx_xc, out_x, out_xc, (gg_back, *gx_core, out_core))
    gx_back = swap(gx_sum, "stream", 1)
    out_back = swap(out_sum, "stream", 1)
    both, up, down = (0, 1), (0,), (1,)
    ea_keep, ea_send = halve_y(first[0], first_arrived, both, (out_sum,))
    ea_arrived = swap(ea_send, "dp", 4)
    order = jnp.arange(4, dtype=jnp.int32) ^ (stream * 2 + core)
    gg = gg_rel.reshape(4, here, rows)[order].reshape(EXPERTS, rows)
    gg = jnp.pad(gg, ((0, 16 - EXPERTS), (0, 0)))

    down_half = touch(second[2], (ea_send,))
    down_half_arrived = swap(down_half, "dp", 2)
    up_keep, up_send, down_keep, down_send, shared_out, shared_gx = shared_call(
        pos, hidden, branch_grad, shared_up, shared_down, (down_half, *gx_core, gg)
    )
    sh_arrived = swap_all([*up_send, *down_send], "dp", 1)

    grad_middle, grad_attended, back, mods_two, drouter = middle_backward(
        (shared_gx, gx_near, *gx_core, gx_back), gg, routes_t, router_t, hidden, cotangent, branch_one,
        patches, mod, out_weight, blocks, (),
    )
    ea_keep, ea_send = halve_z(ea_keep, ea_arrived, both, (grad_attended,))
    ea_arrived = swap(ea_send, "dp", 8)
    bu_keep, bu_send = halve_y(second[0], up_half_arrived, up, (ea_send,))
    bu_arrived = swap(bu_send, "dp", 4)
    sh_keep, sh_send = halve_slices(up_keep, down_keep, sh_arrived, (bu_send,))
    sh_arrived = swap(sh_send, "stream", 1)
    grads = attend_backward(pos, packed, attended, logsum, grad_attended, short, (sh_send,))
    out_back = touch(out_back, (grads[0],))
    bd_keep, bd_send = halve_y(second[0], down_half_arrived, down, (out_back,))
    bd_arrived = swap(bd_send, "dp", 4)
    bu_keep, bu_send = halve_z(bu_keep, bu_arrived, up, (bd_send,))
    bu_arrived = swap(bu_send, "dp", 8)
    ea_arrived = touch(ea_arrived, (bu_send,))
    qk_keep, qk_send = weight_grads(pos, patches, mod, grads, attended, back, (ea_arrived,))
    qk_arrived = swap_all(qk_send, "dp", 1)
    sh_keep, sh_send = halve(sh_keep, sh_arrived, (qk_send[0],))
    sh_arrived = swap(sh_send, "dp", 2)
    qk_keep, qk_send = halve_parts(qk_keep, qk_arrived, (sh_send,))
    qk_arrived = swap(qk_send, "stream", 1)
    mixed, gate_two = mixed_forward(
        (shared_out, out_near, out_core, out_back), cotangent, branch_one, patches, mod, blocks, (qk_send,)
    )
    grad_patches, mods_one = inputs_backward(grads, qkv_weight, patches, grad_middle, mod, blocks, (gate_two,))
    factors = [a[:blocks] for a in (act, *mods_one, *mods_two, gate_two)]
    factors = jnp.concatenate(factors + [drouter[:EXPERTS].reshape(blocks, -1)], 1).astype(BF16)

    def doubled(axis, bit, after):
        return jnp.concatenate([factors, touch(swap(factors, axis, bit), (after,))], 0)

    grad_mod = jnp.concatenate([mods_one, mods_two, gate_two[None]], 0)
    sh_keep, sh_send = halve(sh_keep, sh_arrived, (mods_one,))
    sh_arrived = swap(sh_send, "dp", 4)
    qk_keep, qk_send = halve(qk_keep, qk_arrived, (sh_send,))
    qk_arrived = swap(qk_send, "dp", 2)
    bd_keep, bd_send = halve_z(bd_keep, bd_arrived, down, (qk_send,))
    bd_arrived = swap(bd_send, "dp", 8)
    bu_arrived = touch(bu_arrived, (bd_send,))
    factors = doubled("dp", 8, bu_arrived)
    grad_embedding = used_backward(pos, grad_mod, ada_weight, emb_pad, blocks, (bu_arrived,))
    factors = doubled("dp", 4, grad_embedding)
    qk_keep, qk_send = halve(qk_keep, qk_arrived, (grad_embedding,))
    qk_arrived = swap(qk_send, "dp", 4)
    sh_keep, sh_send = halve(sh_keep, sh_arrived, (qk_send,))
    sh_arrived = swap(sh_send, "dp", 8)
    factors = doubled("dp", 2, sh_send)
    ea_done = finish_kinds(pos, ea_keep, ea_arrived, both, (sh_send,))
    qk_keep, qk_send = halve(qk_keep, qk_arrived, (ea_done[1],))
    qk_arrived = swap(qk_send, "dp", 8)
    bd_arrived = touch(bd_arrived, (qk_send,))
    bu_done = finish_kinds(pos, bu_keep, bu_arrived, up, (bd_arrived,))
    factors_x = touch(swap(factors, "stream", 1), (bu_done[1],))
    bd_done = finish_kinds(pos, bd_keep, bd_arrived, down, (factors_x,))
    bu_others = touch(swap(bu_done[1], "dp", 1), (bd_done[1],))
    ea_others = [touch(swap(a, "dp", 1), (bd_done[1],)) for a in (ea_done[1], ea_done[3])]
    bd_others = touch(swap(bd_done[1], "dp", 1), (bu_others,))
    done = finish_slices(
        pos, sh_keep, sh_arrived, qk_keep, qk_arrived, (bu_others, bd_others, *ea_others)
    )
    pieces = [factors, factors_x, swap(factors, "dp", 1), swap(factors_x, "dp", 1)]

    pieces[:2] = [touch(a, (done[0],)) for a in pieces[:2]]
    ea_others = [touch(a, (done[0],)) for a in ea_others]

    def slices_out(mine, send):
        near = in_order(core, mine, swap(send, "dp", 1), mine.ndim - 1)
        far = in_order(core, swap(mine, "stream", 1), swap_across(send), mine.ndim - 1)
        return in_order(stream, near, far, mine.ndim - 1).astype(F32)

    rows_out = slices_out(*done[:2])
    grad_qkv_out, grad_shared_up = rows_out[0], rows_out[1]
    grad_shared_down = slices_out(*done[2:])

    share = width // dp_size

    def own_share(values):
        return lax.dynamic_slice_in_dim(values, dp * share, share, 1)

    grad_ada, drouter_sum = 0.0, 0.0
    for piece in pieces:
        acts = own_share(piece[:, :width])
        grad_ada = grad_ada + lax.dot_general(
            acts, piece[:, width : 7 * width], (((0,), (0,)), ((), ())), preferred_element_type=F32
        )
        drouter_sum = drouter_sum + jnp.sum(piece[:, 7 * width :].astype(F32).reshape(-1, blocks, 2 * width), 0)
    grad_router = own_share(drouter_sum.reshape(EXPERTS, width)).T

    def experts_out(one, two, one_other, two_other):
        mine, others = jnp.stack([one, two]), jnp.stack([one_other, two_other]).astype(F32)
        return in_order(core, mine, others, 0)

    return (
        mixed, grad_patches, grad_embedding[:blocks], grad_ada, grad_qkv_out[:, : 3 * width],
        grad_qkv_out[:, 3 * width :], grad_shared_up, grad_shared_down, grad_router,
        experts_out(ea_done[0], bu_done[0], ea_others[0], bu_others),
        experts_out(ea_done[2], bd_done[0], ea_others[1], bd_others),
    )


def local(*arrays):
    experts, width, wide = arrays[11].shape
    pair = lax.axis_size("stream") == 2 and experts == 4 and lax.axis_size("dp") == 16
    if pair and wide == 4 * width:
        return local_pair(*arrays)
    return local_general(*arrays)


def solution(mesh):
    return jax.shard_map(
        local,
        mesh=mesh,
        in_specs=(
            P(("dp", "stream"), None),
            P(("dp", "stream"), None),
            P(("dp", "stream")),
            P(("dp", "stream"), None),
            P(("dp", "stream"), None),
            P(),
            P(),
            P(),
            P(),
            P(),
            P(),
            P("stream", None, None),
            P("stream", None, None),
        ),
        out_specs=(
            P(("dp", "stream"), None),
            P(("dp", "stream"), None),
            P(("dp", "stream"), None),
            P("dp", None),
            P("dp", None),
            P("dp", None),
            P("dp", None),
            P("dp", None),
            P("dp", None),
            P("stream", "dp", None),
            P("stream", "dp", None),
        ),
        check_vma=False,
    )
```
